32 devices in a mesh: dp: 8 (over z, x), seq: 4 (over y, core).
Axes of the slice: x: 2, y: 2, z: 4, core: 2. Of those that a mesh axis runs over, the one named last changes fastest.
Arguments:
- x_text: bfloat16 [8192, 768], P(('dp', 'seq')), may hold values from -6 to 6
- x_vis: bfloat16 [2304, 1024], P(('dp', 'seq')), may hold values from -6 to 6
- caption_len: int32 [64], P(('dp', 'seq')), may hold values from 8 to 128, as said below
- cot_text: bfloat16 [8192, 768], P(('dp', 'seq')), may hold values from -6 to 6
- cot_vis: bfloat16 [2304, 1024], P(('dp', 'seq'))
- master_blocks: float32 [5056, 4096], P('dp')
- stat_left: float32 [5056, 4096], P('dp')
- stat_right: float32 [5056, 4096], P('dp')
- root_left: float32 [5056, 4096], P('dp')
- root_right: float32 [5056, 4096], P('dp')
- norm_params: float32 [2, 5376], replicated
- norm_second: float32 [2, 5376], replicated
Outputs:
- out_text: bfloat16 [8192, 768], P(('dp', 'seq'))
- out_vis: bfloat16 [2304, 1024], P(('dp', 'seq'))
- grad_text: float32 [8192, 768], P(('dp', 'seq'))
- grad_vis: float32 [2304, 1024], P(('dp', 'seq'))
- grad_blocks: float32 [5056, 4096], P('dp')
- left_new: float32 [5056, 4096], P('dp')
- right_new: float32 [5056, 4096], P('dp')
- master_new: float32 [5056, 4096], P('dp')
- norm_grads: float32 [2, 5376], replicated
- norm_second_new: float32 [2, 5376], replicated
- norm_new: float32 [2, 5376], replicated
The draws below stay inside these ranges and needn't reach their ends.
Inputs may be any that keep to these rules, and one draw needn't show every extreme that they name: `caption_len`: some pair has exactly 128 live slots and some exactly 8.
All inputs are finite; a program needn't handle non-finite values.
Results may differ from the reference program's by a relative error of at most 0.02.
Values may be sent and summed in bfloat16 or wider, within the bound.
No kernel may reach another device: no remote copies, remote signals or barrier semaphores. Data moves between devices by JAX's collectives and lax.ppermute only.
A program may use at most 448 MiB of HBM per device.

```python
import jax
import jax.numpy as jnp
from jax import lax

TXT = 768
VIS = 1024
BI = 1024
FFT = 3072
FFV = 1024
HEAD = 128
HEAD_T = 64
HEAD_V = 128
REG = 36
CAP = 128
MIN_CAP = 8
BLK = 64
PD = 2
PAIRS = 64
NT = 8192
NV = 2304
NBLK = 5056
NORMW = 5376
N_SEQ = 4


COEFFS = (0.7, 0.1, 0.5, 0.4, 0.4, 0.2, 0.4, 0.15, 0.4, 0.3, 0.3, 0.15)


def weight_layout_drawn():
    return ((VIS, BI, 3), (BI, VIS, 1), (VIS, FFV, 1), (FFV, VIS, 1), (VIS, VIS, 3), (VIS, VIS, 1), (TXT, BI, 3), (BI, TXT, 1), (TXT, FFT, 1), (FFT, TXT, 1), (TXT, TXT, 3), (TXT, TXT, 1))


def kind_table(values):
    area = BLK * BLK
    counts = [count * rows * columns // area for rows, columns, count in weight_layout_drawn()]
    return jnp.concatenate([jnp.full((number,), value, jnp.float32) for number, value in zip(counts, values)])


def stat_sizes():
    rows = [PAIRS * REG] * 6 + [PAIRS * CAP] * 6
    return [BLK * coeff * coeff * number / 9.0 for coeff, number in zip(COEFFS, rows)]


def symmetric_noise(key):
    noise = jnp.clip(jax.random.normal(key, (NBLK, BLK, BLK), jnp.float32), -4.0, 4.0)
    return (noise + jnp.swapaxes(noise, 1, 2)) * 0.7071


def shaped_matrix(key, salt, scales, low_end, high_end):
    first, second = jax.random.split(jax.random.fold_in(key, salt))
    scale = kind_table(scales)[:, None, None]
    diagonal = jax.random.uniform(first, (NBLK, BLK), jnp.float32, low_end, high_end)
    identity = jnp.eye(BLK, dtype=jnp.float32)
    cube = scale * (identity * diagonal[:, :, None] + 0.06 * (1.0 - identity) * symmetric_noise(second))
    return cube.reshape(NBLK, BLK * BLK)


def draw_stat_left(key, part):
    return shaped_matrix(key, 11, stat_sizes(), 1.0, 4.0)


def draw_stat_right(key, part):
    return shaped_matrix(key, 12, stat_sizes(), 1.0, 4.0)


def draw_root_left(key, part):
    return shaped_matrix(key, 13, [(2.5 * stat) ** (-0.25) for stat in stat_sizes()], 0.5, 2.0)


def draw_root_right(key, part):
    return shaped_matrix(key, 14, [(2.5 * stat) ** (-0.25) for stat in stat_sizes()], 0.5, 2.0)


def draw_master_blocks(key, part):
    fans = [VIS, 2 * BI // (MIN_CAP + CAP), VIS, FFV, VIS, VIS // REG, TXT, BI // REG, TXT, FFT, TXT, 2 * TXT // (MIN_CAP + CAP)]
    scale = kind_table([fan ** (-0.5) for fan in fans])[:, None]
    base = jnp.clip(jax.random.normal(key, (NBLK, BLK * BLK), jnp.float32), -4.0, 4.0)
    return scale * base


def draw_cot_vis(key, part):
    inner = jax.random.fold_in(key, 21)
    base = jnp.clip(jax.random.normal(inner, (NV, VIS), jnp.float32), -6.0, 6.0)
    return base.astype(jnp.bfloat16)


def draw_caption_len(key, part):
    first, second, third = jax.random.split(key, 3)
    values = jax.random.randint(first, (PAIRS,), MIN_CAP, CAP + 1)
    longest = jax.random.randint(second, (), 0, PAIRS)
    shortest = (longest + 1 + jax.random.randint(third, (), 0, PAIRS - 1)) % PAIRS
    return values.at[longest].set(CAP).at[shortest].set(MIN_CAP).astype(jnp.int32)


def draw_norm_params(key, part):
    first, second = jax.random.split(jax.random.fold_in(key, 31))
    gains = 1.0 + 0.2 * jnp.clip(jax.random.normal(first, (NORMW,), jnp.float32), -3.0, 3.0)
    biases = 0.3 * jnp.clip(jax.random.normal(second, (NORMW,), jnp.float32), -3.0, 3.0)
    return jnp.stack([gains, biases])


def draw_norm_second(key, part):
    counts = jnp.concatenate([jnp.full((3 * VIS,), PAIRS * REG, jnp.float32), jnp.full((3 * TXT,), PAIRS * CAP, jnp.float32)])
    factor = jax.random.uniform(jax.random.fold_in(key, 41), (2, NORMW), jnp.float32, 1.0, 4.0)
    return factor * counts / 9.0


def block_levels(own_key, extent, shards, low, high):
    level, own = 1.0, jax.random.fold_in(own_key, 6)
    for position, shards_of in shards:
        heights = jnp.exp(jax.random.uniform(jax.random.fold_in(own, position), (shards_of,), jnp.float32, low / len(shards), high / len(shards)))
        level = level * jnp.repeat(heights, extent[position] // shards_of).reshape([-1 if axis == position else 1 for axis in range(len(extent))])
    return level


def bell_draw(key, shape, scale, limit, shards=(), held_as=jnp.bfloat16):
    entries = jax.random.normal(key, shape, jnp.float32) * scale
    if len(shards) > 0:
        entries = block_levels(key, shape, shards, -0.22, 0.18) * entries
    return jnp.clip(entries, min=-limit, max=limit).astype(held_as)


def setup_inputs(seed: int = 0) -> dict:
    key_list = jax.random.split(jax.random.key(seed), 13)
    return {
        "x_text": bell_draw(key_list[0], (NT, TXT), 1.0, 6.0, ((0, 32),)),
        "x_vis": bell_draw(key_list[1], (NV, VIS), 1.0, 6.0, ((0, 32),)),
        "caption_len": draw_caption_len(jax.random.fold_in(key_list[12], 71), 0),
        "cot_text": bell_draw(key_list[3], (NT, TXT), 1.0, 6.0, ((0, 32),)),
        "cot_vis": draw_cot_vis(jax.random.fold_in(key_list[12], 71), 0),
        "master_blocks": draw_master_blocks(jax.random.fold_in(key_list[12], 71), 0),
        "stat_left": draw_stat_left(jax.random.fold_in(key_list[12], 71), 0),
        "stat_right": draw_stat_right(jax.random.fold_in(key_list[12], 71), 0),
        "root_left": draw_root_left(jax.random.fold_in(key_list[12], 71), 0),
        "root_right": draw_root_right(jax.random.fold_in(key_list[12], 71), 0),
        "norm_params": draw_norm_params(jax.random.fold_in(key_list[12], 71), 0),
        "norm_second": draw_norm_second(jax.random.fold_in(key_list[12], 71), 0),
    }


@jax.custom_vjp
def low(v):
    return lax.optimization_barrier(v.astype(jnp.bfloat16)).astype(jnp.float32)

@jax.custom_vjp
def low_back(v):
    return v

def low_keep(v):
    return (low(v), None)

def low_pass(kept, grad):
    return (grad,)

def back_keep(v):
    return (v, None)

def back_low(kept, grad):
    return (low(grad),)
low.defvjp(low_keep, low_pass)
low_back.defvjp(back_keep, back_low)
MASK_FILL = -1000000000.0
STAT_DECAY = 0.9
WEIGHT_RATE = 0.3
NORM_RATE = 0.2
NORM_EPSILON = 1e-05
MOMENT_EPSILON = 1e-08
HIGHEST = lax.Precision.HIGHEST

def product(left, right):
    return jnp.dot(left, right, precision=HIGHEST, preferred_element_type=jnp.float32)

def weight_layout():
    return ((VIS, BI, 3), (BI, VIS, 1), (VIS, FFV, 1), (FFV, VIS, 1), (VIS, VIS, 3), (VIS, VIS, 1), (TXT, BI, 3), (BI, TXT, 1), (TXT, FFT, 1), (FFT, TXT, 1), (TXT, TXT, 3), (TXT, TXT, 1))

def unpack_weights(flat):
    size = BLK
    blocks = flat.reshape(flat.shape[0], size, size)
    begin = 0
    matrices = []
    for rows, columns, count in weight_layout():
        number = count * rows * columns // (size * size)
        shaped = blocks[begin:begin + number].reshape(count, rows // size, columns // size, size, size)
        matrices.append(shaped.transpose(1, 3, 0, 2, 4).reshape(rows, count * columns))
        begin += number
    return matrices

def group_to_blocks(matrix, count):
    size = BLK
    rows, total = matrix.shape
    columns = total // count
    shaped = matrix.reshape(rows // size, size, count, columns // size, size)
    return shaped.transpose(2, 0, 3, 1, 4).reshape(-1, size, size)

def norm_columns(values, stream, which):
    if stream == 0:
        begin = which * VIS
        width = VIS
    else:
        begin = 3 * VIS + which * TXT
        width = TXT
    return values[:, begin:begin + width]

def layer_norm(resid, columns):
    mean = lax.optimization_barrier(jnp.mean(resid, -1, keepdims=True))
    centered = resid - mean
    variance = lax.optimization_barrier(jnp.mean(centered * centered, -1, keepdims=True))
    return centered * lax.rsqrt(variance + NORM_EPSILON) * columns[0] + columns[1]

def ref_heads(side, which, head):
    part = side[:, :, which]
    return part.reshape(part.shape[0], part.shape[1], -1, head)

def ref_attend(query, keys, values, live, head):
    scores = low_back(jnp.einsum('gqhd,gkhd->ghqk', query, keys, precision=HIGHEST) * head ** (-0.5))
    if live is not None:
        scores = jnp.where(live[:, None, None, :], scores, MASK_FILL)
    weights = low(jax.nn.softmax(scores, axis=3))
    found = low_back(low(jnp.einsum('ghqk,gkhd->gqhd', weights, values, precision=HIGHEST)))
    return found.reshape(found.shape[0], found.shape[1], -1)

def ref_pair(vis_side, text_side, live, cross):
    if cross:
        vis_found = ref_attend(ref_heads(vis_side, 0, HEAD), ref_heads(text_side, 1, HEAD), ref_heads(text_side, 2, HEAD), live, HEAD)
        text_found = ref_attend(ref_heads(text_side, 0, HEAD), ref_heads(vis_side, 1, HEAD), ref_heads(vis_side, 2, HEAD), None, HEAD)
    else:
        vis_found = ref_attend(ref_heads(vis_side, 0, HEAD_V), ref_heads(vis_side, 1, HEAD_V), ref_heads(vis_side, 2, HEAD_V), None, HEAD_V)
        text_found = ref_attend(ref_heads(text_side, 0, HEAD_T), ref_heads(text_side, 1, HEAD_T), ref_heads(text_side, 2, HEAD_T), live, HEAD_T)
    return (vis_found, text_found)

def ref_side(rows_in, weight, pairs):
    made = low_back(low(product(low(rows_in), low(weight))))
    return made.reshape(pairs, -1, 3, weight.shape[1] // 3)

def ref_feed(first, up_weight, down_weight, columns):
    pre = low_back(product(low(first), low(up_weight)))
    act = low(jax.nn.gelu(pre, approximate=False))
    return layer_norm(first + low_back(product(act, low(down_weight))), columns)

def group_forward(params, text_rows, vis_rows, lengths):
    co_vis, out_co_vis, up_vis, down_vis, self_vis, out_self_vis, co_text, out_co_text, up_text, down_text, self_text, out_self_text, norm_values = params
    pairs = lengths.shape[0]
    live = lax.broadcasted_iota(jnp.int32, (pairs, CAP), 1) < lengths[:, None]
    vis_found, text_found = ref_pair(ref_side(vis_rows, co_vis, pairs), ref_side(text_rows, co_text, pairs), live, True)
    vis_first = layer_norm(vis_rows + low_back(product(vis_found.reshape(-1, BI), low(out_co_vis))), norm_columns(norm_values, 0, 0))
    text_first = layer_norm(text_rows + low_back(product(text_found.reshape(-1, BI), low(out_co_text))), norm_columns(norm_values, 1, 0))
    vis_second = ref_feed(vis_first, up_vis, down_vis, norm_columns(norm_values, 0, 1))
    text_second = ref_feed(text_first, up_text, down_text, norm_columns(norm_values, 1, 1))
    vis_found, text_found = ref_pair(ref_side(vis_second, self_vis, pairs), ref_side(text_second, self_text, pairs), live, False)
    vis_out = layer_norm(vis_second + low_back(product(vis_found.reshape(-1, VIS), low(out_self_vis))), norm_columns(norm_values, 0, 2))
    text_out = layer_norm(text_second + low_back(product(text_found.reshape(-1, TXT), low(out_self_text))), norm_columns(norm_values, 1, 2))
    return (text_out, vis_out)

def reference(x_text, x_vis, caption_len, cot_text, cot_vis, master_blocks, stat_left, stat_right, root_left, root_right, norm_params, norm_second):
    vis_width = x_vis.shape[1]
    text_width = x_text.shape[1]
    params = tuple(unpack_weights(master_blocks)) + (norm_params,)
    group = PD * N_SEQ
    count = PAIRS // group
    data = (x_text.reshape(count, group * CAP, text_width), x_vis.reshape(count, group * REG, vis_width), caption_len.reshape(count, group), cot_text.reshape(count, group * CAP, text_width), cot_vis.reshape(count, group * REG, vis_width))

    def step(total, item):
        text_rows, vis_rows, lengths, cot_t, cot_v = item

        def forward(weights_in, text_in, vis_in):
            return group_forward(weights_in, text_in, vis_in, lengths)
        outputs, pull = jax.vjp(forward, params, text_rows.astype(jnp.float32), vis_rows.astype(jnp.float32))
        grads, grad_t, grad_v = pull((cot_t.astype(jnp.float32), cot_v.astype(jnp.float32)))
        total = jax.tree.map(jnp.add, total, grads)
        return (total, (outputs[0].astype(jnp.bfloat16), outputs[1].astype(jnp.bfloat16), grad_t, grad_v))
    zeros = jax.tree.map(jnp.zeros_like, params)
    total, (out_t, out_v, grad_t, grad_v) = lax.scan(step, zeros, data)
    layout = weight_layout()
    grad_cube = jnp.concatenate([group_to_blocks(total[index], layout[index][2]) for index in range(12)], 0)
    number = grad_cube.shape[0]
    left_cube = stat_left.reshape(number, BLK, BLK)
    right_cube = stat_right.reshape(number, BLK, BLK)
    rootl_cube = root_left.reshape(number, BLK, BLK)
    rootr_cube = root_right.reshape(number, BLK, BLK)
    left_new = STAT_DECAY * left_cube + (1.0 - STAT_DECAY) * jnp.einsum('bij,bkj->bik', grad_cube, grad_cube, precision=HIGHEST)
    right_new = STAT_DECAY * right_cube + (1.0 - STAT_DECAY) * jnp.einsum('bji,bjk->bik', grad_cube, grad_cube, precision=HIGHEST)
    half = jnp.einsum('bij,bjk->bik', rootl_cube, grad_cube, precision=HIGHEST)
    direction = jnp.einsum('bij,bjk->bik', half, rootr_cube, precision=HIGHEST)
    master_new = master_blocks - WEIGHT_RATE * direction.reshape(number, BLK * BLK)
    norm_grads = total[12]
    second_new = STAT_DECAY * norm_second + (1.0 - STAT_DECAY) * norm_grads * norm_grads
    norm_new = norm_params - NORM_RATE * norm_grads / (jnp.sqrt(second_new) + MOMENT_EPSILON)
    return (out_t.reshape(PAIRS * CAP, text_width), out_v.reshape(PAIRS * REG, vis_width), grad_t.reshape(PAIRS * CAP, text_width), grad_v.reshape(PAIRS * REG, vis_width), grad_cube.reshape(number, BLK * BLK), left_new.reshape(number, BLK * BLK), right_new.reshape(number, BLK * BLK), master_new, norm_grads, second_new, norm_new)
```

```python
import functools

import jax
import jax.numpy as jnp
from jax import lax
from jax.experimental import pallas as pl
from jax.experimental.pallas import tpu as pltpu
from jax.sharding import PartitionSpec as P

TXT = 768
VIS = 1024
BI = 1024
FFT = 3072
FFV = 1024
HEAD = 128
HEAD_T = 64
HEAD_V = 128
BLK = 64


MASK_FILL = -1000000000.0
STAT_DECAY = 0.9
WEIGHT_RATE = 0.3
NORM_RATE = 0.2
NORM_EPSILON = 1e-05
MOMENT_EPSILON = 1e-08
HIGHEST = lax.Precision.HIGHEST
CONTRACT_COLS = (((1,), (1,)), ((), ()))


def weight_layout():
    return (
        (VIS, BI, 3),
        (BI, VIS, 1),
        (VIS, FFV, 1),
        (FFV, VIS, 1),
        (VIS, VIS, 3),
        (VIS, VIS, 1),
        (TXT, BI, 3),
        (BI, TXT, 1),
        (TXT, FFT, 1),
        (FFT, TXT, 1),
        (TXT, TXT, 3),
        (TXT, TXT, 1),
    )


def unpack_weights(flat):
    size = BLK
    blocks = flat.reshape(flat.shape[0], size, size)
    begin = 0
    matrices = []
    for rows, columns, count in weight_layout():
        number = count * rows * columns // (size * size)
        shaped = blocks[begin : begin + number].reshape(
            count, rows // size, columns // size, size, size
        )
        matrices.append(shaped.transpose(1, 3, 0, 2, 4).reshape(rows, count * columns))
        begin += number
    return matrices


def block_grad(inputs, grads, count):
    size = BLK
    left = inputs.reshape(inputs.shape[0], inputs.shape[1] // size, size)
    right = grads.reshape(grads.shape[0], count, grads.shape[1] // (count * size), size)
    return jnp.einsum("nai,nkbj->kabij", left, right, preferred_element_type=jnp.float32).reshape(
        -1, size * size
    )


def norm_columns(values, stream, which):
    if stream == 0:
        begin = which * VIS
        width = VIS
    else:
        begin = 3 * VIS + which * TXT
        width = TXT
    return values[:, begin : begin + width]


def gelu_exact(value):
    return jax.nn.gelu(value, approximate=False)


def heads_of(side, which, head):
    part = side[:, :, which, :]
    return part.reshape(part.shape[0], part.shape[1], part.shape[2] // head, head)


def scores_of(query, keys, live, head):
    scores = jnp.einsum(
        "gqhd,gkhd->ghqk", query, keys, preferred_element_type=jnp.float32
    ) * head ** (-0.5)
    if live is not None:
        scores = jnp.where(live[:, None, None, :], scores, MASK_FILL)
    return scores


def attend_one(query, keys, values, live, head):
    scores = scores_of(query, keys, live, head)
    top = jnp.max(scores, axis=3, keepdims=True)
    raised = jnp.exp(scores - top)
    total = jnp.sum(raised, axis=3, keepdims=True)
    found = jnp.einsum(
        "ghqk,gkhd->gqhd",
        (raised / total).astype(jnp.bfloat16),
        values,
        preferred_element_type=jnp.float32,
    ).astype(jnp.bfloat16)
    return (found.reshape(found.shape[0], found.shape[1], -1), top + jnp.log(total))


def attend_one_back(query, keys, values, live, head, logsum, dfound):
    scale = head ** (-0.5)
    probs = jnp.exp(scores_of(query, keys, live, head) - logsum)
    upstream = dfound.reshape(dfound.shape[0], dfound.shape[1], -1, head)
    dprobs = jnp.einsum("gqhd,gkhd->ghqk", upstream, values, preferred_element_type=jnp.float32)
    dvalues = jnp.einsum(
        "ghqk,gqhd->gkhd", probs.astype(jnp.bfloat16), upstream, preferred_element_type=jnp.float32
    )
    dscores = (probs * (dprobs - jnp.sum(probs * dprobs, axis=3, keepdims=True))).astype(
        jnp.bfloat16
    )
    dquery = (
        jnp.einsum("ghqk,gkhd->gqhd", dscores, keys, preferred_element_type=jnp.float32) * scale
    )
    dkeys = (
        jnp.einsum("ghqk,gqhd->gkhd", dscores, query, preferred_element_type=jnp.float32) * scale
    )
    return (dquery, dkeys, dvalues)


def attention_plan(vis_side, text_side, lengths, cross):
    live = (
        lax.broadcasted_iota(jnp.int32, (lengths.shape[0], text_side.shape[1]), 1)
        < lengths[:, None]
    )
    if cross:
        return ((vis_side, text_side, live, HEAD), (text_side, vis_side, None, HEAD))
    return ((vis_side, vis_side, None, HEAD_V), (text_side, text_side, live, HEAD_T))


def pair_attend(vis_side, text_side, lengths, cross):
    results = []
    for query_side, key_side, live, head in attention_plan(vis_side, text_side, lengths, cross):
        results.append(
            attend_one(
                heads_of(query_side, 0, head),
                heads_of(key_side, 1, head),
                heads_of(key_side, 2, head),
                live,
                head,
            )
        )
    return (results[0][0], results[1][0], results[0][1], results[1][1])


def pair_attend_back(
    vis_side, text_side, lengths, cross, vis_logsum, text_logsum, vis_dfound, text_dfound
):
    plan = attention_plan(vis_side, text_side, lengths, cross)
    parts = []
    for (query_side, key_side, live, head), logsum, dfound in zip(
        plan, (vis_logsum, text_logsum), (vis_dfound, text_dfound)
    ):
        parts.append(
            attend_one_back(
                heads_of(query_side, 0, head),
                heads_of(key_side, 1, head),
                heads_of(key_side, 2, head),
                live,
                head,
                logsum,
                dfound,
            )
        )
    if cross:
        vis_parts = (parts[0][0], parts[1][1], parts[1][2])
        text_parts = (parts[1][0], parts[0][1], parts[0][2])
    else:
        vis_parts = parts[0]
        text_parts = parts[1]
    vis_grad = jnp.stack(vis_parts, axis=2).reshape(vis_side.shape).astype(jnp.bfloat16)
    text_grad = jnp.stack(text_parts, axis=2).reshape(text_side.shape).astype(jnp.bfloat16)
    return (vis_grad, text_grad)


def to_heads(vis_side, text_side):
    return (vis_side, text_side)


def from_heads(vis_found, text_found):
    return (vis_found, text_found)


def dfound_to_heads(vis_dfound, text_dfound):
    return (vis_dfound, text_dfound)


def grads_from_heads(vis_grad, text_grad):
    return (vis_grad, text_grad)


def side_of(rows_in, weight, pairs):
    made = jnp.dot(rows_in, weight, preferred_element_type=jnp.float32).astype(jnp.bfloat16)
    return made.reshape(pairs, -1, 3, weight.shape[1] // 3)


def norm_forward(resid, columns):
    mean = jnp.mean(resid, -1, keepdims=True)
    centered = resid - mean
    scale = lax.rsqrt(jnp.mean(centered * centered, -1, keepdims=True) + NORM_EPSILON)
    normed = centered * scale
    return (normed, scale, normed * columns[0] + columns[1])


def norm_backward(upstream, normed, scale, gain):
    scaled = upstream * gain
    resid_grad = scale * (
        scaled
        - jnp.mean(scaled, -1, keepdims=True)
        - normed * jnp.mean(scaled * normed, -1, keepdims=True)
    )
    return (resid_grad, jnp.sum(upstream * normed, 0), jnp.sum(upstream, 0))


def stream_middle(context_rows, x_rows, weights, values, stream, pairs):
    resid = x_rows.astype(jnp.float32) + jnp.dot(
        context_rows, weights[1], preferred_element_type=jnp.float32
    )
    normed_one, scale_one, first = norm_forward(resid, norm_columns(values, stream, 0))
    first_low = first.astype(jnp.bfloat16)
    pre = jnp.dot(first_low, weights[2], preferred_element_type=jnp.float32)
    act = gelu_exact(pre).astype(jnp.bfloat16)
    resid = first + jnp.dot(act, weights[3], preferred_element_type=jnp.float32)
    normed_two, scale_two, second = norm_forward(resid, norm_columns(values, stream, 1))
    second_low = second.astype(jnp.bfloat16)
    side = side_of(second_low, weights[4], pairs)
    return (
        side,
        (normed_one, scale_one, first_low, pre, act, normed_two, scale_two, second, second_low),
    )


def stream_end(self_rows, second, out_weight, values, stream):
    resid = second + jnp.dot(self_rows, out_weight, preferred_element_type=jnp.float32)
    normed_three, scale_three, third = norm_forward(resid, norm_columns(values, stream, 2))
    return (third.astype(jnp.bfloat16), normed_three, scale_three)


def stream_back_end(
    cotangent, normed_three, scale_three, self_rows, out_weight, values, stream, pairs
):
    resid_three, gain_three, bias_three = norm_backward(
        cotangent.astype(jnp.float32), normed_three, scale_three, norm_columns(values, stream, 2)[0]
    )
    third_back = resid_three.astype(jnp.bfloat16)
    grad_self_out = block_grad(self_rows, third_back, 1)
    dself = lax.dot_general(
        third_back, out_weight, CONTRACT_COLS, preferred_element_type=jnp.float32
    )
    dself = dself.astype(jnp.bfloat16).reshape(pairs, -1, out_weight.shape[0])
    return (resid_three, dself, grad_self_out, gain_three, bias_three)


def stream_back_middle(resid_three, dself_side, kept, context_rows, weights, values, stream, pairs):
    normed_one, scale_one, first_low, pre, act, normed_two, scale_two, second, second_low = kept
    dself_rows = dself_side.reshape(-1, dself_side.shape[2] * dself_side.shape[3])
    grad_self_qkv = block_grad(second_low, dself_rows, 3)
    second_in = resid_three + lax.dot_general(
        dself_rows, weights[4], CONTRACT_COLS, preferred_element_type=jnp.float32
    )
    resid_two, gain_two, bias_two = norm_backward(
        second_in, normed_two, scale_two, norm_columns(values, stream, 1)[0]
    )
    branch_back = resid_two.astype(jnp.bfloat16)
    grad_down = block_grad(act, branch_back, 1)
    act_grad = lax.dot_general(
        branch_back, weights[3], CONTRACT_COLS, preferred_element_type=jnp.float32
    )
    pre_grad = jax.vjp(gelu_exact, pre)[1](act_grad)[0].astype(jnp.bfloat16)
    grad_up = block_grad(first_low, pre_grad, 1)
    first_in = resid_two + lax.dot_general(
        pre_grad, weights[2], CONTRACT_COLS, preferred_element_type=jnp.float32
    )
    resid_one, gain_one, bias_one = norm_backward(
        first_in, normed_one, scale_one, norm_columns(values, stream, 0)[0]
    )
    first_back = resid_one.astype(jnp.bfloat16)
    grad_co_out = block_grad(context_rows, first_back, 1)
    dcontext = lax.dot_general(
        first_back, weights[1], CONTRACT_COLS, preferred_element_type=jnp.float32
    )
    dcontext = dcontext.astype(jnp.bfloat16).reshape(pairs, -1, BI)
    return (
        resid_one,
        dcontext,
        (grad_co_out, grad_up, grad_down, grad_self_qkv),
        (gain_one, gain_two),
        (bias_one, bias_two),
    )


def shards(
    x_text,
    x_vis,
    caption_len,
    cot_text,
    cot_vis,
    master_blocks,
    stat_left,
    stat_right,
    root_left,
    root_right,
    norm_params,
    norm_second,
):
    pairs = caption_len.shape[0]
    width = master_blocks.shape[1] // lax.axis_size("seq")
    mine = lax.dynamic_slice_in_dim(master_blocks, lax.axis_index("seq") * width, width, 1).astype(
        jnp.bfloat16
    )
    partial_value = lax.all_gather(mine, "dp", axis=0, tiled=True)
    every = lax.all_gather(partial_value, "seq", axis=1, tiled=True)
    matrices = unpack_weights(every)
    vis_weights = matrices[:6]
    text_weights = matrices[6:]
    vis_co = side_of(x_vis, vis_weights[0], pairs)
    text_co = side_of(x_text, text_weights[0], pairs)
    lengths = caption_len
    vis_co_use, text_co_use = to_heads(vis_co, text_co)
    vis_found, text_found, vis_co_sum, text_co_sum = pair_attend(
        vis_co_use, text_co_use, lengths, True
    )
    vis_context, text_context = from_heads(vis_found, text_found)
    vis_context_rows = vis_context.reshape(-1, BI)
    text_context_rows = text_context.reshape(-1, BI)
    vis_self, vis_kept = stream_middle(vis_context_rows, x_vis, vis_weights, norm_params, 0, pairs)
    text_self, text_kept = stream_middle(
        text_context_rows, x_text, text_weights, norm_params, 1, pairs
    )
    vis_self_use, text_self_use = to_heads(vis_self, text_self)
    vis_found, text_found, vis_self_sum, text_self_sum = pair_attend(
        vis_self_use, text_self_use, lengths, False
    )
    vis_self_context, text_self_context = from_heads(vis_found, text_found)
    vis_self_rows = vis_self_context.reshape(-1, VIS)
    text_self_rows = text_self_context.reshape(-1, TXT)
    out_vis, vis_normed_three, vis_scale_three = stream_end(
        vis_self_rows, vis_kept[7], vis_weights[5], norm_params, 0
    )
    out_text, text_normed_three, text_scale_three = stream_end(
        text_self_rows, text_kept[7], text_weights[5], norm_params, 1
    )
    vis_resid_three, vis_dself, vis_grad_so, vis_gain_three, vis_bias_three = stream_back_end(
        cot_vis,
        vis_normed_three,
        vis_scale_three,
        vis_self_rows,
        vis_weights[5],
        norm_params,
        0,
        pairs,
    )
    text_resid_three, text_dself, text_grad_so, text_gain_three, text_bias_three = stream_back_end(
        cot_text,
        text_normed_three,
        text_scale_three,
        text_self_rows,
        text_weights[5],
        norm_params,
        1,
        pairs,
    )
    vis_dheads, text_dheads = dfound_to_heads(vis_dself, text_dself)
    vis_dgot, text_dgot = pair_attend_back(
        vis_self_use,
        text_self_use,
        lengths,
        False,
        vis_self_sum,
        text_self_sum,
        vis_dheads,
        text_dheads,
    )
    vis_dself_side, text_dself_side = grads_from_heads(vis_dgot, text_dgot)
    vis_resid_one, vis_dcontext, vis_grads_mid, vis_gains_mid, vis_biases_mid = stream_back_middle(
        vis_resid_three,
        vis_dself_side,
        vis_kept,
        vis_context_rows,
        vis_weights,
        norm_params,
        0,
        pairs,
    )
    text_resid_one, text_dcontext, text_grads_mid, text_gains_mid, text_biases_mid = (
        stream_back_middle(
            text_resid_three,
            text_dself_side,
            text_kept,
            text_context_rows,
            text_weights,
            norm_params,
            1,
            pairs,
        )
    )
    vis_dheads, text_dheads = dfound_to_heads(vis_dcontext, text_dcontext)
    vis_dgot, text_dgot = pair_attend_back(
        vis_co_use, text_co_use, lengths, True, vis_co_sum, text_co_sum, vis_dheads, text_dheads
    )
    vis_dco, text_dco = grads_from_heads(vis_dgot, text_dgot)
    vis_dco_rows = vis_dco.reshape(-1, 3 * BI)
    text_dco_rows = text_dco.reshape(-1, 3 * BI)
    grad_vis = vis_resid_one + lax.dot_general(
        vis_dco_rows, vis_weights[0], CONTRACT_COLS, preferred_element_type=jnp.float32
    )
    grad_text = text_resid_one + lax.dot_general(
        text_dco_rows, text_weights[0], CONTRACT_COLS, preferred_element_type=jnp.float32
    )
    vis_grad_co = block_grad(x_vis, vis_dco_rows, 3)
    text_grad_co = block_grad(x_text, text_dco_rows, 3)
    local_blocks = jnp.concatenate(
        [vis_grad_co]
        + list(vis_grads_mid)
        + [vis_grad_so]
        + [text_grad_co]
        + list(text_grads_mid)
        + [text_grad_so],
        0,
    )
    norm_local = jnp.stack(
        [
            jnp.concatenate(
                [
                    vis_gains_mid[0],
                    vis_gains_mid[1],
                    vis_gain_three,
                    text_gains_mid[0],
                    text_gains_mid[1],
                    text_gain_three,
                ]
            ),
            jnp.concatenate(
                [
                    vis_biases_mid[0],
                    vis_biases_mid[1],
                    vis_bias_three,
                    text_biases_mid[0],
                    text_biases_mid[1],
                    text_bias_three,
                ]
            ),
        ]
    )
    columns = lax.psum_scatter(
        local_blocks.astype(jnp.bfloat16), "seq", scatter_dimension=1, tiled=True
    ).astype(jnp.float32)
    owned_columns = lax.psum_scatter(columns, "dp", scatter_dimension=0, tiled=True)
    owned = lax.all_gather(owned_columns.astype(jnp.bfloat16), "seq", axis=1, tiled=True).astype(
        owned_columns.dtype
    )
    norm_grads = lax.psum(norm_local, ("dp", "seq"))
    number = owned.shape[0]
    grad_cube = owned.reshape(number, BLK, BLK)
    left_cube = stat_left.reshape(number, BLK, BLK)
    right_cube = stat_right.reshape(number, BLK, BLK)
    rootl_cube = root_left.reshape(number, BLK, BLK)
    rootr_cube = root_right.reshape(number, BLK, BLK)
    left_new = STAT_DECAY * left_cube + (1.0 - STAT_DECAY) * jnp.einsum(
        "bij,bkj->bik", grad_cube, grad_cube, precision=HIGHEST
    )
    right_new = STAT_DECAY * right_cube + (1.0 - STAT_DECAY) * jnp.einsum(
        "bji,bjk->bik", grad_cube, grad_cube, precision=HIGHEST
    )
    half = jnp.einsum("bij,bjk->bik", rootl_cube, grad_cube, precision=HIGHEST)
    direction = jnp.einsum("bij,bjk->bik", half, rootr_cube, precision=HIGHEST)
    master_new = master_blocks - WEIGHT_RATE * direction.reshape(number, BLK * BLK)
    second_new = STAT_DECAY * norm_second + (1.0 - STAT_DECAY) * norm_grads * norm_grads
    norm_new = norm_params - NORM_RATE * norm_grads / (jnp.sqrt(second_new) + MOMENT_EPSILON)
    return (
        out_text,
        out_vis,
        grad_text,
        grad_vis,
        owned,
        left_new.reshape(number, BLK * BLK),
        right_new.reshape(number, BLK * BLK),
        master_new,
        norm_grads,
        second_new,
        norm_new,
    )


SUB = 64
WIDE = 256
QUAD = 4
F32 = jnp.float32
BF16 = jnp.bfloat16
VIS_PAD = 48
VMEM_LIMIT = 60 * 1024 * 1024
NT = (((1,), (1,)), ((), ()))
TN = (((0,), (0,)), ((), ()))


def tile_table():
    begin = 0
    table = []
    for rows, columns, count in weight_layout():
        r, g = rows // SUB, columns // WIDE
        table.append((begin, count, r, g))
        begin += count * r * g
    return table


TILES = tile_table()


def dot(left, right, how=None):
    if how is None:
        return jnp.dot(left, right, preferred_element_type=F32)
    return lax.dot_general(left, right, how, preferred_element_type=F32)


def params(**more):
    return pltpu.CompilerParams(vmem_limit_bytes=VMEM_LIMIT, **more)


def whole(count):
    return [pl.BlockSpec(memory_space=pltpu.VMEM)] * count


def lanes_low(rows):
    return lax.broadcasted_iota(jnp.int32, (rows, 2 * SUB), 1) < SUB


def spread_rows(x_ref, scratch):
    for c in range(32):
        scratch[c * 8 : (c + 1) * 8, :] = x_ref[:, c * 128 : (c + 1) * 128]


def pair_natural(scratch, b, place):
    low = lanes_low(32)
    one = scratch[pl.ds(b, 32, stride=8), :]
    two = scratch[pl.ds(b + 1, 32, stride=8), :]
    place[pl.ds(0, 32, stride=2), :] = jnp.where(low, one, pltpu.roll(two, SUB, 1))
    place[pl.ds(1, 32, stride=2), :] = jnp.where(low, pltpu.roll(one, SUB, 1), two)
    return place[...]


def pair_spread(value, place, scratch, b):
    low = lanes_low(32)
    place[...] = value
    even = place[pl.ds(0, 32, stride=2), :]
    odd = place[pl.ds(1, 32, stride=2), :]
    scratch[pl.ds(b, 32, stride=8), :] = jnp.where(low, even, pltpu.roll(odd, SUB, 1))
    scratch[pl.ds(b + 1, 32, stride=8), :] = jnp.where(low, pltpu.roll(even, SUB, 1), odd)


def prep_body(x_ref, o_ref, spread, place):
    spread_rows(x_ref, spread)
    for k in range(2):
        for m in range(2):
            o_ref[k, :, m * 128 : (m + 1) * 128] = pair_natural(
                spread, 4 * k + 2 * m, place.at[2 * k + m]
            ).astype(BF16)


def prep(master_blocks):
    number = master_blocks.shape[0]
    return pl.pallas_call(
        prep_body,
        grid=(number // 8,),
        in_specs=[pl.BlockSpec((8, SUB * SUB), lambda i: (i, 0))],
        out_specs=pl.BlockSpec((2, SUB, WIDE), lambda i: (i, 0, 0)),
        out_shape=jax.ShapeDtypeStruct((number // 4, SUB, WIDE), BF16),
        scratch_shapes=[pltpu.VMEM((256, 128), F32), pltpu.VMEM((4, SUB, 128), F32)],
        compiler_params=params(),
    )(master_blocks)


def block_diagonal(pair):
    low = lanes_low(SUB)
    zero = jnp.zeros_like(pair)
    return jnp.concatenate([jnp.where(low, pair, zero), jnp.where(low, zero, pair)], 0)


def fold(square):
    return square[:SUB] + square[SUB:]


def renew_body(
    g_ref, m_ref, sl_ref, sr_ref, rl_ref, rr_ref,
    go_ref, lo_ref, ro_ref, mo_ref,
    root_l, root_r, out_g, out_l, out_r, out_m, place,
):
    spread_rows(rl_ref, root_l)
    spread_rows(rr_ref, root_r)
    for pair in range(4):
        spots = place.at[pair]
        wide = g_ref[pair // 2, :, (pair % 2) * 128 : (pair % 2 + 1) * 128].astype(F32)
        grad = block_diagonal(wide).astype(BF16)
        left = block_diagonal(pair_natural(root_l, 2 * pair, spots.at[0])).astype(BF16)
        right = block_diagonal(pair_natural(root_r, 2 * pair, spots.at[1])).astype(BF16)
        half = dot(left, grad).astype(BF16)
        pair_spread(wide, spots.at[2], out_g, 2 * pair)
        pair_spread(fold(dot(grad, grad, NT)), spots.at[3], out_l, 2 * pair)
        pair_spread(fold(dot(grad, grad, TN)), spots.at[4], out_r, 2 * pair)
        pair_spread(fold(dot(half, right)), spots.at[5], out_m, 2 * pair)
    for c in range(32):
        lanes = slice(c * 128, (c + 1) * 128)
        rows = slice(c * 8, (c + 1) * 8)
        go_ref[:, lanes] = out_g[rows, :]
        lo_ref[:, lanes] = STAT_DECAY * sl_ref[:, lanes] + (1.0 - STAT_DECAY) * out_l[rows, :]
        ro_ref[:, lanes] = STAT_DECAY * sr_ref[:, lanes] + (1.0 - STAT_DECAY) * out_r[rows, :]
        mo_ref[:, lanes] = m_ref[:, lanes] - WEIGHT_RATE * out_m[rows, :]


def renew(owned, master_blocks, stat_left, stat_right, root_left, root_right):
    number = master_blocks.shape[0]
    flat = pl.BlockSpec((8, SUB * SUB), lambda i: (i, 0))
    shape = jax.ShapeDtypeStruct(master_blocks.shape, F32)
    return pl.pallas_call(
        renew_body,
        grid=(number // 8,),
        in_specs=[pl.BlockSpec((2, SUB, WIDE), lambda i: (i, 0, 0))] + [flat] * 5,
        out_specs=[flat] * 4,
        out_shape=[shape] * 4,
        scratch_shapes=[pltpu.VMEM((256, 128), F32)] * 6 + [pltpu.VMEM((4, 6, SUB, 128), F32)],
        compiler_params=params(),
    )(owned, master_blocks, stat_left, stat_right, root_left, root_right)


def times(rows_in, w, base, r, g, part, col):
    first = base + part * r * g + col
    return dot(rows_in, jnp.concatenate([w[first + a * g] for a in range(r)], 0))


def times_back(d_ref, w, base, r, g, count, r4):
    total = None
    for part in range(count):
        first = base + (part * r + 4 * r4) * g
        wide = jnp.concatenate(
            [
                jnp.concatenate([w[first + a * g + col] for a in range(4)], 0)
                for col in range(g)
            ],
            1,
        )
        made = dot(d_ref[:, part * g * WIDE : (part + 1) * g * WIDE], wide, NT)
        total = made if total is None else total + made
    return total


def at256(i):
    return pl.ds(pl.multiple_of(i * WIDE, WIDE), WIDE)


def softmax_of(query, keys, scale, limit):
    scores = dot(query, keys, NT) * scale
    column = lax.broadcasted_iota(jnp.int32, scores.shape, 1)
    scores = jnp.where(column < limit, scores, MASK_FILL)
    raised = jnp.exp(scores - jnp.max(scores, 1, keepdims=True))
    return raised / jnp.sum(raised, 1, keepdims=True)


def score_grad(probs, dprobs):
    return (probs * (dprobs - jnp.sum(probs * dprobs, 1, keepdims=True))).astype(BF16)


def at128(i):
    return pl.ds(pl.multiple_of(i * 128, 128), 128)


def load(w_any, w, sems, pieces, base):
    copies = []
    for i, which in enumerate(pieces):
        begin, count, r, g = TILES[which]
        n = count * r * g
        copies.append(
            pltpu.make_async_copy(
                w_any.at[pl.ds(begin, n)], w.at[pl.ds(base[i], n)], sems.at[i]
            )
        )
        copies[-1].start()
    return copies


def tiles_of(which):
    _, count, r, g = TILES[which]
    return count * r * g


def co_body(len_ref, xv_ref, xt_ref, w_any, cv_ref, ct_ref, fv_ref, ft_ref, w, sems):
    base = (0, tiles_of(0))
    copies = load(w_any, w, sems, (0, 6), base)
    for which, at, x_ref, o_ref, copy in (
        (0, base[0], xv_ref, cv_ref, copies[0]),
        (6, base[1], xt_ref, ct_ref, copies[1]),
    ):
        _, count, r, g = TILES[which]
        copy.wait()

        def column(i, carry, at=at, r=r, g=g, x_ref=x_ref, o_ref=o_ref):
            o_ref[:, at256(i)] = times(x_ref[...], w, at, r, g, i // g, i % g).astype(BF16)
            return carry

        lax.fori_loop(0, count * g, column, 0)
    scale = HEAD ** (-0.5)
    reg = len_ref[2]
    heads = BI // HEAD
    for pair in range(2):
        vis = slice(pair * VIS_PAD, (pair + 1) * VIS_PAD)
        text = slice(pair * 128, (pair + 1) * 128)
        live = len_ref[pair]

        def head(j, carry, vis=vis, text=text, live=live):
            qv, kv, vv = (cv_ref[vis, at128(j + heads * s)] for s in range(3))
            qt, kt, vt = (ct_ref[text, at128(j + heads * s)] for s in range(3))
            fv_ref[vis, at128(j)] = dot(softmax_of(qv, kt, scale, live).astype(BF16), vt).astype(BF16)
            ft_ref[text, at128(j)] = dot(softmax_of(qt, kv, scale, reg).astype(BF16), vv).astype(BF16)
            return carry

        lax.fori_loop(0, heads, head, 0)


def co_forward(lengths, x_vis, x_text, tiles):
    return pl.pallas_call(
        co_body,
        in_specs=[pl.BlockSpec(memory_space=pltpu.SMEM)] + whole(2) + [pl.BlockSpec(memory_space=pl.ANY)],
        out_specs=whole(4),
        out_shape=[
            jax.ShapeDtypeStruct((x_vis.shape[0], 3 * BI), BF16),
            jax.ShapeDtypeStruct((x_text.shape[0], 3 * BI), BF16),
            jax.ShapeDtypeStruct((x_vis.shape[0], BI), BF16),
            jax.ShapeDtypeStruct((x_text.shape[0], BI), BF16),
        ],
        scratch_shapes=[
            pltpu.VMEM((tiles_of(0) + tiles_of(6), SUB, WIDE), BF16),
            pltpu.SemaphoreType.DMA((2,)),
        ],
        compiler_params=params(),
    )(lengths, x_vis, x_text, tiles)


def co_back_body(
    len_ref, cv_ref, ct_ref, dv_ref, dt_ref, rv_ref, rt_ref, w_any,
    gv_ref, gt_ref, ov_ref, ot_ref, w, sems,
):
    base = (0, tiles_of(0))
    copies = load(w_any, w, sems, (0, 6), base)
    scale = HEAD ** (-0.5)
    reg = len_ref[2]
    heads = BI // HEAD
    for pair in range(2):
        vis = slice(pair * VIS_PAD, (pair + 1) * VIS_PAD)
        text = slice(pair * 128, (pair + 1) * 128)
        live = len_ref[pair]

        def head(j, carry, vis=vis, text=text, live=live):
            qv, kv, vv = (cv_ref[vis, at128(j + heads * s)] for s in range(3))
            qt, kt, vt = (ct_ref[text, at128(j + heads * s)] for s in range(3))
            dv = dv_ref[vis, at128(j)]
            dt = dt_ref[text, at128(j)]
            probs = softmax_of(qv, kt, scale, live)
            ds = score_grad(probs, dot(dv, vt, NT))
            gv_ref[vis, at128(j)] = (dot(ds, kt) * scale).astype(BF16)
            gt_ref[text, at128(j + heads)] = (dot(ds, qv, TN) * scale).astype(BF16)
            gt_ref[text, at128(j + 2 * heads)] = dot(probs.astype(BF16), dv, TN).astype(BF16)
            probs = softmax_of(qt, kv, scale, reg)
            ds = score_grad(probs, dot(dt, vv, NT))
            gt_ref[text, at128(j)] = (dot(ds, kv) * scale).astype(BF16)
            gv_ref[vis, at128(j + heads)] = (dot(ds, qt, TN) * scale).astype(BF16)
            gv_ref[vis, at128(j + 2 * heads)] = dot(probs.astype(BF16), dt, TN).astype(BF16)
            return carry

        lax.fori_loop(0, heads, head, 0)
    for which, at, g_ref, r_ref, o_ref, copy in (
        (0, base[0], gv_ref, rv_ref, ov_ref, copies[0]),
        (6, base[1], gt_ref, rt_ref, ot_ref, copies[1]),
    ):
        _, count, r, g = TILES[which]
        copy.wait()

        def rows4(i, carry, at=at, r=r, g=g, count=count, g_ref=g_ref, r_ref=r_ref, o_ref=o_ref):
            o_ref[:, at256(i)] = r_ref[:, at256(i)] + times_back(g_ref, w, at, r, g, count, i)
            return carry

        lax.fori_loop(0, r // 4, rows4, 0)


def co_backward(lengths, co_vis, co_text, dvis, dtext, resid_vis, resid_text, tiles):
    return pl.pallas_call(
        co_back_body,
        in_specs=[pl.BlockSpec(memory_space=pltpu.SMEM)] + whole(6) + [pl.BlockSpec(memory_space=pl.ANY)],
        out_specs=whole(4),
        out_shape=[
            jax.ShapeDtypeStruct(co_vis.shape, BF16),
            jax.ShapeDtypeStruct(co_text.shape, BF16),
            jax.ShapeDtypeStruct(resid_vis.shape, F32),
            jax.ShapeDtypeStruct(resid_text.shape, F32),
        ],
        scratch_shapes=[
            pltpu.VMEM((tiles_of(0) + tiles_of(6), SUB, WIDE), BF16),
            pltpu.SemaphoreType.DMA((2,)),
        ],
        compiler_params=params(),
    )(lengths, co_vis, co_text, dvis, dtext, resid_vis, resid_text, tiles)


def erf_parts(value):
    return 0.5 * (1.0 + lax.erf(value * 0.7071067811865476))


def middle_body(
    config,
    len_ref, ctx_ref, x_ref, cot_ref, norm_ref, w_any,
    out_ref, first_ref, act_ref, second_ref, sctx_ref,
    fback_ref, pback_ref, bback_ref, dself_ref, tback_ref,
    resid_ref, dctx_ref, sums_ref,
    w, sems, pre, n1, n2, n3, s1, s2, s3, wide, acc, selfs, probs, stat,
):
    begin, rows, span, head, chunk = config
    width = x_ref.shape[1]
    base = []
    at = 0
    for which in range(begin, begin + 5):
        base.append(at)
        at += tiles_of(which)
    copies = load(w_any, w, sems, tuple(range(begin, begin + 5)), base)
    shapes = [TILES[which][1:] for which in range(begin, begin + 5)]
    steps = rows // chunk

    def at_chunk(i):
        return pl.ds(pl.multiple_of(i * chunk, chunk), chunk)

    def norm(resid, which, i, kept, scales):
        mean = jnp.mean(resid, 1, keepdims=True)
        centered = resid - mean
        scale = lax.rsqrt(jnp.mean(centered * centered, 1, keepdims=True) + NORM_EPSILON)
        normed = centered * scale
        kept[at_chunk(i), :] = normed
        scales[at_chunk(i), :] = jnp.broadcast_to(scale, (chunk, 128))
        return normed * norm_ref[0, which : which + 1, :] + norm_ref[1, which : which + 1, :]

    def eight(value):
        return jnp.sum(value.reshape(chunk // 8, 8, width), 0)

    def norm_back(upstream, which, i, kept, scales):
        normed = kept[at_chunk(i), :]
        stat[which] = stat[which] + eight(upstream * normed)
        stat[3 + which] = stat[3 + which] + eight(upstream)
        scaled = upstream * norm_ref[0, which : which + 1, :]
        return scales[at_chunk(i), 0:1] * (
            scaled
            - jnp.mean(scaled, 1, keepdims=True)
            - normed * jnp.mean(scaled * normed, 1, keepdims=True)
        )

    def loop(count, body):
        lax.fori_loop(0, count, lambda i, carry: (body(i), carry)[1], 0)

    stat[...] = jnp.zeros(stat.shape, F32)
    count, r, g = shapes[0]
    copies[0].wait()

    def co_out(i):
        wide[:, at256(i)] = times(ctx_ref[...], w, base[0], r, g, 0, i)

    loop(g, co_out)

    def norm_one(i):
        value = norm(wide[at_chunk(i), :] + x_ref[at_chunk(i), :].astype(F32), 0, i, n1, s1)
        wide[at_chunk(i), :] = value
        first_ref[at_chunk(i), :] = value.astype(BF16)

    loop(steps, norm_one)
    _, r_up, g_up = shapes[1]
    _, r_down, g_down = shapes[2]
    copies[1].wait()
    copies[2].wait()
    acc[...] = jnp.zeros(acc.shape, F32)

    def down_rows(i):
        return jnp.concatenate(
            [
                jnp.concatenate([w[base[2] + (4 * i + a) * g_down + col] for a in range(4)], 0)
                for col in range(g_down)
            ],
            1,
        )

    def feed(i):
        value = times(first_ref[...], w, base[1], r_up, g_up, 0, i)
        pre[i] = value
        act = (value * erf_parts(value)).astype(BF16)
        act_ref[:, at256(i)] = act
        acc[...] += dot(act, down_rows(i))

    loop(g_up, feed)

    def norm_two(i):
        value = norm(wide[at_chunk(i), :] + acc[at_chunk(i), :], 1, i, n2, s2)
        wide[at_chunk(i), :] = value
        second_ref[at_chunk(i), :] = value.astype(BF16)

    loop(steps, norm_two)
    count_s, r_s, g_s = shapes[3]
    copies[3].wait()

    def self_in(i):
        selfs[:, at256(i)] = times(second_ref[...], w, base[3], r_s, g_s, i // g_s, i % g_s).astype(BF16)

    loop(count_s * g_s, self_in)
    scale = head ** (-0.5)
    groups = width // 128
    per = 128 // head
    pairs = rows // span

    def halves(values):
        if per == 1:
            return values[0]
        low = lax.broadcasted_iota(jnp.int32, values[0].shape, 1) < head
        return jnp.where(low, values[0], values[1])

    def only(value, h):
        if per == 1:
            return value
        low = lax.broadcasted_iota(jnp.int32, value.shape, 1) < head
        keep = low if h == 0 else jnp.logical_not(low)
        return jnp.where(keep, value, jnp.zeros_like(value))

    for pair in range(pairs):
        own = slice(pair * span, (pair + 1) * span)
        live = len_ref[pair]

        def attend(j, own=own, live=live, pair=pair):
            q, k, v = (selfs[own, at128(j + groups * s)] for s in range(3))
            found = []
            for h in range(per):
                p = softmax_of(only(q, h), k, scale, live)
                probs[(pair * groups + j) * per + h] = p
                found.append(dot(p.astype(BF16), v))
            sctx_ref[own, at128(j)] = halves(found).astype(BF16)

        loop(groups, attend)
    _, r_o, g_o = shapes[4]
    copies[4].wait()

    def self_out(i):
        acc[:, at256(i)] = times(sctx_ref[...], w, base[4], r_o, g_o, 0, i)

    loop(g_o, self_out)

    def norm_three(i):
        value = norm(wide[at_chunk(i), :] + acc[at_chunk(i), :], 2, i, n3, s3)
        out_ref[at_chunk(i), :] = value.astype(BF16)
        third = norm_back(cot_ref[at_chunk(i), :].astype(F32), 2, i, n3, s3)
        wide[at_chunk(i), :] = third
        tback_ref[at_chunk(i), :] = third.astype(BF16)

    loop(steps, norm_three)

    def self_out_back(i):
        dctx_ref[:, at256(i)] = times_back(tback_ref, w, base[4], r_o, g_o, 1, i).astype(BF16)

    loop(r_o // 4, self_out_back)
    for pair in range(pairs):
        own = slice(pair * span, (pair + 1) * span)

        def attend_back(j, own=own, pair=pair):
            q, k, v = (selfs[own, at128(j + groups * s)] for s in range(3))
            up = dctx_ref[own, at128(j)]
            dq, dk, dv = [], [], []
            for h in range(per):
                p = probs[(pair * groups + j) * per + h]
                ds = score_grad(p, dot(only(up, h), v, NT))
                dq.append(dot(ds, k))
                dk.append(dot(ds, q, TN))
                dv.append(dot(p.astype(BF16), up, TN))
            dself_ref[own, at128(j)] = (halves(dq) * scale).astype(BF16)
            dself_ref[own, at128(j + groups)] = (halves(dk) * scale).astype(BF16)
            dself_ref[own, at128(j + 2 * groups)] = halves(dv).astype(BF16)

        loop(groups, attend_back)

    def self_in_back(i):
        acc[:, at256(i)] = times_back(dself_ref, w, base[3], r_s, g_s, count_s, i)

    loop(r_s // 4, self_in_back)

    def norm_two_back(i):
        value = norm_back(wide[at_chunk(i), :] + acc[at_chunk(i), :], 1, i, n2, s2)
        wide[at_chunk(i), :] = value
        bback_ref[at_chunk(i), :] = value.astype(BF16)

    loop(steps, norm_two_back)

    def feed_back(i):
        act_grad = dot(bback_ref[...], down_rows(i), NT)
        value = pre[i]
        slope = erf_parts(value) + value * (0.3989422804014327 * jnp.exp(-0.5 * value * value))
        pback_ref[:, at256(i)] = (act_grad * slope).astype(BF16)

    loop(g_up, feed_back)

    def up_back(i):
        acc[:, at256(i)] = times_back(pback_ref, w, base[1], r_up, g_up, 1, i)

    loop(r_up // 4, up_back)

    def norm_one_back(i):
        value = norm_back(wide[at_chunk(i), :] + acc[at_chunk(i), :], 0, i, n1, s1)
        resid_ref[at_chunk(i), :] = value
        fback_ref[at_chunk(i), :] = value.astype(BF16)

    loop(steps, norm_one_back)

    def co_out_back(i):
        dctx_ref[:, at256(i)] = times_back(fback_ref, w, base[0], r, g, 1, i).astype(BF16)

    loop(r // 4, co_out_back)
    sums_ref[...] = jnp.sum(stat[...], 1)


def middle(begin, lengths, context, x, cot, norms, tiles, span, head, chunk):
    rows, width = x.shape
    hidden = TILES[begin + 1][3] * WIDE
    number = sum(tiles_of(which) for which in range(begin, begin + 5))
    low = lambda columns: jax.ShapeDtypeStruct((rows, columns), BF16)
    return pl.pallas_call(
        functools.partial(middle_body, (begin, rows, span, head, chunk)),
        in_specs=[pl.BlockSpec(memory_space=pltpu.SMEM)] + whole(4) + [pl.BlockSpec(memory_space=pl.ANY)],
        out_specs=whole(13),
        out_shape=[
            low(width), low(width), low(hidden), low(width), low(width),
            low(width), low(hidden), low(width), low(3 * width), low(width),
            jax.ShapeDtypeStruct((rows, width), F32), low(BI),
            jax.ShapeDtypeStruct((6, width), F32),
        ],
        scratch_shapes=[
            pltpu.VMEM((number, SUB, WIDE), BF16),
            pltpu.SemaphoreType.DMA((5,)),
            pltpu.VMEM((hidden // WIDE, rows, WIDE), F32),
        ]
        + [pltpu.VMEM((rows, width), F32)] * 3
        + [pltpu.VMEM((rows, 128), F32)] * 3
        + [pltpu.VMEM((rows, width), F32)] * 2
        + [
            pltpu.VMEM((rows, 3 * width), BF16),
            pltpu.VMEM((rows // span * (width // head), span, span), F32),
            pltpu.VMEM((6, 8, width), F32),
        ],
        compiler_params=params(),
    )(lengths, context, x, cot, norms, tiles)


def weight_body(kinds, *refs):
    n = len(kinds)
    lefts, rights, out, stage, sems = refs[:n], refs[n : 2 * n], refs[2 * n], refs[2 * n + 1], refs[2 * n + 2]
    offset = 0
    for which, a_ref, b_ref in zip(kinds, lefts, rights):
        _, count, r, g = TILES[which]
        size = 4 * g

        def copy(i, slot, offset=offset, size=size):
            return pltpu.make_async_copy(
                stage.at[slot, pl.ds(0, size)], out.at[pl.ds(offset + i * size, size)], sems.at[slot]
            )

        total = count * (r // 4)

        def step(i, carry, a_ref=a_ref, b_ref=b_ref, r=r, g=g, copy=copy):
            slot = lax.rem(i, 2)

            @pl.when(i >= 2)
            def _():
                copy(i - 2, slot).wait()

            part = i // (r // 4)
            r4 = lax.rem(i, r // 4)
            left = a_ref[:, at256(r4)]
            for col in range(g):
                made = dot(left, b_ref[:, at256(part * g + col)], TN).astype(BF16)
                for a in range(4):
                    stage[slot, a * g + col] = made[a * SUB : (a + 1) * SUB]
            copy(i, slot).start()
            return carry

        lax.fori_loop(0, total, step, 0)
        for i in range(max(0, total - 2), total):
            copy(i, i % 2).wait()
        offset += count * r * g


def weight_grads(kinds, lefts, rights):
    number = sum(tiles_of(which) for which in kinds)
    most = max(4 * TILES[which][3] for which in kinds)
    return pl.pallas_call(
        functools.partial(weight_body, kinds),
        in_specs=whole(2 * len(kinds)),
        out_specs=pl.BlockSpec(memory_space=pl.ANY),
        out_shape=jax.ShapeDtypeStruct((number, SUB, WIDE), BF16),
        scratch_shapes=[
            pltpu.VMEM((2, most, SUB, WIDE), BF16),
            pltpu.SemaphoreType.DMA((2,)),
        ],
        compiler_params=params(),
    )(*lefts, *rights)


def sum_everywhere(value):
    for axis in ("seq", "dp"):
        size = lax.axis_size(axis)
        step = 1
        while step < size:
            value = value + lax.ppermute(value, axis, [(i, i ^ step) for i in range(size)])
            step *= 2
    return value


def gather_tiles(own):
    halves = own.reshape(own.shape[0] * 2, SUB // 2, WIDE)
    size = halves.shape[0] // lax.axis_size("seq")
    mine = lax.dynamic_slice_in_dim(halves, lax.axis_index("seq") * size, size, 0)
    return lax.all_gather(mine, ("dp", "seq"), axis=0, tiled=True).reshape(-1, SUB, WIDE)


def reduce_tiles(grads):
    halves = grads.reshape(grads.shape[0] * 2, SUB // 2, WIDE)
    mine = lax.psum_scatter(halves, ("dp", "seq"), scatter_dimension=0, tiled=True)
    return lax.all_gather(mine, "seq", axis=0, tiled=True).reshape(-1, SUB, WIDE)


def pad_regions(value, pairs):
    reg = value.shape[0] // pairs
    cube = value.reshape(pairs, reg, value.shape[1])
    return jnp.pad(cube, ((0, 0), (0, VIS_PAD - reg), (0, 0))).reshape(pairs * VIS_PAD, -1)


def cut_regions(value, pairs, reg):
    return value.reshape(pairs, VIS_PAD, -1)[:, :reg].reshape(pairs * reg, -1)


def fast_shards(
    x_text, x_vis, caption_len, cot_text, cot_vis, master_blocks,
    stat_left, stat_right, root_left, root_right, norm_params, norm_second,
):
    pairs = caption_len.shape[0]
    reg = x_vis.shape[0] // pairs
    tiles = gather_tiles(prep(master_blocks))
    lengths = jnp.concatenate([caption_len, jnp.full((2,), reg, jnp.int32)])
    regions = jnp.full((2,), reg, jnp.int32)
    xv = pad_regions(x_vis, pairs)
    cv = pad_regions(cot_vis, pairs)
    vis_norms = norm_params[:, : 3 * VIS].reshape(2, 3, VIS)
    text_norms = norm_params[:, 3 * VIS :].reshape(2, 3, TXT)
    co_vis, co_text, vis_ctx, text_ctx = co_forward(lengths, xv, x_text, tiles)
    (out_vis, v_first, v_act, v_second, v_sctx, v_fback, v_pback, v_bback, v_dself, v_tback,
     v_resid, v_dctx, v_sums) = middle(1, regions, vis_ctx, xv, cv, vis_norms, tiles, VIS_PAD, HEAD_V, 32)
    vis_mid = weight_grads(
        (1, 2, 3, 4, 5), (vis_ctx, v_first, v_act, v_second, v_sctx),
        (v_fback, v_pback, v_bback, v_dself, v_tback),
    )
    (out_text, t_first, t_act, t_second, t_sctx, t_fback, t_pback, t_bback, t_dself, t_tback,
     t_resid, t_dctx, t_sums) = middle(
        7, lengths, text_ctx, x_text, cot_text, text_norms, tiles, x_text.shape[0] // pairs, HEAD_T, 32
    )
    text_mid = weight_grads(
        (7, 8, 9, 10, 11), (text_ctx, t_first, t_act, t_second, t_sctx),
        (t_fback, t_pback, t_bback, t_dself, t_tback),
    )
    dco_vis, dco_text, grad_vis, grad_text = co_backward(
        lengths, co_vis, co_text, v_dctx, t_dctx, v_resid, t_resid, tiles
    )
    vis_co = weight_grads((0,), (xv,), (dco_vis,))
    text_co = weight_grads((6,), (x_text,), (dco_text,))
    owned = reduce_tiles(jnp.concatenate([vis_co, vis_mid, text_co, text_mid], 0))
    norm_local = jnp.concatenate([v_sums.reshape(2, -1), t_sums.reshape(2, -1)], 1)
    norm_grads = sum_everywhere(norm_local)
    grad_blocks, left_new, right_new, master_new = renew(
        owned, master_blocks, stat_left, stat_right, root_left, root_right
    )
    second_new = STAT_DECAY * norm_second + (1.0 - STAT_DECAY) * norm_grads * norm_grads
    norm_new = norm_params - NORM_RATE * norm_grads / (jnp.sqrt(second_new) + MOMENT_EPSILON)
    return (
        out_text,
        cut_regions(out_vis, pairs, reg),
        grad_text,
        cut_regions(grad_vis, pairs, reg),
        grad_blocks,
        left_new,
        right_new,
        master_new,
        norm_grads,
        second_new,
        norm_new,
    )


def fits(mesh):
    owners, group = mesh.shape["dp"], mesh.shape["seq"]
    number = sum(rows * columns * count for rows, columns, count in weight_layout()) // (BLK * BLK)
    powers = owners & (owners - 1) == 0 and group & (group - 1) == 0
    return powers and number % (8 * owners) == 0 and number // owners // 2 % group == 0


def solution(mesh):
    placed = (
        P(("dp", "seq"), None),
        P(("dp", "seq"), None),
        P(("dp", "seq")),
        P(("dp", "seq"), None),
        P(("dp", "seq"), None),
        P("dp", None),
        P("dp", None),
        P("dp", None),
        P("dp", None),
        P("dp", None),
        P(),
        P(),
    )
    step = fast_shards if fits(mesh) else shards
    return jax.shard_map(
        step,
        mesh=mesh,
        in_specs=placed,
        out_specs=(
            P(("dp", "seq"), None),
            P(("dp", "seq"), None),
            P(("dp", "seq"), None),
            P(("dp", "seq"), None),
            P("dp", None),
            P("dp", None),
            P("dp", None),
            P("dp", None),
            P(),
            P(),
            P(),
        ),
        check_vma=False,
    )
```

```python
import functools

import jax
import jax.numpy as jnp
from jax import lax
from jax.experimental import pallas as pl
from jax.experimental.pallas import tpu as pltpu
from jax.sharding import PartitionSpec as P

TXT = 768
VIS = 1024
BI = 1024
FFT = 3072
FFV = 1024
HEAD = 128
HEAD_T = 64
HEAD_V = 128
BLK = 64


MASK_FILL = -1000000000.0
STAT_DECAY = 0.9
WEIGHT_RATE = 0.3
NORM_RATE = 0.2
NORM_EPSILON = 1e-05
MOMENT_EPSILON = 1e-08
HIGHEST = lax.Precision.HIGHEST
CONTRACT_COLS = (((1,), (1,)), ((), ()))


def weight_layout():
    return (
        (VIS, BI, 3),
        (BI, VIS, 1),
        (VIS, FFV, 1),
        (FFV, VIS, 1),
        (VIS, VIS, 3),
        (VIS, VIS, 1),
        (TXT, BI, 3),
        (BI, TXT, 1),
        (TXT, FFT, 1),
        (FFT, TXT, 1),
        (TXT, TXT, 3),
        (TXT, TXT, 1),
    )


def unpack_weights(flat):
    size = BLK
    blocks = flat.reshape(flat.shape[0], size, size)
    begin = 0
    matrices = []
    for rows, columns, count in weight_layout():
        number = count * rows * columns // (size * size)
        shaped = blocks[begin : begin + number].reshape(
            count, rows // size, columns // size, size, size
        )
        matrices.append(shaped.transpose(1, 3, 0, 2, 4).reshape(rows, count * columns))
        begin += number
    return matrices


def block_grad(inputs, grads, count):
    size = BLK
    left = inputs.reshape(inputs.shape[0], inputs.shape[1] // size, size)
    right = grads.reshape(grads.shape[0], count, grads.shape[1] // (count * size), size)
    return jnp.einsum("nai,nkbj->kabij", left, right, preferred_element_type=jnp.float32).reshape(
        -1, size * size
    )


def norm_columns(values, stream, which):
    if stream == 0:
        begin = which * VIS
        width = VIS
    else:
        begin = 3 * VIS + which * TXT
        width = TXT
    return values[:, begin : begin + width]


def gelu_exact(value):
    return jax.nn.gelu(value, approximate=False)


def heads_of(side, which, head):
    part = side[:, :, which, :]
    return part.reshape(part.shape[0], part.shape[1], part.shape[2] // head, head)


def scores_of(query, keys, live, head):
    scores = jnp.einsum(
        "gqhd,gkhd->ghqk", query, keys, preferred_element_type=jnp.float32
    ) * head ** (-0.5)
    if live is not None:
        scores = jnp.where(live[:, None, None, :], scores, MASK_FILL)
    return scores


def attend_one(query, keys, values, live, head):
    scores = scores_of(query, keys, live, head)
    top = jnp.max(scores, axis=3, keepdims=True)
    raised = jnp.exp(scores - top)
    total = jnp.sum(raised, axis=3, keepdims=True)
    found = jnp.einsum(
        "ghqk,gkhd->gqhd",
        (raised / total).astype(jnp.bfloat16),
        values,
        preferred_element_type=jnp.float32,
    ).astype(jnp.bfloat16)
    return (found.reshape(found.shape[0], found.shape[1], -1), top + jnp.log(total))


def attend_one_back(query, keys, values, live, head, logsum, dfound):
    scale = head ** (-0.5)
    probs = jnp.exp(scores_of(query, keys, live, head) - logsum)
    upstream = dfound.reshape(dfound.shape[0], dfound.shape[1], -1, head)
    dprobs = jnp.einsum("gqhd,gkhd->ghqk", upstream, values, preferred_element_type=jnp.float32)
    dvalues = jnp.einsum(
        "ghqk,gqhd->gkhd", probs.astype(jnp.bfloat16), upstream, preferred_element_type=jnp.float32
    )
    dscores = (probs * (dprobs - jnp.sum(probs * dprobs, axis=3, keepdims=True))).astype(
        jnp.bfloat16
    )
    dquery = (
        jnp.einsum("ghqk,gkhd->gqhd", dscores, keys, preferred_element_type=jnp.float32) * scale
    )
    dkeys = (
        jnp.einsum("ghqk,gqhd->gkhd", dscores, query, preferred_element_type=jnp.float32) * scale
    )
    return (dquery, dkeys, dvalues)


def attention_plan(vis_side, text_side, lengths, cross):
    live = (
        lax.broadcasted_iota(jnp.int32, (lengths.shape[0], text_side.shape[1]), 1)
        < lengths[:, None]
    )
    if cross:
        return ((vis_side, text_side, live, HEAD), (text_side, vis_side, None, HEAD))
    return ((vis_side, vis_side, None, HEAD_V), (text_side, text_side, live, HEAD_T))


def pair_attend(vis_side, text_side, lengths, cross):
    results = []
    for query_side, key_side, live, head in attention_plan(vis_side, text_side, lengths, cross):
        results.append(
            attend_one(
                heads_of(query_side, 0, head),
                heads_of(key_side, 1, head),
                heads_of(key_side, 2, head),
                live,
                head,
            )
        )
    return (results[0][0], results[1][0], results[0][1], results[1][1])


def pair_attend_back(
    vis_side, text_side, lengths, cross, vis_logsum, text_logsum, vis_dfound, text_dfound
):
    plan = attention_plan(vis_side, text_side, lengths, cross)
    parts = []
    for (query_side, key_side, live, head), logsum, dfound in zip(
        plan, (vis_logsum, text_logsum), (vis_dfound, text_dfound)
    ):
        parts.append(
            attend_one_back(
                heads_of(query_side, 0, head),
                heads_of(key_side, 1, head),
                heads_of(key_side, 2, head),
                live,
                head,
                logsum,
                dfound,
            )
        )
    if cross:
        vis_parts = (parts[0][0], parts[1][1], parts[1][2])
        text_parts = (parts[1][0], parts[0][1], parts[0][2])
    else:
        vis_parts = parts[0]
        text_parts = parts[1]
    vis_grad = jnp.stack(vis_parts, axis=2).reshape(vis_side.shape).astype(jnp.bfloat16)
    text_grad = jnp.stack(text_parts, axis=2).reshape(text_side.shape).astype(jnp.bfloat16)
    return (vis_grad, text_grad)


def to_heads(vis_side, text_side):
    return (vis_side, text_side)


def from_heads(vis_found, text_found):
    return (vis_found, text_found)


def dfound_to_heads(vis_dfound, text_dfound):
    return (vis_dfound, text_dfound)


def grads_from_heads(vis_grad, text_grad):
    return (vis_grad, text_grad)


def side_of(rows_in, weight, pairs):
    made = jnp.dot(rows_in, weight, preferred_element_type=jnp.float32).astype(jnp.bfloat16)
    return made.reshape(pairs, -1, 3, weight.shape[1] // 3)


def norm_forward(resid, columns):
    mean = jnp.mean(resid, -1, keepdims=True)
    centered = resid - mean
    scale = lax.rsqrt(jnp.mean(centered * centered, -1, keepdims=True) + NORM_EPSILON)
    normed = centered * scale
    return (normed, scale, normed * columns[0] + columns[1])


def norm_backward(upstream, normed, scale, gain):
    scaled = upstream * gain
    resid_grad = scale * (
        scaled
        - jnp.mean(scaled, -1, keepdims=True)
        - normed * jnp.mean(scaled * normed, -1, keepdims=True)
    )
    return (resid_grad, jnp.sum(upstream * normed, 0), jnp.sum(upstream, 0))


def stream_middle(context_rows, x_rows, weights, values, stream, pairs):
    resid = x_rows.astype(jnp.float32) + jnp.dot(
        context_rows, weights[1], preferred_element_type=jnp.float32
    )
    normed_one, scale_one, first = norm_forward(resid, norm_columns(values, stream, 0))
    first_low = first.astype(jnp.bfloat16)
    pre = jnp.dot(first_low, weights[2], preferred_element_type=jnp.float32)
    act = gelu_exact(pre).astype(jnp.bfloat16)
    resid = first + jnp.dot(act, weights[3], preferred_element_type=jnp.float32)
    normed_two, scale_two, second = norm_forward(resid, norm_columns(values, stream, 1))
    second_low = second.astype(jnp.bfloat16)
    side = side_of(second_low, weights[4], pairs)
    return (
        side,
        (normed_one, scale_one, first_low, pre, act, normed_two, scale_two, second, second_low),
    )


def stream_end(self_rows, second, out_weight, values, stream):
    resid = second + jnp.dot(self_rows, out_weight, preferred_element_type=jnp.float32)
    normed_three, scale_three, third = norm_forward(resid, norm_columns(values, stream, 2))
    return (third.astype(jnp.bfloat16), normed_three, scale_three)


def stream_back_end(
    cotangent, normed_three, scale_three, self_rows, out_weight, values, stream, pairs
):
    resid_three, gain_three, bias_three = norm_backward(
        cotangent.astype(jnp.float32), normed_three, scale_three, norm_columns(values, stream, 2)[0]
    )
    third_back = resid_three.astype(jnp.bfloat16)
    grad_self_out = block_grad(self_rows, third_back, 1)
    dself = lax.dot_general(
        third_back, out_weight, CONTRACT_COLS, preferred_element_type=jnp.float32
    )
    dself = dself.astype(jnp.bfloat16).reshape(pairs, -1, out_weight.shape[0])
    return (resid_three, dself, grad_self_out, gain_three, bias_three)


def stream_back_middle(resid_three, dself_side, kept, context_rows, weights, values, stream, pairs):
    normed_one, scale_one, first_low, pre, act, normed_two, scale_two, second, second_low = kept
    dself_rows = dself_side.reshape(-1, dself_side.shape[2] * dself_side.shape[3])
    grad_self_qkv = block_grad(second_low, dself_rows, 3)
    second_in = resid_three + lax.dot_general(
        dself_rows, weights[4], CONTRACT_COLS, preferred_element_type=jnp.float32
    )
    resid_two, gain_two, bias_two = norm_backward(
        second_in, normed_two, scale_two, norm_columns(values, stream, 1)[0]
    )
    branch_back = resid_two.astype(jnp.bfloat16)
    grad_down = block_grad(act, branch_back, 1)
    act_grad = lax.dot_general(
        branch_back, weights[3], CONTRACT_COLS, preferred_element_type=jnp.float32
    )
    pre_grad = jax.vjp(gelu_exact, pre)[1](act_grad)[0].astype(jnp.bfloat16)
    grad_up = block_grad(first_low, pre_grad, 1)
    first_in = resid_two + lax.dot_general(
        pre_grad, weights[2], CONTRACT_COLS, preferred_element_type=jnp.float32
    )
    resid_one, gain_one, bias_one = norm_backward(
        first_in, normed_one, scale_one, norm_columns(values, stream, 0)[0]
    )
    first_back = resid_one.astype(jnp.bfloat16)
    grad_co_out = block_grad(context_rows, first_back, 1)
    dcontext = lax.dot_general(
        first_back, weights[1], CONTRACT_COLS, preferred_element_type=jnp.float32
    )
    dcontext = dcontext.astype(jnp.bfloat16).reshape(pairs, -1, BI)
    return (
        resid_one,
        dcontext,
        (grad_co_out, grad_up, grad_down, grad_self_qkv),
        (gain_one, gain_two),
        (bias_one, bias_two),
    )


def shards(
    x_text,
    x_vis,
    caption_len,
    cot_text,
    cot_vis,
    master_blocks,
    stat_left,
    stat_right,
    root_left,
    root_right,
    norm_params,
    norm_second,
):
    pairs = caption_len.shape[0]
    width = master_blocks.shape[1] // lax.axis_size("seq")
    mine = lax.dynamic_slice_in_dim(master_blocks, lax.axis_index("seq") * width, width, 1).astype(
        jnp.bfloat16
    )
    partial_value = lax.all_gather(mine, "dp", axis=0, tiled=True)
    every = lax.all_gather(partial_value, "seq", axis=1, tiled=True)
    matrices = unpack_weights(every)
    vis_weights = matrices[:6]
    text_weights = matrices[6:]
    vis_co = side_of(x_vis, vis_weights[0], pairs)
    text_co = side_of(x_text, text_weights[0], pairs)
    lengths = caption_len
    vis_co_use, text_co_use = to_heads(vis_co, text_co)
    vis_found, text_found, vis_co_sum, text_co_sum = pair_attend(
        vis_co_use, text_co_use, lengths, True
    )
    vis_context, text_context = from_heads(vis_found, text_found)
    vis_context_rows = vis_context.reshape(-1, BI)
    text_context_rows = text_context.reshape(-1, BI)
    vis_self, vis_kept = stream_middle(vis_context_rows, x_vis, vis_weights, norm_params, 0, pairs)
    text_self, text_kept = stream_middle(
        text_context_rows, x_text, text_weights, norm_params, 1, pairs
    )
    vis_self_use, text_self_use = to_heads(vis_self, text_self)
    vis_found, text_found, vis_self_sum, text_self_sum = pair_attend(
        vis_self_use, text_self_use, lengths, False
    )
    vis_self_context, text_self_context = from_heads(vis_found, text_found)
    vis_self_rows = vis_self_context.reshape(-1, VIS)
    text_self_rows = text_self_context.reshape(-1, TXT)
    out_vis, vis_normed_three, vis_scale_three = stream_end(
        vis_self_rows, vis_kept[7], vis_weights[5], norm_params, 0
    )
    out_text, text_normed_three, text_scale_three = stream_end(
        text_self_rows, text_kept[7], text_weights[5], norm_params, 1
    )
    vis_resid_three, vis_dself, vis_grad_so, vis_gain_three, vis_bias_three = stream_back_end(
        cot_vis,
        vis_normed_three,
        vis_scale_three,
        vis_self_rows,
        vis_weights[5],
        norm_params,
        0,
        pairs,
    )
    text_resid_three, text_dself, text_grad_so, text_gain_three, text_bias_three = stream_back_end(
        cot_text,
        text_normed_three,
        text_scale_three,
        text_self_rows,
        text_weights[5],
        norm_params,
        1,
        pairs,
    )
    vis_dheads, text_dheads = dfound_to_heads(vis_dself, text_dself)
    vis_dgot, text_dgot = pair_attend_back(
        vis_self_use,
        text_self_use,
        lengths,
        False,
        vis_self_sum,
        text_self_sum,
        vis_dheads,
        text_dheads,
    )
    vis_dself_side, text_dself_side = grads_from_heads(vis_dgot, text_dgot)
    vis_resid_one, vis_dcontext, vis_grads_mid, vis_gains_mid, vis_biases_mid = stream_back_middle(
        vis_resid_three,
        vis_dself_side,
        vis_kept,
        vis_context_rows,
        vis_weights,
        norm_params,
        0,
        pairs,
    )
    text_resid_one, text_dcontext, text_grads_mid, text_gains_mid, text_biases_mid = (
        stream_back_middle(
            text_resid_three,
            text_dself_side,
            text_kept,
            text_context_rows,
            text_weights,
            norm_params,
            1,
            pairs,
        )
    )
    vis_dheads, text_dheads = dfound_to_heads(vis_dcontext, text_dcontext)
    vis_dgot, text_dgot = pair_attend_back(
        vis_co_use, text_co_use, lengths, True, vis_co_sum, text_co_sum, vis_dheads, text_dheads
    )
    vis_dco, text_dco = grads_from_heads(vis_dgot, text_dgot)
    vis_dco_rows = vis_dco.reshape(-1, 3 * BI)
    text_dco_rows = text_dco.reshape(-1, 3 * BI)
    grad_vis = vis_resid_one + lax.dot_general(
        vis_dco_rows, vis_weights[0], CONTRACT_COLS, preferred_element_type=jnp.float32
    )
    grad_text = text_resid_one + lax.dot_general(
        text_dco_rows, text_weights[0], CONTRACT_COLS, preferred_element_type=jnp.float32
    )
    vis_grad_co = block_grad(x_vis, vis_dco_rows, 3)
    text_grad_co = block_grad(x_text, text_dco_rows, 3)
    local_blocks = jnp.concatenate(
        [vis_grad_co]
        + list(vis_grads_mid)
        + [vis_grad_so]
        + [text_grad_co]
        + list(text_grads_mid)
        + [text_grad_so],
        0,
    )
    norm_local = jnp.stack(
        [
            jnp.concatenate(
                [
                    vis_gains_mid[0],
                    vis_gains_mid[1],
                    vis_gain_three,
                    text_gains_mid[0],
                    text_gains_mid[1],
                    text_gain_three,
                ]
            ),
            jnp.concatenate(
                [
                    vis_biases_mid[0],
                    vis_biases_mid[1],
                    vis_bias_three,
                    text_biases_mid[0],
                    text_biases_mid[1],
                    text_bias_three,
                ]
            ),
        ]
    )
    columns = lax.psum_scatter(
        local_blocks.astype(jnp.bfloat16), "seq", scatter_dimension=1, tiled=True
    ).astype(jnp.float32)
    owned_columns = lax.psum_scatter(columns, "dp", scatter_dimension=0, tiled=True)
    owned = lax.all_gather(owned_columns.astype(jnp.bfloat16), "seq", axis=1, tiled=True).astype(
        owned_columns.dtype
    )
    norm_grads = lax.psum(norm_local, ("dp", "seq"))
    number = owned.shape[0]
    grad_cube = owned.reshape(number, BLK, BLK)
    left_cube = stat_left.reshape(number, BLK, BLK)
    right_cube = stat_right.reshape(number, BLK, BLK)
    rootl_cube = root_left.reshape(number, BLK, BLK)
    rootr_cube = root_right.reshape(number, BLK, BLK)
    left_new = STAT_DECAY * left_cube + (1.0 - STAT_DECAY) * jnp.einsum(
        "bij,bkj->bik", grad_cube, grad_cube, precision=HIGHEST
    )
    right_new = STAT_DECAY * right_cube + (1.0 - STAT_DECAY) * jnp.einsum(
        "bji,bjk->bik", grad_cube, grad_cube, precision=HIGHEST
    )
    half = jnp.einsum("bij,bjk->bik", rootl_cube, grad_cube, precision=HIGHEST)
    direction = jnp.einsum("bij,bjk->bik", half, rootr_cube, precision=HIGHEST)
    master_new = master_blocks - WEIGHT_RATE * direction.reshape(number, BLK * BLK)
    second_new = STAT_DECAY * norm_second + (1.0 - STAT_DECAY) * norm_grads * norm_grads
    norm_new = norm_params - NORM_RATE * norm_grads / (jnp.sqrt(second_new) + MOMENT_EPSILON)
    return (
        out_text,
        out_vis,
        grad_text,
        grad_vis,
        owned,
        left_new.reshape(number, BLK * BLK),
        right_new.reshape(number, BLK * BLK),
        master_new,
        norm_grads,
        second_new,
        norm_new,
    )


SUB = 64
WIDE = 256
QUAD = 4
F32 = jnp.float32
BF16 = jnp.bfloat16
VIS_PAD = 48
VMEM_LIMIT = 60 * 1024 * 1024
NT = (((1,), (1,)), ((), ()))
TN = (((0,), (0,)), ((), ()))


def tile_table():
    begin = 0
    table = []
    for rows, columns, count in weight_layout():
        r, g = rows // SUB, columns // WIDE
        table.append((begin, count, r, g))
        begin += count * r * g
    return table


TILES = tile_table()
SHARD = 158
FAR = 46
G_HALF = 24
G_LONE = 6
R_HALF = 80
R_STEP = 78
R_LONE = 28
CHUNKS = 2
SWAP_CORE = [(i, i ^ 1) for i in range(4)]
SWAP_Y = [(i, i ^ 2) for i in range(4)]
SWAP_X = [(i, i ^ 1) for i in range(8)]


def dot(left, right, how=None):
    if how is None:
        return jnp.dot(left, right, preferred_element_type=F32)
    return lax.dot_general(left, right, how, preferred_element_type=F32)


def params(**more):
    return pltpu.CompilerParams(vmem_limit_bytes=VMEM_LIMIT, **more)


def cost(micros):
    return pl.CostEstimate(flops=0, bytes_accessed=int(micros * 3.4e6), transcendentals=0)


def whole(count):
    return [pl.BlockSpec(memory_space=pltpu.VMEM)] * count


def linear(value):
    groups = value.shape[0] // 8
    return value.reshape(groups, 8, 32, 128).transpose(0, 2, 1, 3).reshape(groups * 256, 128)


def unlinear(value):
    groups = value.shape[0] // 256
    return value.reshape(groups, 32, 8, 128).transpose(0, 2, 1, 3).reshape(groups * 8, SUB * SUB)


def lanes_low(rows):
    return lax.broadcasted_iota(jnp.int32, (rows, 2 * SUB), 1) < SUB


def spread_of(ref, b):
    return ref[pl.ds(b, 32, stride=8), :]


def natural_order():
    row = lax.broadcasted_iota(jnp.int32, (SUB, SUB), 0)
    column = lax.broadcasted_iota(jnp.int32, (SUB, SUB), 1)
    return jnp.where(row == 2 * (column % 32) + column // 32, 1.0, 0.0).astype(BF16)


def prep_rows(pairs_ref, x_ref, o_ref):
    low = lanes_low(32)
    order = natural_order()
    for k in range(2):
        for m in range(2):
            one = spread_of(x_ref, 4 * k + 2 * m)
            two = spread_of(x_ref, 4 * k + 2 * m + 1)
            rows = jnp.concatenate(
                [
                    jnp.where(low, one, pltpu.roll(two, SUB, 1)),
                    jnp.where(low, pltpu.roll(one, SUB, 1), two),
                ],
                0,
            )
            o_ref[k, :, m * 128 : (m + 1) * 128] = dot(order, rows.astype(BF16)).astype(BF16)


def prep(master_blocks, pairs):
    number = pairs.shape[0]
    return pl.pallas_call(
        prep_rows,
        grid_spec=pltpu.PrefetchScalarGridSpec(
            num_scalar_prefetch=1,
            grid=(number,),
            in_specs=[pl.BlockSpec((256, 128), lambda i, which: (which[i], 0))],
            out_specs=pl.BlockSpec((2, SUB, WIDE), lambda i, which: (i, 0, 0)),
        ),
        out_shape=jax.ShapeDtypeStruct((number * 2, SUB, WIDE), BF16),
        compiler_params=params(),
        cost_estimate=cost(0.4 * number),
    )(pairs, linear(master_blocks))


def renew_body(which_ref, g_ref, m_ref, sl_ref, sr_ref, rl_ref, rr_ref, *refs):
    go_ref, lo_ref, ro_ref, mo_ref, place = refs[-5:]
    low = lanes_low(SUB)
    low_half = lanes_low(32)
    nothing = jnp.zeros((SUB, 128), F32)
    pairs = range(4)

    def diagonal(pair):
        return jnp.concatenate([jnp.where(low, pair, nothing), jnp.where(low, nothing, pair)], 0).astype(BF16)

    def mixed(even, odd):
        return (
            jnp.where(low_half, even, pltpu.roll(odd, SUB, 1)),
            jnp.where(low_half, pltpu.roll(even, SUB, 1), odd),
        )

    def natural(ref, pair, spot):
        even, odd = mixed(spread_of(ref, 2 * pair), spread_of(ref, 2 * pair + 1))
        spot[pl.ds(0, 32, stride=2), :] = even
        spot[pl.ds(1, 32, stride=2), :] = odd
        return spot[...]

    def spread(value, spot):
        spot[...] = value
        return mixed(spot[pl.ds(0, 32, stride=2), :], spot[pl.ds(1, 32, stride=2), :])

    tiles = [g_ref[pair // 2, :, (pair % 2) * 128 : (pair % 2 + 1) * 128] for pair in pairs]
    wide = [tile.astype(F32) for tile in tiles]
    grads = [diagonal(value) for value in wide]
    lefts = [natural(rl_ref, pair, place.at[pair, 0]).astype(BF16) for pair in pairs]
    rights = [diagonal(natural(rr_ref, pair, place.at[pair, 1])) for pair in pairs]
    halves = [dot(lefts[pair], grads[pair]).astype(BF16) for pair in pairs]
    left_parts = [dot(tiles[pair], grads[pair], NT) for pair in pairs]
    squares = [dot(tiles[pair], tiles[pair], TN) for pair in pairs]
    right_parts = [jnp.where(low, square[:SUB], square[SUB:]) for square in squares]
    steps = [dot(halves[pair], rights[pair]) for pair in pairs]
    for pair in pairs:
        made = [
            spread(value[pair], place.at[pair, 2 + k])
            for k, value in enumerate((wide, left_parts, right_parts, steps))
        ]
        for i in range(2):
            at = pl.ds(2 * pair + i, 32, stride=8)
            go_ref[at, :] = made[0][i]
            lo_ref[at, :] = STAT_DECAY * sl_ref[at, :] + (1.0 - STAT_DECAY) * made[1][i]
            ro_ref[at, :] = STAT_DECAY * sr_ref[at, :] + (1.0 - STAT_DECAY) * made[2][i]
            mo_ref[at, :] = m_ref[at, :] - WEIGHT_RATE * made[3][i]


def renew(which, owned, master_blocks, stat_left, stat_right, root_left, root_right, before):
    steps = which.shape[0]
    flat = pl.BlockSpec((256, 128), lambda i, which: (which[i], 0))
    shape = jax.ShapeDtypeStruct((master_blocks.shape[0] * 32, 128), F32)
    made = pl.pallas_call(
        renew_body,
        grid_spec=pltpu.PrefetchScalarGridSpec(
            num_scalar_prefetch=1,
            grid=(steps,),
            in_specs=[pl.BlockSpec((2, SUB, WIDE), lambda i, which: (i, 0, 0))]
            + [flat] * 5
            + [pl.BlockSpec(memory_space=pl.ANY)] * len(before),
            out_specs=[flat] * 4,
            scratch_shapes=[pltpu.VMEM((4, 6, SUB, 128), F32)],
        ),
        out_shape=[shape] * 4,
        input_output_aliases={7 + i: i for i in range(len(before))},
        compiler_params=params(),
        cost_estimate=cost(0.7 * steps),
    )(
        which,
        owned,
        *(linear(value) for value in (master_blocks, stat_left, stat_right, root_left, root_right)),
        *(linear(value) for value in before),
    )
    return [unlinear(value) for value in made]


def times(rows_in, w, base, r, g, part, col):
    first = base + part * r * g + col
    return dot(rows_in, jnp.concatenate([w[first + a * g] for a in range(r)], 0))


def times_back(d_ref, w, base, r, g, count, r4):
    total = None
    for part in range(count):
        first = base + (part * r + 4 * r4) * g
        wide = jnp.concatenate(
            [
                jnp.concatenate([w[first + a * g + col] for a in range(4)], 0)
                for col in range(g)
            ],
            1,
        )
        made = dot(d_ref[:, part * g * WIDE : (part + 1) * g * WIDE], wide, NT)
        total = made if total is None else total + made
    return total


def at256(i):
    return pl.ds(pl.multiple_of(i * WIDE, WIDE), WIDE)


def softmax_of(query, keys, scale, limit):
    scores = dot(query, keys, NT) * scale
    column = lax.broadcasted_iota(jnp.int32, scores.shape, 1)
    scores = jnp.where(column < limit, scores, MASK_FILL)
    raised = jnp.exp(scores - jnp.max(scores, 1, keepdims=True))
    return raised / jnp.sum(raised, 1, keepdims=True)


def score_grad(probs, dprobs):
    return (probs * (dprobs - jnp.sum(probs * dprobs, 1, keepdims=True))).astype(BF16)


def at128(i):
    return pl.ds(pl.multiple_of(i * 128, 128), 128)


def load(near, far, w, sems, pieces, base):
    started = []
    used = 0
    for i, which in enumerate(pieces):
        begin, count, r, g = TILES[which]
        end = begin + count * r * g
        copies = []
        for owner in range(begin // SHARD, (end - 1) // SHARD + 1):
            first = max(begin, owner * SHARD)
            last = min(end, (owner + 1) * SHARD)
            middle = min(max(owner * SHARD + FAR, first), last)
            for source, lo, hi, at in (
                (near, first, middle, owner * (2 * G_HALF) + first - owner * SHARD),
                (far, middle, last, owner * (SHARD - FAR) + middle - owner * SHARD - FAR),
            ):
                if lo < hi:
                    copies.append(
                        pltpu.make_async_copy(
                            source.at[pl.ds(at, hi - lo)],
                            w.at[pl.ds(base[i] + lo - begin, hi - lo)],
                            sems.at[used],
                        )
                    )
                    copies[-1].start()
                    used += 1
        started.append(copies)
    return started


def arrive(copies):
    for copy in copies:
        copy.wait()


def tiles_of(which):
    _, count, r, g = TILES[which]
    return count * r * g


def co_body(len_ref, xv_ref, xt_ref, near, far, cv_ref, ct_ref, fv_ref, ft_ref, w, sems):
    base = (0, tiles_of(0))
    copies = load(near, far, w, sems, (0, 6), base)
    for which, at, x_ref, o_ref, copy in (
        (0, base[0], xv_ref, cv_ref, copies[0]),
        (6, base[1], xt_ref, ct_ref, copies[1]),
    ):
        _, count, r, g = TILES[which]
        arrive(copy)

        def column(i, carry, at=at, r=r, g=g, x_ref=x_ref, o_ref=o_ref):
            o_ref[:, at256(i)] = times(x_ref[...], w, at, r, g, i // g, i % g).astype(BF16)
            return carry

        lax.fori_loop(0, count * g, column, 0, unroll=2)
    scale = HEAD ** (-0.5)
    reg = len_ref[2]
    heads = BI // HEAD
    def head(j, carry):
        for pair in range(2):
            vis = slice(pair * VIS_PAD, (pair + 1) * VIS_PAD)
            text = slice(pair * 128, (pair + 1) * 128)
            live = len_ref[pair]
            qv, kv, vv = (cv_ref[vis, at128(j + heads * s)] for s in range(3))
            qt, kt, vt = (ct_ref[text, at128(j + heads * s)] for s in range(3))
            fv_ref[vis, at128(j)] = dot(softmax_of(qv, kt, scale, live).astype(BF16), vt).astype(BF16)
            ft_ref[text, at128(j)] = dot(softmax_of(qt, kv, scale, reg).astype(BF16), vv).astype(BF16)
        return carry

    lax.fori_loop(0, heads, head, 0, unroll=2)


def co_forward(lengths, x_vis, x_text, near, far):
    return pl.pallas_call(
        co_body,
        in_specs=[pl.BlockSpec(memory_space=pltpu.SMEM)] + whole(2) + [pl.BlockSpec(memory_space=pl.ANY)] * 2,
        out_specs=whole(4),
        out_shape=[
            jax.ShapeDtypeStruct((x_vis.shape[0], 3 * BI), BF16),
            jax.ShapeDtypeStruct((x_text.shape[0], 3 * BI), BF16),
            jax.ShapeDtypeStruct((x_vis.shape[0], BI), BF16),
            jax.ShapeDtypeStruct((x_text.shape[0], BI), BF16),
        ],
        scratch_shapes=[
            pltpu.VMEM((tiles_of(0) + tiles_of(6), SUB, WIDE), BF16),
            pltpu.SemaphoreType.DMA((16,)),
        ],
        compiler_params=params(),
        cost_estimate=cost(22),
    )(lengths, x_vis, x_text, near, far)


def co_back_body(
    len_ref, cv_ref, ct_ref, dv_ref, dt_ref, rv_ref, rt_ref, near, far,
    gv_ref, gt_ref, ov_ref, ot_ref, w, sems,
):
    base = (0, tiles_of(0))
    copies = load(near, far, w, sems, (0, 6), base)
    scale = HEAD ** (-0.5)
    reg = len_ref[2]
    heads = BI // HEAD
    def head(j, carry):
        for pair in range(2):
            vis = slice(pair * VIS_PAD, (pair + 1) * VIS_PAD)
            text = slice(pair * 128, (pair + 1) * 128)
            live = len_ref[pair]
            qv, kv, vv = (cv_ref[vis, at128(j + heads * s)] for s in range(3))
            qt, kt, vt = (ct_ref[text, at128(j + heads * s)] for s in range(3))
            dv = dv_ref[vis, at128(j)]
            dt = dt_ref[text, at128(j)]
            probs = softmax_of(qv, kt, scale, live)
            ds = score_grad(probs, dot(dv, vt, NT))
            gv_ref[vis, at128(j)] = (dot(ds, kt) * scale).astype(BF16)
            gt_ref[text, at128(j + heads)] = (dot(ds, qv, TN) * scale).astype(BF16)
            gt_ref[text, at128(j + 2 * heads)] = dot(probs.astype(BF16), dv, TN).astype(BF16)
            probs = softmax_of(qt, kv, scale, reg)
            ds = score_grad(probs, dot(dt, vv, NT))
            gt_ref[text, at128(j)] = (dot(ds, kv) * scale).astype(BF16)
            gv_ref[vis, at128(j + heads)] = (dot(ds, qt, TN) * scale).astype(BF16)
            gv_ref[vis, at128(j + 2 * heads)] = dot(probs.astype(BF16), dt, TN).astype(BF16)
        return carry

    lax.fori_loop(0, heads, head, 0)
    for which, at, g_ref, r_ref, o_ref, copy in (
        (0, base[0], gv_ref, rv_ref, ov_ref, copies[0]),
        (6, base[1], gt_ref, rt_ref, ot_ref, copies[1]),
    ):
        _, count, r, g = TILES[which]
        arrive(copy)

        def rows4(i, carry, at=at, r=r, g=g, count=count, g_ref=g_ref, r_ref=r_ref, o_ref=o_ref):
            o_ref[:, at256(i)] = r_ref[:, at256(i)] + times_back(g_ref, w, at, r, g, count, i)
            return carry

        lax.fori_loop(0, r // 4, rows4, 0)


def co_backward(lengths, co_vis, co_text, dvis, dtext, resid_vis, resid_text, near, far):
    return pl.pallas_call(
        co_back_body,
        in_specs=[pl.BlockSpec(memory_space=pltpu.SMEM)] + whole(6) + [pl.BlockSpec(memory_space=pl.ANY)] * 2,
        out_specs=whole(4),
        out_shape=[
            jax.ShapeDtypeStruct(co_vis.shape, BF16),
            jax.ShapeDtypeStruct(co_text.shape, BF16),
            jax.ShapeDtypeStruct(resid_vis.shape, F32),
            jax.ShapeDtypeStruct(resid_text.shape, F32),
        ],
        scratch_shapes=[
            pltpu.VMEM((tiles_of(0) + tiles_of(6), SUB, WIDE), BF16),
            pltpu.SemaphoreType.DMA((16,)),
        ],
        compiler_params=params(),
        cost_estimate=cost(23),
    )(lengths, co_vis, co_text, dvis, dtext, resid_vis, resid_text, near, far)


def erf_parts(value):
    return 0.5 * (1.0 + lax.erf(value * 0.7071067811865476))


def middle_body(
    config,
    len_ref, ctx_ref, x_ref, cot_ref, norm_ref, near, far,
    out_ref, first_ref, act_ref, second_ref, sctx_ref,
    fback_ref, pback_ref, bback_ref, dself_ref, tback_ref,
    resid_ref, dctx_ref, sums_ref,
    w, sems, pre, n1, n2, n3, s1, s2, s3, wide, acc, selfs, probs, stat,
):
    begin, rows, span, head, chunk = config
    width = x_ref.shape[1]
    base = []
    at = 0
    for which in range(begin, begin + 5):
        base.append(at)
        at += tiles_of(which)
    copies = load(near, far, w, sems, tuple(range(begin, begin + 5)), base)
    shapes = [TILES[which][1:] for which in range(begin, begin + 5)]
    steps = rows // chunk

    def at_chunk(i):
        return pl.ds(pl.multiple_of(i * chunk, chunk), chunk)

    def norm(resid, which, i, kept, scales):
        mean = jnp.mean(resid, 1, keepdims=True)
        centered = resid - mean
        scale = lax.rsqrt(jnp.mean(centered * centered, 1, keepdims=True) + NORM_EPSILON)
        normed = centered * scale
        kept[at_chunk(i), :] = normed
        scales[at_chunk(i), :] = jnp.broadcast_to(scale, (chunk, 128))
        return normed * norm_ref[0, which : which + 1, :] + norm_ref[1, which : which + 1, :]

    def eight(value):
        return jnp.sum(value.reshape(chunk // 8, 8, width), 0)

    def norm_back(upstream, which, i, kept, scales):
        normed = kept[at_chunk(i), :]
        stat[which] = stat[which] + eight(upstream * normed)
        stat[3 + which] = stat[3 + which] + eight(upstream)
        scaled = upstream * norm_ref[0, which : which + 1, :]
        return scales[at_chunk(i), 0:1] * (
            scaled
            - jnp.mean(scaled, 1, keepdims=True)
            - normed * jnp.mean(scaled * normed, 1, keepdims=True)
        )

    def loop(count, body, unroll=1):
        lax.fori_loop(0, count, lambda i, carry: (body(i), carry)[1], 0, unroll=unroll)

    stat[...] = jnp.zeros(stat.shape, F32)
    count, r, g = shapes[0]
    arrive(copies[0])

    def co_out(i):
        wide[:, at256(i)] = times(ctx_ref[...], w, base[0], r, g, 0, i)

    loop(g, co_out)

    def norm_one(i):
        value = norm(wide[at_chunk(i), :] + x_ref[at_chunk(i), :].astype(F32), 0, i, n1, s1)
        wide[at_chunk(i), :] = value
        first_ref[at_chunk(i), :] = value.astype(BF16)

    loop(steps, norm_one, 2 if steps % 2 == 0 else steps)
    _, r_up, g_up = shapes[1]
    _, r_down, g_down = shapes[2]
    arrive(copies[1])
    arrive(copies[2])
    acc[...] = jnp.zeros(acc.shape, F32)

    def down_rows(i):
        return jnp.concatenate(
            [
                jnp.concatenate([w[base[2] + (4 * i + a) * g_down + col] for a in range(4)], 0)
                for col in range(g_down)
            ],
            1,
        )

    def feed(i):
        value = times(first_ref[...], w, base[1], r_up, g_up, 0, i)
        part = erf_parts(value)
        pre[i] = part + value * (0.3989422804014327 * jnp.exp(-0.5 * value * value))
        act = (value * part).astype(BF16)
        act_ref[:, at256(i)] = act
        acc[...] += dot(act, down_rows(i))

    loop(g_up, feed, 2)

    def norm_two(i):
        value = norm(wide[at_chunk(i), :] + acc[at_chunk(i), :], 1, i, n2, s2)
        wide[at_chunk(i), :] = value
        second_ref[at_chunk(i), :] = value.astype(BF16)

    loop(steps, norm_two, 2 if steps % 2 == 0 else steps)
    count_s, r_s, g_s = shapes[3]
    arrive(copies[3])

    def self_in(i):
        selfs[:, at256(i)] = times(second_ref[...], w, base[3], r_s, g_s, i // g_s, i % g_s).astype(BF16)

    loop(count_s * g_s, self_in, 3)
    scale = head ** (-0.5)
    groups = width // 128
    per = 128 // head
    pairs = rows // span

    def halves(values):
        if per == 1:
            return values[0]
        low = lax.broadcasted_iota(jnp.int32, values[0].shape, 1) < head
        return jnp.where(low, values[0], values[1])

    def only(value, h):
        if per == 1:
            return value
        low = lax.broadcasted_iota(jnp.int32, value.shape, 1) < head
        keep = low if h == 0 else jnp.logical_not(low)
        return jnp.where(keep, value, jnp.zeros_like(value))

    def attend(j):
        for pair in range(pairs):
            own = slice(pair * span, (pair + 1) * span)
            live = len_ref[pair]
            q, k, v = (selfs[own, at128(j + groups * s)] for s in range(3))
            found = []
            for h in range(per):
                p = softmax_of(only(q, h), k, scale, live)
                probs[(pair * groups + j) * per + h] = p
                found.append(dot(p.astype(BF16), v))
            sctx_ref[own, at128(j)] = halves(found).astype(BF16)

    loop(groups, attend)
    _, r_o, g_o = shapes[4]
    arrive(copies[4])

    def self_out(i):
        acc[:, at256(i)] = times(sctx_ref[...], w, base[4], r_o, g_o, 0, i)

    loop(g_o, self_out)

    def norm_three(i):
        value = norm(wide[at_chunk(i), :] + acc[at_chunk(i), :], 2, i, n3, s3)
        out_ref[at_chunk(i), :] = value.astype(BF16)
        third = norm_back(cot_ref[at_chunk(i), :].astype(F32), 2, i, n3, s3)
        wide[at_chunk(i), :] = third
        tback_ref[at_chunk(i), :] = third.astype(BF16)

    loop(steps, norm_three, 2 if steps % 2 == 0 else steps)

    def self_out_back(i):
        dctx_ref[:, at256(i)] = times_back(tback_ref, w, base[4], r_o, g_o, 1, i).astype(BF16)

    loop(r_o // 4, self_out_back)
    def attend_back(j):
        for pair in range(pairs):
            own = slice(pair * span, (pair + 1) * span)
            q, k, v = (selfs[own, at128(j + groups * s)] for s in range(3))
            up = dctx_ref[own, at128(j)]
            dq, dk, dv = [], [], []
            for h in range(per):
                p = probs[(pair * groups + j) * per + h]
                ds = score_grad(p, dot(only(up, h), v, NT))
                dq.append(dot(ds, k))
                dk.append(dot(ds, q, TN))
                dv.append(dot(p.astype(BF16), up, TN))
            dself_ref[own, at128(j)] = (halves(dq) * scale).astype(BF16)
            dself_ref[own, at128(j + groups)] = (halves(dk) * scale).astype(BF16)
            dself_ref[own, at128(j + 2 * groups)] = halves(dv).astype(BF16)

    loop(groups, attend_back)

    def self_in_back(i):
        acc[:, at256(i)] = times_back(dself_ref, w, base[3], r_s, g_s, count_s, i)

    loop(r_s // 4, self_in_back)

    def norm_two_back(i):
        value = norm_back(wide[at_chunk(i), :] + acc[at_chunk(i), :], 1, i, n2, s2)
        wide[at_chunk(i), :] = value
        bback_ref[at_chunk(i), :] = value.astype(BF16)

    loop(steps, norm_two_back, 2 if steps % 2 == 0 else steps)

    def feed_back(i):
        act_grad = dot(bback_ref[...], down_rows(i), NT)
        pback_ref[:, at256(i)] = (act_grad * pre[i]).astype(BF16)

    loop(g_up, feed_back, 2)

    def up_back(i):
        acc[:, at256(i)] = times_back(pback_ref, w, base[1], r_up, g_up, 1, i)

    loop(r_up // 4, up_back)

    def norm_one_back(i):
        value = norm_back(wide[at_chunk(i), :] + acc[at_chunk(i), :], 0, i, n1, s1)
        resid_ref[at_chunk(i), :] = value
        fback_ref[at_chunk(i), :] = value.astype(BF16)

    loop(steps, norm_one_back, 2 if steps % 2 == 0 else steps)

    def co_out_back(i):
        dctx_ref[:, at256(i)] = times_back(fback_ref, w, base[0], r, g, 1, i).astype(BF16)

    loop(r // 4, co_out_back)
    sums_ref[...] = jnp.sum(stat[...], 1)


def middle(begin, lengths, context, x, cot, norms, near, far, span, head, chunk):
    rows, width = x.shape
    hidden = TILES[begin + 1][3] * WIDE
    number = sum(tiles_of(which) for which in range(begin, begin + 5))
    low = lambda columns: jax.ShapeDtypeStruct((rows, columns), BF16)
    return pl.pallas_call(
        functools.partial(middle_body, (begin, rows, span, head, chunk)),
        in_specs=[pl.BlockSpec(memory_space=pltpu.SMEM)] + whole(4) + [pl.BlockSpec(memory_space=pl.ANY)] * 2,
        out_specs=whole(13),
        out_shape=[
            low(width), low(width), low(hidden), low(width), low(width),
            low(width), low(hidden), low(width), low(3 * width), low(width),
            jax.ShapeDtypeStruct((rows, width), F32), low(BI),
            jax.ShapeDtypeStruct((6, width), F32),
        ],
        scratch_shapes=[
            pltpu.VMEM((number, SUB, WIDE), BF16),
            pltpu.SemaphoreType.DMA((24,)),
            pltpu.VMEM((hidden // WIDE, rows, WIDE), F32),
        ]
        + [pltpu.VMEM((rows, width), F32)] * 3
        + [pltpu.VMEM((rows, 128), F32)] * 3
        + [pltpu.VMEM((rows, width), F32)] * 2
        + [
            pltpu.VMEM((rows, 3 * width), BF16),
            pltpu.VMEM((rows // span * (width // head), span, span), F32),
            pltpu.VMEM((6, 8, width), F32),
        ],
        compiler_params=params(),
        cost_estimate=cost(40),
    )(lengths, context, x, cot, norms, near, far)


def weight_body(kinds, *refs):
    n = len(kinds)
    lefts, rights = refs[:n], refs[n : 2 * n]
    out, stage, across, sems = refs[2 * n :]
    offset = 0
    for which, a_ref, b_ref in zip(kinds, lefts, rights):
        _, count, r, g = TILES[which]
        size = 4 * g

        def copy(i, slot, offset=offset, size=size):
            return pltpu.make_async_copy(
                stage.at[slot, pl.ds(0, size)], out.at[pl.ds(offset + i * size, size)], sems.at[slot]
            )

        total = count * (r // 4)

        def step(i, carry, a_ref=a_ref, b_ref=b_ref, r=r, g=g, copy=copy):
            slot = lax.rem(i, 4)

            @pl.when(i >= 4)
            def _():
                copy(i - 4, slot).wait()

            part = i // (r // 4)
            r4 = lax.rem(i, r // 4)
            across[...] = jnp.transpose(a_ref[:, at256(r4)])
            left = across[...]
            for col in range(g):
                made = dot(left, b_ref[:, at256(part * g + col)]).astype(BF16)
                for a in range(4):
                    stage[slot, a * g + col] = made[a * SUB : (a + 1) * SUB]
            copy(i, slot).start()
            return carry

        lax.fori_loop(0, total, step, 0)
        for i in range(max(0, total - 4), total):
            copy(i, i % 4).wait()
        offset += count * r * g


def weight_grads(kinds, lefts, rights):
    number = sum(tiles_of(which) for which in kinds)
    most = max(4 * TILES[which][3] for which in kinds)
    return pl.pallas_call(
        functools.partial(weight_body, kinds),
        in_specs=whole(2 * len(kinds)),
        out_specs=pl.BlockSpec(memory_space=pl.ANY),
        out_shape=jax.ShapeDtypeStruct((number, SUB, WIDE), BF16),
        scratch_shapes=[
            pltpu.VMEM((4, most, SUB, WIDE), BF16),
            pltpu.VMEM((WIDE, lefts[0].shape[0]), BF16),
            pltpu.SemaphoreType.DMA((4,)),
        ],
        compiler_params=params(),
        cost_estimate=cost(number * 0.04),
    )(*lefts, *rights)


def spot():
    dp = lax.axis_index("dp")
    seq = lax.axis_index("seq")
    return dp // 2, dp % 2, seq // 2, seq % 2


def along_z(value, moves):
    return lax.ppermute(value, "dp", [(2 * a + x, 2 * b + x) for a, b in moves for x in (0, 1)])


def cut(value, begin, size):
    return lax.dynamic_slice_in_dim(value, begin, size, 0)


def join(parts):
    return jnp.concatenate(parts) if len(parts) > 1 else parts[0]


def add(left, right):
    return (left.astype(F32) + right.astype(F32)).astype(BF16)


def by_y(y, mine, other):
    return [jnp.where(y == 0, mine, other), jnp.where(y == 0, other, mine)]


def blank(shape):
    return pl.pallas_call(
        lambda out: None,
        out_specs=pl.BlockSpec(memory_space=pl.ANY),
        out_shape=jax.ShapeDtypeStruct(shape, BF16),
        compiler_params=params(),
    )()


def gather_tiles(master_blocks):
    z, x, y, core = spot()
    lone, both, half = G_LONE // 2, (G_HALF - 2 * G_LONE) // 2, G_HALF // 2
    fourth = (SHARD - FAR) // 4
    mine = prep(
        master_blocks,
        jnp.concatenate(
            [half * core + lone * y + jnp.arange(lone), half * core + 2 * lone + jnp.arange(both)]
        ).astype(jnp.int32),
    )
    last = prep(
        master_blocks,
        ((FAR + fourth * lax.axis_index("seq")) // 2 + jnp.arange(fourth // 2)).astype(jnp.int32),
    )
    far = lax.all_gather(last, ("dp", "seq"), axis=0, tiled=True)
    ring = [(0, 1), (1, 2), (2, 3), (3, 0)]
    near = blank((8, 2 * G_HALF, SUB, WIDE))
    rows = [mine]
    cross = []
    halves = []
    for phase in range(6):
        out = {}
        if phase < 3:
            out["z"] = along_z(rows[phase], ring)
        if phase < 4:
            out["x"] = lax.ppermute(rows[phase], "dp", SWAP_X)
        if 1 <= phase < 5:
            here = [rows[phase - 1], cross[phase - 1]]
            out["y"] = lax.ppermute(join([part[:G_LONE] for part in here]), "seq", SWAP_Y)
        if phase >= 2:
            out["core"] = lax.ppermute(join(halves[phase - 2]), "seq", SWAP_CORE)
        out, rows, cross, halves = lax.optimization_barrier((out, rows, cross, halves))
        if "z" in out:
            rows = rows + [out["z"]]
        if "x" in out:
            cross = cross + [out["x"]]
        if "y" in out:
            halves = halves + [
                [
                    join(by_y(y, part[:G_LONE], out["y"][G_LONE * i : G_LONE * (i + 1)]) + [part[G_LONE:]])
                    for i, part in enumerate(here)
                ]
            ]
        if "core" in out:
            step = phase - 2
            for side in range(2):
                owner = 2 * ((z - step) % 4) + (x + side) % 2
                own = halves[step][side][None]
                got = out["core"][None, G_HALF * side : G_HALF * (side + 1)]
                near = lax.dynamic_update_slice(near, own, (owner, G_HALF * core, 0, 0))
                near = lax.dynamic_update_slice(near, got, (owner, G_HALF * (1 - core), 0, 0))
    return near.reshape(-1, SUB, WIDE), far


ROUTES = (
    (((3, 2),), ((2, 1),), ((1, 0),)),
    (((3, 2), (0, 1)), ((2, 1),)),
    (((0, 1), (3, 2)), ((1, 2),)),
    (((0, 1),), ((1, 2),), ((2, 3),)),
)
LONE = R_LONE // CHUNKS
BOTH = (R_HALF - 2 * R_LONE) // CHUNKS


def chunk_pairs(k):
    table = []
    for core in range(2):
        begin = R_STEP * core // 2
        for y in range(2):
            table += [begin + (R_LONE * y + LONE * k) // 2 + i for i in range(LONE // 2)]
        table += [begin + R_LONE + BOTH * k // 2 + i for i in range(BOTH // 2)]
    return jnp.asarray(table, jnp.int32)


class Sums:
    def __init__(self):
        self.at = spot()
        self.state = {}

    def group(self, zi, place):
        pair = (2 * zi, 2 * zi + 1)

        def part(o, core, begin, size):
            array, offset = place[o]
            begin += offset + R_STEP * core
            return array[begin : begin + size]

        lone = jnp.concatenate(
            [part(o, core, R_LONE * y, R_LONE) for y in range(2) for core in range(2) for o in pair]
        )
        lone = lax.psum_scatter(lone, "seq", scatter_dimension=0, tiled=True)
        self.state["lone", zi] = lone.reshape(2, R_LONE, SUB, WIDE)
        self.state["both", zi] = tuple(place[o] for o in pair)

    def both_of(self, zi, core):
        size = R_HALF - 2 * R_LONE
        return jnp.stack(
            [cut(array, offset + R_STEP * core + 2 * R_LONE, size) for array, offset in self.state["both", zi]]
        )

    def send(self, task):
        z, x, y, core = self.at
        state = self.state
        kind, who = task[0], task[1]
        if kind == "C":
            array, offset = state["place", who]
            return lax.ppermute(cut(array, offset + R_STEP * (1 - core), R_HALF), "seq", SWAP_CORE)
        if kind == "B":
            return lax.ppermute(self.both_of(who, 1 - core), "seq", SWAP_CORE)
        if kind == "Y":
            k = task[2]
            return lax.ppermute(
                jnp.stack([cut(state["half", o], R_LONE * (1 - y) + LONE * k, LONE) for o in (2 * who, 2 * who + 1)]),
                "seq",
                SWAP_Y,
            )
        if kind == "X":
            lone, both = state["kept", who, task[2]]
            return lax.ppermute(join([cut(lone, 1 - x, 1)[0], cut(both, 1 - x, 1)[0]]), "dp", SWAP_X)
        if kind == "Z":
            return along_z(state["value", who, task[2]], ROUTES[who][task[3]])
        if kind == "F":
            values = [state["value", zi, who] for zi in range(4)]
            mine = jnp.where(z == 0, values[0], jnp.where(z == 1, values[1], jnp.where(z == 2, values[2], values[3])))
            state["mine", who] = mine
            return lax.ppermute(mine, "seq", SWAP_Y)
        if kind == "G":
            return lax.ppermute(state["whole", who], "seq", SWAP_CORE)
        axis, step = (("seq", 1), ("seq", 2), ("dp", 1), ("dp", 2), ("dp", 4))[who]
        size = lax.axis_size(axis)
        return lax.ppermute(state["norms", 0], axis, [(i, i ^ step) for i in range(size)])

    def take(self, task, got):
        z, x, y, core = self.at
        state = self.state
        kind, who = task[0], task[1]
        if kind == "C":
            array, offset = state["place", who]
            state["half", who] = add(cut(array, offset + R_STEP * core, R_HALF), got)
        elif kind == "B":
            both = add(self.both_of(who, core), got)
            lone = state.pop(("lone", who))
            state.pop(("both", who))
            for k in range(CHUNKS):
                state["kept", who, k] = (
                    lone[:, LONE * k : LONE * (k + 1)],
                    both[:, BOTH * k : BOTH * (k + 1)],
                )
        elif kind == "Y":
            k = task[2]
            halves = [state["half", o] for o in (2 * who, 2 * who + 1)]
            lone = add(jnp.stack([cut(h, R_LONE * y + LONE * k, LONE) for h in halves]), got)
            both = jnp.stack([h[2 * R_LONE + BOTH * k : 2 * R_LONE + BOTH * (k + 1)] for h in halves])
            state["kept", who, k] = (lone, both)
        elif kind == "X":
            lone, both = state.pop(("kept", who, task[2]))
            state["value", who, task[2]] = add(join([cut(lone, x, 1)[0], cut(both, x, 1)[0]]), got)
        elif kind == "Z":
            state["value", who, task[2]] = add(state["value", who, task[2]], got)
        elif kind == "F":
            mine = state.pop(("mine", who))
            state["whole", who] = join(by_y(y, mine[:LONE], got[:LONE]) + [add(mine[LONE:], got[LONE:])])
        elif kind == "G":
            half = state.pop(("whole", who))
            state["owned", who] = join([jnp.where(core == 0, half, got), jnp.where(core == 0, got, half)])
        else:
            state["norms", 0] = state["norms", 0] + got

    def step(self, tasks, beside=None):
        out = [self.send(task) for task in tasks]
        work = beside() if beside is not None else ()
        fixed = {key: value for key, value in self.state.items() if key[0] in ("place", "both")}
        moving = {key: value for key, value in self.state.items() if key not in fixed}
        out, work, moving = lax.optimization_barrier((out, work, moving))
        self.state = {**moving, **fixed}
        for task, got in zip(tasks, out):
            self.take(task, got)
        return work


def pad_regions(value, pairs):
    reg = value.shape[0] // pairs
    cube = value.reshape(pairs, reg, value.shape[1])
    return jnp.pad(cube, ((0, 0), (0, VIS_PAD - reg), (0, 0))).reshape(pairs * VIS_PAD, -1)


def cut_regions(value, pairs, reg):
    return value.reshape(pairs, VIS_PAD, -1)[:, :reg].reshape(pairs * reg, -1)


def fast_shards(
    x_text, x_vis, caption_len, cot_text, cot_vis, master_blocks,
    stat_left, stat_right, root_left, root_right, norm_params, norm_second,
):
    pairs = caption_len.shape[0]
    reg = x_vis.shape[0] // pairs
    near, far = gather_tiles(master_blocks)
    lengths = jnp.concatenate([caption_len, jnp.full((2,), reg, jnp.int32)])
    regions = jnp.full((2,), reg, jnp.int32)
    xv = pad_regions(x_vis, pairs)
    cv = pad_regions(cot_vis, pairs)
    vis_norms = norm_params[:, : 3 * VIS].reshape(2, 3, VIS)
    text_norms = norm_params[:, 3 * VIS :].reshape(2, 3, TXT)
    co_vis, co_text, vis_ctx, text_ctx = co_forward(lengths, xv, x_text, near, far)
    (out_vis, v_first, v_act, v_second, v_sctx, v_fback, v_pback, v_bback, v_dself, v_tback,
     v_resid, v_dctx, v_sums) = middle(1, regions, vis_ctx, xv, cv, vis_norms, near, far, VIS_PAD, HEAD_V, 32)
    vis_mid = weight_grads(
        (1, 2, 3, 4, 5), (vis_ctx, v_first, v_act, v_second, v_sctx),
        (v_fback, v_pback, v_bback, v_dself, v_tback),
    )
    sums = Sums()
    vis_at = TILES[1][0]
    text_at = TILES[7][0]
    sums.group(1, {o: (vis_mid, SHARD * o - vis_at) for o in (2, 3)})
    (out_text, t_first, t_act, t_second, t_sctx, t_fback, t_pback, t_bback, t_dself, t_tback,
     t_resid, t_dctx, t_sums) = middle(
        7, lengths, text_ctx, x_text, cot_text, text_norms, near, far, x_text.shape[0] // pairs, HEAD_T, 32
    )
    sums.state["norms", 0] = jnp.concatenate([v_sums.reshape(2, -1), t_sums.reshape(2, -1)], 1)
    lefts = (text_ctx, t_first, t_act, t_second, t_sctx)
    rights = (t_fback, t_pback, t_bback, t_dself, t_tback)
    later = sums.state.pop(("lone", 1))
    lefts, rights, later = sums.step([], lambda: (lefts, rights, later))
    sums.state["lone", 1] = later
    sums.step([("B", 1)])
    text_mid, back = sums.step(
        [("X", 1, 0)],
        lambda: (
            weight_grads((7, 8, 9, 10, 11), lefts, rights),
            (co_vis, co_text, v_dctx, t_dctx, v_resid, t_resid),
        ),
    )
    sums.group(3, {o: (text_mid, SHARD * o - text_at) for o in (6, 7)})
    later = sums.state.pop(("lone", 3))
    dco_vis, dco_text, grad_vis, grad_text = sums.step(
        [("X", 1, 1), ("Z", 1, 0, 0)], lambda: co_backward(lengths, *back, near, far)
    )
    vis_co, text_co = sums.step(
        [("Z", 1, 1, 0), ("Z", 1, 0, 1)],
        lambda: (weight_grads((0,), (xv,), (dco_vis,)), weight_grads((6,), (x_text,), (dco_text,))),
    )
    sums.state["lone", 3] = later
    sums.state["place", 0] = (vis_co, 0)
    sums.state["place", 1] = (jnp.concatenate([vis_co[SHARD:], vis_mid[: 2 * SHARD - vis_at]]), 0)
    sums.state["place", 4] = (
        jnp.concatenate([vis_mid[4 * SHARD - vis_at :], text_co, text_mid[: 5 * SHARD - text_at]]), 0
    )
    sums.state["place", 5] = (text_mid, 5 * SHARD - text_at)
    for tasks in (
        [("C", 0), ("C", 1), ("B", 3), ("Z", 1, 1, 1), ("N", 0)],
        [("C", 4), ("C", 5), ("Y", 0, 0), ("X", 3, 0)],
        [("Y", 2, 0), ("X", 0, 0), ("Z", 3, 0, 0), ("N", 1)],
        [("Y", 0, 1), ("X", 2, 0), ("Z", 3, 0, 1), ("Z", 0, 0, 0), ("N", 2)],
        [("Y", 2, 1), ("X", 3, 1), ("Z", 3, 0, 2), ("Z", 0, 0, 1), ("Z", 2, 0, 0)],
        [("X", 0, 1), ("Z", 3, 1, 0), ("Z", 0, 0, 2), ("Z", 2, 0, 1), ("N", 3)],
        [("F", 0), ("X", 2, 1), ("Z", 3, 1, 1), ("Z", 0, 1, 0), ("N", 4)],
        [("G", 0), ("Z", 3, 1, 2), ("Z", 0, 1, 1), ("Z", 2, 1, 0)],
    ):
        sums.step(tasks)
    statistics = (master_blocks, stat_left, stat_right, root_left, root_right)
    early = chunk_pairs(0)
    count = early.shape[0] // 2
    renewed = sums.step(
        [("Z", 0, 1, 2), ("Z", 2, 1, 1)],
        lambda: renew(early[:count], sums.state["owned", 0][: 2 * count], *statistics, ()),
    )
    renewed = sums.step(
        [("F", 1)],
        lambda: renew(early[count:], sums.state["owned", 0][2 * count :], *statistics, renewed),
    )
    sums.step([("G", 1)])
    grad_blocks, left_new, right_new, master_new = renew(
        chunk_pairs(1), sums.state["owned", 1], *statistics, renewed
    )
    norm_grads = sums.state["norms", 0]
    second_new = STAT_DECAY * norm_second + (1.0 - STAT_DECAY) * norm_grads * norm_grads
    norm_new = norm_params - NORM_RATE * norm_grads / (jnp.sqrt(second_new) + MOMENT_EPSILON)
    return (
        out_text,
        cut_regions(out_vis, pairs, reg),
        grad_text,
        cut_regions(grad_vis, pairs, reg),
        grad_blocks,
        left_new,
        right_new,
        master_new,
        norm_grads,
        second_new,
        norm_new,
    )


def fits(mesh):
    return mesh.shape["dp"] == 8 and mesh.shape["seq"] == 4


def solution(mesh):
    placed = (
        P(("dp", "seq"), None),
        P(("dp", "seq"), None),
        P(("dp", "seq")),
        P(("dp", "seq"), None),
        P(("dp", "seq"), None),
        P("dp", None),
        P("dp", None),
        P("dp", None),
        P("dp", None),
        P("dp", None),
        P(),
        P(),
    )
    step = fast_shards if fits(mesh) else shards
    return jax.shard_map(
        step,
        mesh=mesh,
        in_specs=placed,
        out_specs=(
            P(("dp", "seq"), None),
            P(("dp", "seq"), None),
            P(("dp", "seq"), None),
            P(("dp", "seq"), None),
            P("dp", None),
            P("dp", None),
            P("dp", None),
            P("dp", None),
            P(),
            P(),
            P(),
        ),
        check_vma=False,
    )
```

```python
import functools

import jax
import jax.numpy as jnp
from jax import lax
from jax.experimental import pallas as pl
from jax.experimental.pallas import tpu as pltpu
from jax.sharding import PartitionSpec as P

TXT = 768
VIS = 1024
BI = 1024
FFT = 3072
FFV = 1024
HEAD = 128
HEAD_T = 64
HEAD_V = 128
BLK = 64


MASK_FILL = -1000000000.0
STAT_DECAY = 0.9
WEIGHT_RATE = 0.3
NORM_RATE = 0.2
NORM_EPSILON = 1e-05
MOMENT_EPSILON = 1e-08
HIGHEST = lax.Precision.HIGHEST
CONTRACT_COLS = (((1,), (1,)), ((), ()))


def weight_layout():
    return (
        (VIS, BI, 3),
        (BI, VIS, 1),
        (VIS, FFV, 1),
        (FFV, VIS, 1),
        (VIS, VIS, 3),
        (VIS, VIS, 1),
        (TXT, BI, 3),
        (BI, TXT, 1),
        (TXT, FFT, 1),
        (FFT, TXT, 1),
        (TXT, TXT, 3),
        (TXT, TXT, 1),
    )


def unpack_weights(flat):
    size = BLK
    blocks = flat.reshape(flat.shape[0], size, size)
    begin = 0
    matrices = []
    for rows, columns, count in weight_layout():
        number = count * rows * columns // (size * size)
        shaped = blocks[begin : begin + number].reshape(
            count, rows // size, columns // size, size, size
        )
        matrices.append(shaped.transpose(1, 3, 0, 2, 4).reshape(rows, count * columns))
        begin += number
    return matrices


def block_grad(inputs, grads, count):
    size = BLK
    left = inputs.reshape(inputs.shape[0], inputs.shape[1] // size, size)
    right = grads.reshape(grads.shape[0], count, grads.shape[1] // (count * size), size)
    return jnp.einsum("nai,nkbj->kabij", left, right, preferred_element_type=jnp.float32).reshape(
        -1, size * size
    )


def norm_columns(values, stream, which):
    if stream == 0:
        begin = which * VIS
        width = VIS
    else:
        begin = 3 * VIS + which * TXT
        width = TXT
    return values[:, begin : begin + width]


def gelu_exact(value):
    return jax.nn.gelu(value, approximate=False)


def heads_of(side, which, head):
    part = side[:, :, which, :]
    return part.reshape(part.shape[0], part.shape[1], part.shape[2] // head, head)


def scores_of(query, keys, live, head):
    scores = jnp.einsum(
        "gqhd,gkhd->ghqk", query, keys, preferred_element_type=jnp.float32
    ) * head ** (-0.5)
    if live is not None:
        scores = jnp.where(live[:, None, None, :], scores, MASK_FILL)
    return scores


def attend_one(query, keys, values, live, head):
    scores = scores_of(query, keys, live, head)
    top = jnp.max(scores, axis=3, keepdims=True)
    raised = jnp.exp(scores - top)
    total = jnp.sum(raised, axis=3, keepdims=True)
    found = jnp.einsum(
        "ghqk,gkhd->gqhd",
        (raised / total).astype(jnp.bfloat16),
        values,
        preferred_element_type=jnp.float32,
    ).astype(jnp.bfloat16)
    return (found.reshape(found.shape[0], found.shape[1], -1), top + jnp.log(total))


def attend_one_back(query, keys, values, live, head, logsum, dfound):
    scale = head ** (-0.5)
    probs = jnp.exp(scores_of(query, keys, live, head) - logsum)
    upstream = dfound.reshape(dfound.shape[0], dfound.shape[1], -1, head)
    dprobs = jnp.einsum("gqhd,gkhd->ghqk", upstream, values, preferred_element_type=jnp.float32)
    dvalues = jnp.einsum(
        "ghqk,gqhd->gkhd", probs.astype(jnp.bfloat16), upstream, preferred_element_type=jnp.float32
    )
    dscores = (probs * (dprobs - jnp.sum(probs * dprobs, axis=3, keepdims=True))).astype(
        jnp.bfloat16
    )
    dquery = (
        jnp.einsum("ghqk,gkhd->gqhd", dscores, keys, preferred_element_type=jnp.float32) * scale
    )
    dkeys = (
        jnp.einsum("ghqk,gqhd->gkhd", dscores, query, preferred_element_type=jnp.float32) * scale
    )
    return (dquery, dkeys, dvalues)


def attention_plan(vis_side, text_side, lengths, cross):
    live = (
        lax.broadcasted_iota(jnp.int32, (lengths.shape[0], text_side.shape[1]), 1)
        < lengths[:, None]
    )
    if cross:
        return ((vis_side, text_side, live, HEAD), (text_side, vis_side, None, HEAD))
    return ((vis_side, vis_side, None, HEAD_V), (text_side, text_side, live, HEAD_T))


def pair_attend(vis_side, text_side, lengths, cross):
    results = []
    for query_side, key_side, live, head in attention_plan(vis_side, text_side, lengths, cross):
        results.append(
            attend_one(
                heads_of(query_side, 0, head),
                heads_of(key_side, 1, head),
                heads_of(key_side, 2, head),
                live,
                head,
            )
        )
    return (results[0][0], results[1][0], results[0][1], results[1][1])


def pair_attend_back(
    vis_side, text_side, lengths, cross, vis_logsum, text_logsum, vis_dfound, text_dfound
):
    plan = attention_plan(vis_side, text_side, lengths, cross)
    parts = []
    for (query_side, key_side, live, head), logsum, dfound in zip(
        plan, (vis_logsum, text_logsum), (vis_dfound, text_dfound)
    ):
        parts.append(
            attend_one_back(
                heads_of(query_side, 0, head),
                heads_of(key_side, 1, head),
                heads_of(key_side, 2, head),
                live,
                head,
                logsum,
                dfound,
            )
        )
    if cross:
        vis_parts = (parts[0][0], parts[1][1], parts[1][2])
        text_parts = (parts[1][0], parts[0][1], parts[0][2])
    else:
        vis_parts = parts[0]
        text_parts = parts[1]
    vis_grad = jnp.stack(vis_parts, axis=2).reshape(vis_side.shape).astype(jnp.bfloat16)
    text_grad = jnp.stack(text_parts, axis=2).reshape(text_side.shape).astype(jnp.bfloat16)
    return (vis_grad, text_grad)


def to_heads(vis_side, text_side):
    return (vis_side, text_side)


def from_heads(vis_found, text_found):
    return (vis_found, text_found)


def dfound_to_heads(vis_dfound, text_dfound):
    return (vis_dfound, text_dfound)


def grads_from_heads(vis_grad, text_grad):
    return (vis_grad, text_grad)


def side_of(rows_in, weight, pairs):
    made = jnp.dot(rows_in, weight, preferred_element_type=jnp.float32).astype(jnp.bfloat16)
    return made.reshape(pairs, -1, 3, weight.shape[1] // 3)


def norm_forward(resid, columns):
    mean = jnp.mean(resid, -1, keepdims=True)
    centered = resid - mean
    scale = lax.rsqrt(jnp.mean(centered * centered, -1, keepdims=True) + NORM_EPSILON)
    normed = centered * scale
    return (normed, scale, normed * columns[0] + columns[1])


def norm_backward(upstream, normed, scale, gain):
    scaled = upstream * gain
    resid_grad = scale * (
        scaled
        - jnp.mean(scaled, -1, keepdims=True)
        - normed * jnp.mean(scaled * normed, -1, keepdims=True)
    )
    return (resid_grad, jnp.sum(upstream * normed, 0), jnp.sum(upstream, 0))


def stream_middle(context_rows, x_rows, weights, values, stream, pairs):
    resid = x_rows.astype(jnp.float32) + jnp.dot(
        context_rows, weights[1], preferred_element_type=jnp.float32
    )
    normed_one, scale_one, first = norm_forward(resid, norm_columns(values, stream, 0))
    first_low = first.astype(jnp.bfloat16)
    pre = jnp.dot(first_low, weights[2], preferred_element_type=jnp.float32)
    act = gelu_exact(pre).astype(jnp.bfloat16)
    resid = first + jnp.dot(act, weights[3], preferred_element_type=jnp.float32)
    normed_two, scale_two, second = norm_forward(resid, norm_columns(values, stream, 1))
    second_low = second.astype(jnp.bfloat16)
    side = side_of(second_low, weights[4], pairs)
    return (
        side,
        (normed_one, scale_one, first_low, pre, act, normed_two, scale_two, second, second_low),
    )


def stream_end(self_rows, second, out_weight, values, stream):
    resid = second + jnp.dot(self_rows, out_weight, preferred_element_type=jnp.float32)
    normed_three, scale_three, third = norm_forward(resid, norm_columns(values, stream, 2))
    return (third.astype(jnp.bfloat16), normed_three, scale_three)


def stream_back_end(
    cotangent, normed_three, scale_three, self_rows, out_weight, values, stream, pairs
):
    resid_three, gain_three, bias_three = norm_backward(
        cotangent.astype(jnp.float32), normed_three, scale_three, norm_columns(values, stream, 2)[0]
    )
    third_back = resid_three.astype(jnp.bfloat16)
    grad_self_out = block_grad(self_rows, third_back, 1)
    dself = lax.dot_general(
        third_back, out_weight, CONTRACT_COLS, preferred_element_type=jnp.float32
    )
    dself = dself.astype(jnp.bfloat16).reshape(pairs, -1, out_weight.shape[0])
    return (resid_three, dself, grad_self_out, gain_three, bias_three)


def stream_back_middle(resid_three, dself_side, kept, context_rows, weights, values, stream, pairs):
    normed_one, scale_one, first_low, pre, act, normed_two, scale_two, second, second_low = kept
    dself_rows = dself_side.reshape(-1, dself_side.shape[2] * dself_side.shape[3])
    grad_self_qkv = block_grad(second_low, dself_rows, 3)
    second_in = resid_three + lax.dot_general(
        dself_rows, weights[4], CONTRACT_COLS, preferred_element_type=jnp.float32
    )
    resid_two, gain_two, bias_two = norm_backward(
        second_in, normed_two, scale_two, norm_columns(values, stream, 1)[0]
    )
    branch_back = resid_two.astype(jnp.bfloat16)
    grad_down = block_grad(act, branch_back, 1)
    act_grad = lax.dot_general(
        branch_back, weights[3], CONTRACT_COLS, preferred_element_type=jnp.float32
    )
    pre_grad = jax.vjp(gelu_exact, pre)[1](act_grad)[0].astype(jnp.bfloat16)
    grad_up = block_grad(first_low, pre_grad, 1)
    first_in = resid_two + lax.dot_general(
        pre_grad, weights[2], CONTRACT_COLS, preferred_element_type=jnp.float32
    )
    resid_one, gain_one, bias_one = norm_backward(
        first_in, normed_one, scale_one, norm_columns(values, stream, 0)[0]
    )
    first_back = resid_one.astype(jnp.bfloat16)
    grad_co_out = block_grad(context_rows, first_back, 1)
    dcontext = lax.dot_general(
        first_back, weights[1], CONTRACT_COLS, preferred_element_type=jnp.float32
    )
    dcontext = dcontext.astype(jnp.bfloat16).reshape(pairs, -1, BI)
    return (
        resid_one,
        dcontext,
        (grad_co_out, grad_up, grad_down, grad_self_qkv),
        (gain_one, gain_two),
        (bias_one, bias_two),
    )


def shards(
    x_text,
    x_vis,
    caption_len,
    cot_text,
    cot_vis,
    master_blocks,
    stat_left,
    stat_right,
    root_left,
    root_right,
    norm_params,
    norm_second,
):
    pairs = caption_len.shape[0]
    width = master_blocks.shape[1] // lax.axis_size("seq")
    mine = lax.dynamic_slice_in_dim(master_blocks, lax.axis_index("seq") * width, width, 1).astype(
        jnp.bfloat16
    )
    partial_value = lax.all_gather(mine, "dp", axis=0, tiled=True)
    every = lax.all_gather(partial_value, "seq", axis=1, tiled=True)
    matrices = unpack_weights(every)
    vis_weights = matrices[:6]
    text_weights = matrices[6:]
    vis_co = side_of(x_vis, vis_weights[0], pairs)
    text_co = side_of(x_text, text_weights[0], pairs)
    lengths = caption_len
    vis_co_use, text_co_use = to_heads(vis_co, text_co)
    vis_found, text_found, vis_co_sum, text_co_sum = pair_attend(
        vis_co_use, text_co_use, lengths, True
    )
    vis_context, text_context = from_heads(vis_found, text_found)
    vis_context_rows = vis_context.reshape(-1, BI)
    text_context_rows = text_context.reshape(-1, BI)
    vis_self, vis_kept = stream_middle(vis_context_rows, x_vis, vis_weights, norm_params, 0, pairs)
    text_self, text_kept = stream_middle(
        text_context_rows, x_text, text_weights, norm_params, 1, pairs
    )
    vis_self_use, text_self_use = to_heads(vis_self, text_self)
    vis_found, text_found, vis_self_sum, text_self_sum = pair_attend(
        vis_self_use, text_self_use, lengths, False
    )
    vis_self_context, text_self_context = from_heads(vis_found, text_found)
    vis_self_rows = vis_self_context.reshape(-1, VIS)
    text_self_rows = text_self_context.reshape(-1, TXT)
    out_vis, vis_normed_three, vis_scale_three = stream_end(
        vis_self_rows, vis_kept[7], vis_weights[5], norm_params, 0
    )
    out_text, text_normed_three, text_scale_three = stream_end(
        text_self_rows, text_kept[7], text_weights[5], norm_params, 1
    )
    vis_resid_three, vis_dself, vis_grad_so, vis_gain_three, vis_bias_three = stream_back_end(
        cot_vis,
        vis_normed_three,
        vis_scale_three,
        vis_self_rows,
        vis_weights[5],
        norm_params,
        0,
        pairs,
    )
    text_resid_three, text_dself, text_grad_so, text_gain_three, text_bias_three = stream_back_end(
        cot_text,
        text_normed_three,
        text_scale_three,
        text_self_rows,
        text_weights[5],
        norm_params,
        1,
        pairs,
    )
    vis_dheads, text_dheads = dfound_to_heads(vis_dself, text_dself)
    vis_dgot, text_dgot = pair_attend_back(
        vis_self_use,
        text_self_use,
        lengths,
        False,
        vis_self_sum,
        text_self_sum,
        vis_dheads,
        text_dheads,
    )
    vis_dself_side, text_dself_side = grads_from_heads(vis_dgot, text_dgot)
    vis_resid_one, vis_dcontext, vis_grads_mid, vis_gains_mid, vis_biases_mid = stream_back_middle(
        vis_resid_three,
        vis_dself_side,
        vis_kept,
        vis_context_rows,
        vis_weights,
        norm_params,
        0,
        pairs,
    )
    text_resid_one, text_dcontext, text_grads_mid, text_gains_mid, text_biases_mid = (
        stream_back_middle(
            text_resid_three,
            text_dself_side,
            text_kept,
            text_context_rows,
            text_weights,
            norm_params,
            1,
            pairs,
        )
    )
    vis_dheads, text_dheads = dfound_to_heads(vis_dcontext, text_dcontext)
    vis_dgot, text_dgot = pair_attend_back(
        vis_co_use, text_co_use, lengths, True, vis_co_sum, text_co_sum, vis_dheads, text_dheads
    )
    vis_dco, text_dco = grads_from_heads(vis_dgot, text_dgot)
    vis_dco_rows = vis_dco.reshape(-1, 3 * BI)
    text_dco_rows = text_dco.reshape(-1, 3 * BI)
    grad_vis = vis_resid_one + lax.dot_general(
        vis_dco_rows, vis_weights[0], CONTRACT_COLS, preferred_element_type=jnp.float32
    )
    grad_text = text_resid_one + lax.dot_general(
        text_dco_rows, text_weights[0], CONTRACT_COLS, preferred_element_type=jnp.float32
    )
    vis_grad_co = block_grad(x_vis, vis_dco_rows, 3)
    text_grad_co = block_grad(x_text, text_dco_rows, 3)
    local_blocks = jnp.concatenate(
        [vis_grad_co]
        + list(vis_grads_mid)
        + [vis_grad_so]
        + [text_grad_co]
        + list(text_grads_mid)
        + [text_grad_so],
        0,
    )
    norm_local = jnp.stack(
        [
            jnp.concatenate(
                [
                    vis_gains_mid[0],
                    vis_gains_mid[1],
                    vis_gain_three,
                    text_gains_mid[0],
                    text_gains_mid[1],
                    text_gain_three,
                ]
            ),
            jnp.concatenate(
                [
                    vis_biases_mid[0],
                    vis_biases_mid[1],
                    vis_bias_three,
                    text_biases_mid[0],
                    text_biases_mid[1],
                    text_bias_three,
                ]
            ),
        ]
    )
    columns = lax.psum_scatter(
        local_blocks.astype(jnp.bfloat16), "seq", scatter_dimension=1, tiled=True
    ).astype(jnp.float32)
    owned_columns = lax.psum_scatter(columns, "dp", scatter_dimension=0, tiled=True)
    owned = lax.all_gather(owned_columns.astype(jnp.bfloat16), "seq", axis=1, tiled=True).astype(
        owned_columns.dtype
    )
    norm_grads = lax.psum(norm_local, ("dp", "seq"))
    number = owned.shape[0]
    grad_cube = owned.reshape(number, BLK, BLK)
    left_cube = stat_left.reshape(number, BLK, BLK)
    right_cube = stat_right.reshape(number, BLK, BLK)
    rootl_cube = root_left.reshape(number, BLK, BLK)
    rootr_cube = root_right.reshape(number, BLK, BLK)
    left_new = STAT_DECAY * left_cube + (1.0 - STAT_DECAY) * jnp.einsum(
        "bij,bkj->bik", grad_cube, grad_cube, precision=HIGHEST
    )
    right_new = STAT_DECAY * right_cube + (1.0 - STAT_DECAY) * jnp.einsum(
        "bji,bjk->bik", grad_cube, grad_cube, precision=HIGHEST
    )
    half = jnp.einsum("bij,bjk->bik", rootl_cube, grad_cube, precision=HIGHEST)
    direction = jnp.einsum("bij,bjk->bik", half, rootr_cube, precision=HIGHEST)
    master_new = master_blocks - WEIGHT_RATE * direction.reshape(number, BLK * BLK)
    second_new = STAT_DECAY * norm_second + (1.0 - STAT_DECAY) * norm_grads * norm_grads
    norm_new = norm_params - NORM_RATE * norm_grads / (jnp.sqrt(second_new) + MOMENT_EPSILON)
    return (
        out_text,
        out_vis,
        grad_text,
        grad_vis,
        owned,
        left_new.reshape(number, BLK * BLK),
        right_new.reshape(number, BLK * BLK),
        master_new,
        norm_grads,
        second_new,
        norm_new,
    )


SUB = 64
WIDE = 256
QUAD = 4
F32 = jnp.float32
BF16 = jnp.bfloat16
VIS_PAD = 48
VMEM_LIMIT = 60 * 1024 * 1024
NT = (((1,), (1,)), ((), ()))
TN = (((0,), (0,)), ((), ()))


def tile_table():
    begin = 0
    table = []
    for rows, columns, count in weight_layout():
        r, g = rows // SUB, columns // WIDE
        table.append((begin, count, r, g))
        begin += count * r * g
    return table


TILES = tile_table()
SHARD = 158
FAR = 46
G_HALF = 24
G_LONE = 6
R_LONE = 28
R_BOTH = 24
R_HALF = 2 * R_LONE + R_BOTH
CHUNKS = 2
SWAP_CORE = [(i, i ^ 1) for i in range(4)]
SWAP_Y = [(i, i ^ 2) for i in range(4)]
SWAP_X = [(i, i ^ 1) for i in range(8)]


def dot(left, right, how=None):
    if how is None:
        return jnp.dot(left, right, preferred_element_type=F32)
    return lax.dot_general(left, right, how, preferred_element_type=F32)


def params(**more):
    return pltpu.CompilerParams(vmem_limit_bytes=VMEM_LIMIT, **more)


def cost(micros):
    return pl.CostEstimate(flops=0, bytes_accessed=int(micros * 3.4e6), transcendentals=0)


def whole(count):
    return [pl.BlockSpec(memory_space=pltpu.VMEM)] * count


def linear(value):
    groups = value.shape[0] // 8
    return value.reshape(groups, 8, 32, 128).transpose(0, 2, 1, 3).reshape(groups * 256, 128)


def unlinear(value):
    groups = value.shape[0] // 256
    return value.reshape(groups, 32, 8, 128).transpose(0, 2, 1, 3).reshape(groups * 8, SUB * SUB)


def lanes_low(rows):
    return lax.broadcasted_iota(jnp.int32, (rows, 2 * SUB), 1) < SUB


def spread_of(ref, b):
    return ref[pl.ds(b, 32, stride=8), :]


def natural_order():
    row = lax.broadcasted_iota(jnp.int32, (SUB, SUB), 0)
    column = lax.broadcasted_iota(jnp.int32, (SUB, SUB), 1)
    return jnp.where(row == 2 * (column % 32) + column // 32, 1.0, 0.0).astype(BF16)


def prep_rows(number, pairs_ref, x_any, o_ref, rows_in, sems):
    def fetch(i):
        rows = pl.ds(pl.multiple_of(pairs_ref[i] * 256, 256), 256)
        return pltpu.make_async_copy(x_any.at[rows], rows_in.at[i], sems.at[i])

    for i in range(number):
        fetch(i).start()
    low = lanes_low(32)
    order = natural_order()

    def step(i, carry):
        fetch(i).wait()
        x_ref = rows_in.at[i]
        spots = range(4)
        one = [spread_of(x_ref, 2 * m) for m in spots]
        two = [spread_of(x_ref, 2 * m + 1) for m in spots]
        rows = [
            jnp.concatenate(
                [
                    jnp.where(low, one[m], pltpu.roll(two[m], SUB, 1)),
                    jnp.where(low, pltpu.roll(one[m], SUB, 1), two[m]),
                ],
                0,
            ).astype(BF16)
            for m in spots
        ]
        made = [dot(order, rows[m]).astype(BF16) for m in spots]
        for m in spots:
            o_ref[2 * i + m // 2, :, (m % 2) * 128 : (m % 2 + 1) * 128] = made[m]
        return carry

    lax.fori_loop(0, number, step, 0, unroll=2 if number % 2 == 0 else 3)


def prep(master_blocks, pairs):
    number = pairs.shape[0]
    return pl.pallas_call(
        functools.partial(prep_rows, number),
        in_specs=[pl.BlockSpec(memory_space=pltpu.SMEM), pl.BlockSpec(memory_space=pl.ANY)],
        out_specs=pl.BlockSpec(memory_space=pltpu.VMEM),
        out_shape=jax.ShapeDtypeStruct((number * 2, SUB, WIDE), BF16),
        scratch_shapes=[pltpu.VMEM((number, 256, 128), F32), pltpu.SemaphoreType.DMA((number,))],
        compiler_params=params(),
        cost_estimate=cost(0.4 * number),
    )(pairs, linear(master_blocks))


def renew_eight(g_ref, m_ref, sl_ref, sr_ref, rl_ref, rr_ref, go_ref, lo_ref, ro_ref, mo_ref, place):
    low = lanes_low(SUB)
    low_half = lanes_low(32)
    nothing = jnp.zeros((SUB, 128), F32)
    pairs = range(4)

    def diagonal(pair):
        return jnp.concatenate([jnp.where(low, pair, nothing), jnp.where(low, nothing, pair)], 0).astype(BF16)

    def mixed(even, odd):
        return (
            jnp.where(low_half, even, pltpu.roll(odd, SUB, 1)),
            jnp.where(low_half, pltpu.roll(even, SUB, 1), odd),
        )

    def natural(ref, pair, spot):
        even, odd = mixed(spread_of(ref, 2 * pair), spread_of(ref, 2 * pair + 1))
        spot[pl.ds(0, 32, stride=2), :] = even
        spot[pl.ds(1, 32, stride=2), :] = odd
        return spot[...]

    def spread(value, spot):
        spot[...] = value
        return mixed(spot[pl.ds(0, 32, stride=2), :], spot[pl.ds(1, 32, stride=2), :])

    tiles = [g_ref[pair // 2, :, (pair % 2) * 128 : (pair % 2 + 1) * 128] for pair in pairs]
    wide = [tile.astype(F32) for tile in tiles]
    grads = [diagonal(value) for value in wide]
    lefts = [natural(rl_ref, pair, place.at[pair, 0]).astype(BF16) for pair in pairs]
    rights = [diagonal(natural(rr_ref, pair, place.at[pair, 1])) for pair in pairs]
    halves = [dot(lefts[pair], grads[pair]).astype(BF16) for pair in pairs]
    left_parts = [dot(tiles[pair], grads[pair], NT) for pair in pairs]
    squares = [dot(tiles[pair], tiles[pair], TN) for pair in pairs]
    right_parts = [jnp.where(low, square[:SUB], square[SUB:]) for square in squares]
    steps = [dot(halves[pair], rights[pair]) for pair in pairs]
    for pair in pairs:
        made = [
            spread(value[pair], place.at[pair, 2 + k])
            for k, value in enumerate((wide, left_parts, right_parts, steps))
        ]
        for i in range(2):
            at = pl.ds(2 * pair + i, 32, stride=8)
            go_ref[at, :] = made[0][i]
            lo_ref[at, :] = STAT_DECAY * sl_ref[at, :] + (1.0 - STAT_DECAY) * made[1][i]
            ro_ref[at, :] = STAT_DECAY * sr_ref[at, :] + (1.0 - STAT_DECAY) * made[2][i]
            mo_ref[at, :] = m_ref[at, :] - WEIGHT_RATE * made[3][i]


SLOTS = 4


def renew_body(steps, which_ref, g_any, *refs):
    ins = refs[:5]
    outs = refs[-9:-5]
    gbuf, inbuf, outbuf, place, sems = refs[-5:]

    def rows(i):
        return pl.ds(pl.multiple_of(which_ref[i] * 256, 256), 256)

    def fetch(i):
        slot = lax.rem(i, SLOTS)
        copies = [pltpu.make_async_copy(g_any.at[pl.ds(2 * i, 2)], gbuf.at[slot], sems.at[slot, 0])]
        for k, ref in enumerate(ins):
            copies.append(
                pltpu.make_async_copy(ref.at[rows(i)], inbuf.at[slot, k], sems.at[slot, 1 + k])
            )
        return copies

    def put(i):
        slot = lax.rem(i, SLOTS)
        return [
            pltpu.make_async_copy(outbuf.at[slot, k], ref.at[rows(i)], sems.at[slot, 6 + k])
            for k, ref in enumerate(outs)
        ]

    def start(copies):
        for copy in copies:
            copy.start()

    def wait(copies):
        for copy in copies:
            copy.wait()

    for i in range(min(SLOTS, steps)):
        start(fetch(i))

    def step(i, carry):
        slot = lax.rem(i, SLOTS)
        wait(fetch(i))

        @pl.when(i >= SLOTS)
        def _():
            wait(put(i - SLOTS))

        renew_eight(
            gbuf.at[slot], *(inbuf.at[slot, k] for k in range(5)), *(outbuf.at[slot, k] for k in range(4)), place
        )
        start(put(i))

        @pl.when(i + SLOTS < steps)
        def _():
            start(fetch(i + SLOTS))

        return carry

    lax.fori_loop(0, steps, step, 0)
    for i in range(max(0, steps - SLOTS), steps):
        wait(put(i))


def renew(which, owned, master_blocks, stat_left, stat_right, root_left, root_right, before):
    steps = which.shape[0]
    shape = jax.ShapeDtypeStruct((master_blocks.shape[0] * 32, 128), F32)
    anywhere = pl.BlockSpec(memory_space=pl.ANY)
    made = pl.pallas_call(
        functools.partial(renew_body, steps),
        in_specs=[pl.BlockSpec(memory_space=pltpu.SMEM)] + [anywhere] * (6 + len(before)),
        out_specs=[anywhere] * 4,
        out_shape=[shape] * 4,
        scratch_shapes=[
            pltpu.VMEM((SLOTS, 2, SUB, WIDE), BF16),
            pltpu.VMEM((SLOTS, 5, 256, 128), F32),
            pltpu.VMEM((SLOTS, 4, 256, 128), F32),
            pltpu.VMEM((4, 6, SUB, 128), F32),
            pltpu.SemaphoreType.DMA((SLOTS, 10)),
        ],
        input_output_aliases={7 + i: i for i in range(len(before))},
        compiler_params=params(),
        cost_estimate=cost(0.7 * steps),
    )(
        which,
        owned,
        *(linear(value) for value in (master_blocks, stat_left, stat_right, root_left, root_right)),
        *(linear(value) for value in before),
    )
    return [unlinear(value) for value in made]


def times(rows_in, w, base, r, g, part, col):
    first = base + part * r * g + col
    return dot(rows_in, jnp.concatenate([w[first + a * g] for a in range(r)], 0))


def times_back(d_ref, w, base, r, g, count, r4):
    total = None
    for part in range(count):
        first = base + (part * r + 4 * r4) * g
        wide = jnp.concatenate(
            [
                jnp.concatenate([w[first + a * g + col] for a in range(4)], 0)
                for col in range(g)
            ],
            1,
        )
        made = dot(d_ref[:, part * g * WIDE : (part + 1) * g * WIDE], wide, NT)
        total = made if total is None else total + made
    return total


def at256(i):
    return pl.ds(pl.multiple_of(i * WIDE, WIDE), WIDE)


def softmax_all(products, scale, limits):
    scores = []
    for product, limit in zip(products, limits):
        column = lax.broadcasted_iota(jnp.int32, product.shape, 1)
        scores.append(jnp.where(column < limit, product * scale, MASK_FILL))
    tops = [jnp.max(score, 1, keepdims=True) for score in scores]
    raised = [jnp.exp(score - top) for score, top in zip(scores, tops)]
    shares = [1.0 / jnp.sum(value, 1, keepdims=True) for value in raised]
    return [value * share for value, share in zip(raised, shares)]


def score_grads(probs, dprobs):
    weighted = [p * d for p, d in zip(probs, dprobs)]
    totals = [jnp.sum(value, 1, keepdims=True) for value in weighted]
    return [(value - p * total).astype(BF16) for value, p, total in zip(weighted, probs, totals)]


def at128(i):
    return pl.ds(pl.multiple_of(i * 128, 128), 128)


def load(near, far, w, sems, pieces, base):
    started = []
    used = 0
    for i, which in enumerate(pieces):
        begin, count, r, g = TILES[which]
        end = begin + count * r * g
        copies = []
        for owner in range(begin // SHARD, (end - 1) // SHARD + 1):
            first = max(begin, owner * SHARD)
            last = min(end, (owner + 1) * SHARD)
            middle = min(max(owner * SHARD + FAR, first), last)
            for source, lo, hi, at in (
                (near, first, middle, owner * (2 * G_HALF) + first - owner * SHARD),
                (far, middle, last, owner * (SHARD - FAR) + middle - owner * SHARD - FAR),
            ):
                if lo < hi:
                    copies.append(
                        pltpu.make_async_copy(
                            source.at[pl.ds(at, hi - lo)],
                            w.at[pl.ds(base[i] + lo - begin, hi - lo)],
                            sems.at[used],
                        )
                    )
                    copies[-1].start()
                    used += 1
        started.append(copies)
    return started


def arrive(copies):
    for copy in copies:
        copy.wait()


def tiles_of(which):
    _, count, r, g = TILES[which]
    return count * r * g


def co_body(len_ref, xv_ref, xt_ref, near, far, cv_ref, ct_ref, fv_ref, ft_ref, w, sems):
    base = (0, tiles_of(0))
    copies = load(near, far, w, sems, (0, 6), base)
    for which, at, x_ref, o_ref, copy in (
        (0, base[0], xv_ref, cv_ref, copies[0]),
        (6, base[1], xt_ref, ct_ref, copies[1]),
    ):
        _, count, r, g = TILES[which]
        arrive(copy)

        def column(i, carry, at=at, r=r, g=g, x_ref=x_ref, o_ref=o_ref):
            o_ref[:, at256(i)] = times(x_ref[...], w, at, r, g, i // g, i % g).astype(BF16)
            return carry

        lax.fori_loop(0, count * g, column, 0, unroll=2)
    scale = HEAD ** (-0.5)
    reg = len_ref[2]
    heads = BI // HEAD
    vis = [slice(pair * VIS_PAD, (pair + 1) * VIS_PAD) for pair in range(2)]
    text = [slice(pair * 128, (pair + 1) * 128) for pair in range(2)]
    limits = [len_ref[0], len_ref[1], reg, reg]

    def head(j, carry):
        qv, kv, vv = ([cv_ref[rows, at128(j + heads * s)] for rows in vis] for s in range(3))
        qt, kt, vt = ([ct_ref[rows, at128(j + heads * s)] for rows in text] for s in range(3))
        probs = softmax_all([dot(q, k, NT) for q, k in zip(qv + qt, kt + kv)], scale, limits)
        found = [dot(p.astype(BF16), v).astype(BF16) for p, v in zip(probs, vt + vv)]
        for pair in range(2):
            fv_ref[vis[pair], at128(j)] = found[pair]
            ft_ref[text[pair], at128(j)] = found[2 + pair]
        return carry

    lax.fori_loop(0, heads, head, 0, unroll=2)


def co_forward(lengths, x_vis, x_text, near, far):
    return pl.pallas_call(
        co_body,
        in_specs=[pl.BlockSpec(memory_space=pltpu.SMEM)] + whole(2) + [pl.BlockSpec(memory_space=pl.ANY)] * 2,
        out_specs=whole(4),
        out_shape=[
            jax.ShapeDtypeStruct((x_vis.shape[0], 3 * BI), BF16),
            jax.ShapeDtypeStruct((x_text.shape[0], 3 * BI), BF16),
            jax.ShapeDtypeStruct((x_vis.shape[0], BI), BF16),
            jax.ShapeDtypeStruct((x_text.shape[0], BI), BF16),
        ],
        scratch_shapes=[
            pltpu.VMEM((tiles_of(0) + tiles_of(6), SUB, WIDE), BF16),
            pltpu.SemaphoreType.DMA((16,)),
        ],
        compiler_params=params(),
        cost_estimate=cost(22),
    )(lengths, x_vis, x_text, near, far)


def co_back_body(
    len_ref, cv_ref, ct_ref, dv_ref, dt_ref, rv_ref, rt_ref, near, far,
    gv_ref, gt_ref, ov_ref, ot_ref, w, sems,
):
    base = (0, tiles_of(0))
    copies = load(near, far, w, sems, (0, 6), base)
    scale = HEAD ** (-0.5)
    reg = len_ref[2]
    heads = BI // HEAD
    vis = [slice(pair * VIS_PAD, (pair + 1) * VIS_PAD) for pair in range(2)]
    text = [slice(pair * 128, (pair + 1) * 128) for pair in range(2)]
    limits = [len_ref[0], len_ref[1], reg, reg]

    def head(j, carry):
        qv, kv, vv = ([cv_ref[rows, at128(j + heads * s)] for rows in vis] for s in range(3))
        qt, kt, vt = ([ct_ref[rows, at128(j + heads * s)] for rows in text] for s in range(3))
        up = [dv_ref[rows, at128(j)] for rows in vis] + [dt_ref[rows, at128(j)] for rows in text]
        queries, keys, values = qv + qt, kt + kv, vt + vv
        products = [dot(q, k, NT) for q, k in zip(queries, keys)]
        dprobs = [dot(u, v, NT) for u, v in zip(up, values)]
        probs = softmax_all(products, scale, limits)
        ds = score_grads(probs, dprobs)
        dvalues = [dot(p.astype(BF16), u, TN).astype(BF16) for p, u in zip(probs, up)]
        dqueries = [(dot(d, k) * scale).astype(BF16) for d, k in zip(ds, keys)]
        dkeys = [(dot(d, q, TN) * scale).astype(BF16) for d, q in zip(ds, queries)]
        for pair in range(2):
            gv_ref[vis[pair], at128(j)] = dqueries[pair]
            gt_ref[text[pair], at128(j + heads)] = dkeys[pair]
            gt_ref[text[pair], at128(j + 2 * heads)] = dvalues[pair]
            gt_ref[text[pair], at128(j)] = dqueries[2 + pair]
            gv_ref[vis[pair], at128(j + heads)] = dkeys[2 + pair]
            gv_ref[vis[pair], at128(j + 2 * heads)] = dvalues[2 + pair]
        return carry

    lax.fori_loop(0, heads, head, 0, unroll=2)
    for which, at, g_ref, r_ref, o_ref, copy in (
        (0, base[0], gv_ref, rv_ref, ov_ref, copies[0]),
        (6, base[1], gt_ref, rt_ref, ot_ref, copies[1]),
    ):
        _, count, r, g = TILES[which]
        arrive(copy)

        def rows4(i, carry, at=at, r=r, g=g, count=count, g_ref=g_ref, r_ref=r_ref, o_ref=o_ref):
            o_ref[:, at256(i)] = r_ref[:, at256(i)] + times_back(g_ref, w, at, r, g, count, i)
            return carry

        lax.fori_loop(0, r // 4, rows4, 0)


def co_backward(lengths, co_vis, co_text, dvis, dtext, resid_vis, resid_text, near, far):
    return pl.pallas_call(
        co_back_body,
        in_specs=[pl.BlockSpec(memory_space=pltpu.SMEM)] + whole(6) + [pl.BlockSpec(memory_space=pl.ANY)] * 2,
        out_specs=whole(4),
        out_shape=[
            jax.ShapeDtypeStruct(co_vis.shape, BF16),
            jax.ShapeDtypeStruct(co_text.shape, BF16),
            jax.ShapeDtypeStruct(resid_vis.shape, F32),
            jax.ShapeDtypeStruct(resid_text.shape, F32),
        ],
        scratch_shapes=[
            pltpu.VMEM((tiles_of(0) + tiles_of(6), SUB, WIDE), BF16),
            pltpu.SemaphoreType.DMA((16,)),
        ],
        compiler_params=params(),
        cost_estimate=cost(23),
    )(lengths, co_vis, co_text, dvis, dtext, resid_vis, resid_text, near, far)


def erf_parts(value):
    return 0.5 * (1.0 + lax.erf(value * 0.7071067811865476))


def middle_body(
    config,
    len_ref, ctx_ref, x_ref, cot_ref, norm_ref, near, far,
    out_ref, first_ref, act_ref, second_ref, sctx_ref,
    fback_ref, pback_ref, bback_ref, dself_ref, tback_ref,
    resid_ref, dctx_ref, sums_ref,
    w, sems, pre, n1, n2, n3, s1, s2, s3, wide, acc, selfs, probs, stat,
):
    begin, rows, span, head, chunk = config
    width = x_ref.shape[1]
    base = []
    at = 0
    for which in range(begin, begin + 5):
        base.append(at)
        at += tiles_of(which)
    copies = load(near, far, w, sems, tuple(range(begin, begin + 5)), base)
    shapes = [TILES[which][1:] for which in range(begin, begin + 5)]
    steps = rows // chunk

    def at_chunk(i):
        return pl.ds(pl.multiple_of(i * chunk, chunk), chunk)

    def norm(resid, which, i, kept, scales):
        mean = jnp.mean(resid, 1, keepdims=True)
        centered = resid - mean
        scale = lax.rsqrt(jnp.mean(centered * centered, 1, keepdims=True) + NORM_EPSILON)
        normed = centered * scale
        kept[at_chunk(i), :] = normed
        scales[at_chunk(i), :] = jnp.broadcast_to(scale, (chunk, 128))
        return normed * norm_ref[0, which : which + 1, :] + norm_ref[1, which : which + 1, :]

    def eight(value):
        return jnp.sum(value.reshape(chunk // 8, 8, width), 0)

    def norm_back(upstream, which, i, kept, scales):
        normed = kept[at_chunk(i), :]
        stat[which] = stat[which] + eight(upstream * normed)
        stat[3 + which] = stat[3 + which] + eight(upstream)
        scaled = upstream * norm_ref[0, which : which + 1, :]
        return scales[at_chunk(i), 0:1] * (
            scaled
            - jnp.mean(scaled, 1, keepdims=True)
            - normed * jnp.mean(scaled * normed, 1, keepdims=True)
        )

    def loop(count, body, unroll=1):
        lax.fori_loop(0, count, lambda i, carry: (body(i), carry)[1], 0, unroll=unroll)

    stat[...] = jnp.zeros(stat.shape, F32)
    count, r, g = shapes[0]
    arrive(copies[0])

    def co_out(i):
        wide[:, at256(i)] = times(ctx_ref[...], w, base[0], r, g, 0, i)

    loop(g, co_out, g)

    def norm_one(i):
        value = norm(wide[at_chunk(i), :] + x_ref[at_chunk(i), :].astype(F32), 0, i, n1, s1)
        wide[at_chunk(i), :] = value
        first_ref[at_chunk(i), :] = value.astype(BF16)

    loop(steps, norm_one, 2 if steps % 2 == 0 else steps)
    _, r_up, g_up = shapes[1]
    _, r_down, g_down = shapes[2]
    arrive(copies[1])
    arrive(copies[2])
    acc[...] = jnp.zeros(acc.shape, F32)

    def down_rows(i):
        return jnp.concatenate(
            [
                jnp.concatenate([w[base[2] + (4 * i + a) * g_down + col] for a in range(4)], 0)
                for col in range(g_down)
            ],
            1,
        )

    def feed(i):
        value = times(first_ref[...], w, base[1], r_up, g_up, 0, i)
        part = erf_parts(value)
        pre[i] = part + value * (0.3989422804014327 * jnp.exp(-0.5 * value * value))
        act = (value * part).astype(BF16)
        act_ref[:, at256(i)] = act
        acc[...] += dot(act, down_rows(i))

    loop(g_up, feed, 4)

    def norm_two(i):
        value = norm(wide[at_chunk(i), :] + acc[at_chunk(i), :], 1, i, n2, s2)
        wide[at_chunk(i), :] = value
        second_ref[at_chunk(i), :] = value.astype(BF16)

    loop(steps, norm_two, 2 if steps % 2 == 0 else steps)
    count_s, r_s, g_s = shapes[3]
    arrive(copies[3])

    def self_in(i):
        selfs[:, at256(i)] = times(second_ref[...], w, base[3], r_s, g_s, i // g_s, i % g_s).astype(BF16)

    loop(count_s * g_s, self_in, g_s)
    scale = head ** (-0.5)
    groups = width // 128
    per = 128 // head
    pairs = rows // span

    def halves(values):
        if per == 1:
            return values[0]
        low = lax.broadcasted_iota(jnp.int32, values[0].shape, 1) < head
        return jnp.where(low, values[0], values[1])

    def only(value, h):
        if per == 1:
            return value
        low = lax.broadcasted_iota(jnp.int32, value.shape, 1) < head
        keep = low if h == 0 else jnp.logical_not(low)
        return jnp.where(keep, value, jnp.zeros_like(value))

    own = [slice(pair * span, (pair + 1) * span) for pair in range(pairs)]
    each = [(pair, h) for pair in range(pairs) for h in range(per)]

    def attend(j):
        q, k, v = ([selfs[rows_of, at128(j + groups * s)] for rows_of in own] for s in range(3))
        products = [dot(only(q[pair], h), k[pair], NT) for pair, h in each]
        p = softmax_all(products, scale, [len_ref[pair] for pair, _ in each])
        found = [dot(value.astype(BF16), v[pair]) for value, (pair, _) in zip(p, each)]
        for i, value in enumerate(p):
            probs[j * len(each) + i] = value
        for pair in range(pairs):
            sctx_ref[own[pair], at128(j)] = halves(found[pair * per : (pair + 1) * per]).astype(BF16)

    loop(groups, attend, 2)
    _, r_o, g_o = shapes[4]
    arrive(copies[4])

    def self_out(i):
        acc[:, at256(i)] = times(sctx_ref[...], w, base[4], r_o, g_o, 0, i)

    loop(g_o, self_out, g_o)

    def norm_three(i):
        value = norm(wide[at_chunk(i), :] + acc[at_chunk(i), :], 2, i, n3, s3)
        out_ref[at_chunk(i), :] = value.astype(BF16)
        third = norm_back(cot_ref[at_chunk(i), :].astype(F32), 2, i, n3, s3)
        wide[at_chunk(i), :] = third
        tback_ref[at_chunk(i), :] = third.astype(BF16)

    loop(steps, norm_three, 2 if steps % 2 == 0 else steps)

    def self_out_back(i):
        dctx_ref[:, at256(i)] = times_back(tback_ref, w, base[4], r_o, g_o, 1, i).astype(BF16)

    loop(r_o // 4, self_out_back, r_o // 4)
    def attend_back(j):
        q, k, v = ([selfs[rows_of, at128(j + groups * s)] for rows_of in own] for s in range(3))
        up = [dctx_ref[rows_of, at128(j)] for rows_of in own]
        p = [probs[j * len(each) + i] for i in range(len(each))]
        dprobs = [dot(only(up[pair], h), v[pair], NT) for pair, h in each]
        dv = [dot(value.astype(BF16), up[pair], TN) for value, (pair, _) in zip(p, each)]
        ds = score_grads(p, dprobs)
        dq = [dot(value, k[pair]) for value, (pair, _) in zip(ds, each)]
        dk = [dot(value, q[pair], TN) for value, (pair, _) in zip(ds, each)]
        for pair in range(pairs):
            mine = slice(pair * per, (pair + 1) * per)
            dself_ref[own[pair], at128(j)] = (halves(dq[mine]) * scale).astype(BF16)
            dself_ref[own[pair], at128(j + groups)] = (halves(dk[mine]) * scale).astype(BF16)
            dself_ref[own[pair], at128(j + 2 * groups)] = halves(dv[mine]).astype(BF16)

    loop(groups, attend_back, 2)

    def self_in_back(i):
        acc[:, at256(i)] = times_back(dself_ref, w, base[3], r_s, g_s, count_s, i)

    loop(r_s // 4, self_in_back, r_s // 4)

    def norm_two_back(i):
        value = norm_back(wide[at_chunk(i), :] + acc[at_chunk(i), :], 1, i, n2, s2)
        wide[at_chunk(i), :] = value
        bback_ref[at_chunk(i), :] = value.astype(BF16)

    loop(steps, norm_two_back, 2 if steps % 2 == 0 else steps)

    def feed_back(i):
        act_grad = dot(bback_ref[...], down_rows(i), NT)
        pback_ref[:, at256(i)] = (act_grad * pre[i]).astype(BF16)

    loop(g_up, feed_back, 4)

    def up_back(i):
        acc[:, at256(i)] = times_back(pback_ref, w, base[1], r_up, g_up, 1, i)

    loop(r_up // 4, up_back, r_up // 4)

    def norm_one_back(i):
        value = norm_back(wide[at_chunk(i), :] + acc[at_chunk(i), :], 0, i, n1, s1)
        resid_ref[at_chunk(i), :] = value
        fback_ref[at_chunk(i), :] = value.astype(BF16)

    loop(steps, norm_one_back, 2 if steps % 2 == 0 else steps)

    def co_out_back(i):
        dctx_ref[:, at256(i)] = times_back(fback_ref, w, base[0], r, g, 1, i).astype(BF16)

    loop(r // 4, co_out_back, r // 4)
    sums_ref[...] = jnp.sum(stat[...], 1)


def middle(begin, lengths, context, x, cot, norms, near, far, span, head, chunk):
    rows, width = x.shape
    hidden = TILES[begin + 1][3] * WIDE
    number = sum(tiles_of(which) for which in range(begin, begin + 5))
    low = lambda columns: jax.ShapeDtypeStruct((rows, columns), BF16)
    return pl.pallas_call(
        functools.partial(middle_body, (begin, rows, span, head, chunk)),
        in_specs=[pl.BlockSpec(memory_space=pltpu.SMEM)] + whole(4) + [pl.BlockSpec(memory_space=pl.ANY)] * 2,
        out_specs=whole(13),
        out_shape=[
            low(width), low(width), low(hidden), low(width), low(width),
            low(width), low(hidden), low(width), low(3 * width), low(width),
            jax.ShapeDtypeStruct((rows, width), F32), low(BI),
            jax.ShapeDtypeStruct((6, width), F32),
        ],
        scratch_shapes=[
            pltpu.VMEM((number, SUB, WIDE), BF16),
            pltpu.SemaphoreType.DMA((24,)),
            pltpu.VMEM((hidden // WIDE, rows, WIDE), F32),
        ]
        + [pltpu.VMEM((rows, width), F32)] * 3
        + [pltpu.VMEM((rows, 128), F32)] * 3
        + [pltpu.VMEM((rows, width), F32)] * 2
        + [
            pltpu.VMEM((rows, 3 * width), BF16),
            pltpu.VMEM((rows // span * (width // head), span, span), F32),
            pltpu.VMEM((6, 8, width), F32),
        ],
        compiler_params=params(),
        cost_estimate=cost(40),
    )(lengths, context, x, cot, norms, near, far)


def weight_body(kinds, *refs):
    n = len(kinds)
    lefts, rights = refs[:n], refs[n : 2 * n]
    out, stage, across, sems = refs[2 * n :]
    offset = 0
    for which, a_ref, b_ref in zip(kinds, lefts, rights):
        _, count, r, g = TILES[which]
        size = 4 * g

        def copy(i, slot, offset=offset, size=size):
            return pltpu.make_async_copy(
                stage.at[slot, pl.ds(0, size)], out.at[pl.ds(offset + i * size, size)], sems.at[slot]
            )

        total = count * (r // 4)

        def step(i, carry, a_ref=a_ref, b_ref=b_ref, r=r, g=g, copy=copy):
            slot = lax.rem(i, 4)

            @pl.when(i >= 4)
            def _():
                copy(i - 4, slot).wait()

            part = i // (r // 4)
            r4 = lax.rem(i, r // 4)
            across[...] = jnp.transpose(a_ref[:, at256(r4)])
            left = across[...]
            for first in range(0, g, 4 if g % 4 == 0 else 3):
                columns = range(first, first + (4 if g % 4 == 0 else 3))
                made = [dot(left, b_ref[:, at256(part * g + col)]).astype(BF16) for col in columns]
                for col, value in zip(columns, made):
                    for a in range(4):
                        stage[slot, a * g + col] = value[a * SUB : (a + 1) * SUB]
            copy(i, slot).start()
            return carry

        lax.fori_loop(0, total, step, 0, unroll=2 if total % 2 == 0 else 3)
        for i in range(max(0, total - 4), total):
            copy(i, i % 4).wait()
        offset += count * r * g


def weight_grads(kinds, lefts, rights):
    number = sum(tiles_of(which) for which in kinds)
    most = max(4 * TILES[which][3] for which in kinds)
    return pl.pallas_call(
        functools.partial(weight_body, kinds),
        in_specs=whole(2 * len(kinds)),
        out_specs=pl.BlockSpec(memory_space=pl.ANY),
        out_shape=jax.ShapeDtypeStruct((number, SUB, WIDE), BF16),
        scratch_shapes=[
            pltpu.VMEM((4, most, SUB, WIDE), BF16),
            pltpu.VMEM((WIDE, lefts[0].shape[0]), BF16),
            pltpu.SemaphoreType.DMA((4,)),
        ],
        compiler_params=params(),
        cost_estimate=cost(number * 0.04),
    )(*lefts, *rights)


def spot():
    dp = lax.axis_index("dp")
    seq = lax.axis_index("seq")
    return dp // 2, dp % 2, seq // 2, seq % 2


def along_z(value, moves):
    return lax.ppermute(value, "dp", [(2 * a + x, 2 * b + x) for a, b in moves for x in (0, 1)])


def cut(value, begin, size):
    return lax.dynamic_slice_in_dim(value, begin, size, 0)


def join(parts):
    return jnp.concatenate(parts) if len(parts) > 1 else parts[0]


def add(left, right):
    return (left.astype(F32) + right.astype(F32)).astype(BF16)


def by_y(y, mine, other):
    return [jnp.where(y == 0, mine, other), jnp.where(y == 0, other, mine)]


def blank(shape):
    return pl.pallas_call(
        lambda out: None,
        out_specs=pl.BlockSpec(memory_space=pl.ANY),
        out_shape=jax.ShapeDtypeStruct(shape, BF16),
        compiler_params=params(),
    )()


def gather_tiles(master_blocks):
    z, x, y, core = spot()
    lone, both, half = G_LONE // 2, (G_HALF - 2 * G_LONE) // 2, G_HALF // 2
    fourth = (SHARD - FAR) // 4
    mine = prep(
        master_blocks,
        jnp.concatenate(
            [half * core + lone * y + jnp.arange(lone), half * core + 2 * lone + jnp.arange(both)]
        ).astype(jnp.int32),
    )
    last = prep(
        master_blocks,
        ((FAR + fourth * lax.axis_index("seq")) // 2 + jnp.arange(fourth // 2)).astype(jnp.int32),
    )
    far = lax.all_gather(last, ("dp", "seq"), axis=0, tiled=True)
    ring = [(0, 1), (1, 2), (2, 3), (3, 0)]
    near = blank((8, 2 * G_HALF, SUB, WIDE))
    rows = [mine]
    cross = []
    halves = []
    for phase in range(6):
        out = {}
        if phase < 3:
            out["z"] = along_z(rows[phase], ring)
        if phase < 4:
            out["x"] = lax.ppermute(rows[phase], "dp", SWAP_X)
        if 1 <= phase < 5:
            here = [rows[phase - 1], cross[phase - 1]]
            out["y"] = lax.ppermute(join([part[:G_LONE] for part in here]), "seq", SWAP_Y)
        if phase >= 2:
            out["core"] = lax.ppermute(join(halves[phase - 2]), "seq", SWAP_CORE)
        out, rows, cross, halves = lax.optimization_barrier((out, rows, cross, halves))
        if "z" in out:
            rows = rows + [out["z"]]
        if "x" in out:
            cross = cross + [out["x"]]
        if "y" in out:
            halves = halves + [
                [
                    join(by_y(y, part[:G_LONE], out["y"][G_LONE * i : G_LONE * (i + 1)]) + [part[G_LONE:]])
                    for i, part in enumerate(here)
                ]
            ]
        if "core" in out:
            step = phase - 2
            for side in range(2):
                owner = 2 * ((z - step) % 4) + (x + side) % 2
                own = halves[step][side][None]
                got = out["core"][None, G_HALF * side : G_HALF * (side + 1)]
                near = lax.dynamic_update_slice(near, own, (owner, G_HALF * core, 0, 0))
                near = lax.dynamic_update_slice(near, got, (owner, G_HALF * (1 - core), 0, 0))
    return near.reshape(-1, SUB, WIDE), far


ROUTES = (
    (((3, 2),), ((2, 1),), ((1, 0),)),
    (((3, 2), (0, 1)), ((2, 1),)),
    (((0, 1), (3, 2)), ((1, 2),)),
    (((0, 1),), ((1, 2),), ((2, 3),)),
)
LONE = R_LONE // CHUNKS
BOTH = R_BOTH // CHUNKS
GROUP_ORDER = [[0, 2, 1, 3]]


def lone_at(core):
    return 2 * R_LONE * core


def both_at(core):
    return 4 * R_LONE + (SHARD - 4 * R_LONE - R_BOTH) * core


def chunk_pairs(k):
    table = []
    for core in range(2):
        for y in range(2):
            table += [(lone_at(core) + R_LONE * y + LONE * k) // 2 + i for i in range(LONE // 2)]
        table += [(both_at(core) + BOTH * k) // 2 + i for i in range(BOTH // 2)]
    return jnp.asarray(table, jnp.int32)


def half_of(source, core):
    array, offset = source
    return join([cut(array, offset + lone_at(core), 2 * R_LONE), cut(array, offset + both_at(core), R_BOTH)])


def group_lone(array, offset):
    return lax.psum_scatter(
        array[offset : offset + 4 * R_LONE], "seq", scatter_dimension=0, tiled=True,
        axis_index_groups=GROUP_ORDER,
    )


def both_parts(array, offset, core):
    return jnp.stack([cut(array, offset + SHARD * i + both_at(core), R_BOTH) for i in range(2)])


def chunks_of(lone, both):
    return [
        (lone[:, LONE * k : LONE * (k + 1)], both[:, BOTH * k : BOTH * (k + 1)]) for k in range(CHUNKS)
    ]


class Sums:
    def __init__(self):
        self.at = spot()
        self.state = {}

    def send(self, task):
        z, x, y, core = self.at
        state = self.state
        kind, who = task[0], task[1]
        if kind == "Y":
            return lax.ppermute(cut(state["lone", who], 1 - y, 1)[0], "seq", SWAP_Y)
        if kind == "X":
            lone, both = state["kept", who]
            return lax.ppermute(join([cut(lone, 1 - x, 1)[0], cut(both, 1 - x, 1)[0]]), "dp", SWAP_X)
        if kind == "Z":
            return along_z(state["value", who], ROUTES[who][task[2]])
        if kind == "F":
            values = [state["value", zi] for zi in range(4)]
            mine = jnp.where(z == 0, values[0], jnp.where(z == 1, values[1], jnp.where(z == 2, values[2], values[3])))
            state["mine", 0] = mine
            return lax.ppermute(mine, "seq", SWAP_Y)
        if kind == "G":
            return lax.ppermute(state["whole", 0], "seq", SWAP_CORE)
        axis, step = (("seq", 1), ("seq", 2), ("dp", 1), ("dp", 2), ("dp", 4))[who]
        size = lax.axis_size(axis)
        return lax.ppermute(state["norms", 0], axis, [(i, i ^ step) for i in range(size)])

    def take(self, task, got):
        z, x, y, core = self.at
        state = self.state
        kind, who = task[0], task[1]
        if kind == "Y":
            state["kept", who] = (add(cut(state.pop(("lone", who)), y, 1)[0], got), state.pop(("both", who)))
        elif kind == "X":
            lone, both = state.pop(("kept", who))
            state["value", who] = add(join([cut(lone, x, 1)[0], cut(both, x, 1)[0]]), got)
        elif kind == "Z":
            state["value", who] = add(state["value", who], got)
        elif kind == "F":
            mine = state.pop(("mine", 0))
            state["whole", 0] = join(by_y(y, mine[:LONE], got[:LONE]) + [add(mine[LONE:], got[LONE:])])
        elif kind == "G":
            half = state.pop(("whole", 0))
            state["owned", 0] = join([jnp.where(core == 0, half, got), jnp.where(core == 0, got, half)])
        else:
            state["norms", 0] = state["norms", 0] + got

    def step(self, tasks):
        out = [self.send(task) for task in tasks]
        out, self.state = lax.optimization_barrier((out, self.state))
        for task, got in zip(tasks, out):
            self.take(task, got)


def beside(chunks, tasks, work):
    out = [chunks[k].send(task) for k, task in tasks]
    made = work()
    out, made, states = lax.optimization_barrier((out, made, [chunk.state for chunk in chunks]))
    for chunk, state in zip(chunks, states):
        chunk.state = state
    for (k, task), got in zip(tasks, out):
        chunks[k].take(task, got)
    return made


def pair_up(halves, chunks, zi):
    for k, chunk in enumerate(chunks):
        chunk.state["lone", zi] = jnp.stack(
            [
                jnp.stack([half[R_LONE * y + LONE * k : R_LONE * y + LONE * (k + 1)] for half in halves])
                for y in range(2)
            ]
        )
        chunk.state["both", zi] = jnp.stack(
            [half[2 * R_LONE + BOTH * k : 2 * R_LONE + BOTH * (k + 1)] for half in halves]
        )


def pad_regions(value, pairs):
    reg = value.shape[0] // pairs
    cube = value.reshape(pairs, reg, value.shape[1])
    return jnp.pad(cube, ((0, 0), (0, VIS_PAD - reg), (0, 0))).reshape(pairs * VIS_PAD, -1)


def cut_regions(value, pairs, reg):
    return value.reshape(pairs, VIS_PAD, -1)[:, :reg].reshape(pairs * reg, -1)


def fast_shards(
    x_text, x_vis, caption_len, cot_text, cot_vis, master_blocks,
    stat_left, stat_right, root_left, root_right, norm_params, norm_second,
):
    pairs = caption_len.shape[0]
    reg = x_vis.shape[0] // pairs
    near, far = gather_tiles(master_blocks)
    lengths = jnp.concatenate([caption_len, jnp.full((2,), reg, jnp.int32)])
    regions = jnp.full((2,), reg, jnp.int32)
    xv = pad_regions(x_vis, pairs)
    cv = pad_regions(cot_vis, pairs)
    vis_norms = norm_params[:, : 3 * VIS].reshape(2, 3, VIS)
    text_norms = norm_params[:, 3 * VIS :].reshape(2, 3, TXT)
    co_vis, co_text, vis_ctx, text_ctx = co_forward(lengths, xv, x_text, near, far)
    (out_vis, v_first, v_act, v_second, v_sctx, v_fback, v_pback, v_bback, v_dself, v_tback,
     v_resid, v_dctx, v_sums) = middle(1, regions, vis_ctx, xv, cv, vis_norms, near, far, VIS_PAD, HEAD_V, 32)
    vis_mid = weight_grads(
        (1, 2, 3, 4, 5), (vis_ctx, v_first, v_act, v_second, v_sctx),
        (v_fback, v_pback, v_bback, v_dself, v_tback),
    )
    _, _, _, core = spot()
    chunks = [Sums() for _ in range(CHUNKS)]
    vis_at, text_at = TILES[1][0], TILES[7][0]
    vis_pair, text_pair = (vis_mid, 2 * SHARD - vis_at), 6 * SHARD - text_at
    lone = [group_lone(vis_mid, vis_pair[1] + SHARD * i) for i in range(2)]
    far_both = lax.ppermute(both_parts(*vis_pair, 1 - core), "seq", SWAP_CORE)
    (out_text, t_first, t_act, t_second, t_sctx, t_fback, t_pback, t_bback, t_dself, t_tback,
     t_resid, t_dctx, t_sums) = middle(
        7, lengths, text_ctx, x_text, cot_text, text_norms, near, far, x_text.shape[0] // pairs, HEAD_T, 32
    )
    chunks[0].state["norms", 0] = jnp.concatenate([v_sums.reshape(2, -1), t_sums.reshape(2, -1)], 1)
    lefts = (text_ctx, t_first, t_act, t_second, t_sctx)
    rights = (t_fback, t_pback, t_bback, t_dself, t_tback)
    lefts, rights, far_both = lax.optimization_barrier((lefts, rights, far_both))
    text_mid = weight_grads((7, 8, 9, 10, 11), lefts, rights)
    both = add(both_parts(*vis_pair, core), far_both)
    far_both = lax.ppermute(both_parts(text_mid, text_pair, 1 - core), "seq", SWAP_CORE)
    back = (co_vis, co_text, v_dctx, t_dctx, v_resid, t_resid)
    back, lone, both, text_mid = lax.optimization_barrier((back, lone, both, text_mid))
    for k, kept in enumerate(chunks_of(jnp.stack(lone), both)):
        chunks[k].state["kept", 1] = kept
    lone = [group_lone(text_mid, text_pair + SHARD * i) for i in range(2)]
    dco_vis, dco_text, grad_vis, grad_text, far_both = beside(
        chunks,
        [(0, ("X", 1)), (0, ("N", 0))],
        lambda: (*co_backward(lengths, *back, near, far), far_both),
    )
    vis_co, text_co = beside(
        chunks,
        [(1, ("X", 1)), (0, ("Z", 1, 0)), (0, ("N", 1))],
        lambda: (weight_grads((0,), (xv,), (dco_vis,)), weight_grads((6,), (x_text,), (dco_text,))),
    )
    both = add(both_parts(text_mid, text_pair, core), far_both)
    place = {
        0: (vis_co, 0),
        1: (jnp.concatenate([vis_co[SHARD:], vis_mid[: 2 * SHARD - vis_at]]), 0),
        4: (jnp.concatenate([vis_mid[4 * SHARD - vis_at :], text_co, text_mid[: 5 * SHARD - text_at]]), 0),
        5: (text_mid, 5 * SHARD - text_at),
    }

    def swap_halves(tasks, owners):
        got = beside(
            chunks, tasks, lambda: [lax.ppermute(half_of(place[o], 1 - core), "seq", SWAP_CORE) for o in owners]
        )
        pair_up([add(half_of(place[o], core), part) for o, part in zip(owners, got)], chunks, owners[0] // 2)

    swap_halves([(0, ("Z", 1, 1)), (1, ("Z", 1, 0)), (0, ("N", 2))], (0, 1))
    for k, kept in enumerate(chunks_of(jnp.stack(lone), both)):
        chunks[k].state["kept", 3] = kept
    swap_halves([(0, ("Y", 0)), (0, ("X", 3)), (1, ("Z", 1, 1))], (4, 5))
    beside(chunks, [(0, ("Y", 2)), (0, ("X", 0)), (0, ("Z", 3, 0)), (1, ("X", 3)), (0, ("N", 3))], lambda: ())
    chunks[1].step([("Y", 0), ("Z", 3, 0)])
    chunks[0].step([("X", 2), ("Z", 0, 0), ("Z", 3, 1), ("N", 4)])
    chunks[1].step([("Y", 2), ("X", 0), ("Z", 3, 1)])
    chunks[0].step([("Z", 0, 1), ("Z", 2, 0), ("Z", 3, 2)])
    chunks[1].step([("X", 2), ("Z", 0, 0), ("Z", 3, 2)])
    chunks[0].step([("Z", 0, 2), ("Z", 2, 1)])
    chunks[1].step([("Z", 0, 1), ("Z", 2, 0)])
    chunks[0].step([("F", 0)])
    beside(chunks, [(0, ("G", 0)), (1, ("Z", 0, 2)), (1, ("Z", 2, 1))], lambda: ())
    statistics = (master_blocks, stat_left, stat_right, root_left, root_right)
    early = chunk_pairs(0)
    count = 3 * early.shape[0] // 4
    owned = chunks[0].state["owned", 0]
    renewed = beside(chunks, [(1, ("F", 0))], lambda: renew(early[:count], owned[: 2 * count], *statistics, ()))
    renewed = beside(
        chunks, [(1, ("G", 0))], lambda: renew(early[count:], owned[2 * count :], *statistics, renewed)
    )
    grad_blocks, left_new, right_new, master_new = renew(
        chunk_pairs(1), chunks[1].state["owned", 0], *statistics, renewed
    )
    norm_grads = chunks[0].state["norms", 0]
    second_new = STAT_DECAY * norm_second + (1.0 - STAT_DECAY) * norm_grads * norm_grads
    norm_new = norm_params - NORM_RATE * norm_grads / (jnp.sqrt(second_new) + MOMENT_EPSILON)
    return (
        out_text,
        cut_regions(out_vis, pairs, reg),
        grad_text,
        cut_regions(grad_vis, pairs, reg),
        grad_blocks,
        left_new,
        right_new,
        master_new,
        norm_grads,
        second_new,
        norm_new,
    )


def fits(mesh):
    return mesh.shape["dp"] == 8 and mesh.shape["seq"] == 4


def solution(mesh):
    placed = (
        P(("dp", "seq"), None),
        P(("dp", "seq"), None),
        P(("dp", "seq")),
        P(("dp", "seq"), None),
        P(("dp", "seq"), None),
        P("dp", None),
        P("dp", None),
        P("dp", None),
        P("dp", None),
        P("dp", None),
        P(),
        P(),
    )
    step = fast_shards if fits(mesh) else shards
    return jax.shard_map(
        step,
        mesh=mesh,
        in_specs=placed,
        out_specs=(
            P(("dp", "seq"), None),
            P(("dp", "seq"), None),
            P(("dp", "seq"), None),
            P(("dp", "seq"), None),
            P("dp", None),
            P("dp", None),
            P("dp", None),
            P("dp", None),
            P(),
            P(),
            P(),
        ),
        check_vma=False,
    )
```

```python
import functools

import jax
import jax.numpy as jnp
from jax import lax
from jax.experimental import pallas as pl
from jax.experimental.pallas import tpu as pltpu
from jax.sharding import PartitionSpec as P

TXT = 768
VIS = 1024
BI = 1024
FFT = 3072
FFV = 1024
HEAD = 128
HEAD_T = 64
HEAD_V = 128
BLK = 64


MASK_FILL = -1000000000.0
STAT_DECAY = 0.9
WEIGHT_RATE = 0.3
NORM_RATE = 0.2
NORM_EPSILON = 1e-05
MOMENT_EPSILON = 1e-08
HIGHEST = lax.Precision.HIGHEST
CONTRACT_COLS = (((1,), (1,)), ((), ()))


def weight_layout():
    return (
        (VIS, BI, 3),
        (BI, VIS, 1),
        (VIS, FFV, 1),
        (FFV, VIS, 1),
        (VIS, VIS, 3),
        (VIS, VIS, 1),
        (TXT, BI, 3),
        (BI, TXT, 1),
        (TXT, FFT, 1),
        (FFT, TXT, 1),
        (TXT, TXT, 3),
        (TXT, TXT, 1),
    )


def unpack_weights(flat):
    size = BLK
    blocks = flat.reshape(flat.shape[0], size, size)
    begin = 0
    matrices = []
    for rows, columns, count in weight_layout():
        number = count * rows * columns // (size * size)
        shaped = blocks[begin : begin + number].reshape(
            count, rows // size, columns // size, size, size
        )
        matrices.append(shaped.transpose(1, 3, 0, 2, 4).reshape(rows, count * columns))
        begin += number
    return matrices


def block_grad(inputs, grads, count):
    size = BLK
    left = inputs.reshape(inputs.shape[0], inputs.shape[1] // size, size)
    right = grads.reshape(grads.shape[0], count, grads.shape[1] // (count * size), size)
    return jnp.einsum("nai,nkbj->kabij", left, right, preferred_element_type=jnp.float32).reshape(
        -1, size * size
    )


def norm_columns(values, stream, which):
    if stream == 0:
        begin = which * VIS
        width = VIS
    else:
        begin = 3 * VIS + which * TXT
        width = TXT
    return values[:, begin : begin + width]


def gelu_exact(value):
    return jax.nn.gelu(value, approximate=False)


def heads_of(side, which, head):
    part = side[:, :, which, :]
    return part.reshape(part.shape[0], part.shape[1], part.shape[2] // head, head)


def scores_of(query, keys, live, head):
    scores = jnp.einsum(
        "gqhd,gkhd->ghqk", query, keys, preferred_element_type=jnp.float32
    ) * head ** (-0.5)
    if live is not None:
        scores = jnp.where(live[:, None, None, :], scores, MASK_FILL)
    return scores


def attend_one(query, keys, values, live, head):
    scores = scores_of(query, keys, live, head)
    top = jnp.max(scores, axis=3, keepdims=True)
    raised = jnp.exp(scores - top)
    total = jnp.sum(raised, axis=3, keepdims=True)
    found = jnp.einsum(
        "ghqk,gkhd->gqhd",
        (raised / total).astype(jnp.bfloat16),
        values,
        preferred_element_type=jnp.float32,
    ).astype(jnp.bfloat16)
    return (found.reshape(found.shape[0], found.shape[1], -1), top + jnp.log(total))


def attend_one_back(query, keys, values, live, head, logsum, dfound):
    scale = head ** (-0.5)
    probs = jnp.exp(scores_of(query, keys, live, head) - logsum)
    upstream = dfound.reshape(dfound.shape[0], dfound.shape[1], -1, head)
    dprobs = jnp.einsum("gqhd,gkhd->ghqk", upstream, values, preferred_element_type=jnp.float32)
    dvalues = jnp.einsum(
        "ghqk,gqhd->gkhd", probs.astype(jnp.bfloat16), upstream, preferred_element_type=jnp.float32
    )
    dscores = (probs * (dprobs - jnp.sum(probs * dprobs, axis=3, keepdims=True))).astype(
        jnp.bfloat16
    )
    dquery = (
        jnp.einsum("ghqk,gkhd->gqhd", dscores, keys, preferred_element_type=jnp.float32) * scale
    )
    dkeys = (
        jnp.einsum("ghqk,gqhd->gkhd", dscores, query, preferred_element_type=jnp.float32) * scale
    )
    return (dquery, dkeys, dvalues)


def attention_plan(vis_side, text_side, lengths, cross):
    live = (
        lax.broadcasted_iota(jnp.int32, (lengths.shape[0], text_side.shape[1]), 1)
        < lengths[:, None]
    )
    if cross:
        return ((vis_side, text_side, live, HEAD), (text_side, vis_side, None, HEAD))
    return ((vis_side, vis_side, None, HEAD_V), (text_side, text_side, live, HEAD_T))


def pair_attend(vis_side, text_side, lengths, cross):
    results = []
    for query_side, key_side, live, head in attention_plan(vis_side, text_side, lengths, cross):
        results.append(
            attend_one(
                heads_of(query_side, 0, head),
                heads_of(key_side, 1, head),
                heads_of(key_side, 2, head),
                live,
                head,
            )
        )
    return (results[0][0], results[1][0], results[0][1], results[1][1])


def pair_attend_back(
    vis_side, text_side, lengths, cross, vis_logsum, text_logsum, vis_dfound, text_dfound
):
    plan = attention_plan(vis_side, text_side, lengths, cross)
    parts = []
    for (query_side, key_side, live, head), logsum, dfound in zip(
        plan, (vis_logsum, text_logsum), (vis_dfound, text_dfound)
    ):
        parts.append(
            attend_one_back(
                heads_of(query_side, 0, head),
                heads_of(key_side, 1, head),
                heads_of(key_side, 2, head),
                live,
                head,
                logsum,
                dfound,
            )
        )
    if cross:
        vis_parts = (parts[0][0], parts[1][1], parts[1][2])
        text_parts = (parts[1][0], parts[0][1], parts[0][2])
    else:
        vis_parts = parts[0]
        text_parts = parts[1]
    vis_grad = jnp.stack(vis_parts, axis=2).reshape(vis_side.shape).astype(jnp.bfloat16)
    text_grad = jnp.stack(text_parts, axis=2).reshape(text_side.shape).astype(jnp.bfloat16)
    return (vis_grad, text_grad)


def to_heads(vis_side, text_side):
    return (vis_side, text_side)


def from_heads(vis_found, text_found):
    return (vis_found, text_found)


def dfound_to_heads(vis_dfound, text_dfound):
    return (vis_dfound, text_dfound)


def grads_from_heads(vis_grad, text_grad):
    return (vis_grad, text_grad)


def side_of(rows_in, weight, pairs):
    made = jnp.dot(rows_in, weight, preferred_element_type=jnp.float32).astype(jnp.bfloat16)
    return made.reshape(pairs, -1, 3, weight.shape[1] // 3)


def norm_forward(resid, columns):
    mean = jnp.mean(resid, -1, keepdims=True)
    centered = resid - mean
    scale = lax.rsqrt(jnp.mean(centered * centered, -1, keepdims=True) + NORM_EPSILON)
    normed = centered * scale
    return (normed, scale, normed * columns[0] + columns[1])


def norm_backward(upstream, normed, scale, gain):
    scaled = upstream * gain
    resid_grad = scale * (
        scaled
        - jnp.mean(scaled, -1, keepdims=True)
        - normed * jnp.mean(scaled * normed, -1, keepdims=True)
    )
    return (resid_grad, jnp.sum(upstream * normed, 0), jnp.sum(upstream, 0))


def stream_middle(context_rows, x_rows, weights, values, stream, pairs):
    resid = x_rows.astype(jnp.float32) + jnp.dot(
        context_rows, weights[1], preferred_element_type=jnp.float32
    )
    normed_one, scale_one, first = norm_forward(resid, norm_columns(values, stream, 0))
    first_low = first.astype(jnp.bfloat16)
    pre = jnp.dot(first_low, weights[2], preferred_element_type=jnp.float32)
    act = gelu_exact(pre).astype(jnp.bfloat16)
    resid = first + jnp.dot(act, weights[3], preferred_element_type=jnp.float32)
    normed_two, scale_two, second = norm_forward(resid, norm_columns(values, stream, 1))
    second_low = second.astype(jnp.bfloat16)
    side = side_of(second_low, weights[4], pairs)
    return (
        side,
        (normed_one, scale_one, first_low, pre, act, normed_two, scale_two, second, second_low),
    )


def stream_end(self_rows, second, out_weight, values, stream):
    resid = second + jnp.dot(self_rows, out_weight, preferred_element_type=jnp.float32)
    normed_three, scale_three, third = norm_forward(resid, norm_columns(values, stream, 2))
    return (third.astype(jnp.bfloat16), normed_three, scale_three)


def stream_back_end(
    cotangent, normed_three, scale_three, self_rows, out_weight, values, stream, pairs
):
    resid_three, gain_three, bias_three = norm_backward(
        cotangent.astype(jnp.float32), normed_three, scale_three, norm_columns(values, stream, 2)[0]
    )
    third_back = resid_three.astype(jnp.bfloat16)
    grad_self_out = block_grad(self_rows, third_back, 1)
    dself = lax.dot_general(
        third_back, out_weight, CONTRACT_COLS, preferred_element_type=jnp.float32
    )
    dself = dself.astype(jnp.bfloat16).reshape(pairs, -1, out_weight.shape[0])
    return (resid_three, dself, grad_self_out, gain_three, bias_three)


def stream_back_middle(resid_three, dself_side, kept, context_rows, weights, values, stream, pairs):
    normed_one, scale_one, first_low, pre, act, normed_two, scale_two, second, second_low = kept
    dself_rows = dself_side.reshape(-1, dself_side.shape[2] * dself_side.shape[3])
    grad_self_qkv = block_grad(second_low, dself_rows, 3)
    second_in = resid_three + lax.dot_general(
        dself_rows, weights[4], CONTRACT_COLS, preferred_element_type=jnp.float32
    )
    resid_two, gain_two, bias_two = norm_backward(
        second_in, normed_two, scale_two, norm_columns(values, stream, 1)[0]
    )
    branch_back = resid_two.astype(jnp.bfloat16)
    grad_down = block_grad(act, branch_back, 1)
    act_grad = lax.dot_general(
        branch_back, weights[3], CONTRACT_COLS, preferred_element_type=jnp.float32
    )
    pre_grad = jax.vjp(gelu_exact, pre)[1](act_grad)[0].astype(jnp.bfloat16)
    grad_up = block_grad(first_low, pre_grad, 1)
    first_in = resid_two + lax.dot_general(
        pre_grad, weights[2], CONTRACT_COLS, preferred_element_type=jnp.float32
    )
    resid_one, gain_one, bias_one = norm_backward(
        first_in, normed_one, scale_one, norm_columns(values, stream, 0)[0]
    )
    first_back = resid_one.astype(jnp.bfloat16)
    grad_co_out = block_grad(context_rows, first_back, 1)
    dcontext = lax.dot_general(
        first_back, weights[1], CONTRACT_COLS, preferred_element_type=jnp.float32
    )
    dcontext = dcontext.astype(jnp.bfloat16).reshape(pairs, -1, BI)
    return (
        resid_one,
        dcontext,
        (grad_co_out, grad_up, grad_down, grad_self_qkv),
        (gain_one, gain_two),
        (bias_one, bias_two),
    )


def shards(
    x_text,
    x_vis,
    caption_len,
    cot_text,
    cot_vis,
    master_blocks,
    stat_left,
    stat_right,
    root_left,
    root_right,
    norm_params,
    norm_second,
):
    pairs = caption_len.shape[0]
    width = master_blocks.shape[1] // lax.axis_size("seq")
    mine = lax.dynamic_slice_in_dim(master_blocks, lax.axis_index("seq") * width, width, 1).astype(
        jnp.bfloat16
    )
    partial_value = lax.all_gather(mine, "dp", axis=0, tiled=True)
    every = lax.all_gather(partial_value, "seq", axis=1, tiled=True)
    matrices = unpack_weights(every)
    vis_weights = matrices[:6]
    text_weights = matrices[6:]
    vis_co = side_of(x_vis, vis_weights[0], pairs)
    text_co = side_of(x_text, text_weights[0], pairs)
    lengths = caption_len
    vis_co_use, text_co_use = to_heads(vis_co, text_co)
    vis_found, text_found, vis_co_sum, text_co_sum = pair_attend(
        vis_co_use, text_co_use, lengths, True
    )
    vis_context, text_context = from_heads(vis_found, text_found)
    vis_context_rows = vis_context.reshape(-1, BI)
    text_context_rows = text_context.reshape(-1, BI)
    vis_self, vis_kept = stream_middle(vis_context_rows, x_vis, vis_weights, norm_params, 0, pairs)
    text_self, text_kept = stream_middle(
        text_context_rows, x_text, text_weights, norm_params, 1, pairs
    )
    vis_self_use, text_self_use = to_heads(vis_self, text_self)
    vis_found, text_found, vis_self_sum, text_self_sum = pair_attend(
        vis_self_use, text_self_use, lengths, False
    )
    vis_self_context, text_self_context = from_heads(vis_found, text_found)
    vis_self_rows = vis_self_context.reshape(-1, VIS)
    text_self_rows = text_self_context.reshape(-1, TXT)
    out_vis, vis_normed_three, vis_scale_three = stream_end(
        vis_self_rows, vis_kept[7], vis_weights[5], norm_params, 0
    )
    out_text, text_normed_three, text_scale_three = stream_end(
        text_self_rows, text_kept[7], text_weights[5], norm_params, 1
    )
    vis_resid_three, vis_dself, vis_grad_so, vis_gain_three, vis_bias_three = stream_back_end(
        cot_vis,
        vis_normed_three,
        vis_scale_three,
        vis_self_rows,
        vis_weights[5],
        norm_params,
        0,
        pairs,
    )
    text_resid_three, text_dself, text_grad_so, text_gain_three, text_bias_three = stream_back_end(
        cot_text,
        text_normed_three,
        text_scale_three,
        text_self_rows,
        text_weights[5],
        norm_params,
        1,
        pairs,
    )
    vis_dheads, text_dheads = dfound_to_heads(vis_dself, text_dself)
    vis_dgot, text_dgot = pair_attend_back(
        vis_self_use,
        text_self_use,
        lengths,
        False,
        vis_self_sum,
        text_self_sum,
        vis_dheads,
        text_dheads,
    )
    vis_dself_side, text_dself_side = grads_from_heads(vis_dgot, text_dgot)
    vis_resid_one, vis_dcontext, vis_grads_mid, vis_gains_mid, vis_biases_mid = stream_back_middle(
        vis_resid_three,
        vis_dself_side,
        vis_kept,
        vis_context_rows,
        vis_weights,
        norm_params,
        0,
        pairs,
    )
    text_resid_one, text_dcontext, text_grads_mid, text_gains_mid, text_biases_mid = (
        stream_back_middle(
            text_resid_three,
            text_dself_side,
            text_kept,
            text_context_rows,
            text_weights,
            norm_params,
            1,
            pairs,
        )
    )
    vis_dheads, text_dheads = dfound_to_heads(vis_dcontext, text_dcontext)
    vis_dgot, text_dgot = pair_attend_back(
        vis_co_use, text_co_use, lengths, True, vis_co_sum, text_co_sum, vis_dheads, text_dheads
    )
    vis_dco, text_dco = grads_from_heads(vis_dgot, text_dgot)
    vis_dco_rows = vis_dco.reshape(-1, 3 * BI)
    text_dco_rows = text_dco.reshape(-1, 3 * BI)
    grad_vis = vis_resid_one + lax.dot_general(
        vis_dco_rows, vis_weights[0], CONTRACT_COLS, preferred_element_type=jnp.float32
    )
    grad_text = text_resid_one + lax.dot_general(
        text_dco_rows, text_weights[0], CONTRACT_COLS, preferred_element_type=jnp.float32
    )
    vis_grad_co = block_grad(x_vis, vis_dco_rows, 3)
    text_grad_co = block_grad(x_text, text_dco_rows, 3)
    local_blocks = jnp.concatenate(
        [vis_grad_co]
        + list(vis_grads_mid)
        + [vis_grad_so]
        + [text_grad_co]
        + list(text_grads_mid)
        + [text_grad_so],
        0,
    )
    norm_local = jnp.stack(
        [
            jnp.concatenate(
                [
                    vis_gains_mid[0],
                    vis_gains_mid[1],
                    vis_gain_three,
                    text_gains_mid[0],
                    text_gains_mid[1],
                    text_gain_three,
                ]
            ),
            jnp.concatenate(
                [
                    vis_biases_mid[0],
                    vis_biases_mid[1],
                    vis_bias_three,
                    text_biases_mid[0],
                    text_biases_mid[1],
                    text_bias_three,
                ]
            ),
        ]
    )
    columns = lax.psum_scatter(
        local_blocks.astype(jnp.bfloat16), "seq", scatter_dimension=1, tiled=True
    ).astype(jnp.float32)
    owned_columns = lax.psum_scatter(columns, "dp", scatter_dimension=0, tiled=True)
    owned = lax.all_gather(owned_columns.astype(jnp.bfloat16), "seq", axis=1, tiled=True).astype(
        owned_columns.dtype
    )
    norm_grads = lax.psum(norm_local, ("dp", "seq"))
    number = owned.shape[0]
    grad_cube = owned.reshape(number, BLK, BLK)
    left_cube = stat_left.reshape(number, BLK, BLK)
    right_cube = stat_right.reshape(number, BLK, BLK)
    rootl_cube = root_left.reshape(number, BLK, BLK)
    rootr_cube = root_right.reshape(number, BLK, BLK)
    left_new = STAT_DECAY * left_cube + (1.0 - STAT_DECAY) * jnp.einsum(
        "bij,bkj->bik", grad_cube, grad_cube, precision=HIGHEST
    )
    right_new = STAT_DECAY * right_cube + (1.0 - STAT_DECAY) * jnp.einsum(
        "bji,bjk->bik", grad_cube, grad_cube, precision=HIGHEST
    )
    half = jnp.einsum("bij,bjk->bik", rootl_cube, grad_cube, precision=HIGHEST)
    direction = jnp.einsum("bij,bjk->bik", half, rootr_cube, precision=HIGHEST)
    master_new = master_blocks - WEIGHT_RATE * direction.reshape(number, BLK * BLK)
    second_new = STAT_DECAY * norm_second + (1.0 - STAT_DECAY) * norm_grads * norm_grads
    norm_new = norm_params - NORM_RATE * norm_grads / (jnp.sqrt(second_new) + MOMENT_EPSILON)
    return (
        out_text,
        out_vis,
        grad_text,
        grad_vis,
        owned,
        left_new.reshape(number, BLK * BLK),
        right_new.reshape(number, BLK * BLK),
        master_new,
        norm_grads,
        second_new,
        norm_new,
    )


SUB = 64
WIDE = 256
QUAD = 4
F32 = jnp.float32
BF16 = jnp.bfloat16
VIS_PAD = 48
VMEM_LIMIT = 60 * 1024 * 1024
NT = (((1,), (1,)), ((), ()))
TN = (((0,), (0,)), ((), ()))


def tile_table():
    begin = 0
    table = []
    for rows, columns, count in weight_layout():
        r, g = rows // SUB, columns // WIDE
        table.append((begin, count, r, g))
        begin += count * r * g
    return table


TILES = tile_table()
SHARD = 158
FAR = 62
G_HALF = 32
G_LONE = 8
R_LONE = 28
R_BOTH = 24
R_HALF = 2 * R_LONE + R_BOTH
CHUNKS = 2
SWAP_CORE = [(i, i ^ 1) for i in range(4)]
SWAP_Y = [(i, i ^ 2) for i in range(4)]
SWAP_X = [(i, i ^ 1) for i in range(8)]


def dot(left, right, how=None):
    if how is None:
        return jnp.dot(left, right, preferred_element_type=F32)
    return lax.dot_general(left, right, how, preferred_element_type=F32)


def params(**more):
    return pltpu.CompilerParams(vmem_limit_bytes=VMEM_LIMIT, **more)


def cost(micros):
    return pl.CostEstimate(flops=0, bytes_accessed=int(micros * 3.4e6), transcendentals=0)


def whole(count):
    return [pl.BlockSpec(memory_space=pltpu.VMEM)] * count


def linear(value):
    groups = value.shape[0] // 8
    return value.reshape(groups, 8, 32, 128).transpose(0, 2, 1, 3).reshape(groups * 256, 128)


def unlinear(value):
    groups = value.shape[0] // 256
    return value.reshape(groups, 32, 8, 128).transpose(0, 2, 1, 3).reshape(groups * 8, SUB * SUB)


def lanes_low(rows):
    return lax.broadcasted_iota(jnp.int32, (rows, 2 * SUB), 1) < SUB


def spread_of(ref, b):
    return ref[pl.ds(b, 32, stride=8), :]


def natural_order():
    row = lax.broadcasted_iota(jnp.int32, (SUB, SUB), 0)
    column = lax.broadcasted_iota(jnp.int32, (SUB, SUB), 1)
    return jnp.where(row == 2 * (column % 32) + column // 32, 1.0, 0.0).astype(BF16)


def prep_rows(number, pairs_ref, x_any, o_ref, rows_in, sems):
    def fetch(i):
        rows = pl.ds(pl.multiple_of(pairs_ref[i] * 256, 256), 256)
        return pltpu.make_async_copy(x_any.at[rows], rows_in.at[i], sems.at[i])

    for i in range(number):
        fetch(i).start()
    low = lanes_low(32)
    order = natural_order()

    def step(i, carry):
        fetch(i).wait()
        x_ref = rows_in.at[i]
        spots = range(4)
        one = [spread_of(x_ref, 2 * m) for m in spots]
        two = [spread_of(x_ref, 2 * m + 1) for m in spots]
        rows = [
            jnp.concatenate(
                [
                    jnp.where(low, one[m], pltpu.roll(two[m], SUB, 1)),
                    jnp.where(low, pltpu.roll(one[m], SUB, 1), two[m]),
                ],
                0,
            ).astype(BF16)
            for m in spots
        ]
        made = [dot(order, rows[m]).astype(BF16) for m in spots]
        for m in spots:
            o_ref[2 * i + m // 2, :, (m % 2) * 128 : (m % 2 + 1) * 128] = made[m]
        return carry

    lax.fori_loop(0, number, step, 0, unroll=2 if number % 2 == 0 else 3)


def prep(master_blocks, pairs):
    number = pairs.shape[0]
    return pl.pallas_call(
        functools.partial(prep_rows, number),
        in_specs=[pl.BlockSpec(memory_space=pltpu.SMEM), pl.BlockSpec(memory_space=pl.ANY)],
        out_specs=pl.BlockSpec(memory_space=pltpu.VMEM),
        out_shape=jax.ShapeDtypeStruct((number * 2, SUB, WIDE), BF16),
        scratch_shapes=[pltpu.VMEM((number, 256, 128), F32), pltpu.SemaphoreType.DMA((number,))],
        compiler_params=params(),
        cost_estimate=cost(0.4 * number),
    )(pairs, linear(master_blocks))


def renew_eight(g_ref, m_ref, sl_ref, sr_ref, rl_ref, rr_ref, go_ref, lo_ref, ro_ref, mo_ref, place):
    low = lanes_low(SUB)
    low_half = lanes_low(32)
    nothing = jnp.zeros((SUB, 128), F32)
    pairs = range(4)

    def diagonal(pair):
        return jnp.concatenate([jnp.where(low, pair, nothing), jnp.where(low, nothing, pair)], 0).astype(BF16)

    def mixed(even, odd):
        return (
            jnp.where(low_half, even, pltpu.roll(odd, SUB, 1)),
            jnp.where(low_half, pltpu.roll(even, SUB, 1), odd),
        )

    def natural(ref, pair, spot):
        even, odd = mixed(spread_of(ref, 2 * pair), spread_of(ref, 2 * pair + 1))
        spot[pl.ds(0, 32, stride=2), :] = even
        spot[pl.ds(1, 32, stride=2), :] = odd
        return spot[...]

    def spread(value, spot):
        spot[...] = value
        return mixed(spot[pl.ds(0, 32, stride=2), :], spot[pl.ds(1, 32, stride=2), :])

    tiles = [g_ref[pair // 2, :, (pair % 2) * 128 : (pair % 2 + 1) * 128] for pair in pairs]
    wide = [tile.astype(F32) for tile in tiles]
    grads = [diagonal(value) for value in wide]
    lefts = [natural(rl_ref, pair, place.at[pair, 0]).astype(BF16) for pair in pairs]
    rights = [diagonal(natural(rr_ref, pair, place.at[pair, 1])) for pair in pairs]
    halves = [dot(lefts[pair], grads[pair]).astype(BF16) for pair in pairs]
    left_parts = [dot(tiles[pair], grads[pair], NT) for pair in pairs]
    squares = [dot(tiles[pair], tiles[pair], TN) for pair in pairs]
    right_parts = [jnp.where(low, square[:SUB], square[SUB:]) for square in squares]
    steps = [dot(halves[pair], rights[pair]) for pair in pairs]
    for pair in pairs:
        made = [
            spread(value[pair], place.at[pair, 2 + k])
            for k, value in enumerate((wide, left_parts, right_parts, steps))
        ]
        for i in range(2):
            at = pl.ds(2 * pair + i, 32, stride=8)
            go_ref[at, :] = made[0][i]
            lo_ref[at, :] = STAT_DECAY * sl_ref[at, :] + (1.0 - STAT_DECAY) * made[1][i]
            ro_ref[at, :] = STAT_DECAY * sr_ref[at, :] + (1.0 - STAT_DECAY) * made[2][i]
            mo_ref[at, :] = m_ref[at, :] - WEIGHT_RATE * made[3][i]


SLOTS = 4


def renew_body(steps, which_ref, g_any, *refs):
    ins = refs[:5]
    outs = refs[-9:-5]
    gbuf, inbuf, outbuf, place, sems = refs[-5:]

    def rows(i):
        return pl.ds(pl.multiple_of(which_ref[i] * 256, 256), 256)

    def fetch(i):
        slot = lax.rem(i, SLOTS)
        copies = [pltpu.make_async_copy(g_any.at[pl.ds(2 * i, 2)], gbuf.at[slot], sems.at[slot, 0])]
        for k, ref in enumerate(ins):
            copies.append(
                pltpu.make_async_copy(ref.at[rows(i)], inbuf.at[slot, k], sems.at[slot, 1 + k])
            )
        return copies

    def put(i):
        slot = lax.rem(i, SLOTS)
        return [
            pltpu.make_async_copy(outbuf.at[slot, k], ref.at[rows(i)], sems.at[slot, 6 + k])
            for k, ref in enumerate(outs)
        ]

    def start(copies):
        for copy in copies:
            copy.start()

    def wait(copies):
        for copy in copies:
            copy.wait()

    for i in range(min(SLOTS, steps)):
        start(fetch(i))

    def step(i, carry):
        slot = lax.rem(i, SLOTS)
        wait(fetch(i))

        @pl.when(i >= SLOTS)
        def _():
            wait(put(i - SLOTS))

        renew_eight(
            gbuf.at[slot], *(inbuf.at[slot, k] for k in range(5)), *(outbuf.at[slot, k] for k in range(4)), place
        )
        start(put(i))

        @pl.when(i + SLOTS < steps)
        def _():
            start(fetch(i + SLOTS))

        return carry

    lax.fori_loop(0, steps, step, 0)
    for i in range(max(0, steps - SLOTS), steps):
        wait(put(i))


def renew(which, owned, master_blocks, stat_left, stat_right, root_left, root_right, before):
    steps = which.shape[0]
    shape = jax.ShapeDtypeStruct((master_blocks.shape[0] * 32, 128), F32)
    anywhere = pl.BlockSpec(memory_space=pl.ANY)
    made = pl.pallas_call(
        functools.partial(renew_body, steps),
        in_specs=[pl.BlockSpec(memory_space=pltpu.SMEM)] + [anywhere] * (6 + len(before)),
        out_specs=[anywhere] * 4,
        out_shape=[shape] * 4,
        scratch_shapes=[
            pltpu.VMEM((SLOTS, 2, SUB, WIDE), BF16),
            pltpu.VMEM((SLOTS, 5, 256, 128), F32),
            pltpu.VMEM((SLOTS, 4, 256, 128), F32),
            pltpu.VMEM((4, 6, SUB, 128), F32),
            pltpu.SemaphoreType.DMA((SLOTS, 10)),
        ],
        input_output_aliases={7 + i: i for i in range(len(before))},
        compiler_params=params(),
        cost_estimate=cost(0.7 * steps),
    )(
        which,
        owned,
        *(linear(value) for value in (master_blocks, stat_left, stat_right, root_left, root_right)),
        *(linear(value) for value in before),
    )
    return [unlinear(value) for value in made]


def times(rows_in, w, base, r, g, part, col):
    first = base + part * r * g + col
    return dot(rows_in, jnp.concatenate([w[first + a * g] for a in range(r)], 0))


def times_back(d_ref, w, base, r, g, count, r4):
    total = None
    for part in range(count):
        first = base + (part * r + 4 * r4) * g
        wide = jnp.concatenate(
            [
                jnp.concatenate([w[first + a * g + col] for a in range(4)], 0)
                for col in range(g)
            ],
            1,
        )
        made = dot(d_ref[:, part * g * WIDE : (part + 1) * g * WIDE], wide, NT)
        total = made if total is None else total + made
    return total


def at256(i):
    return pl.ds(pl.multiple_of(i * WIDE, WIDE), WIDE)


def softmax_all(products, scale, limits):
    scores = []
    for product, limit in zip(products, limits):
        column = lax.broadcasted_iota(jnp.int32, product.shape, 1)
        scores.append(jnp.where(column < limit, product * scale, MASK_FILL))
    tops = [jnp.max(score, 1, keepdims=True) for score in scores]
    raised = [jnp.exp(score - top) for score, top in zip(scores, tops)]
    shares = [1.0 / jnp.sum(value, 1, keepdims=True) for value in raised]
    return [value * share for value, share in zip(raised, shares)]


def score_grads(probs, dprobs):
    weighted = [p * d for p, d in zip(probs, dprobs)]
    totals = [jnp.sum(value, 1, keepdims=True) for value in weighted]
    return [(value - p * total).astype(BF16) for value, p, total in zip(weighted, probs, totals)]


def at128(i):
    return pl.ds(pl.multiple_of(i * 128, 128), 128)


def load(near, far, w, sems, pieces, base):
    started = []
    used = 0
    for i, which in enumerate(pieces):
        begin, count, r, g = TILES[which]
        end = begin + count * r * g
        copies = []
        for owner in range(begin // SHARD, (end - 1) // SHARD + 1):
            first = max(begin, owner * SHARD)
            last = min(end, (owner + 1) * SHARD)
            middle = min(max(owner * SHARD + FAR, first), last)
            for source, lo, hi, at in (
                (near, first, middle, owner * (2 * G_HALF) + first - owner * SHARD),
                (far, middle, last, owner * (SHARD - FAR) + middle - owner * SHARD - FAR),
            ):
                if lo < hi:
                    copies.append(
                        pltpu.make_async_copy(
                            source.at[pl.ds(at, hi - lo)],
                            w.at[pl.ds(base[i] + lo - begin, hi - lo)],
                            sems.at[used],
                        )
                    )
                    copies[-1].start()
                    used += 1
        started.append(copies)
    return started


def arrive(copies):
    for copy in copies:
        copy.wait()


def tiles_of(which):
    _, count, r, g = TILES[which]
    return count * r * g


def co_body(len_ref, xv_ref, xt_ref, near, far, cv_ref, ct_ref, fv_ref, ft_ref, w, sems):
    base = (0, tiles_of(0))
    copies = load(near, far, w, sems, (0, 6), base)
    for which, at, x_ref, o_ref, copy in (
        (0, base[0], xv_ref, cv_ref, copies[0]),
        (6, base[1], xt_ref, ct_ref, copies[1]),
    ):
        _, count, r, g = TILES[which]
        arrive(copy)

        def column(i, carry, at=at, r=r, g=g, x_ref=x_ref, o_ref=o_ref):
            o_ref[:, at256(i)] = times(x_ref[...], w, at, r, g, i // g, i % g).astype(BF16)
            return carry

        lax.fori_loop(0, count * g, column, 0, unroll=2)
    scale = HEAD ** (-0.5)
    reg = len_ref[2]
    heads = BI // HEAD
    vis = [slice(pair * VIS_PAD, (pair + 1) * VIS_PAD) for pair in range(2)]
    text = [slice(pair * 128, (pair + 1) * 128) for pair in range(2)]
    limits = [len_ref[0], len_ref[1], reg, reg]

    def head(j, carry):
        qv, kv, vv = ([cv_ref[rows, at128(j + heads * s)] for rows in vis] for s in range(3))
        qt, kt, vt = ([ct_ref[rows, at128(j + heads * s)] for rows in text] for s in range(3))
        probs = softmax_all([dot(q, k, NT) for q, k in zip(qv + qt, kt + kv)], scale, limits)
        found = [dot(p.astype(BF16), v).astype(BF16) for p, v in zip(probs, vt + vv)]
        for pair in range(2):
            fv_ref[vis[pair], at128(j)] = found[pair]
            ft_ref[text[pair], at128(j)] = found[2 + pair]
        return carry

    lax.fori_loop(0, heads, head, 0, unroll=2)


def co_forward(lengths, x_vis, x_text, near, far):
    return pl.pallas_call(
        co_body,
        in_specs=[pl.BlockSpec(memory_space=pltpu.SMEM)] + whole(2) + [pl.BlockSpec(memory_space=pl.ANY)] * 2,
        out_specs=whole(4),
        out_shape=[
            jax.ShapeDtypeStruct((x_vis.shape[0], 3 * BI), BF16),
            jax.ShapeDtypeStruct((x_text.shape[0], 3 * BI), BF16),
            jax.ShapeDtypeStruct((x_vis.shape[0], BI), BF16),
            jax.ShapeDtypeStruct((x_text.shape[0], BI), BF16),
        ],
        scratch_shapes=[
            pltpu.VMEM((tiles_of(0) + tiles_of(6), SUB, WIDE), BF16),
            pltpu.SemaphoreType.DMA((16,)),
        ],
        compiler_params=params(),
        cost_estimate=cost(22),
    )(lengths, x_vis, x_text, near, far)


def co_back_body(
    len_ref, cv_ref, ct_ref, dv_ref, dt_ref, rv_ref, rt_ref, near, far,
    gv_ref, gt_ref, ov_ref, ot_ref, w, sems,
):
    base = (0, tiles_of(0))
    copies = load(near, far, w, sems, (0, 6), base)
    scale = HEAD ** (-0.5)
    reg = len_ref[2]
    heads = BI // HEAD
    vis = [slice(pair * VIS_PAD, (pair + 1) * VIS_PAD) for pair in range(2)]
    text = [slice(pair * 128, (pair + 1) * 128) for pair in range(2)]
    limits = [len_ref[0], len_ref[1], reg, reg]

    def head(j, carry):
        qv, kv, vv = ([cv_ref[rows, at128(j + heads * s)] for rows in vis] for s in range(3))
        qt, kt, vt = ([ct_ref[rows, at128(j + heads * s)] for rows in text] for s in range(3))
        up = [dv_ref[rows, at128(j)] for rows in vis] + [dt_ref[rows, at128(j)] for rows in text]
        queries, keys, values = qv + qt, kt + kv, vt + vv
        products = [dot(q, k, NT) for q, k in zip(queries, keys)]
        dprobs = [dot(u, v, NT) for u, v in zip(up, values)]
        probs = softmax_all(products, scale, limits)
        ds = score_grads(probs, dprobs)
        dvalues = [dot(p.astype(BF16), u, TN).astype(BF16) for p, u in zip(probs, up)]
        dqueries = [(dot(d, k) * scale).astype(BF16) for d, k in zip(ds, keys)]
        dkeys = [(dot(d, q, TN) * scale).astype(BF16) for d, q in zip(ds, queries)]
        for pair in range(2):
            gv_ref[vis[pair], at128(j)] = dqueries[pair]
            gt_ref[text[pair], at128(j + heads)] = dkeys[pair]
            gt_ref[text[pair], at128(j + 2 * heads)] = dvalues[pair]
            gt_ref[text[pair], at128(j)] = dqueries[2 + pair]
            gv_ref[vis[pair], at128(j + heads)] = dkeys[2 + pair]
            gv_ref[vis[pair], at128(j + 2 * heads)] = dvalues[2 + pair]
        return carry

    lax.fori_loop(0, heads, head, 0, unroll=2)
    for which, at, g_ref, r_ref, o_ref, copy in (
        (0, base[0], gv_ref, rv_ref, ov_ref, copies[0]),
        (6, base[1], gt_ref, rt_ref, ot_ref, copies[1]),
    ):
        _, count, r, g = TILES[which]
        arrive(copy)

        def rows4(i, carry, at=at, r=r, g=g, count=count, g_ref=g_ref, r_ref=r_ref, o_ref=o_ref):
            o_ref[:, at256(i)] = r_ref[:, at256(i)] + times_back(g_ref, w, at, r, g, count, i)
            return carry

        lax.fori_loop(0, r // 4, rows4, 0)


def co_backward(lengths, co_vis, co_text, dvis, dtext, resid_vis, resid_text, near, far):
    return pl.pallas_call(
        co_back_body,
        in_specs=[pl.BlockSpec(memory_space=pltpu.SMEM)] + whole(6) + [pl.BlockSpec(memory_space=pl.ANY)] * 2,
        out_specs=whole(4),
        out_shape=[
            jax.ShapeDtypeStruct(co_vis.shape, BF16),
            jax.ShapeDtypeStruct(co_text.shape, BF16),
            jax.ShapeDtypeStruct(resid_vis.shape, F32),
            jax.ShapeDtypeStruct(resid_text.shape, F32),
        ],
        scratch_shapes=[
            pltpu.VMEM((tiles_of(0) + tiles_of(6), SUB, WIDE), BF16),
            pltpu.SemaphoreType.DMA((16,)),
        ],
        compiler_params=params(),
        cost_estimate=cost(23),
    )(lengths, co_vis, co_text, dvis, dtext, resid_vis, resid_text, near, far)


def erf_parts(value):
    return 0.5 * (1.0 + lax.erf(value * 0.7071067811865476))


def middle_body(
    config,
    len_ref, ctx_ref, x_ref, cot_ref, norm_ref, near, far,
    out_ref, first_ref, act_ref, second_ref, sctx_ref,
    fback_ref, pback_ref, bback_ref, dself_ref, tback_ref,
    resid_ref, dctx_ref, sums_ref,
    w, sems, pre, n1, n2, n3, s1, s2, s3, wide, acc, selfs, probs, stat,
):
    begin, rows, span, head, chunk = config
    width = x_ref.shape[1]
    base = []
    at = 0
    for which in range(begin, begin + 5):
        base.append(at)
        at += tiles_of(which)
    copies = load(near, far, w, sems, tuple(range(begin, begin + 5)), base)
    shapes = [TILES[which][1:] for which in range(begin, begin + 5)]
    steps = rows // chunk

    def at_chunk(i):
        return pl.ds(pl.multiple_of(i * chunk, chunk), chunk)

    def norm(resid, which, i, kept, scales):
        mean = jnp.mean(resid, 1, keepdims=True)
        centered = resid - mean
        scale = lax.rsqrt(jnp.mean(centered * centered, 1, keepdims=True) + NORM_EPSILON)
        normed = centered * scale
        kept[at_chunk(i), :] = normed
        scales[at_chunk(i), :] = jnp.broadcast_to(scale, (chunk, 128))
        return normed * norm_ref[0, which : which + 1, :] + norm_ref[1, which : which + 1, :]

    def eight(value):
        return jnp.sum(value.reshape(chunk // 8, 8, width), 0)

    def norm_back(upstream, which, i, kept, scales):
        normed = kept[at_chunk(i), :]
        stat[which] = stat[which] + eight(upstream * normed)
        stat[3 + which] = stat[3 + which] + eight(upstream)
        scaled = upstream * norm_ref[0, which : which + 1, :]
        return scales[at_chunk(i), 0:1] * (
            scaled
            - jnp.mean(scaled, 1, keepdims=True)
            - normed * jnp.mean(scaled * normed, 1, keepdims=True)
        )

    def loop(count, body, unroll=1):
        lax.fori_loop(0, count, lambda i, carry: (body(i), carry)[1], 0, unroll=unroll)

    stat[...] = jnp.zeros(stat.shape, F32)
    count, r, g = shapes[0]
    arrive(copies[0])

    def co_out(i):
        wide[:, at256(i)] = times(ctx_ref[...], w, base[0], r, g, 0, i)

    loop(g, co_out, g)

    def norm_one(i):
        value = norm(wide[at_chunk(i), :] + x_ref[at_chunk(i), :].astype(F32), 0, i, n1, s1)
        wide[at_chunk(i), :] = value
        first_ref[at_chunk(i), :] = value.astype(BF16)

    loop(steps, norm_one, 2 if steps % 2 == 0 else steps)
    _, r_up, g_up = shapes[1]
    _, r_down, g_down = shapes[2]
    arrive(copies[1])
    arrive(copies[2])
    acc[...] = jnp.zeros(acc.shape, F32)

    def down_rows(i):
        return jnp.concatenate(
            [
                jnp.concatenate([w[base[2] + (4 * i + a) * g_down + col] for a in range(4)], 0)
                for col in range(g_down)
            ],
            1,
        )

    def feed(i):
        value = times(first_ref[...], w, base[1], r_up, g_up, 0, i)
        part = erf_parts(value)
        pre[i] = part + value * (0.3989422804014327 * jnp.exp(-0.5 * value * value))
        act = (value * part).astype(BF16)
        act_ref[:, at256(i)] = act
        acc[...] += dot(act, down_rows(i))

    loop(g_up, feed, 4)

    def norm_two(i):
        value = norm(wide[at_chunk(i), :] + acc[at_chunk(i), :], 1, i, n2, s2)
        wide[at_chunk(i), :] = value
        second_ref[at_chunk(i), :] = value.astype(BF16)

    loop(steps, norm_two, 2 if steps % 2 == 0 else steps)
    count_s, r_s, g_s = shapes[3]
    arrive(copies[3])

    def self_in(i):
        selfs[:, at256(i)] = times(second_ref[...], w, base[3], r_s, g_s, i // g_s, i % g_s).astype(BF16)

    loop(count_s * g_s, self_in, g_s)
    scale = head ** (-0.5)
    groups = width // 128
    per = 128 // head
    pairs = rows // span

    def halves(values):
        if per == 1:
            return values[0]
        low = lax.broadcasted_iota(jnp.int32, values[0].shape, 1) < head
        return jnp.where(low, values[0], values[1])

    def only(value, h):
        if per == 1:
            return value
        low = lax.broadcasted_iota(jnp.int32, value.shape, 1) < head
        keep = low if h == 0 else jnp.logical_not(low)
        return jnp.where(keep, value, jnp.zeros_like(value))

    own = [slice(pair * span, (pair + 1) * span) for pair in range(pairs)]
    each = [(pair, h) for pair in range(pairs) for h in range(per)]

    def attend(j):
        q, k, v = ([selfs[rows_of, at128(j + groups * s)] for rows_of in own] for s in range(3))
        products = [dot(only(q[pair], h), k[pair], NT) for pair, h in each]
        p = softmax_all(products, scale, [len_ref[pair] for pair, _ in each])
        found = [dot(value.astype(BF16), v[pair]) for value, (pair, _) in zip(p, each)]
        for i, value in enumerate(p):
            probs[j * len(each) + i] = value
        for pair in range(pairs):
            sctx_ref[own[pair], at128(j)] = halves(found[pair * per : (pair + 1) * per]).astype(BF16)

    loop(groups, attend, 2)
    _, r_o, g_o = shapes[4]
    arrive(copies[4])

    def self_out(i):
        acc[:, at256(i)] = times(sctx_ref[...], w, base[4], r_o, g_o, 0, i)

    loop(g_o, self_out, g_o)

    def norm_three(i):
        value = norm(wide[at_chunk(i), :] + acc[at_chunk(i), :], 2, i, n3, s3)
        out_ref[at_chunk(i), :] = value.astype(BF16)
        third = norm_back(cot_ref[at_chunk(i), :].astype(F32), 2, i, n3, s3)
        wide[at_chunk(i), :] = third
        tback_ref[at_chunk(i), :] = third.astype(BF16)

    loop(steps, norm_three, 2 if steps % 2 == 0 else steps)

    def self_out_back(i):
        dctx_ref[:, at256(i)] = times_back(tback_ref, w, base[4], r_o, g_o, 1, i).astype(BF16)

    loop(r_o // 4, self_out_back, r_o // 4)
    def attend_back(j):
        q, k, v = ([selfs[rows_of, at128(j + groups * s)] for rows_of in own] for s in range(3))
        up = [dctx_ref[rows_of, at128(j)] for rows_of in own]
        p = [probs[j * len(each) + i] for i in range(len(each))]
        dprobs = [dot(only(up[pair], h), v[pair], NT) for pair, h in each]
        dv = [dot(value.astype(BF16), up[pair], TN) for value, (pair, _) in zip(p, each)]
        ds = score_grads(p, dprobs)
        dq = [dot(value, k[pair]) for value, (pair, _) in zip(ds, each)]
        dk = [dot(value, q[pair], TN) for value, (pair, _) in zip(ds, each)]
        for pair in range(pairs):
            mine = slice(pair * per, (pair + 1) * per)
            dself_ref[own[pair], at128(j)] = (halves(dq[mine]) * scale).astype(BF16)
            dself_ref[own[pair], at128(j + groups)] = (halves(dk[mine]) * scale).astype(BF16)
            dself_ref[own[pair], at128(j + 2 * groups)] = halves(dv[mine]).astype(BF16)

    loop(groups, attend_back, 2)

    def self_in_back(i):
        acc[:, at256(i)] = times_back(dself_ref, w, base[3], r_s, g_s, count_s, i)

    loop(r_s // 4, self_in_back, r_s // 4)

    def norm_two_back(i):
        value = norm_back(wide[at_chunk(i), :] + acc[at_chunk(i), :], 1, i, n2, s2)
        wide[at_chunk(i), :] = value
        bback_ref[at_chunk(i), :] = value.astype(BF16)

    loop(steps, norm_two_back, 2 if steps % 2 == 0 else steps)

    def feed_back(i):
        act_grad = dot(bback_ref[...], down_rows(i), NT)
        pback_ref[:, at256(i)] = (act_grad * pre[i]).astype(BF16)

    loop(g_up, feed_back, 4)

    def up_back(i):
        acc[:, at256(i)] = times_back(pback_ref, w, base[1], r_up, g_up, 1, i)

    loop(r_up // 4, up_back, r_up // 4)

    def norm_one_back(i):
        value = norm_back(wide[at_chunk(i), :] + acc[at_chunk(i), :], 0, i, n1, s1)
        resid_ref[at_chunk(i), :] = value
        fback_ref[at_chunk(i), :] = value.astype(BF16)

    loop(steps, norm_one_back, 2 if steps % 2 == 0 else steps)

    def co_out_back(i):
        dctx_ref[:, at256(i)] = times_back(fback_ref, w, base[0], r, g, 1, i).astype(BF16)

    loop(r // 4, co_out_back, r // 4)
    sums_ref[...] = jnp.sum(stat[...], 1)


def middle(begin, lengths, context, x, cot, norms, near, far, span, head, chunk):
    rows, width = x.shape
    hidden = TILES[begin + 1][3] * WIDE
    number = sum(tiles_of(which) for which in range(begin, begin + 5))
    low = lambda columns: jax.ShapeDtypeStruct((rows, columns), BF16)
    return pl.pallas_call(
        functools.partial(middle_body, (begin, rows, span, head, chunk)),
        in_specs=[pl.BlockSpec(memory_space=pltpu.SMEM)] + whole(4) + [pl.BlockSpec(memory_space=pl.ANY)] * 2,
        out_specs=whole(13),
        out_shape=[
            low(width), low(width), low(hidden), low(width), low(width),
            low(width), low(hidden), low(width), low(3 * width), low(width),
            jax.ShapeDtypeStruct((rows, width), F32), low(BI),
            jax.ShapeDtypeStruct((6, width), F32),
        ],
        scratch_shapes=[
            pltpu.VMEM((number, SUB, WIDE), BF16),
            pltpu.SemaphoreType.DMA((24,)),
            pltpu.VMEM((hidden // WIDE, rows, WIDE), F32),
        ]
        + [pltpu.VMEM((rows, width), F32)] * 3
        + [pltpu.VMEM((rows, 128), F32)] * 3
        + [pltpu.VMEM((rows, width), F32)] * 2
        + [
            pltpu.VMEM((rows, 3 * width), BF16),
            pltpu.VMEM((rows // span * (width // head), span, span), F32),
            pltpu.VMEM((6, 8, width), F32),
        ],
        compiler_params=params(),
        cost_estimate=cost(40),
    )(lengths, context, x, cot, norms, near, far)


def weight_body(kinds, *refs):
    n = len(kinds)
    lefts, rights = refs[:n], refs[n : 2 * n]
    out, stage, across, sems = refs[2 * n :]
    offset = 0
    for which, a_ref, b_ref in zip(kinds, lefts, rights):
        _, count, r, g = TILES[which]
        size = 4 * g

        def copy(i, slot, offset=offset, size=size):
            return pltpu.make_async_copy(
                stage.at[slot, pl.ds(0, size)], out.at[pl.ds(offset + i * size, size)], sems.at[slot]
            )

        total = count * (r // 4)

        def step(i, carry, a_ref=a_ref, b_ref=b_ref, r=r, g=g, copy=copy):
            slot = lax.rem(i, 4)

            @pl.when(i >= 4)
            def _():
                copy(i - 4, slot).wait()

            part = i // (r // 4)
            r4 = lax.rem(i, r // 4)
            across[...] = jnp.transpose(a_ref[:, at256(r4)])
            left = across[...]
            for first in range(0, g, 4 if g % 4 == 0 else 3):
                columns = range(first, first + (4 if g % 4 == 0 else 3))
                made = [dot(left, b_ref[:, at256(part * g + col)]).astype(BF16) for col in columns]
                for col, value in zip(columns, made):
                    for a in range(4):
                        stage[slot, a * g + col] = value[a * SUB : (a + 1) * SUB]
            copy(i, slot).start()
            return carry

        lax.fori_loop(0, total, step, 0, unroll=2 if total % 2 == 0 else 3)
        for i in range(max(0, total - 4), total):
            copy(i, i % 4).wait()
        offset += count * r * g


def weight_grads(kinds, lefts, rights):
    number = sum(tiles_of(which) for which in kinds)
    most = max(4 * TILES[which][3] for which in kinds)
    return pl.pallas_call(
        functools.partial(weight_body, kinds),
        in_specs=whole(2 * len(kinds)),
        out_specs=pl.BlockSpec(memory_space=pl.ANY),
        out_shape=jax.ShapeDtypeStruct((number, SUB, WIDE), BF16),
        scratch_shapes=[
            pltpu.VMEM((4, most, SUB, WIDE), BF16),
            pltpu.VMEM((WIDE, lefts[0].shape[0]), BF16),
            pltpu.SemaphoreType.DMA((4,)),
        ],
        compiler_params=params(),
        cost_estimate=cost(number * 0.04),
    )(*lefts, *rights)


def spot():
    dp = lax.axis_index("dp")
    seq = lax.axis_index("seq")
    return dp // 2, dp % 2, seq // 2, seq % 2


def along_z(value, moves):
    return lax.ppermute(value, "dp", [(2 * a + x, 2 * b + x) for a, b in moves for x in (0, 1)])


def cut(value, begin, size):
    return lax.dynamic_slice_in_dim(value, begin, size, 0)


def join(parts):
    return jnp.concatenate(parts) if len(parts) > 1 else parts[0]


def add(left, right):
    return (left.astype(F32) + right.astype(F32)).astype(BF16)


def by_y(y, mine, other):
    return [jnp.where(y == 0, mine, other), jnp.where(y == 0, other, mine)]


def blank(shape):
    return pl.pallas_call(
        lambda out: None,
        out_specs=pl.BlockSpec(memory_space=pl.ANY),
        out_shape=jax.ShapeDtypeStruct(shape, BF16),
        compiler_params=params(),
    )()


def gather_tiles(master_blocks):
    z, x, y, core = spot()
    lone, both, half = G_LONE // 2, (G_HALF - 2 * G_LONE) // 2, G_HALF // 2
    fourth = (SHARD - FAR) // 4
    mine = prep(
        master_blocks,
        jnp.concatenate(
            [half * core + lone * y + jnp.arange(lone), half * core + 2 * lone + jnp.arange(both)]
        ).astype(jnp.int32),
    )
    last = prep(
        master_blocks,
        ((FAR + fourth * lax.axis_index("seq")) // 2 + jnp.arange(fourth // 2)).astype(jnp.int32),
    )
    far = lax.all_gather(last, ("dp", "seq"), axis=0, tiled=True)
    ring = [(0, 1), (1, 2), (2, 3), (3, 0)]
    near = blank((8, 2 * G_HALF, SUB, WIDE))
    rows = [mine]
    cross = []
    halves = []
    for phase in range(6):
        out = {}
        if phase < 3:
            out["z"] = along_z(rows[phase], ring)
        if phase < 4:
            out["x"] = lax.ppermute(rows[phase], "dp", SWAP_X)
        if 1 <= phase < 5:
            here = [rows[phase - 1], cross[phase - 1]]
            out["y"] = lax.ppermute(join([part[:G_LONE] for part in here]), "seq", SWAP_Y)
        if phase >= 2:
            out["core"] = lax.ppermute(join(halves[phase - 2]), "seq", SWAP_CORE)
        out, rows, cross, halves = lax.optimization_barrier((out, rows, cross, halves))
        if "z" in out:
            rows = rows + [out["z"]]
        if "x" in out:
            cross = cross + [out["x"]]
        if "y" in out:
            halves = halves + [
                [
                    join(by_y(y, part[:G_LONE], out["y"][G_LONE * i : G_LONE * (i + 1)]) + [part[G_LONE:]])
                    for i, part in enumerate(here)
                ]
            ]
        if "core" in out:
            step = phase - 2
            for side in range(2):
                owner = 2 * ((z - step) % 4) + (x + side) % 2
                own = halves[step][side][None]
                got = out["core"][None, G_HALF * side : G_HALF * (side + 1)]
                near = lax.dynamic_update_slice(near, own, (owner, G_HALF * core, 0, 0))
                near = lax.dynamic_update_slice(near, got, (owner, G_HALF * (1 - core), 0, 0))
    return near.reshape(-1, SUB, WIDE), far


ROUTES = (
    (((3, 2),), ((2, 1),), ((1, 0),)),
    (((3, 2), (0, 1)), ((2, 1),)),
    (((0, 1), (3, 2)), ((1, 2),)),
    (((0, 1),), ((1, 2),), ((2, 3),)),
)
LONE = R_LONE // CHUNKS
BOTH = R_BOTH // CHUNKS
GROUP_ORDER = [[0, 2, 1, 3]]


def lone_at(core):
    return 2 * R_LONE * core


def both_at(core):
    return 4 * R_LONE + (SHARD - 4 * R_LONE - R_BOTH) * core


def chunk_pairs(k):
    table = []
    for core in range(2):
        for y in range(2):
            table += [(lone_at(core) + R_LONE * y + LONE * k) // 2 + i for i in range(LONE // 2)]
        table += [(both_at(core) + BOTH * k) // 2 + i for i in range(BOTH // 2)]
    return jnp.asarray(table, jnp.int32)


def pieces_of(owner, ranges, begins):
    pieces = []
    at = 0
    for begin, size in ranges:
        first, last = SHARD * owner + begin, SHARD * owner + begin + size
        for which, (lo, hi) in enumerate(begins):
            start, end = max(first, lo), min(last, hi)
            if start < end:
                pieces.append((which, start - lo, end - start, at + start - first))
        at += size
    return pieces


def half_plan(owner, begins, other):
    return [
        pieces_of(owner, ((lone_at(core ^ other), 2 * R_LONE), (both_at(core ^ other), R_BOTH)), begins)
        for core in range(2)
    ]


def both_plan(owner, begins, other):
    plan = []
    for core in range(2):
        pieces = []
        for i in range(2):
            for which, begin, size, at in pieces_of(owner + i, ((both_at(core ^ other), R_BOTH),), begins):
                pieces.append((which, begin, size, at + R_BOTH * i))
        plan.append(pieces)
    return plan


def follow(core_ref, plans, arrays, outs, sems):
    for core in range(2):

        @pl.when(core_ref[0] == core)
        def _(core=core):
            copies = []
            for j, plan in enumerate(plans):
                for i, (which, begin, size, at) in enumerate(plan[core]):
                    copies.append(
                        pltpu.make_async_copy(
                            arrays[which].at[pl.ds(begin, size)], outs[j].at[pl.ds(at, size)], sems.at[j, i]
                        )
                    )
            for copy in copies:
                copy.start()
            for copy in copies:
                copy.wait()


def pick_body(plans, number, core_ref, *refs):
    follow(core_ref, plans, refs[:number], refs[number:-1], refs[-1])


def pick(core, sources, plans, sizes):
    arrays = [array for _, array in sources]
    return pl.pallas_call(
        functools.partial(pick_body, plans, len(arrays)),
        in_specs=[pl.BlockSpec(memory_space=pltpu.SMEM)] + [pl.BlockSpec(memory_space=pl.ANY)] * len(arrays),
        out_specs=whole(len(plans)),
        out_shape=[jax.ShapeDtypeStruct((size, SUB, WIDE), BF16) for size in sizes],
        scratch_shapes=[pltpu.SemaphoreType.DMA((len(plans), 6))],
        compiler_params=params(),
        cost_estimate=cost(2 * len(plans)),
    )(core.reshape(1), *arrays)


def begins_of(sources):
    return [(begin, begin + array.shape[0]) for begin, array in sources]


def merge_body(plans, number, core_ref, *refs):
    arrays, got = refs[:number], refs[number : number + 2]
    outs = refs[number + 2 : -2]
    own, sems = refs[-2:]
    follow(core_ref, plans, arrays, [own.at[0], own.at[1]], sems)

    def total(out, size, i, begin):
        def tile(t, carry):
            out[t] = add(own[i, begin + t], got[i][begin + t])
            return carry

        lax.fori_loop(0, size, tile, 0, unroll=2)

    for k in range(CHUNKS):
        for i in range(2):
            for y in range(2):
                total(outs[2 * k].at[y, i], LONE, i, R_LONE * y + LONE * k)
            total(outs[2 * k + 1].at[i], BOTH, i, 2 * R_LONE + BOTH * k)


def merge(core, sources, zi, got, chunks):
    arrays = [array for _, array in sources]
    plans = [half_plan(2 * zi + i, begins_of(sources), 0) for i in range(2)]
    shapes = []
    for _ in range(CHUNKS):
        shapes += [(2, 2, LONE, SUB, WIDE), (2, BOTH, SUB, WIDE)]
    made = pl.pallas_call(
        functools.partial(merge_body, plans, len(arrays)),
        in_specs=[pl.BlockSpec(memory_space=pltpu.SMEM)]
        + [pl.BlockSpec(memory_space=pl.ANY)] * len(arrays)
        + whole(2),
        out_specs=whole(len(shapes)),
        out_shape=[jax.ShapeDtypeStruct(shape, BF16) for shape in shapes],
        scratch_shapes=[
            pltpu.VMEM((2, R_HALF, SUB, WIDE), BF16),
            pltpu.SemaphoreType.DMA((2, 6)),
        ],
        compiler_params=params(),
        cost_estimate=cost(8),
    )(core.reshape(1), *arrays, *got)
    for k, chunk in enumerate(chunks):
        chunk.state["lone", zi], chunk.state["both", zi] = made[2 * k : 2 * k + 2]


def arrange_body(pieces, x_any, o_any, held, sems):
    arrivals = []
    at = 0
    for i, (begin, size) in enumerate(pieces):
        spot_of = pl.ds(at, size)
        arrivals.append(
            (
                pltpu.make_async_copy(x_any.at[pl.ds(begin, size)], held.at[spot_of], sems.at[0, i]),
                pltpu.make_async_copy(held.at[spot_of], o_any.at[spot_of], sems.at[1, i]),
            )
        )
        arrivals[-1][0].start()
        at += size
    for came, goes in arrivals:
        came.wait()
        goes.start()
    for _, goes in arrivals:
        goes.wait()


def arrange(array, pieces):
    number = sum(size for _, size in pieces)
    return pl.pallas_call(
        functools.partial(arrange_body, pieces),
        in_specs=[pl.BlockSpec(memory_space=pl.ANY)],
        out_specs=pl.BlockSpec(memory_space=pl.ANY),
        out_shape=jax.ShapeDtypeStruct((number, SUB, WIDE), BF16),
        scratch_shapes=[
            pltpu.VMEM((number, SUB, WIDE), BF16),
            pltpu.SemaphoreType.DMA((2, len(pieces))),
        ],
        compiler_params=params(),
        cost_estimate=cost(6),
    )(array)


def group_lone(array, offset):
    pieces = tuple(
        (offset + SHARD * o + R_LONE * part, R_LONE) for part in range(4) for o in range(2)
    )
    made = lax.psum_scatter(
        arrange(array, pieces), "seq", scatter_dimension=0, tiled=True, axis_index_groups=GROUP_ORDER
    )
    return made.reshape(2, R_LONE, SUB, WIDE)


def chunks_of(lone, both):
    return [
        (lone[:, LONE * k : LONE * (k + 1)], both[:, BOTH * k : BOTH * (k + 1)]) for k in range(CHUNKS)
    ]


class Sums:
    def __init__(self):
        self.at = spot()
        self.state = {}

    def send(self, task):
        z, x, y, core = self.at
        state = self.state
        kind, who = task[0], task[1]
        if kind == "Y":
            return lax.ppermute(cut(state["lone", who], 1 - y, 1)[0], "seq", SWAP_Y)
        if kind == "X":
            lone, both = state["kept", who]
            return lax.ppermute(join([cut(lone, 1 - x, 1)[0], cut(both, 1 - x, 1)[0]]), "dp", SWAP_X)
        if kind == "Z":
            return along_z(state["value", who], ROUTES[who][task[2]])
        if kind == "F":
            values = [state["value", zi] for zi in range(4)]
            mine = jnp.where(z == 0, values[0], jnp.where(z == 1, values[1], jnp.where(z == 2, values[2], values[3])))
            state["mine", 0] = mine
            return lax.ppermute(mine, "seq", SWAP_Y)
        if kind == "G":
            return lax.ppermute(state["whole", 0], "seq", SWAP_CORE)
        axis, step = (("seq", 1), ("seq", 2), ("dp", 1), ("dp", 2), ("dp", 4))[who]
        size = lax.axis_size(axis)
        return lax.ppermute(state["norms", 0], axis, [(i, i ^ step) for i in range(size)])

    def take(self, task, got):
        z, x, y, core = self.at
        state = self.state
        kind, who = task[0], task[1]
        if kind == "Y":
            state["kept", who] = (add(cut(state.pop(("lone", who)), y, 1)[0], got), state.pop(("both", who)))
        elif kind == "X":
            lone, both = state.pop(("kept", who))
            state["value", who] = add(join([cut(lone, x, 1)[0], cut(both, x, 1)[0]]), got)
        elif kind == "Z":
            state["value", who] = add(state["value", who], got)
        elif kind == "F":
            mine = state.pop(("mine", 0))
            state["whole", 0] = join(by_y(y, mine[:LONE], got[:LONE]) + [add(mine[LONE:], got[LONE:])])
        elif kind == "G":
            half = state.pop(("whole", 0))
            state["owned", 0] = join([jnp.where(core == 0, half, got), jnp.where(core == 0, got, half)])
        else:
            state["norms", 0] = state["norms", 0] + got

    def step(self, tasks):
        out = [self.send(task) for task in tasks]
        out, self.state = lax.optimization_barrier((out, self.state))
        for task, got in zip(tasks, out):
            self.take(task, got)


def beside(chunks, tasks, work):
    out = [chunks[k].send(task) for k, task in tasks]
    made = work()
    out, made, states = lax.optimization_barrier((out, made, [chunk.state for chunk in chunks]))
    for chunk, state in zip(chunks, states):
        chunk.state = state
    for (k, task), got in zip(tasks, out):
        chunks[k].take(task, got)
    return made


def pad_regions(value, pairs):
    reg = value.shape[0] // pairs
    cube = value.reshape(pairs, reg, value.shape[1])
    return jnp.pad(cube, ((0, 0), (0, VIS_PAD - reg), (0, 0))).reshape(pairs * VIS_PAD, -1)


def cut_regions(value, pairs, reg):
    return value.reshape(pairs, VIS_PAD, -1)[:, :reg].reshape(pairs * reg, -1)


def fast_shards(
    x_text, x_vis, caption_len, cot_text, cot_vis, master_blocks,
    stat_left, stat_right, root_left, root_right, norm_params, norm_second,
):
    pairs = caption_len.shape[0]
    reg = x_vis.shape[0] // pairs
    near, far = gather_tiles(master_blocks)
    lengths = jnp.concatenate([caption_len, jnp.full((2,), reg, jnp.int32)])
    regions = jnp.full((2,), reg, jnp.int32)
    xv = pad_regions(x_vis, pairs)
    cv = pad_regions(cot_vis, pairs)
    vis_norms = norm_params[:, : 3 * VIS].reshape(2, 3, VIS)
    text_norms = norm_params[:, 3 * VIS :].reshape(2, 3, TXT)
    co_vis, co_text, vis_ctx, text_ctx = co_forward(lengths, xv, x_text, near, far)
    (out_vis, v_first, v_act, v_second, v_sctx, v_fback, v_pback, v_bback, v_dself, v_tback,
     v_resid, v_dctx, v_sums) = middle(1, regions, vis_ctx, xv, cv, vis_norms, near, far, VIS_PAD, HEAD_V, 32)
    vis_mid = weight_grads(
        (1, 2, 3, 4, 5), (vis_ctx, v_first, v_act, v_second, v_sctx),
        (v_fback, v_pback, v_bback, v_dself, v_tback),
    )
    _, _, _, core = spot()
    chunks = [Sums() for _ in range(CHUNKS)]
    vis_at, text_at = TILES[1][0], TILES[7][0]
    vis_pair, text_pair = (vis_mid, 2 * SHARD - vis_at), 6 * SHARD - text_at
    lone = group_lone(*vis_pair)
    vis_source = (vis_at, vis_mid)

    def pick_both(source, owner):
        begins = begins_of([source])
        plans = [both_plan(owner, begins, 1), both_plan(owner, begins, 0)]
        send, own = pick(core, [source], plans, [2 * R_BOTH] * 2)
        return own, lax.ppermute(send, "seq", SWAP_CORE)

    def both_sum(own, got):
        return add(own, got).reshape(2, R_BOTH, SUB, WIDE)

    own_both, far_both = pick_both(vis_source, 2)
    (out_text, t_first, t_act, t_second, t_sctx, t_fback, t_pback, t_bback, t_dself, t_tback,
     t_resid, t_dctx, t_sums) = middle(
        7, lengths, text_ctx, x_text, cot_text, text_norms, near, far, x_text.shape[0] // pairs, HEAD_T, 32
    )
    chunks[0].state["norms", 0] = jnp.concatenate([v_sums.reshape(2, -1), t_sums.reshape(2, -1)], 1)
    lefts = (text_ctx, t_first, t_act, t_second, t_sctx)
    rights = (t_fback, t_pback, t_bback, t_dself, t_tback)
    lefts, rights, far_both = lax.optimization_barrier((lefts, rights, far_both))
    text_mid = weight_grads((7, 8, 9, 10, 11), lefts, rights)
    text_source = (text_at, text_mid)
    both = both_sum(own_both, far_both)
    own_both, far_both = pick_both(text_source, 6)
    back = (co_vis, co_text, v_dctx, t_dctx, v_resid, t_resid)
    back, lone, both, text_mid = lax.optimization_barrier((back, lone, both, text_mid))
    for k, kept in enumerate(chunks_of(lone, both)):
        chunks[k].state["kept", 1] = kept
    lone = group_lone(text_mid, text_pair)
    def swap_halves(sources, owners):
        plans = [half_plan(o, begins_of(sources), 1) for o in owners]
        return [
            lax.ppermute(part, "seq", SWAP_CORE) for part in pick(core, sources, plans, [R_HALF] * len(owners))
        ]

    dco_vis, dco_text, grad_vis, grad_text, far_both, far_half = beside(
        chunks,
        [(0, ("X", 1)), (0, ("N", 0))],
        lambda: (*co_backward(lengths, *back, near, far), far_both, swap_halves([text_source], (5,))[0]),
    )
    late_sources = [vis_source, None, text_source]

    def co_grads():
        text_co = weight_grads((6,), (x_text,), (dco_text,))
        late_sources[1] = (TILES[6][0], text_co)
        return text_co, swap_halves(late_sources, (4,))[0], weight_grads((0,), (xv,), (dco_vis,))

    text_co, far_four, vis_co = beside(
        chunks, [(1, ("X", 1)), (0, ("Z", 1, 0)), (0, ("N", 1))], co_grads
    )
    early_sources = [(0, vis_co), vis_source]
    late_sources[1] = (TILES[6][0], text_co)

    def merge_late():
        merge(core, late_sources, 2, [far_four, far_half], chunks)
        return swap_halves(early_sources, (0, 1))

    got = beside(chunks, [(0, ("Z", 1, 1)), (1, ("Z", 1, 0))], merge_late)
    for k, kept in enumerate(chunks_of(lone, both_sum(own_both, far_both))):
        chunks[k].state["kept", 3] = kept
    beside(
        chunks,
        [(0, ("Y", 2)), (0, ("X", 3)), (1, ("Z", 1, 1))],
        lambda: merge(core, early_sources, 0, got, chunks),
    )
    beside(chunks, [(0, ("Y", 0)), (0, ("X", 2)), (0, ("Z", 3, 0)), (1, ("X", 3)), (0, ("N", 2))], lambda: ())
    chunks[1].step([("Y", 2), ("Z", 3, 0)])
    chunks[0].step([("X", 0), ("Z", 2, 0), ("Z", 3, 1), ("N", 3)])
    chunks[1].step([("Y", 0), ("X", 2), ("Z", 3, 1)])
    chunks[0].step([("Z", 0, 0), ("Z", 2, 1), ("Z", 3, 2), ("N", 4)])
    chunks[1].step([("X", 0), ("Z", 2, 0), ("Z", 3, 2)])
    chunks[0].step([("Z", 0, 1)])
    chunks[1].step([("Z", 0, 0), ("Z", 2, 1)])
    chunks[0].step([("Z", 0, 2)])
    chunks[1].step([("Z", 0, 1)])
    chunks[0].step([("F", 0)])
    chunks[0].step([("G", 0)])
    statistics = (master_blocks, stat_left, stat_right, root_left, root_right)
    early = chunk_pairs(0)
    count = early.shape[0] // 2
    owned = chunks[0].state["owned", 0]
    renewed = beside(
        chunks, [(1, ("Z", 0, 2))], lambda: renew(early[:count], owned[: 2 * count], *statistics, ())
    )
    renewed = beside(
        chunks, [(1, ("F", 0))], lambda: renew(early[count:], owned[2 * count :], *statistics, renewed)
    )
    chunks[1].step([("G", 0)])
    grad_blocks, left_new, right_new, master_new = renew(
        chunk_pairs(1), chunks[1].state["owned", 0], *statistics, renewed
    )
    norm_grads = chunks[0].state["norms", 0]
    second_new = STAT_DECAY * norm_second + (1.0 - STAT_DECAY) * norm_grads * norm_grads
    norm_new = norm_params - NORM_RATE * norm_grads / (jnp.sqrt(second_new) + MOMENT_EPSILON)
    return (
        out_text,
        cut_regions(out_vis, pairs, reg),
        grad_text,
        cut_regions(grad_vis, pairs, reg),
        grad_blocks,
        left_new,
        right_new,
        master_new,
        norm_grads,
        second_new,
        norm_new,
    )


def fits(mesh):
    return mesh.shape["dp"] == 8 and mesh.shape["seq"] == 4


def solution(mesh):
    placed = (
        P(("dp", "seq"), None),
        P(("dp", "seq"), None),
        P(("dp", "seq")),
        P(("dp", "seq"), None),
        P(("dp", "seq"), None),
        P("dp", None),
        P("dp", None),
        P("dp", None),
        P("dp", None),
        P("dp", None),
        P(),
        P(),
    )
    step = fast_shards if fits(mesh) else shards
    return jax.shard_map(
        step,
        mesh=mesh,
        in_specs=placed,
        out_specs=(
            P(("dp", "seq"), None),
            P(("dp", "seq"), None),
            P(("dp", "seq"), None),
            P(("dp", "seq"), None),
            P("dp", None),
            P("dp", None),
            P("dp", None),
            P("dp", None),
            P(),
            P(),
            P(),
        ),
        check_vma=False,
    )
```

```python
import functools

import jax
import jax.numpy as jnp
from jax import lax
from jax.experimental import pallas as pl
from jax.experimental.pallas import tpu as pltpu
from jax.sharding import PartitionSpec as P

TXT = 768
VIS = 1024
BI = 1024
FFT = 3072
FFV = 1024
HEAD = 128
HEAD_T = 64
HEAD_V = 128
BLK = 64


MASK_FILL = -1000000000.0
STAT_DECAY = 0.9
WEIGHT_RATE = 0.3
NORM_RATE = 0.2
NORM_EPSILON = 1e-05
MOMENT_EPSILON = 1e-08
HIGHEST = lax.Precision.HIGHEST
CONTRACT_COLS = (((1,), (1,)), ((), ()))


def weight_layout():
    return (
        (VIS, BI, 3),
        (BI, VIS, 1),
        (VIS, FFV, 1),
        (FFV, VIS, 1),
        (VIS, VIS, 3),
        (VIS, VIS, 1),
        (TXT, BI, 3),
        (BI, TXT, 1),
        (TXT, FFT, 1),
        (FFT, TXT, 1),
        (TXT, TXT, 3),
        (TXT, TXT, 1),
    )


def unpack_weights(flat):
    size = BLK
    blocks = flat.reshape(flat.shape[0], size, size)
    begin = 0
    matrices = []
    for rows, columns, count in weight_layout():
        number = count * rows * columns // (size * size)
        shaped = blocks[begin : begin + number].reshape(
            count, rows // size, columns // size, size, size
        )
        matrices.append(shaped.transpose(1, 3, 0, 2, 4).reshape(rows, count * columns))
        begin += number
    return matrices


def block_grad(inputs, grads, count):
    size = BLK
    left = inputs.reshape(inputs.shape[0], inputs.shape[1] // size, size)
    right = grads.reshape(grads.shape[0], count, grads.shape[1] // (count * size), size)
    return jnp.einsum("nai,nkbj->kabij", left, right, preferred_element_type=jnp.float32).reshape(
        -1, size * size
    )


def norm_columns(values, stream, which):
    if stream == 0:
        begin = which * VIS
        width = VIS
    else:
        begin = 3 * VIS + which * TXT
        width = TXT
    return values[:, begin : begin + width]


def gelu_exact(value):
    return jax.nn.gelu(value, approximate=False)


def heads_of(side, which, head):
    part = side[:, :, which, :]
    return part.reshape(part.shape[0], part.shape[1], part.shape[2] // head, head)


def scores_of(query, keys, live, head):
    scores = jnp.einsum(
        "gqhd,gkhd->ghqk", query, keys, preferred_element_type=jnp.float32
    ) * head ** (-0.5)
    if live is not None:
        scores = jnp.where(live[:, None, None, :], scores, MASK_FILL)
    return scores


def attend_one(query, keys, values, live, head):
    scores = scores_of(query, keys, live, head)
    top = jnp.max(scores, axis=3, keepdims=True)
    raised = jnp.exp(scores - top)
    total = jnp.sum(raised, axis=3, keepdims=True)
    found = jnp.einsum(
        "ghqk,gkhd->gqhd",
        (raised / total).astype(jnp.bfloat16),
        values,
        preferred_element_type=jnp.float32,
    ).astype(jnp.bfloat16)
    return (found.reshape(found.shape[0], found.shape[1], -1), top + jnp.log(total))


def attend_one_back(query, keys, values, live, head, logsum, dfound):
    scale = head ** (-0.5)
    probs = jnp.exp(scores_of(query, keys, live, head) - logsum)
    upstream = dfound.reshape(dfound.shape[0], dfound.shape[1], -1, head)
    dprobs = jnp.einsum("gqhd,gkhd->ghqk", upstream, values, preferred_element_type=jnp.float32)
    dvalues = jnp.einsum(
        "ghqk,gqhd->gkhd", probs.astype(jnp.bfloat16), upstream, preferred_element_type=jnp.float32
    )
    dscores = (probs * (dprobs - jnp.sum(probs * dprobs, axis=3, keepdims=True))).astype(
        jnp.bfloat16
    )
    dquery = (
        jnp.einsum("ghqk,gkhd->gqhd", dscores, keys, preferred_element_type=jnp.float32) * scale
    )
    dkeys = (
        jnp.einsum("ghqk,gqhd->gkhd", dscores, query, preferred_element_type=jnp.float32) * scale
    )
    return (dquery, dkeys, dvalues)


def attention_plan(vis_side, text_side, lengths, cross):
    live = (
        lax.broadcasted_iota(jnp.int32, (lengths.shape[0], text_side.shape[1]), 1)
        < lengths[:, None]
    )
    if cross:
        return ((vis_side, text_side, live, HEAD), (text_side, vis_side, None, HEAD))
    return ((vis_side, vis_side, None, HEAD_V), (text_side, text_side, live, HEAD_T))


def pair_attend(vis_side, text_side, lengths, cross):
    results = []
    for query_side, key_side, live, head in attention_plan(vis_side, text_side, lengths, cross):
        results.append(
            attend_one(
                heads_of(query_side, 0, head),
                heads_of(key_side, 1, head),
                heads_of(key_side, 2, head),
                live,
                head,
            )
        )
    return (results[0][0], results[1][0], results[0][1], results[1][1])


def pair_attend_back(
    vis_side, text_side, lengths, cross, vis_logsum, text_logsum, vis_dfound, text_dfound
):
    plan = attention_plan(vis_side, text_side, lengths, cross)
    parts = []
    for (query_side, key_side, live, head), logsum, dfound in zip(
        plan, (vis_logsum, text_logsum), (vis_dfound, text_dfound)
    ):
        parts.append(
            attend_one_back(
                heads_of(query_side, 0, head),
                heads_of(key_side, 1, head),
                heads_of(key_side, 2, head),
                live,
                head,
                logsum,
                dfound,
            )
        )
    if cross:
        vis_parts = (parts[0][0], parts[1][1], parts[1][2])
        text_parts = (parts[1][0], parts[0][1], parts[0][2])
    else:
        vis_parts = parts[0]
        text_parts = parts[1]
    vis_grad = jnp.stack(vis_parts, axis=2).reshape(vis_side.shape).astype(jnp.bfloat16)
    text_grad = jnp.stack(text_parts, axis=2).reshape(text_side.shape).astype(jnp.bfloat16)
    return (vis_grad, text_grad)


def to_heads(vis_side, text_side):
    return (vis_side, text_side)


def from_heads(vis_found, text_found):
    return (vis_found, text_found)


def dfound_to_heads(vis_dfound, text_dfound):
    return (vis_dfound, text_dfound)


def grads_from_heads(vis_grad, text_grad):
    return (vis_grad, text_grad)


def side_of(rows_in, weight, pairs):
    made = jnp.dot(rows_in, weight, preferred_element_type=jnp.float32).astype(jnp.bfloat16)
    return made.reshape(pairs, -1, 3, weight.shape[1] // 3)


def norm_forward(resid, columns):
    mean = jnp.mean(resid, -1, keepdims=True)
    centered = resid - mean
    scale = lax.rsqrt(jnp.mean(centered * centered, -1, keepdims=True) + NORM_EPSILON)
    normed = centered * scale
    return (normed, scale, normed * columns[0] + columns[1])


def norm_backward(upstream, normed, scale, gain):
    scaled = upstream * gain
    resid_grad = scale * (
        scaled
        - jnp.mean(scaled, -1, keepdims=True)
        - normed * jnp.mean(scaled * normed, -1, keepdims=True)
    )
    return (resid_grad, jnp.sum(upstream * normed, 0), jnp.sum(upstream, 0))


def stream_middle(context_rows, x_rows, weights, values, stream, pairs):
    resid = x_rows.astype(jnp.float32) + jnp.dot(
        context_rows, weights[1], preferred_element_type=jnp.float32
    )
    normed_one, scale_one, first = norm_forward(resid, norm_columns(values, stream, 0))
    first_low = first.astype(jnp.bfloat16)
    pre = jnp.dot(first_low, weights[2], preferred_element_type=jnp.float32)
    act = gelu_exact(pre).astype(jnp.bfloat16)
    resid = first + jnp.dot(act, weights[3], preferred_element_type=jnp.float32)
    normed_two, scale_two, second = norm_forward(resid, norm_columns(values, stream, 1))
    second_low = second.astype(jnp.bfloat16)
    side = side_of(second_low, weights[4], pairs)
    return (
        side,
        (normed_one, scale_one, first_low, pre, act, normed_two, scale_two, second, second_low),
    )


def stream_end(self_rows, second, out_weight, values, stream):
    resid = second + jnp.dot(self_rows, out_weight, preferred_element_type=jnp.float32)
    normed_three, scale_three, third = norm_forward(resid, norm_columns(values, stream, 2))
    return (third.astype(jnp.bfloat16), normed_three, scale_three)


def stream_back_end(
    cotangent, normed_three, scale_three, self_rows, out_weight, values, stream, pairs
):
    resid_three, gain_three, bias_three = norm_backward(
        cotangent.astype(jnp.float32), normed_three, scale_three, norm_columns(values, stream, 2)[0]
    )
    third_back = resid_three.astype(jnp.bfloat16)
    grad_self_out = block_grad(self_rows, third_back, 1)
    dself = lax.dot_general(
        third_back, out_weight, CONTRACT_COLS, preferred_element_type=jnp.float32
    )
    dself = dself.astype(jnp.bfloat16).reshape(pairs, -1, out_weight.shape[0])
    return (resid_three, dself, grad_self_out, gain_three, bias_three)


def stream_back_middle(resid_three, dself_side, kept, context_rows, weights, values, stream, pairs):
    normed_one, scale_one, first_low, pre, act, normed_two, scale_two, second, second_low = kept
    dself_rows = dself_side.reshape(-1, dself_side.shape[2] * dself_side.shape[3])
    grad_self_qkv = block_grad(second_low, dself_rows, 3)
    second_in = resid_three + lax.dot_general(
        dself_rows, weights[4], CONTRACT_COLS, preferred_element_type=jnp.float32
    )
    resid_two, gain_two, bias_two = norm_backward(
        second_in, normed_two, scale_two, norm_columns(values, stream, 1)[0]
    )
    branch_back = resid_two.astype(jnp.bfloat16)
    grad_down = block_grad(act, branch_back, 1)
    act_grad = lax.dot_general(
        branch_back, weights[3], CONTRACT_COLS, preferred_element_type=jnp.float32
    )
    pre_grad = jax.vjp(gelu_exact, pre)[1](act_grad)[0].astype(jnp.bfloat16)
    grad_up = block_grad(first_low, pre_grad, 1)
    first_in = resid_two + lax.dot_general(
        pre_grad, weights[2], CONTRACT_COLS, preferred_element_type=jnp.float32
    )
    resid_one, gain_one, bias_one = norm_backward(
        first_in, normed_one, scale_one, norm_columns(values, stream, 0)[0]
    )
    first_back = resid_one.astype(jnp.bfloat16)
    grad_co_out = block_grad(context_rows, first_back, 1)
    dcontext = lax.dot_general(
        first_back, weights[1], CONTRACT_COLS, preferred_element_type=jnp.float32
    )
    dcontext = dcontext.astype(jnp.bfloat16).reshape(pairs, -1, BI)
    return (
        resid_one,
        dcontext,
        (grad_co_out, grad_up, grad_down, grad_self_qkv),
        (gain_one, gain_two),
        (bias_one, bias_two),
    )


def shards(
    x_text,
    x_vis,
    caption_len,
    cot_text,
    cot_vis,
    master_blocks,
    stat_left,
    stat_right,
    root_left,
    root_right,
    norm_params,
    norm_second,
):
    pairs = caption_len.shape[0]
    width = master_blocks.shape[1] // lax.axis_size("seq")
    mine = lax.dynamic_slice_in_dim(master_blocks, lax.axis_index("seq") * width, width, 1).astype(
        jnp.bfloat16
    )
    partial_value = lax.all_gather(mine, "dp", axis=0, tiled=True)
    every = lax.all_gather(partial_value, "seq", axis=1, tiled=True)
    matrices = unpack_weights(every)
    vis_weights = matrices[:6]
    text_weights = matrices[6:]
    vis_co = side_of(x_vis, vis_weights[0], pairs)
    text_co = side_of(x_text, text_weights[0], pairs)
    lengths = caption_len
    vis_co_use, text_co_use = to_heads(vis_co, text_co)
    vis_found, text_found, vis_co_sum, text_co_sum = pair_attend(
        vis_co_use, text_co_use, lengths, True
    )
    vis_context, text_context = from_heads(vis_found, text_found)
    vis_context_rows = vis_context.reshape(-1, BI)
    text_context_rows = text_context.reshape(-1, BI)
    vis_self, vis_kept = stream_middle(vis_context_rows, x_vis, vis_weights, norm_params, 0, pairs)
    text_self, text_kept = stream_middle(
        text_context_rows, x_text, text_weights, norm_params, 1, pairs
    )
    vis_self_use, text_self_use = to_heads(vis_self, text_self)
    vis_found, text_found, vis_self_sum, text_self_sum = pair_attend(
        vis_self_use, text_self_use, lengths, False
    )
    vis_self_context, text_self_context = from_heads(vis_found, text_found)
    vis_self_rows = vis_self_context.reshape(-1, VIS)
    text_self_rows = text_self_context.reshape(-1, TXT)
    out_vis, vis_normed_three, vis_scale_three = stream_end(
        vis_self_rows, vis_kept[7], vis_weights[5], norm_params, 0
    )
    out_text, text_normed_three, text_scale_three = stream_end(
        text_self_rows, text_kept[7], text_weights[5], norm_params, 1
    )
    vis_resid_three, vis_dself, vis_grad_so, vis_gain_three, vis_bias_three = stream_back_end(
        cot_vis,
        vis_normed_three,
        vis_scale_three,
        vis_self_rows,
        vis_weights[5],
        norm_params,
        0,
        pairs,
    )
    text_resid_three, text_dself, text_grad_so, text_gain_three, text_bias_three = stream_back_end(
        cot_text,
        text_normed_three,
        text_scale_three,
        text_self_rows,
        text_weights[5],
        norm_params,
        1,
        pairs,
    )
    vis_dheads, text_dheads = dfound_to_heads(vis_dself, text_dself)
    vis_dgot, text_dgot = pair_attend_back(
        vis_self_use,
        text_self_use,
        lengths,
        False,
        vis_self_sum,
        text_self_sum,
        vis_dheads,
        text_dheads,
    )
    vis_dself_side, text_dself_side = grads_from_heads(vis_dgot, text_dgot)
    vis_resid_one, vis_dcontext, vis_grads_mid, vis_gains_mid, vis_biases_mid = stream_back_middle(
        vis_resid_three,
        vis_dself_side,
        vis_kept,
        vis_context_rows,
        vis_weights,
        norm_params,
        0,
        pairs,
    )
    text_resid_one, text_dcontext, text_grads_mid, text_gains_mid, text_biases_mid = (
        stream_back_middle(
            text_resid_three,
            text_dself_side,
            text_kept,
            text_context_rows,
            text_weights,
            norm_params,
            1,
            pairs,
        )
    )
    vis_dheads, text_dheads = dfound_to_heads(vis_dcontext, text_dcontext)
    vis_dgot, text_dgot = pair_attend_back(
        vis_co_use, text_co_use, lengths, True, vis_co_sum, text_co_sum, vis_dheads, text_dheads
    )
    vis_dco, text_dco = grads_from_heads(vis_dgot, text_dgot)
    vis_dco_rows = vis_dco.reshape(-1, 3 * BI)
    text_dco_rows = text_dco.reshape(-1, 3 * BI)
    grad_vis = vis_resid_one + lax.dot_general(
        vis_dco_rows, vis_weights[0], CONTRACT_COLS, preferred_element_type=jnp.float32
    )
    grad_text = text_resid_one + lax.dot_general(
        text_dco_rows, text_weights[0], CONTRACT_COLS, preferred_element_type=jnp.float32
    )
    vis_grad_co = block_grad(x_vis, vis_dco_rows, 3)
    text_grad_co = block_grad(x_text, text_dco_rows, 3)
    local_blocks = jnp.concatenate(
        [vis_grad_co]
        + list(vis_grads_mid)
        + [vis_grad_so]
        + [text_grad_co]
        + list(text_grads_mid)
        + [text_grad_so],
        0,
    )
    norm_local = jnp.stack(
        [
            jnp.concatenate(
                [
                    vis_gains_mid[0],
                    vis_gains_mid[1],
                    vis_gain_three,
                    text_gains_mid[0],
                    text_gains_mid[1],
                    text_gain_three,
                ]
            ),
            jnp.concatenate(
                [
                    vis_biases_mid[0],
                    vis_biases_mid[1],
                    vis_bias_three,
                    text_biases_mid[0],
                    text_biases_mid[1],
                    text_bias_three,
                ]
            ),
        ]
    )
    columns = lax.psum_scatter(
        local_blocks.astype(jnp.bfloat16), "seq", scatter_dimension=1, tiled=True
    ).astype(jnp.float32)
    owned_columns = lax.psum_scatter(columns, "dp", scatter_dimension=0, tiled=True)
    owned = lax.all_gather(owned_columns.astype(jnp.bfloat16), "seq", axis=1, tiled=True).astype(
        owned_columns.dtype
    )
    norm_grads = lax.psum(norm_local, ("dp", "seq"))
    number = owned.shape[0]
    grad_cube = owned.reshape(number, BLK, BLK)
    left_cube = stat_left.reshape(number, BLK, BLK)
    right_cube = stat_right.reshape(number, BLK, BLK)
    rootl_cube = root_left.reshape(number, BLK, BLK)
    rootr_cube = root_right.reshape(number, BLK, BLK)
    left_new = STAT_DECAY * left_cube + (1.0 - STAT_DECAY) * jnp.einsum(
        "bij,bkj->bik", grad_cube, grad_cube, precision=HIGHEST
    )
    right_new = STAT_DECAY * right_cube + (1.0 - STAT_DECAY) * jnp.einsum(
        "bji,bjk->bik", grad_cube, grad_cube, precision=HIGHEST
    )
    half = jnp.einsum("bij,bjk->bik", rootl_cube, grad_cube, precision=HIGHEST)
    direction = jnp.einsum("bij,bjk->bik", half, rootr_cube, precision=HIGHEST)
    master_new = master_blocks - WEIGHT_RATE * direction.reshape(number, BLK * BLK)
    second_new = STAT_DECAY * norm_second + (1.0 - STAT_DECAY) * norm_grads * norm_grads
    norm_new = norm_params - NORM_RATE * norm_grads / (jnp.sqrt(second_new) + MOMENT_EPSILON)
    return (
        out_text,
        out_vis,
        grad_text,
        grad_vis,
        owned,
        left_new.reshape(number, BLK * BLK),
        right_new.reshape(number, BLK * BLK),
        master_new,
        norm_grads,
        second_new,
        norm_new,
    )


SUB = 64
WIDE = 256
QUAD = 4
F32 = jnp.float32
BF16 = jnp.bfloat16
VIS_PAD = 48
VMEM_LIMIT = 60 * 1024 * 1024
NT = (((1,), (1,)), ((), ()))
TN = (((0,), (0,)), ((), ()))


def tile_table():
    begin = 0
    table = []
    for rows, columns, count in weight_layout():
        r, g = rows // SUB, columns // WIDE
        table.append((begin, count, r, g))
        begin += count * r * g
    return table


TILES = tile_table()
SHARD = 158
FAR = 62
G_HALF = 32
G_LONE = 8
R_LONE = 32
R_BOTH = 16
R_HALF = 2 * R_LONE + R_BOTH
CHUNKS = 2
SWAP_CORE = [(i, i ^ 1) for i in range(4)]
SWAP_Y = [(i, i ^ 2) for i in range(4)]
SWAP_X = [(i, i ^ 1) for i in range(8)]


def dot(left, right, how=None):
    if how is None:
        return jnp.dot(left, right, preferred_element_type=F32)
    return lax.dot_general(left, right, how, preferred_element_type=F32)


def params(**more):
    return pltpu.CompilerParams(vmem_limit_bytes=VMEM_LIMIT, **more)


def cost(micros):
    return pl.CostEstimate(flops=0, bytes_accessed=int(micros * 3.4e6), transcendentals=0)


def whole(count):
    return [pl.BlockSpec(memory_space=pltpu.VMEM)] * count


def linear(value):
    groups = value.shape[0] // 8
    return value.reshape(groups, 8, 32, 128).transpose(0, 2, 1, 3).reshape(groups * 256, 128)


def unlinear(value):
    groups = value.shape[0] // 256
    return value.reshape(groups, 32, 8, 128).transpose(0, 2, 1, 3).reshape(groups * 8, SUB * SUB)


def lanes_low(rows):
    return lax.broadcasted_iota(jnp.int32, (rows, 2 * SUB), 1) < SUB


def spread_of(ref, b):
    return ref[pl.ds(b, 32, stride=8), :]


def natural_order():
    row = lax.broadcasted_iota(jnp.int32, (SUB, SUB), 0)
    column = lax.broadcasted_iota(jnp.int32, (SUB, SUB), 1)
    return jnp.where(row == 2 * (column % 32) + column // 32, 1.0, 0.0).astype(BF16)


def prep_rows(number, pairs_ref, x_any, o_ref, rows_in, sems):
    def fetch(i):
        rows = pl.ds(pl.multiple_of(pairs_ref[i] * 256, 256), 256)
        return pltpu.make_async_copy(x_any.at[rows], rows_in.at[i], sems.at[i])

    for i in range(number):
        fetch(i).start()
    low = lanes_low(32)
    order = natural_order()

    def step(i, carry):
        fetch(i).wait()
        x_ref = rows_in.at[i]
        spots = range(4)
        one = [spread_of(x_ref, 2 * m) for m in spots]
        two = [spread_of(x_ref, 2 * m + 1) for m in spots]
        rows = [
            jnp.concatenate(
                [
                    jnp.where(low, one[m], pltpu.roll(two[m], SUB, 1)),
                    jnp.where(low, pltpu.roll(one[m], SUB, 1), two[m]),
                ],
                0,
            ).astype(BF16)
            for m in spots
        ]
        made = [dot(order, rows[m]).astype(BF16) for m in spots]
        for m in spots:
            o_ref[2 * i + m // 2, :, (m % 2) * 128 : (m % 2 + 1) * 128] = made[m]
        return carry

    lax.fori_loop(0, number, step, 0, unroll=2 if number % 2 == 0 else 3)


def prep(master_blocks, pairs):
    number = pairs.shape[0]
    return pl.pallas_call(
        functools.partial(prep_rows, number),
        in_specs=[pl.BlockSpec(memory_space=pltpu.SMEM), pl.BlockSpec(memory_space=pl.ANY)],
        out_specs=pl.BlockSpec(memory_space=pltpu.VMEM),
        out_shape=jax.ShapeDtypeStruct((number * 2, SUB, WIDE), BF16),
        scratch_shapes=[pltpu.VMEM((number, 256, 128), F32), pltpu.SemaphoreType.DMA((number,))],
        compiler_params=params(),
        cost_estimate=cost(0.4 * number),
    )(pairs, linear(master_blocks))


def renew_eight(g_ref, m_ref, sl_ref, sr_ref, rl_ref, rr_ref, go_ref, lo_ref, ro_ref, mo_ref, place):
    low = lanes_low(SUB)
    low_half = lanes_low(32)
    nothing = jnp.zeros((SUB, 128), F32)
    pairs = range(4)

    def diagonal(pair):
        return jnp.concatenate([jnp.where(low, pair, nothing), jnp.where(low, nothing, pair)], 0).astype(BF16)

    def mixed(even, odd):
        return (
            jnp.where(low_half, even, pltpu.roll(odd, SUB, 1)),
            jnp.where(low_half, pltpu.roll(even, SUB, 1), odd),
        )

    def natural(ref, pair, spot):
        even, odd = mixed(spread_of(ref, 2 * pair), spread_of(ref, 2 * pair + 1))
        spot[pl.ds(0, 32, stride=2), :] = even
        spot[pl.ds(1, 32, stride=2), :] = odd
        return spot[...]

    def spread(value, spot):
        spot[...] = value
        return mixed(spot[pl.ds(0, 32, stride=2), :], spot[pl.ds(1, 32, stride=2), :])

    tiles = [g_ref[pair // 2, :, (pair % 2) * 128 : (pair % 2 + 1) * 128] for pair in pairs]
    wide = [tile.astype(F32) for tile in tiles]
    grads = [diagonal(value) for value in wide]
    lefts = [natural(rl_ref, pair, place.at[pair, 0]).astype(BF16) for pair in pairs]
    rights = [diagonal(natural(rr_ref, pair, place.at[pair, 1])) for pair in pairs]
    halves = [dot(lefts[pair], grads[pair]).astype(BF16) for pair in pairs]
    left_parts = [dot(tiles[pair], grads[pair], NT) for pair in pairs]
    squares = [dot(tiles[pair], tiles[pair], TN) for pair in pairs]
    right_parts = [jnp.where(low, square[:SUB], square[SUB:]) for square in squares]
    steps = [dot(halves[pair], rights[pair]) for pair in pairs]
    for pair in pairs:
        made = [
            spread(value[pair], place.at[pair, 2 + k])
            for k, value in enumerate((wide, left_parts, right_parts, steps))
        ]
        for i in range(2):
            at = pl.ds(2 * pair + i, 32, stride=8)
            go_ref[at, :] = made[0][i]
            lo_ref[at, :] = STAT_DECAY * sl_ref[at, :] + (1.0 - STAT_DECAY) * made[1][i]
            ro_ref[at, :] = STAT_DECAY * sr_ref[at, :] + (1.0 - STAT_DECAY) * made[2][i]
            mo_ref[at, :] = m_ref[at, :] - WEIGHT_RATE * made[3][i]


SLOTS = 4


def renew_body(steps, which_ref, g_any, *refs):
    ins = refs[:5]
    outs = refs[-9:-5]
    gbuf, inbuf, outbuf, place, sems = refs[-5:]

    def rows(i):
        return pl.ds(pl.multiple_of(which_ref[i] * 256, 256), 256)

    def fetch(i):
        slot = lax.rem(i, SLOTS)
        copies = [pltpu.make_async_copy(g_any.at[pl.ds(2 * i, 2)], gbuf.at[slot], sems.at[slot, 0])]
        for k, ref in enumerate(ins):
            copies.append(
                pltpu.make_async_copy(ref.at[rows(i)], inbuf.at[slot, k], sems.at[slot, 1 + k])
            )
        return copies

    def put(i):
        slot = lax.rem(i, SLOTS)
        return [
            pltpu.make_async_copy(outbuf.at[slot, k], ref.at[rows(i)], sems.at[slot, 6 + k])
            for k, ref in enumerate(outs)
        ]

    def start(copies):
        for copy in copies:
            copy.start()

    def wait(copies):
        for copy in copies:
            copy.wait()

    for i in range(min(SLOTS, steps)):
        start(fetch(i))

    def step(i, carry):
        slot = lax.rem(i, SLOTS)
        wait(fetch(i))

        @pl.when(i >= SLOTS)
        def _():
            wait(put(i - SLOTS))

        renew_eight(
            gbuf.at[slot], *(inbuf.at[slot, k] for k in range(5)), *(outbuf.at[slot, k] for k in range(4)), place
        )
        start(put(i))

        @pl.when(i + SLOTS < steps)
        def _():
            start(fetch(i + SLOTS))

        return carry

    lax.fori_loop(0, steps, step, 0)
    for i in range(max(0, steps - SLOTS), steps):
        wait(put(i))


def renew(which, owned, master_blocks, stat_left, stat_right, root_left, root_right, before):
    steps = which.shape[0]
    shape = jax.ShapeDtypeStruct((master_blocks.shape[0] * 32, 128), F32)
    anywhere = pl.BlockSpec(memory_space=pl.ANY)
    made = pl.pallas_call(
        functools.partial(renew_body, steps),
        in_specs=[pl.BlockSpec(memory_space=pltpu.SMEM)] + [anywhere] * (6 + len(before)),
        out_specs=[anywhere] * 4,
        out_shape=[shape] * 4,
        scratch_shapes=[
            pltpu.VMEM((SLOTS, 2, SUB, WIDE), BF16),
            pltpu.VMEM((SLOTS, 5, 256, 128), F32),
            pltpu.VMEM((SLOTS, 4, 256, 128), F32),
            pltpu.VMEM((4, 6, SUB, 128), F32),
            pltpu.SemaphoreType.DMA((SLOTS, 10)),
        ],
        input_output_aliases={7 + i: i for i in range(len(before))},
        compiler_params=params(),
        cost_estimate=cost(0.7 * steps),
    )(
        which,
        owned,
        *(linear(value) for value in (master_blocks, stat_left, stat_right, root_left, root_right)),
        *(linear(value) for value in before),
    )
    return [unlinear(value) for value in made]


def times(rows_in, w, base, r, g, part, col):
    first = base + part * r * g + col
    return dot(rows_in, jnp.concatenate([w[first + a * g] for a in range(r)], 0))


def times_back(d_ref, w, base, r, g, count, r4):
    total = None
    for part in range(count):
        first = base + (part * r + 4 * r4) * g
        wide = jnp.concatenate(
            [
                jnp.concatenate([w[first + a * g + col] for a in range(4)], 0)
                for col in range(g)
            ],
            1,
        )
        made = dot(d_ref[:, part * g * WIDE : (part + 1) * g * WIDE], wide, NT)
        total = made if total is None else total + made
    return total


def at256(i):
    return pl.ds(pl.multiple_of(i * WIDE, WIDE), WIDE)


def softmax_all(products, scale, limits):
    scores = []
    for product, limit in zip(products, limits):
        column = lax.broadcasted_iota(jnp.int32, product.shape, 1)
        scores.append(jnp.where(column < limit, product * scale, MASK_FILL))
    tops = [jnp.max(score, 1, keepdims=True) for score in scores]
    raised = [jnp.exp(score - top) for score, top in zip(scores, tops)]
    shares = [1.0 / jnp.sum(value, 1, keepdims=True) for value in raised]
    return [value * share for value, share in zip(raised, shares)]


def score_grads(probs, dprobs):
    weighted = [p * d for p, d in zip(probs, dprobs)]
    totals = [jnp.sum(value, 1, keepdims=True) for value in weighted]
    return [(value - p * total).astype(BF16) for value, p, total in zip(weighted, probs, totals)]


def at128(i):
    return pl.ds(pl.multiple_of(i * 128, 128), 128)


def load(near, far, w, sems, pieces, base):
    started = []
    used = 0
    for i, which in enumerate(pieces):
        begin, count, r, g = TILES[which]
        end = begin + count * r * g
        copies = []
        for owner in range(begin // SHARD, (end - 1) // SHARD + 1):
            first = max(begin, owner * SHARD)
            last = min(end, (owner + 1) * SHARD)
            middle = min(max(owner * SHARD + FAR, first), last)
            for source, lo, hi, at in (
                (near, first, middle, owner * (2 * G_HALF) + first - owner * SHARD),
                (far, middle, last, owner * (SHARD - FAR) + middle - owner * SHARD - FAR),
            ):
                if lo < hi:
                    copies.append(
                        pltpu.make_async_copy(
                            source.at[pl.ds(at, hi - lo)],
                            w.at[pl.ds(base[i] + lo - begin, hi - lo)],
                            sems.at[used],
                        )
                    )
                    copies[-1].start()
                    used += 1
        started.append(copies)
    return started


def arrive(copies):
    for copy in copies:
        copy.wait()


def tiles_of(which):
    _, count, r, g = TILES[which]
    return count * r * g


def co_body(len_ref, xv_ref, xt_ref, near, far, cv_ref, ct_ref, fv_ref, ft_ref, w, sems):
    base = (0, tiles_of(0))
    copies = load(near, far, w, sems, (0, 6), base)
    for which, at, x_ref, o_ref, copy in (
        (0, base[0], xv_ref, cv_ref, copies[0]),
        (6, base[1], xt_ref, ct_ref, copies[1]),
    ):
        _, count, r, g = TILES[which]
        arrive(copy)

        def column(i, carry, at=at, r=r, g=g, x_ref=x_ref, o_ref=o_ref):
            o_ref[:, at256(i)] = times(x_ref[...], w, at, r, g, i // g, i % g).astype(BF16)
            return carry

        lax.fori_loop(0, count * g, column, 0, unroll=2)
    scale = HEAD ** (-0.5)
    reg = len_ref[2]
    heads = BI // HEAD
    vis = [slice(pair * VIS_PAD, (pair + 1) * VIS_PAD) for pair in range(2)]
    text = [slice(pair * 128, (pair + 1) * 128) for pair in range(2)]
    limits = [len_ref[0], len_ref[1], reg, reg]

    def head(j, carry):
        qv, kv, vv = ([cv_ref[rows, at128(j + heads * s)] for rows in vis] for s in range(3))
        qt, kt, vt = ([ct_ref[rows, at128(j + heads * s)] for rows in text] for s in range(3))
        probs = softmax_all([dot(q, k, NT) for q, k in zip(qv + qt, kt + kv)], scale, limits)
        found = [dot(p.astype(BF16), v).astype(BF16) for p, v in zip(probs, vt + vv)]
        for pair in range(2):
            fv_ref[vis[pair], at128(j)] = found[pair]
            ft_ref[text[pair], at128(j)] = found[2 + pair]
        return carry

    lax.fori_loop(0, heads, head, 0, unroll=2)


def co_forward(lengths, x_vis, x_text, near, far):
    return pl.pallas_call(
        co_body,
        in_specs=[pl.BlockSpec(memory_space=pltpu.SMEM)] + whole(2) + [pl.BlockSpec(memory_space=pl.ANY)] * 2,
        out_specs=whole(4),
        out_shape=[
            jax.ShapeDtypeStruct((x_vis.shape[0], 3 * BI), BF16),
            jax.ShapeDtypeStruct((x_text.shape[0], 3 * BI), BF16),
            jax.ShapeDtypeStruct((x_vis.shape[0], BI), BF16),
            jax.ShapeDtypeStruct((x_text.shape[0], BI), BF16),
        ],
        scratch_shapes=[
            pltpu.VMEM((tiles_of(0) + tiles_of(6), SUB, WIDE), BF16),
            pltpu.SemaphoreType.DMA((16,)),
        ],
        compiler_params=params(),
        cost_estimate=cost(22),
    )(lengths, x_vis, x_text, near, far)


def co_back_body(
    len_ref, cv_ref, ct_ref, dv_ref, dt_ref, rv_ref, rt_ref, near, far,
    gv_ref, gt_ref, ov_ref, ot_ref, w, sems,
):
    base = (0, tiles_of(0))
    copies = load(near, far, w, sems, (0, 6), base)
    scale = HEAD ** (-0.5)
    reg = len_ref[2]
    heads = BI // HEAD
    vis = [slice(pair * VIS_PAD, (pair + 1) * VIS_PAD) for pair in range(2)]
    text = [slice(pair * 128, (pair + 1) * 128) for pair in range(2)]
    limits = [len_ref[0], len_ref[1], reg, reg]

    def head(j, carry):
        qv, kv, vv = ([cv_ref[rows, at128(j + heads * s)] for rows in vis] for s in range(3))
        qt, kt, vt = ([ct_ref[rows, at128(j + heads * s)] for rows in text] for s in range(3))
        up = [dv_ref[rows, at128(j)] for rows in vis] + [dt_ref[rows, at128(j)] for rows in text]
        queries, keys, values = qv + qt, kt + kv, vt + vv
        products = [dot(q, k, NT) for q, k in zip(queries, keys)]
        dprobs = [dot(u, v, NT) for u, v in zip(up, values)]
        probs = softmax_all(products, scale, limits)
        ds = score_grads(probs, dprobs)
        dvalues = [dot(p.astype(BF16), u, TN).astype(BF16) for p, u in zip(probs, up)]
        dqueries = [(dot(d, k) * scale).astype(BF16) for d, k in zip(ds, keys)]
        dkeys = [(dot(d, q, TN) * scale).astype(BF16) for d, q in zip(ds, queries)]
        for pair in range(2):
            gv_ref[vis[pair], at128(j)] = dqueries[pair]
            gt_ref[text[pair], at128(j + heads)] = dkeys[pair]
            gt_ref[text[pair], at128(j + 2 * heads)] = dvalues[pair]
            gt_ref[text[pair], at128(j)] = dqueries[2 + pair]
            gv_ref[vis[pair], at128(j + heads)] = dkeys[2 + pair]
            gv_ref[vis[pair], at128(j + 2 * heads)] = dvalues[2 + pair]
        return carry

    lax.fori_loop(0, heads, head, 0, unroll=2)
    for which, at, g_ref, r_ref, o_ref, copy in (
        (0, base[0], gv_ref, rv_ref, ov_ref, copies[0]),
        (6, base[1], gt_ref, rt_ref, ot_ref, copies[1]),
    ):
        _, count, r, g = TILES[which]
        arrive(copy)

        def rows4(i, carry, at=at, r=r, g=g, count=count, g_ref=g_ref, r_ref=r_ref, o_ref=o_ref):
            o_ref[:, at256(i)] = r_ref[:, at256(i)] + times_back(g_ref, w, at, r, g, count, i)
            return carry

        lax.fori_loop(0, r // 4, rows4, 0)


def co_backward(lengths, co_vis, co_text, dvis, dtext, resid_vis, resid_text, near, far):
    return pl.pallas_call(
        co_back_body,
        in_specs=[pl.BlockSpec(memory_space=pltpu.SMEM)] + whole(6) + [pl.BlockSpec(memory_space=pl.ANY)] * 2,
        out_specs=whole(4),
        out_shape=[
            jax.ShapeDtypeStruct(co_vis.shape, BF16),
            jax.ShapeDtypeStruct(co_text.shape, BF16),
            jax.ShapeDtypeStruct(resid_vis.shape, F32),
            jax.ShapeDtypeStruct(resid_text.shape, F32),
        ],
        scratch_shapes=[
            pltpu.VMEM((tiles_of(0) + tiles_of(6), SUB, WIDE), BF16),
            pltpu.SemaphoreType.DMA((16,)),
        ],
        compiler_params=params(),
        cost_estimate=cost(23),
    )(lengths, co_vis, co_text, dvis, dtext, resid_vis, resid_text, near, far)


def erf_parts(value):
    return 0.5 * (1.0 + lax.erf(value * 0.7071067811865476))


def middle_body(
    config,
    len_ref, ctx_ref, x_ref, cot_ref, norm_ref, near, far,
    out_ref, first_ref, act_ref, second_ref, sctx_ref,
    fback_ref, pback_ref, bback_ref, dself_ref, tback_ref,
    resid_ref, dctx_ref, sums_ref,
    w, sems, pre, n1, n2, n3, s1, s2, s3, wide, acc, selfs, probs, stat,
):
    begin, rows, span, head, chunk = config
    width = x_ref.shape[1]
    base = []
    at = 0
    for which in range(begin, begin + 5):
        base.append(at)
        at += tiles_of(which)
    copies = load(near, far, w, sems, tuple(range(begin, begin + 5)), base)
    shapes = [TILES[which][1:] for which in range(begin, begin + 5)]
    steps = rows // chunk

    def at_chunk(i):
        return pl.ds(pl.multiple_of(i * chunk, chunk), chunk)

    def norm(resid, which, i, kept, scales):
        mean = jnp.mean(resid, 1, keepdims=True)
        centered = resid - mean
        scale = lax.rsqrt(jnp.mean(centered * centered, 1, keepdims=True) + NORM_EPSILON)
        normed = centered * scale
        kept[at_chunk(i), :] = normed
        scales[at_chunk(i), :] = jnp.broadcast_to(scale, (chunk, 128))
        return normed * norm_ref[0, which : which + 1, :] + norm_ref[1, which : which + 1, :]

    def eight(value):
        return jnp.sum(value.reshape(chunk // 8, 8, width), 0)

    def norm_back(upstream, which, i, kept, scales):
        normed = kept[at_chunk(i), :]
        stat[which] = stat[which] + eight(upstream * normed)
        stat[3 + which] = stat[3 + which] + eight(upstream)
        scaled = upstream * norm_ref[0, which : which + 1, :]
        return scales[at_chunk(i), 0:1] * (
            scaled
            - jnp.mean(scaled, 1, keepdims=True)
            - normed * jnp.mean(scaled * normed, 1, keepdims=True)
        )

    def loop(count, body, unroll=1):
        lax.fori_loop(0, count, lambda i, carry: (body(i), carry)[1], 0, unroll=unroll)

    stat[...] = jnp.zeros(stat.shape, F32)
    count, r, g = shapes[0]
    arrive(copies[0])

    def co_out(i):
        wide[:, at256(i)] = times(ctx_ref[...], w, base[0], r, g, 0, i)

    loop(g, co_out, g)

    def norm_one(i):
        value = norm(wide[at_chunk(i), :] + x_ref[at_chunk(i), :].astype(F32), 0, i, n1, s1)
        wide[at_chunk(i), :] = value
        first_ref[at_chunk(i), :] = value.astype(BF16)

    loop(steps, norm_one, 2 if steps % 2 == 0 else steps)
    _, r_up, g_up = shapes[1]
    _, r_down, g_down = shapes[2]
    arrive(copies[1])
    arrive(copies[2])
    acc[...] = jnp.zeros(acc.shape, F32)

    def down_rows(i):
        return jnp.concatenate(
            [
                jnp.concatenate([w[base[2] + (4 * i + a) * g_down + col] for a in range(4)], 0)
                for col in range(g_down)
            ],
            1,
        )

    def feed(i):
        value = times(first_ref[...], w, base[1], r_up, g_up, 0, i)
        part = erf_parts(value)
        pre[i] = part + value * (0.3989422804014327 * jnp.exp(-0.5 * value * value))
        act = (value * part).astype(BF16)
        act_ref[:, at256(i)] = act
        acc[...] += dot(act, down_rows(i))

    loop(g_up, feed, 4)

    def norm_two(i):
        value = norm(wide[at_chunk(i), :] + acc[at_chunk(i), :], 1, i, n2, s2)
        wide[at_chunk(i), :] = value
        second_ref[at_chunk(i), :] = value.astype(BF16)

    loop(steps, norm_two, 2 if steps % 2 == 0 else steps)
    count_s, r_s, g_s = shapes[3]
    arrive(copies[3])

    def self_in(i):
        selfs[:, at256(i)] = times(second_ref[...], w, base[3], r_s, g_s, i // g_s, i % g_s).astype(BF16)

    loop(count_s * g_s, self_in, g_s)
    scale = head ** (-0.5)
    groups = width // 128
    per = 128 // head
    pairs = rows // span

    def halves(values):
        if per == 1:
            return values[0]
        low = lax.broadcasted_iota(jnp.int32, values[0].shape, 1) < head
        return jnp.where(low, values[0], values[1])

    def only(value, h):
        if per == 1:
            return value
        low = lax.broadcasted_iota(jnp.int32, value.shape, 1) < head
        keep = low if h == 0 else jnp.logical_not(low)
        return jnp.where(keep, value, jnp.zeros_like(value))

    own = [slice(pair * span, (pair + 1) * span) for pair in range(pairs)]
    each = [(pair, h) for pair in range(pairs) for h in range(per)]

    def attend(j):
        q, k, v = ([selfs[rows_of, at128(j + groups * s)] for rows_of in own] for s in range(3))
        products = [dot(only(q[pair], h), k[pair], NT) for pair, h in each]
        p = softmax_all(products, scale, [len_ref[pair] for pair, _ in each])
        found = [dot(value.astype(BF16), v[pair]) for value, (pair, _) in zip(p, each)]
        for i, value in enumerate(p):
            probs[j * len(each) + i] = value
        for pair in range(pairs):
            sctx_ref[own[pair], at128(j)] = halves(found[pair * per : (pair + 1) * per]).astype(BF16)

    loop(groups, attend, 2)
    _, r_o, g_o = shapes[4]
    arrive(copies[4])

    def self_out(i):
        acc[:, at256(i)] = times(sctx_ref[...], w, base[4], r_o, g_o, 0, i)

    loop(g_o, self_out, g_o)

    def norm_three(i):
        value = norm(wide[at_chunk(i), :] + acc[at_chunk(i), :], 2, i, n3, s3)
        out_ref[at_chunk(i), :] = value.astype(BF16)
        third = norm_back(cot_ref[at_chunk(i), :].astype(F32), 2, i, n3, s3)
        wide[at_chunk(i), :] = third
        tback_ref[at_chunk(i), :] = third.astype(BF16)

    loop(steps, norm_three, 2 if steps % 2 == 0 else steps)

    def self_out_back(i):
        dctx_ref[:, at256(i)] = times_back(tback_ref, w, base[4], r_o, g_o, 1, i).astype(BF16)

    loop(r_o // 4, self_out_back, r_o // 4)
    def attend_back(j):
        q, k, v = ([selfs[rows_of, at128(j + groups * s)] for rows_of in own] for s in range(3))
        up = [dctx_ref[rows_of, at128(j)] for rows_of in own]
        p = [probs[j * len(each) + i] for i in range(len(each))]
        dprobs = [dot(only(up[pair], h), v[pair], NT) for pair, h in each]
        dv = [dot(value.astype(BF16), up[pair], TN) for value, (pair, _) in zip(p, each)]
        ds = score_grads(p, dprobs)
        dq = [dot(value, k[pair]) for value, (pair, _) in zip(ds, each)]
        dk = [dot(value, q[pair], TN) for value, (pair, _) in zip(ds, each)]
        for pair in range(pairs):
            mine = slice(pair * per, (pair + 1) * per)
            dself_ref[own[pair], at128(j)] = (halves(dq[mine]) * scale).astype(BF16)
            dself_ref[own[pair], at128(j + groups)] = (halves(dk[mine]) * scale).astype(BF16)
            dself_ref[own[pair], at128(j + 2 * groups)] = halves(dv[mine]).astype(BF16)

    loop(groups, attend_back, 2)

    def self_in_back(i):
        acc[:, at256(i)] = times_back(dself_ref, w, base[3], r_s, g_s, count_s, i)

    loop(r_s // 4, self_in_back, r_s // 4)

    def norm_two_back(i):
        value = norm_back(wide[at_chunk(i), :] + acc[at_chunk(i), :], 1, i, n2, s2)
        wide[at_chunk(i), :] = value
        bback_ref[at_chunk(i), :] = value.astype(BF16)

    loop(steps, norm_two_back, 2 if steps % 2 == 0 else steps)

    def feed_back(i):
        act_grad = dot(bback_ref[...], down_rows(i), NT)
        pback_ref[:, at256(i)] = (act_grad * pre[i]).astype(BF16)

    loop(g_up, feed_back, 4)

    def up_back(i):
        acc[:, at256(i)] = times_back(pback_ref, w, base[1], r_up, g_up, 1, i)

    loop(r_up // 4, up_back, r_up // 4)

    def norm_one_back(i):
        value = norm_back(wide[at_chunk(i), :] + acc[at_chunk(i), :], 0, i, n1, s1)
        resid_ref[at_chunk(i), :] = value
        fback_ref[at_chunk(i), :] = value.astype(BF16)

    loop(steps, norm_one_back, 2 if steps % 2 == 0 else steps)

    def co_out_back(i):
        dctx_ref[:, at256(i)] = times_back(fback_ref, w, base[0], r, g, 1, i).astype(BF16)

    loop(r // 4, co_out_back, r // 4)
    sums_ref[...] = jnp.sum(stat[...], 1)


def middle(begin, lengths, context, x, cot, norms, near, far, span, head, chunk):
    rows, width = x.shape
    hidden = TILES[begin + 1][3] * WIDE
    number = sum(tiles_of(which) for which in range(begin, begin + 5))
    low = lambda columns: jax.ShapeDtypeStruct((rows, columns), BF16)
    return pl.pallas_call(
        functools.partial(middle_body, (begin, rows, span, head, chunk)),
        in_specs=[pl.BlockSpec(memory_space=pltpu.SMEM)] + whole(4) + [pl.BlockSpec(memory_space=pl.ANY)] * 2,
        out_specs=whole(13),
        out_shape=[
            low(width), low(width), low(hidden), low(width), low(width),
            low(width), low(hidden), low(width), low(3 * width), low(width),
            jax.ShapeDtypeStruct((rows, width), F32), low(BI),
            jax.ShapeDtypeStruct((6, width), F32),
        ],
        scratch_shapes=[
            pltpu.VMEM((number, SUB, WIDE), BF16),
            pltpu.SemaphoreType.DMA((24,)),
            pltpu.VMEM((hidden // WIDE, rows, WIDE), F32),
        ]
        + [pltpu.VMEM((rows, width), F32)] * 3
        + [pltpu.VMEM((rows, 128), F32)] * 3
        + [pltpu.VMEM((rows, width), F32)] * 2
        + [
            pltpu.VMEM((rows, 3 * width), BF16),
            pltpu.VMEM((rows // span * (width // head), span, span), F32),
            pltpu.VMEM((6, 8, width), F32),
        ],
        compiler_params=params(),
        cost_estimate=cost(40),
    )(lengths, context, x, cot, norms, near, far)


def weight_body(kinds, *refs):
    n = len(kinds)
    lefts, rights = refs[:n], refs[n : 2 * n]
    out, stage, across, sems = refs[2 * n :]
    offset = 0
    for which, a_ref, b_ref in zip(kinds, lefts, rights):
        _, count, r, g = TILES[which]
        size = 4 * g

        def copy(i, slot, offset=offset, size=size):
            return pltpu.make_async_copy(
                stage.at[slot, pl.ds(0, size)], out.at[pl.ds(offset + i * size, size)], sems.at[slot]
            )

        total = count * (r // 4)

        def step(i, carry, a_ref=a_ref, b_ref=b_ref, r=r, g=g, copy=copy):
            slot = lax.rem(i, 4)

            @pl.when(i >= 4)
            def _():
                copy(i - 4, slot).wait()

            part = i // (r // 4)
            r4 = lax.rem(i, r // 4)
            across[...] = jnp.transpose(a_ref[:, at256(r4)])
            left = across[...]
            for first in range(0, g, 4 if g % 4 == 0 else 3):
                columns = range(first, first + (4 if g % 4 == 0 else 3))
                made = [dot(left, b_ref[:, at256(part * g + col)]).astype(BF16) for col in columns]
                for col, value in zip(columns, made):
                    for a in range(4):
                        stage[slot, a * g + col] = value[a * SUB : (a + 1) * SUB]
            copy(i, slot).start()
            return carry

        lax.fori_loop(0, total, step, 0, unroll=2 if total % 2 == 0 else 3)
        for i in range(max(0, total - 4), total):
            copy(i, i % 4).wait()
        offset += count * r * g


def weight_grads(kinds, lefts, rights):
    number = sum(tiles_of(which) for which in kinds)
    most = max(4 * TILES[which][3] for which in kinds)
    return pl.pallas_call(
        functools.partial(weight_body, kinds),
        in_specs=whole(2 * len(kinds)),
        out_specs=pl.BlockSpec(memory_space=pl.ANY),
        out_shape=jax.ShapeDtypeStruct((number, SUB, WIDE), BF16),
        scratch_shapes=[
            pltpu.VMEM((4, most, SUB, WIDE), BF16),
            pltpu.VMEM((WIDE, lefts[0].shape[0]), BF16),
            pltpu.SemaphoreType.DMA((4,)),
        ],
        compiler_params=params(),
        cost_estimate=cost(number * 0.04),
    )(*lefts, *rights)


def spot():
    dp = lax.axis_index("dp")
    seq = lax.axis_index("seq")
    return dp // 2, dp % 2, seq // 2, seq % 2


def along_z(value, moves):
    return lax.ppermute(value, "dp", [(2 * a + x, 2 * b + x) for a, b in moves for x in (0, 1)])


def cut(value, begin, size):
    return lax.dynamic_slice_in_dim(value, begin, size, 0)


def join(parts):
    return jnp.concatenate(parts) if len(parts) > 1 else parts[0]


def add(left, right):
    return (left.astype(F32) + right.astype(F32)).astype(BF16)


def by_y(y, mine, other):
    return [jnp.where(y == 0, mine, other), jnp.where(y == 0, other, mine)]


def blank(shape):
    return pl.pallas_call(
        lambda out: None,
        out_specs=pl.BlockSpec(memory_space=pl.ANY),
        out_shape=jax.ShapeDtypeStruct(shape, BF16),
        compiler_params=params(),
    )()


def gather_tiles(master_blocks, others):
    z, x, y, core = spot()
    lone, both, half = G_LONE // 2, (G_HALF - 2 * G_LONE) // 2, G_HALF // 2
    fourth = (SHARD - FAR) // 4
    mine = prep(
        master_blocks,
        jnp.concatenate(
            [half * core + lone * y + jnp.arange(lone), half * core + 2 * lone + jnp.arange(both)]
        ).astype(jnp.int32),
    )
    last = prep(
        master_blocks,
        ((FAR + fourth * lax.axis_index("seq")) // 2 + jnp.arange(fourth // 2)).astype(jnp.int32),
    )
    far = lax.all_gather(last, ("dp", "seq"), axis=0, tiled=True)
    ring = [(0, 1), (1, 2), (2, 3), (3, 0)]
    near = blank((8, 2 * G_HALF, SUB, WIDE))
    rows = [mine]
    cross = []
    halves = []
    for phase in range(6):
        out = {}
        if phase < 3:
            out["z"] = along_z(rows[phase], ring)
        if phase < 4:
            out["x"] = lax.ppermute(rows[phase], "dp", SWAP_X)
        if 1 <= phase < 5:
            here = [rows[phase - 1], cross[phase - 1]]
            out["y"] = lax.ppermute(join([part[:G_LONE] for part in here]), "seq", SWAP_Y)
        if phase >= 2:
            out["core"] = lax.ppermute(join(halves[phase - 2]), "seq", SWAP_CORE)
        out, rows, cross, halves, near, others = lax.optimization_barrier(
            (out, rows, cross, halves, near, others)
        )
        if "z" in out:
            rows = rows + [out["z"]]
        if "x" in out:
            cross = cross + [out["x"]]
        if "y" in out:
            halves = halves + [
                [
                    join(by_y(y, part[:G_LONE], out["y"][G_LONE * i : G_LONE * (i + 1)]) + [part[G_LONE:]])
                    for i, part in enumerate(here)
                ]
            ]
        if "core" in out:
            step = phase - 2
            for side in range(2):
                owner = 2 * ((z - step) % 4) + (x + side) % 2
                own = halves[step][side][None]
                got = out["core"][None, G_HALF * side : G_HALF * (side + 1)]
                near = lax.dynamic_update_slice(near, own, (owner, G_HALF * core, 0, 0))
                near = lax.dynamic_update_slice(near, got, (owner, G_HALF * (1 - core), 0, 0))
    return near.reshape(-1, SUB, WIDE), far, others


ROUTES = (
    (((3, 2),), ((2, 1),), ((1, 0),)),
    (((3, 2), (0, 1)), ((2, 1),)),
    (((0, 1), (3, 2)), ((1, 2),)),
    (((0, 1),), ((1, 2),), ((2, 3),)),
)
LONE = R_LONE // CHUNKS
BOTH = R_BOTH // CHUNKS
GROUP_ORDER = [[0, 2, 1, 3]]


def lone_at(core):
    return 2 * R_LONE * core


def both_at(core):
    return 4 * R_LONE + (SHARD - 4 * R_LONE - R_BOTH) * core


def chunk_pairs(k):
    table = []
    for core in range(2):
        for y in range(2):
            table += [(lone_at(core) + R_LONE * y + LONE * k) // 2 + i for i in range(LONE // 2)]
        table += [(both_at(core) + BOTH * k) // 2 + i for i in range(BOTH // 2)]
    return jnp.asarray(table, jnp.int32)


def pieces_of(owner, ranges, begins):
    pieces = []
    at = 0
    for begin, size in ranges:
        first, last = SHARD * owner + begin, SHARD * owner + begin + size
        for which, (lo, hi) in enumerate(begins):
            start, end = max(first, lo), min(last, hi)
            if start < end:
                pieces.append((which, start - lo, end - start, at + start - first))
        at += size
    return pieces


def half_plan(owner, begins, other):
    return [
        pieces_of(owner, ((lone_at(core ^ other), 2 * R_LONE), (both_at(core ^ other), R_BOTH)), begins)
        for core in range(2)
    ]


def both_plan(owner, begins, other):
    plan = []
    for core in range(2):
        pieces = []
        for i in range(2):
            for which, begin, size, at in pieces_of(owner + i, ((both_at(core ^ other), R_BOTH),), begins):
                pieces.append((which, begin, size, at + R_BOTH * i))
        plan.append(pieces)
    return plan


def follow(core_ref, plans, arrays, outs, sems):
    for core in range(2):

        @pl.when(core_ref[0] == core)
        def _(core=core):
            copies = []
            for j, plan in enumerate(plans):
                for i, (which, begin, size, at) in enumerate(plan[core]):
                    copies.append(
                        pltpu.make_async_copy(
                            arrays[which].at[pl.ds(begin, size)], outs[j].at[pl.ds(at, size)], sems.at[j, i]
                        )
                    )
            for copy in copies:
                copy.start()
            for copy in copies:
                copy.wait()


def pick_body(plans, number, core_ref, *refs):
    follow(core_ref, plans, refs[:number], refs[number:-1], refs[-1])


def pick(core, sources, plans, sizes):
    arrays = [array for _, array in sources]
    return pl.pallas_call(
        functools.partial(pick_body, plans, len(arrays)),
        in_specs=[pl.BlockSpec(memory_space=pltpu.SMEM)] + [pl.BlockSpec(memory_space=pl.ANY)] * len(arrays),
        out_specs=whole(len(plans)),
        out_shape=[jax.ShapeDtypeStruct((size, SUB, WIDE), BF16) for size in sizes],
        scratch_shapes=[pltpu.SemaphoreType.DMA((len(plans), 6))],
        compiler_params=params(),
        cost_estimate=cost(2 * len(plans)),
    )(core.reshape(1), *arrays)


def begins_of(sources):
    return [(begin, begin + array.shape[0]) for begin, array in sources]


def merge_body(plans, number, core_ref, *refs):
    arrays, got = refs[:number], refs[number : number + 2]
    outs = refs[number + 2 : -2]
    own, sems = refs[-2:]
    follow(core_ref, plans, arrays, [own.at[0], own.at[1]], sems)

    def total(out, size, i, begin):
        def tile(t, carry):
            out[t] = add(own[i, begin + t], got[i][begin + t])
            return carry

        lax.fori_loop(0, size, tile, 0, unroll=2)

    for k in range(CHUNKS):
        for i in range(2):
            for y in range(2):
                total(outs[2 * k].at[y, i], LONE, i, R_LONE * y + LONE * k)
            total(outs[2 * k + 1].at[i], BOTH, i, 2 * R_LONE + BOTH * k)


def merge(core, sources, zi, got, chunks):
    arrays = [array for _, array in sources]
    plans = [half_plan(2 * zi + i, begins_of(sources), 0) for i in range(2)]
    shapes = []
    for _ in range(CHUNKS):
        shapes += [(2, 2, LONE, SUB, WIDE), (2, BOTH, SUB, WIDE)]
    made = pl.pallas_call(
        functools.partial(merge_body, plans, len(arrays)),
        in_specs=[pl.BlockSpec(memory_space=pltpu.SMEM)]
        + [pl.BlockSpec(memory_space=pl.ANY)] * len(arrays)
        + whole(2),
        out_specs=whole(len(shapes)),
        out_shape=[jax.ShapeDtypeStruct(shape, BF16) for shape in shapes],
        scratch_shapes=[
            pltpu.VMEM((2, R_HALF, SUB, WIDE), BF16),
            pltpu.SemaphoreType.DMA((2, 6)),
        ],
        compiler_params=params(),
        cost_estimate=cost(8),
    )(core.reshape(1), *arrays, *got)
    for k, chunk in enumerate(chunks):
        chunk.state["lone", zi], chunk.state["both", zi] = made[2 * k : 2 * k + 2]


def arrange_body(pieces, x_any, o_any, held, sems):
    arrivals = []
    at = 0
    for i, (begin, size) in enumerate(pieces):
        spot_of = pl.ds(at, size)
        arrivals.append(
            (
                pltpu.make_async_copy(x_any.at[pl.ds(begin, size)], held.at[spot_of], sems.at[0, i]),
                pltpu.make_async_copy(held.at[spot_of], o_any.at[spot_of], sems.at[1, i]),
            )
        )
        arrivals[-1][0].start()
        at += size
    for came, goes in arrivals:
        came.wait()
        goes.start()
    for _, goes in arrivals:
        goes.wait()


def arrange(array, pieces):
    number = sum(size for _, size in pieces)
    return pl.pallas_call(
        functools.partial(arrange_body, pieces),
        in_specs=[pl.BlockSpec(memory_space=pl.ANY)],
        out_specs=pl.BlockSpec(memory_space=pl.ANY),
        out_shape=jax.ShapeDtypeStruct((number, SUB, WIDE), BF16),
        scratch_shapes=[
            pltpu.VMEM((number, SUB, WIDE), BF16),
            pltpu.SemaphoreType.DMA((2, len(pieces))),
        ],
        compiler_params=params(),
        cost_estimate=cost(6),
    )(array)


def group_lone(array, offset):
    pieces = tuple(
        (offset + SHARD * o + R_LONE * part, R_LONE) for part in range(4) for o in range(2)
    )
    made = lax.psum_scatter(
        arrange(array, pieces), "seq", scatter_dimension=0, tiled=True, axis_index_groups=GROUP_ORDER
    )
    return made.reshape(2, R_LONE, SUB, WIDE)


def chunks_of(lone, both):
    return [
        (lone[:, LONE * k : LONE * (k + 1)], both[:, BOTH * k : BOTH * (k + 1)]) for k in range(CHUNKS)
    ]


class Sums:
    def __init__(self):
        self.at = spot()
        self.state = {}

    def send(self, task):
        z, x, y, core = self.at
        state = self.state
        kind, who = task[0], task[1]
        if kind == "Y":
            return lax.ppermute(cut(state["lone", who], 1 - y, 1)[0], "seq", SWAP_Y)
        if kind == "X":
            lone, both = state["kept", who]
            return lax.ppermute(join([cut(lone, 1 - x, 1)[0], cut(both, 1 - x, 1)[0]]), "dp", SWAP_X)
        if kind == "Z":
            return along_z(state["value", who], ROUTES[who][task[2]])
        if kind == "F":
            values = [state["value", zi] for zi in range(4)]
            mine = jnp.where(z == 0, values[0], jnp.where(z == 1, values[1], jnp.where(z == 2, values[2], values[3])))
            state["mine", 0] = mine
            return lax.ppermute(mine, "seq", SWAP_Y)
        if kind == "G":
            return lax.ppermute(state["whole", 0], "seq", SWAP_CORE)
        axis, step = (("seq", 1), ("seq", 2), ("dp", 1), ("dp", 2), ("dp", 4))[who]
        size = lax.axis_size(axis)
        return lax.ppermute(state["norms", 0], axis, [(i, i ^ step) for i in range(size)])

    def take(self, task, got):
        z, x, y, core = self.at
        state = self.state
        kind, who = task[0], task[1]
        if kind == "Y":
            state["kept", who] = (add(cut(state.pop(("lone", who)), y, 1)[0], got), state.pop(("both", who)))
        elif kind == "X":
            lone, both = state.pop(("kept", who))
            state["value", who] = add(join([cut(lone, x, 1)[0], cut(both, x, 1)[0]]), got)
        elif kind == "Z":
            state["value", who] = add(state["value", who], got)
        elif kind == "F":
            mine = state.pop(("mine", 0))
            state["whole", 0] = join(by_y(y, mine[:LONE], got[:LONE]) + [add(mine[LONE:], got[LONE:])])
        elif kind == "G":
            half = state.pop(("whole", 0))
            state["owned", 0] = join([jnp.where(core == 0, half, got), jnp.where(core == 0, got, half)])
        else:
            state["norms", 0] = state["norms", 0] + got

    def step(self, tasks):
        out = [self.send(task) for task in tasks]
        out, self.state = lax.optimization_barrier((out, self.state))
        for task, got in zip(tasks, out):
            self.take(task, got)


def beside(chunks, tasks, work):
    out = [chunks[k].send(task) for k, task in tasks]
    made = work()
    out, made, states = lax.optimization_barrier((out, made, [chunk.state for chunk in chunks]))
    for chunk, state in zip(chunks, states):
        chunk.state = state
    for (k, task), got in zip(tasks, out):
        chunks[k].take(task, got)
    return made


def pad_regions(value, pairs):
    reg = value.shape[0] // pairs
    cube = value.reshape(pairs, reg, value.shape[1])
    return jnp.pad(cube, ((0, 0), (0, VIS_PAD - reg), (0, 0))).reshape(pairs * VIS_PAD, -1)


def cut_regions(value, pairs, reg):
    return value.reshape(pairs, VIS_PAD, -1)[:, :reg].reshape(pairs * reg, -1)


def fast_shards(
    x_text, x_vis, caption_len, cot_text, cot_vis, master_blocks,
    stat_left, stat_right, root_left, root_right, norm_params, norm_second,
):
    pairs = caption_len.shape[0]
    reg = x_vis.shape[0] // pairs
    xv = pad_regions(x_vis, pairs)
    cv = pad_regions(cot_vis, pairs)
    near, far, (xv, cv) = gather_tiles(master_blocks, (xv, cv))
    lengths = jnp.concatenate([caption_len, jnp.full((2,), reg, jnp.int32)])
    regions = jnp.full((2,), reg, jnp.int32)
    vis_norms = norm_params[:, : 3 * VIS].reshape(2, 3, VIS)
    text_norms = norm_params[:, 3 * VIS :].reshape(2, 3, TXT)
    co_vis, co_text, vis_ctx, text_ctx = co_forward(lengths, xv, x_text, near, far)
    (out_vis, v_first, v_act, v_second, v_sctx, v_fback, v_pback, v_bback, v_dself, v_tback,
     v_resid, v_dctx, v_sums) = middle(1, regions, vis_ctx, xv, cv, vis_norms, near, far, VIS_PAD, HEAD_V, 32)
    vis_mid = weight_grads(
        (1, 2, 3, 4, 5), (vis_ctx, v_first, v_act, v_second, v_sctx),
        (v_fback, v_pback, v_bback, v_dself, v_tback),
    )
    _, _, _, core = spot()
    chunks = [Sums() for _ in range(CHUNKS)]
    vis_at, text_at = TILES[1][0], TILES[7][0]
    vis_pair, text_pair = (vis_mid, 2 * SHARD - vis_at), 6 * SHARD - text_at
    lone = group_lone(*vis_pair)
    vis_source = (vis_at, vis_mid)

    def pick_both(source, owner):
        begins = begins_of([source])
        plans = [both_plan(owner, begins, 1), both_plan(owner, begins, 0)]
        send, own = pick(core, [source], plans, [2 * R_BOTH] * 2)
        return own, lax.ppermute(send, "seq", SWAP_CORE)

    def both_sum(own, got):
        return add(own, got).reshape(2, R_BOTH, SUB, WIDE)

    own_both, far_both = pick_both(vis_source, 2)
    (out_text, t_first, t_act, t_second, t_sctx, t_fback, t_pback, t_bback, t_dself, t_tback,
     t_resid, t_dctx, t_sums) = middle(
        7, lengths, text_ctx, x_text, cot_text, text_norms, near, far, x_text.shape[0] // pairs, HEAD_T, 32
    )
    chunks[0].state["norms", 0] = jnp.concatenate([v_sums.reshape(2, -1), t_sums.reshape(2, -1)], 1)
    lefts = (text_ctx, t_first, t_act, t_second, t_sctx)
    rights = (t_fback, t_pback, t_bback, t_dself, t_tback)
    lefts, rights, far_both = lax.optimization_barrier((lefts, rights, far_both))
    text_mid = weight_grads((7, 8, 9, 10, 11), lefts, rights)
    text_source = (text_at, text_mid)
    both = both_sum(own_both, far_both)
    own_both, far_both = pick_both(text_source, 6)
    back = (co_vis, co_text, v_dctx, t_dctx, v_resid, t_resid)
    back, both, text_mid = lax.optimization_barrier((back, both, text_mid))
    for k, kept in enumerate(chunks_of(lone, both)):
        chunks[k].state["kept", 1] = kept
    lone = group_lone(text_mid, text_pair)
    def swap_halves(sources, owners):
        plans = [half_plan(o, begins_of(sources), 1) for o in owners]
        return [
            lax.ppermute(part, "seq", SWAP_CORE) for part in pick(core, sources, plans, [R_HALF] * len(owners))
        ]

    dco_vis, dco_text, grad_vis, grad_text, far_both, far_half = beside(
        chunks,
        [(0, ("X", 1)), (0, ("N", 0))],
        lambda: (*co_backward(lengths, *back, near, far), far_both, swap_halves([text_source], (5,))[0]),
    )
    late_sources = [vis_source, None, text_source]

    def co_grads():
        text_co = weight_grads((6,), (x_text,), (dco_text,))
        late_sources[1] = (TILES[6][0], text_co)
        return text_co, swap_halves(late_sources, (4,))[0], weight_grads((0,), (xv,), (dco_vis,))

    text_co, far_four, vis_co = beside(
        chunks, [(1, ("X", 1)), (0, ("Z", 1, 0)), (0, ("N", 1))], co_grads
    )
    early_sources = [(0, vis_co), vis_source]
    late_sources[1] = (TILES[6][0], text_co)

    def merge_late():
        merge(core, late_sources, 2, [far_four, far_half], chunks)
        return swap_halves(early_sources, (0, 1))

    got = beside(chunks, [(0, ("Z", 1, 1)), (1, ("Z", 1, 0))], merge_late)
    for k, kept in enumerate(chunks_of(lone, both_sum(own_both, far_both))):
        chunks[k].state["kept", 3] = kept
    beside(
        chunks,
        [(0, ("Y", 2)), (0, ("X", 3)), (1, ("Z", 1, 1))],
        lambda: merge(core, early_sources, 0, got, chunks),
    )
    beside(chunks, [(0, ("Y", 0)), (0, ("X", 2)), (0, ("Z", 3, 0)), (1, ("X", 3)), (0, ("N", 2))], lambda: ())
    chunks[1].step([("Y", 2), ("Z", 3, 0)])
    chunks[0].step([("X", 0), ("Z", 2, 0), ("Z", 3, 1), ("N", 3)])
    chunks[1].step([("Y", 0), ("X", 2), ("Z", 3, 1)])
    chunks[0].step([("Z", 0, 0), ("Z", 2, 1), ("Z", 3, 2), ("N", 4)])
    chunks[1].step([("X", 0), ("Z", 2, 0), ("Z", 3, 2)])
    chunks[0].step([("Z", 0, 1)])
    chunks[1].step([("Z", 0, 0), ("Z", 2, 1)])
    chunks[0].step([("Z", 0, 2)])
    chunks[1].step([("Z", 0, 1)])
    chunks[0].step([("F", 0)])
    chunks[0].step([("G", 0)])
    statistics = (master_blocks, stat_left, stat_right, root_left, root_right)
    early = chunk_pairs(0)
    count = early.shape[0] // 2
    owned = chunks[0].state["owned", 0]
    renewed = beside(
        chunks, [(1, ("Z", 0, 2))], lambda: renew(early[:count], owned[: 2 * count], *statistics, ())
    )
    renewed = beside(
        chunks, [(1, ("F", 0))], lambda: renew(early[count:], owned[2 * count :], *statistics, renewed)
    )
    chunks[1].step([("G", 0)])
    grad_blocks, left_new, right_new, master_new = renew(
        chunk_pairs(1), chunks[1].state["owned", 0], *statistics, renewed
    )
    norm_grads = chunks[0].state["norms", 0]
    second_new = STAT_DECAY * norm_second + (1.0 - STAT_DECAY) * norm_grads * norm_grads
    norm_new = norm_params - NORM_RATE * norm_grads / (jnp.sqrt(second_new) + MOMENT_EPSILON)
    return (
        out_text,
        cut_regions(out_vis, pairs, reg),
        grad_text,
        cut_regions(grad_vis, pairs, reg),
        grad_blocks,
        left_new,
        right_new,
        master_new,
        norm_grads,
        second_new,
        norm_new,
    )


def fits(mesh):
    return mesh.shape["dp"] == 8 and mesh.shape["seq"] == 4


def solution(mesh):
    placed = (
        P(("dp", "seq"), None),
        P(("dp", "seq"), None),
        P(("dp", "seq")),
        P(("dp", "seq"), None),
        P(("dp", "seq"), None),
        P("dp", None),
        P("dp", None),
        P("dp", None),
        P("dp", None),
        P("dp", None),
        P(),
        P(),
    )
    step = fast_shards if fits(mesh) else shards
    return jax.shard_map(
        step,
        mesh=mesh,
        in_specs=placed,
        out_specs=(
            P(("dp", "seq"), None),
            P(("dp", "seq"), None),
            P(("dp", "seq"), None),
            P(("dp", "seq"), None),
            P("dp", None),
            P("dp", None),
            P("dp", None),
            P("dp", None),
            P(),
            P(),
            P(),
        ),
        check_vma=False,
    )
```

```python
import functools

import jax
import jax.numpy as jnp
from jax import lax
from jax.experimental import pallas as pl
from jax.experimental.pallas import tpu as pltpu
from jax.sharding import PartitionSpec as P

TXT = 768
VIS = 1024
BI = 1024
FFT = 3072
FFV = 1024
HEAD = 128
HEAD_T = 64
HEAD_V = 128
BLK = 64


MASK_FILL = -1000000000.0
STAT_DECAY = 0.9
WEIGHT_RATE = 0.3
NORM_RATE = 0.2
NORM_EPSILON = 1e-05
MOMENT_EPSILON = 1e-08
HIGHEST = lax.Precision.HIGHEST
CONTRACT_COLS = (((1,), (1,)), ((), ()))


def weight_layout():
    return (
        (VIS, BI, 3),
        (BI, VIS, 1),
        (VIS, FFV, 1),
        (FFV, VIS, 1),
        (VIS, VIS, 3),
        (VIS, VIS, 1),
        (TXT, BI, 3),
        (BI, TXT, 1),
        (TXT, FFT, 1),
        (FFT, TXT, 1),
        (TXT, TXT, 3),
        (TXT, TXT, 1),
    )


def unpack_weights(flat):
    size = BLK
    blocks = flat.reshape(flat.shape[0], size, size)
    begin = 0
    matrices = []
    for rows, columns, count in weight_layout():
        number = count * rows * columns // (size * size)
        shaped = blocks[begin : begin + number].reshape(
            count, rows // size, columns // size, size, size
        )
        matrices.append(shaped.transpose(1, 3, 0, 2, 4).reshape(rows, count * columns))
        begin += number
    return matrices


def block_grad(inputs, grads, count):
    size = BLK
    left = inputs.reshape(inputs.shape[0], inputs.shape[1] // size, size)
    right = grads.reshape(grads.shape[0], count, grads.shape[1] // (count * size), size)
    return jnp.einsum("nai,nkbj->kabij", left, right, preferred_element_type=jnp.float32).reshape(
        -1, size * size
    )


def norm_columns(values, stream, which):
    if stream == 0:
        begin = which * VIS
        width = VIS
    else:
        begin = 3 * VIS + which * TXT
        width = TXT
    return values[:, begin : begin + width]


def gelu_exact(value):
    return jax.nn.gelu(value, approximate=False)


def heads_of(side, which, head):
    part = side[:, :, which, :]
    return part.reshape(part.shape[0], part.shape[1], part.shape[2] // head, head)


def scores_of(query, keys, live, head):
    scores = jnp.einsum(
        "gqhd,gkhd->ghqk", query, keys, preferred_element_type=jnp.float32
    ) * head ** (-0.5)
    if live is not None:
        scores = jnp.where(live[:, None, None, :], scores, MASK_FILL)
    return scores


def attend_one(query, keys, values, live, head):
    scores = scores_of(query, keys, live, head)
    top = jnp.max(scores, axis=3, keepdims=True)
    raised = jnp.exp(scores - top)
    total = jnp.sum(raised, axis=3, keepdims=True)
    found = jnp.einsum(
        "ghqk,gkhd->gqhd",
        (raised / total).astype(jnp.bfloat16),
        values,
        preferred_element_type=jnp.float32,
    ).astype(jnp.bfloat16)
    return (found.reshape(found.shape[0], found.shape[1], -1), top + jnp.log(total))


def attend_one_back(query, keys, values, live, head, logsum, dfound):
    scale = head ** (-0.5)
    probs = jnp.exp(scores_of(query, keys, live, head) - logsum)
    upstream = dfound.reshape(dfound.shape[0], dfound.shape[1], -1, head)
    dprobs = jnp.einsum("gqhd,gkhd->ghqk", upstream, values, preferred_element_type=jnp.float32)
    dvalues = jnp.einsum(
        "ghqk,gqhd->gkhd", probs.astype(jnp.bfloat16), upstream, preferred_element_type=jnp.float32
    )
    dscores = (probs * (dprobs - jnp.sum(probs * dprobs, axis=3, keepdims=True))).astype(
        jnp.bfloat16
    )
    dquery = (
        jnp.einsum("ghqk,gkhd->gqhd", dscores, keys, preferred_element_type=jnp.float32) * scale
    )
    dkeys = (
        jnp.einsum("ghqk,gqhd->gkhd", dscores, query, preferred_element_type=jnp.float32) * scale
    )
    return (dquery, dkeys, dvalues)


def attention_plan(vis_side, text_side, lengths, cross):
    live = (
        lax.broadcasted_iota(jnp.int32, (lengths.shape[0], text_side.shape[1]), 1)
        < lengths[:, None]
    )
    if cross:
        return ((vis_side, text_side, live, HEAD), (text_side, vis_side, None, HEAD))
    return ((vis_side, vis_side, None, HEAD_V), (text_side, text_side, live, HEAD_T))


def pair_attend(vis_side, text_side, lengths, cross):
    results = []
    for query_side, key_side, live, head in attention_plan(vis_side, text_side, lengths, cross):
        results.append(
            attend_one(
                heads_of(query_side, 0, head),
                heads_of(key_side, 1, head),
                heads_of(key_side, 2, head),
                live,
                head,
            )
        )
    return (results[0][0], results[1][0], results[0][1], results[1][1])


def pair_attend_back(
    vis_side, text_side, lengths, cross, vis_logsum, text_logsum, vis_dfound, text_dfound
):
    plan = attention_plan(vis_side, text_side, lengths, cross)
    parts = []
    for (query_side, key_side, live, head), logsum, dfound in zip(
        plan, (vis_logsum, text_logsum), (vis_dfound, text_dfound)
    ):
        parts.append(
            attend_one_back(
                heads_of(query_side, 0, head),
                heads_of(key_side, 1, head),
                heads_of(key_side, 2, head),
                live,
                head,
                logsum,
                dfound,
            )
        )
    if cross:
        vis_parts = (parts[0][0], parts[1][1], parts[1][2])
        text_parts = (parts[1][0], parts[0][1], parts[0][2])
    else:
        vis_parts = parts[0]
        text_parts = parts[1]
    vis_grad = jnp.stack(vis_parts, axis=2).reshape(vis_side.shape).astype(jnp.bfloat16)
    text_grad = jnp.stack(text_parts, axis=2).reshape(text_side.shape).astype(jnp.bfloat16)
    return (vis_grad, text_grad)


def to_heads(vis_side, text_side):
    return (vis_side, text_side)


def from_heads(vis_found, text_found):
    return (vis_found, text_found)


def dfound_to_heads(vis_dfound, text_dfound):
    return (vis_dfound, text_dfound)


def grads_from_heads(vis_grad, text_grad):
    return (vis_grad, text_grad)


def side_of(rows_in, weight, pairs):
    made = jnp.dot(rows_in, weight, preferred_element_type=jnp.float32).astype(jnp.bfloat16)
    return made.reshape(pairs, -1, 3, weight.shape[1] // 3)


def norm_forward(resid, columns):
    mean = jnp.mean(resid, -1, keepdims=True)
    centered = resid - mean
    scale = lax.rsqrt(jnp.mean(centered * centered, -1, keepdims=True) + NORM_EPSILON)
    normed = centered * scale
    return (normed, scale, normed * columns[0] + columns[1])


def norm_backward(upstream, normed, scale, gain):
    scaled = upstream * gain
    resid_grad = scale * (
        scaled
        - jnp.mean(scaled, -1, keepdims=True)
        - normed * jnp.mean(scaled * normed, -1, keepdims=True)
    )
    return (resid_grad, jnp.sum(upstream * normed, 0), jnp.sum(upstream, 0))


def stream_middle(context_rows, x_rows, weights, values, stream, pairs):
    resid = x_rows.astype(jnp.float32) + jnp.dot(
        context_rows, weights[1], preferred_element_type=jnp.float32
    )
    normed_one, scale_one, first = norm_forward(resid, norm_columns(values, stream, 0))
    first_low = first.astype(jnp.bfloat16)
    pre = jnp.dot(first_low, weights[2], preferred_element_type=jnp.float32)
    act = gelu_exact(pre).astype(jnp.bfloat16)
    resid = first + jnp.dot(act, weights[3], preferred_element_type=jnp.float32)
    normed_two, scale_two, second = norm_forward(resid, norm_columns(values, stream, 1))
    second_low = second.astype(jnp.bfloat16)
    side = side_of(second_low, weights[4], pairs)
    return (
        side,
        (normed_one, scale_one, first_low, pre, act, normed_two, scale_two, second, second_low),
    )


def stream_end(self_rows, second, out_weight, values, stream):
    resid = second + jnp.dot(self_rows, out_weight, preferred_element_type=jnp.float32)
    normed_three, scale_three, third = norm_forward(resid, norm_columns(values, stream, 2))
    return (third.astype(jnp.bfloat16), normed_three, scale_three)


def stream_back_end(
    cotangent, normed_three, scale_three, self_rows, out_weight, values, stream, pairs
):
    resid_three, gain_three, bias_three = norm_backward(
        cotangent.astype(jnp.float32), normed_three, scale_three, norm_columns(values, stream, 2)[0]
    )
    third_back = resid_three.astype(jnp.bfloat16)
    grad_self_out = block_grad(self_rows, third_back, 1)
    dself = lax.dot_general(
        third_back, out_weight, CONTRACT_COLS, preferred_element_type=jnp.float32
    )
    dself = dself.astype(jnp.bfloat16).reshape(pairs, -1, out_weight.shape[0])
    return (resid_three, dself, grad_self_out, gain_three, bias_three)


def stream_back_middle(resid_three, dself_side, kept, context_rows, weights, values, stream, pairs):
    normed_one, scale_one, first_low, pre, act, normed_two, scale_two, second, second_low = kept
    dself_rows = dself_side.reshape(-1, dself_side.shape[2] * dself_side.shape[3])
    grad_self_qkv = block_grad(second_low, dself_rows, 3)
    second_in = resid_three + lax.dot_general(
        dself_rows, weights[4], CONTRACT_COLS, preferred_element_type=jnp.float32
    )
    resid_two, gain_two, bias_two = norm_backward(
        second_in, normed_two, scale_two, norm_columns(values, stream, 1)[0]
    )
    branch_back = resid_two.astype(jnp.bfloat16)
    grad_down = block_grad(act, branch_back, 1)
    act_grad = lax.dot_general(
        branch_back, weights[3], CONTRACT_COLS, preferred_element_type=jnp.float32
    )
    pre_grad = jax.vjp(gelu_exact, pre)[1](act_grad)[0].astype(jnp.bfloat16)
    grad_up = block_grad(first_low, pre_grad, 1)
    first_in = resid_two + lax.dot_general(
        pre_grad, weights[2], CONTRACT_COLS, preferred_element_type=jnp.float32
    )
    resid_one, gain_one, bias_one = norm_backward(
        first_in, normed_one, scale_one, norm_columns(values, stream, 0)[0]
    )
    first_back = resid_one.astype(jnp.bfloat16)
    grad_co_out = block_grad(context_rows, first_back, 1)
    dcontext = lax.dot_general(
        first_back, weights[1], CONTRACT_COLS, preferred_element_type=jnp.float32
    )
    dcontext = dcontext.astype(jnp.bfloat16).reshape(pairs, -1, BI)
    return (
        resid_one,
        dcontext,
        (grad_co_out, grad_up, grad_down, grad_self_qkv),
        (gain_one, gain_two),
        (bias_one, bias_two),
    )


def shards(
    x_text,
    x_vis,
    caption_len,
    cot_text,
    cot_vis,
    master_blocks,
    stat_left,
    stat_right,
    root_left,
    root_right,
    norm_params,
    norm_second,
):
    pairs = caption_len.shape[0]
    width = master_blocks.shape[1] // lax.axis_size("seq")
    mine = lax.dynamic_slice_in_dim(master_blocks, lax.axis_index("seq") * width, width, 1).astype(
        jnp.bfloat16
    )
    partial_value = lax.all_gather(mine, "dp", axis=0, tiled=True)
    every = lax.all_gather(partial_value, "seq", axis=1, tiled=True)
    matrices = unpack_weights(every)
    vis_weights = matrices[:6]
    text_weights = matrices[6:]
    vis_co = side_of(x_vis, vis_weights[0], pairs)
    text_co = side_of(x_text, text_weights[0], pairs)
    lengths = caption_len
    vis_co_use, text_co_use = to_heads(vis_co, text_co)
    vis_found, text_found, vis_co_sum, text_co_sum = pair_attend(
        vis_co_use, text_co_use, lengths, True
    )
    vis_context, text_context = from_heads(vis_found, text_found)
    vis_context_rows = vis_context.reshape(-1, BI)
    text_context_rows = text_context.reshape(-1, BI)
    vis_self, vis_kept = stream_middle(vis_context_rows, x_vis, vis_weights, norm_params, 0, pairs)
    text_self, text_kept = stream_middle(
        text_context_rows, x_text, text_weights, norm_params, 1, pairs
    )
    vis_self_use, text_self_use = to_heads(vis_self, text_self)
    vis_found, text_found, vis_self_sum, text_self_sum = pair_attend(
        vis_self_use, text_self_use, lengths, False
    )
    vis_self_context, text_self_context = from_heads(vis_found, text_found)
    vis_self_rows = vis_self_context.reshape(-1, VIS)
    text_self_rows = text_self_context.reshape(-1, TXT)
    out_vis, vis_normed_three, vis_scale_three = stream_end(
        vis_self_rows, vis_kept[7], vis_weights[5], norm_params, 0
    )
    out_text, text_normed_three, text_scale_three = stream_end(
        text_self_rows, text_kept[7], text_weights[5], norm_params, 1
    )
    vis_resid_three, vis_dself, vis_grad_so, vis_gain_three, vis_bias_three = stream_back_end(
        cot_vis,
        vis_normed_three,
        vis_scale_three,
        vis_self_rows,
        vis_weights[5],
        norm_params,
        0,
        pairs,
    )
    text_resid_three, text_dself, text_grad_so, text_gain_three, text_bias_three = stream_back_end(
        cot_text,
        text_normed_three,
        text_scale_three,
        text_self_rows,
        text_weights[5],
        norm_params,
        1,
        pairs,
    )
    vis_dheads, text_dheads = dfound_to_heads(vis_dself, text_dself)
    vis_dgot, text_dgot = pair_attend_back(
        vis_self_use,
        text_self_use,
        lengths,
        False,
        vis_self_sum,
        text_self_sum,
        vis_dheads,
        text_dheads,
    )
    vis_dself_side, text_dself_side = grads_from_heads(vis_dgot, text_dgot)
    vis_resid_one, vis_dcontext, vis_grads_mid, vis_gains_mid, vis_biases_mid = stream_back_middle(
        vis_resid_three,
        vis_dself_side,
        vis_kept,
        vis_context_rows,
        vis_weights,
        norm_params,
        0,
        pairs,
    )
    text_resid_one, text_dcontext, text_grads_mid, text_gains_mid, text_biases_mid = (
        stream_back_middle(
            text_resid_three,
            text_dself_side,
            text_kept,
            text_context_rows,
            text_weights,
            norm_params,
            1,
            pairs,
        )
    )
    vis_dheads, text_dheads = dfound_to_heads(vis_dcontext, text_dcontext)
    vis_dgot, text_dgot = pair_attend_back(
        vis_co_use, text_co_use, lengths, True, vis_co_sum, text_co_sum, vis_dheads, text_dheads
    )
    vis_dco, text_dco = grads_from_heads(vis_dgot, text_dgot)
    vis_dco_rows = vis_dco.reshape(-1, 3 * BI)
    text_dco_rows = text_dco.reshape(-1, 3 * BI)
    grad_vis = vis_resid_one + lax.dot_general(
        vis_dco_rows, vis_weights[0], CONTRACT_COLS, preferred_element_type=jnp.float32
    )
    grad_text = text_resid_one + lax.dot_general(
        text_dco_rows, text_weights[0], CONTRACT_COLS, preferred_element_type=jnp.float32
    )
    vis_grad_co = block_grad(x_vis, vis_dco_rows, 3)
    text_grad_co = block_grad(x_text, text_dco_rows, 3)
    local_blocks = jnp.concatenate(
        [vis_grad_co]
        + list(vis_grads_mid)
        + [vis_grad_so]
        + [text_grad_co]
        + list(text_grads_mid)
        + [text_grad_so],
        0,
    )
    norm_local = jnp.stack(
        [
            jnp.concatenate(
                [
                    vis_gains_mid[0],
                    vis_gains_mid[1],
                    vis_gain_three,
                    text_gains_mid[0],
                    text_gains_mid[1],
                    text_gain_three,
                ]
            ),
            jnp.concatenate(
                [
                    vis_biases_mid[0],
                    vis_biases_mid[1],
                    vis_bias_three,
                    text_biases_mid[0],
                    text_biases_mid[1],
                    text_bias_three,
                ]
            ),
        ]
    )
    columns = lax.psum_scatter(
        local_blocks.astype(jnp.bfloat16), "seq", scatter_dimension=1, tiled=True
    ).astype(jnp.float32)
    owned_columns = lax.psum_scatter(columns, "dp", scatter_dimension=0, tiled=True)
    owned = lax.all_gather(owned_columns.astype(jnp.bfloat16), "seq", axis=1, tiled=True).astype(
        owned_columns.dtype
    )
    norm_grads = lax.psum(norm_local, ("dp", "seq"))
    number = owned.shape[0]
    grad_cube = owned.reshape(number, BLK, BLK)
    left_cube = stat_left.reshape(number, BLK, BLK)
    right_cube = stat_right.reshape(number, BLK, BLK)
    rootl_cube = root_left.reshape(number, BLK, BLK)
    rootr_cube = root_right.reshape(number, BLK, BLK)
    left_new = STAT_DECAY * left_cube + (1.0 - STAT_DECAY) * jnp.einsum(
        "bij,bkj->bik", grad_cube, grad_cube, precision=HIGHEST
    )
    right_new = STAT_DECAY * right_cube + (1.0 - STAT_DECAY) * jnp.einsum(
        "bji,bjk->bik", grad_cube, grad_cube, precision=HIGHEST
    )
    half = jnp.einsum("bij,bjk->bik", rootl_cube, grad_cube, precision=HIGHEST)
    direction = jnp.einsum("bij,bjk->bik", half, rootr_cube, precision=HIGHEST)
    master_new = master_blocks - WEIGHT_RATE * direction.reshape(number, BLK * BLK)
    second_new = STAT_DECAY * norm_second + (1.0 - STAT_DECAY) * norm_grads * norm_grads
    norm_new = norm_params - NORM_RATE * norm_grads / (jnp.sqrt(second_new) + MOMENT_EPSILON)
    return (
        out_text,
        out_vis,
        grad_text,
        grad_vis,
        owned,
        left_new.reshape(number, BLK * BLK),
        right_new.reshape(number, BLK * BLK),
        master_new,
        norm_grads,
        second_new,
        norm_new,
    )


SUB = 64
WIDE = 256
QUAD = 4
F32 = jnp.float32
BF16 = jnp.bfloat16
VIS_PAD = 48
VMEM_LIMIT = 60 * 1024 * 1024
NT = (((1,), (1,)), ((), ()))
TN = (((0,), (0,)), ((), ()))


def tile_table():
    begin = 0
    table = []
    for rows, columns, count in weight_layout():
        r, g = rows // SUB, columns // WIDE
        table.append((begin, count, r, g))
        begin += count * r * g
    return table


TILES = tile_table()
SHARD = 158
FAR = 62
G_HALF = 32
G_LONE = 8
R_LONE = 32
R_BOTH = 16
R_HALF = 2 * R_LONE + R_BOTH
CHUNKS = 2
SWAP_CORE = [(i, i ^ 1) for i in range(4)]
SWAP_Y = [(i, i ^ 2) for i in range(4)]
SWAP_X = [(i, i ^ 1) for i in range(8)]


def dot(left, right, how=None):
    if how is None:
        return jnp.dot(left, right, preferred_element_type=F32)
    return lax.dot_general(left, right, how, preferred_element_type=F32)


def params(**more):
    return pltpu.CompilerParams(vmem_limit_bytes=VMEM_LIMIT, **more)


def cost(micros):
    return pl.CostEstimate(flops=0, bytes_accessed=int(micros * 3.4e6), transcendentals=0)


def whole(count):
    return [pl.BlockSpec(memory_space=pltpu.VMEM)] * count


def linear(value):
    groups = value.shape[0] // 8
    return value.reshape(groups, 8, 32, 128).transpose(0, 2, 1, 3).reshape(groups * 256, 128)


def unlinear(value):
    groups = value.shape[0] // 256
    return value.reshape(groups, 32, 8, 128).transpose(0, 2, 1, 3).reshape(groups * 8, SUB * SUB)


def lanes_low(rows):
    return lax.broadcasted_iota(jnp.int32, (rows, 2 * SUB), 1) < SUB


def spread_of(ref, b):
    return ref[pl.ds(b, 32, stride=8), :]


def natural_order():
    row = lax.broadcasted_iota(jnp.int32, (SUB, SUB), 0)
    column = lax.broadcasted_iota(jnp.int32, (SUB, SUB), 1)
    return jnp.where(row == 2 * (column % 32) + column // 32, 1.0, 0.0).astype(BF16)


def prep_rows(number, pairs_ref, x_any, o_ref, rows_in, sems):
    def fetch(i):
        rows = pl.ds(pl.multiple_of(pairs_ref[i] * 256, 256), 256)
        return pltpu.make_async_copy(x_any.at[rows], rows_in.at[i], sems.at[i])

    for i in range(number):
        fetch(i).start()
    low = lanes_low(32)
    order = natural_order()

    def step(i, carry):
        fetch(i).wait()
        x_ref = rows_in.at[i]
        spots = range(4)
        one = [spread_of(x_ref, 2 * m) for m in spots]
        two = [spread_of(x_ref, 2 * m + 1) for m in spots]
        rows = [
            jnp.concatenate(
                [
                    jnp.where(low, one[m], pltpu.roll(two[m], SUB, 1)),
                    jnp.where(low, pltpu.roll(one[m], SUB, 1), two[m]),
                ],
                0,
            ).astype(BF16)
            for m in spots
        ]
        made = [dot(order, rows[m]).astype(BF16) for m in spots]
        for m in spots:
            o_ref[2 * i + m // 2, :, (m % 2) * 128 : (m % 2 + 1) * 128] = made[m]
        return carry

    lax.fori_loop(0, number, step, 0, unroll=2 if number % 2 == 0 else 3)


def prep(master_blocks, pairs):
    number = pairs.shape[0]
    return pl.pallas_call(
        functools.partial(prep_rows, number),
        in_specs=[pl.BlockSpec(memory_space=pltpu.SMEM), pl.BlockSpec(memory_space=pl.ANY)],
        out_specs=pl.BlockSpec(memory_space=pltpu.VMEM),
        out_shape=jax.ShapeDtypeStruct((number * 2, SUB, WIDE), BF16),
        scratch_shapes=[pltpu.VMEM((number, 256, 128), F32), pltpu.SemaphoreType.DMA((number,))],
        compiler_params=params(),
        cost_estimate=cost(0.4 * number),
    )(pairs, linear(master_blocks))


def renew_eight(g_ref, m_ref, sl_ref, sr_ref, rl_ref, rr_ref, go_ref, lo_ref, ro_ref, mo_ref, place):
    low = lanes_low(SUB)
    low_half = lanes_low(32)
    nothing = jnp.zeros((SUB, 128), F32)
    pairs = range(4)

    def diagonal(pair):
        return jnp.concatenate([jnp.where(low, pair, nothing), jnp.where(low, nothing, pair)], 0).astype(BF16)

    def mixed(even, odd):
        return (
            jnp.where(low_half, even, pltpu.roll(odd, SUB, 1)),
            jnp.where(low_half, pltpu.roll(even, SUB, 1), odd),
        )

    def natural(ref, pair, spot):
        even, odd = mixed(spread_of(ref, 2 * pair), spread_of(ref, 2 * pair + 1))
        spot[pl.ds(0, 32, stride=2), :] = even
        spot[pl.ds(1, 32, stride=2), :] = odd
        return spot[...]

    def spread(value, spot):
        spot[...] = value
        return mixed(spot[pl.ds(0, 32, stride=2), :], spot[pl.ds(1, 32, stride=2), :])

    tiles = [g_ref[pair // 2, :, (pair % 2) * 128 : (pair % 2 + 1) * 128] for pair in pairs]
    wide = [tile.astype(F32) for tile in tiles]
    grads = [diagonal(value) for value in wide]
    lefts = [natural(rl_ref, pair, place.at[pair, 0]).astype(BF16) for pair in pairs]
    rights = [diagonal(natural(rr_ref, pair, place.at[pair, 1])) for pair in pairs]
    halves = [dot(lefts[pair], grads[pair]).astype(BF16) for pair in pairs]
    left_parts = [dot(tiles[pair], grads[pair], NT) for pair in pairs]
    squares = [dot(tiles[pair], tiles[pair], TN) for pair in pairs]
    right_parts = [jnp.where(low, square[:SUB], square[SUB:]) for square in squares]
    steps = [dot(halves[pair], rights[pair]) for pair in pairs]
    for pair in pairs:
        made = [
            spread(value[pair], place.at[pair, 2 + k])
            for k, value in enumerate((wide, left_parts, right_parts, steps))
        ]
        for i in range(2):
            at = pl.ds(2 * pair + i, 32, stride=8)
            go_ref[at, :] = made[0][i]
            lo_ref[at, :] = STAT_DECAY * sl_ref[at, :] + (1.0 - STAT_DECAY) * made[1][i]
            ro_ref[at, :] = STAT_DECAY * sr_ref[at, :] + (1.0 - STAT_DECAY) * made[2][i]
            mo_ref[at, :] = m_ref[at, :] - WEIGHT_RATE * made[3][i]


SLOTS = 4


def renew_body(steps, which_ref, g_any, *refs):
    ins = refs[:5]
    outs = refs[-9:-5]
    gbuf, inbuf, outbuf, place, sems = refs[-5:]

    def rows(i):
        return pl.ds(pl.multiple_of(which_ref[i] * 256, 256), 256)

    def fetch(i):
        slot = lax.rem(i, SLOTS)
        copies = [pltpu.make_async_copy(g_any.at[pl.ds(2 * i, 2)], gbuf.at[slot], sems.at[slot, 0])]
        for k, ref in enumerate(ins):
            copies.append(
                pltpu.make_async_copy(ref.at[rows(i)], inbuf.at[slot, k], sems.at[slot, 1 + k])
            )
        return copies

    def put(i):
        slot = lax.rem(i, SLOTS)
        return [
            pltpu.make_async_copy(outbuf.at[slot, k], ref.at[rows(i)], sems.at[slot, 6 + k])
            for k, ref in enumerate(outs)
        ]

    def start(copies):
        for copy in copies:
            copy.start()

    def wait(copies):
        for copy in copies:
            copy.wait()

    for i in range(min(SLOTS, steps)):
        start(fetch(i))

    def step(i, carry):
        slot = lax.rem(i, SLOTS)
        wait(fetch(i))

        @pl.when(i >= SLOTS)
        def _():
            wait(put(i - SLOTS))

        renew_eight(
            gbuf.at[slot], *(inbuf.at[slot, k] for k in range(5)), *(outbuf.at[slot, k] for k in range(4)), place
        )
        start(put(i))

        @pl.when(i + SLOTS < steps)
        def _():
            start(fetch(i + SLOTS))

        return carry

    lax.fori_loop(0, steps, step, 0)
    for i in range(max(0, steps - SLOTS), steps):
        wait(put(i))


def renew(which, owned, master_blocks, stat_left, stat_right, root_left, root_right, before):
    steps = which.shape[0]
    shape = jax.ShapeDtypeStruct((master_blocks.shape[0] * 32, 128), F32)
    anywhere = pl.BlockSpec(memory_space=pl.ANY)
    made = pl.pallas_call(
        functools.partial(renew_body, steps),
        in_specs=[pl.BlockSpec(memory_space=pltpu.SMEM)] + [anywhere] * (6 + len(before)),
        out_specs=[anywhere] * 4,
        out_shape=[shape] * 4,
        scratch_shapes=[
            pltpu.VMEM((SLOTS, 2, SUB, WIDE), BF16),
            pltpu.VMEM((SLOTS, 5, 256, 128), F32),
            pltpu.VMEM((SLOTS, 4, 256, 128), F32),
            pltpu.VMEM((4, 6, SUB, 128), F32),
            pltpu.SemaphoreType.DMA((SLOTS, 10)),
        ],
        input_output_aliases={7 + i: i for i in range(len(before))},
        compiler_params=params(),
        cost_estimate=cost(0.7 * steps),
    )(
        which,
        owned,
        *(linear(value) for value in (master_blocks, stat_left, stat_right, root_left, root_right)),
        *(linear(value) for value in before),
    )
    return [unlinear(value) for value in made]


def times(rows_in, w, base, r, g, part, col):
    first = base + part * r * g + col
    return dot(rows_in, jnp.concatenate([w[first + a * g] for a in range(r)], 0))


def times_back(d_ref, w, base, r, g, count, r4):
    total = None
    for part in range(count):
        first = base + (part * r + 4 * r4) * g
        wide = jnp.concatenate(
            [
                jnp.concatenate([w[first + a * g + col] for a in range(4)], 0)
                for col in range(g)
            ],
            1,
        )
        made = dot(d_ref[:, part * g * WIDE : (part + 1) * g * WIDE], wide, NT)
        total = made if total is None else total + made
    return total


def at256(i):
    return pl.ds(pl.multiple_of(i * WIDE, WIDE), WIDE)


def softmax_all(products, scale, limits):
    scores = []
    for product, limit in zip(products, limits):
        column = lax.broadcasted_iota(jnp.int32, product.shape, 1)
        scores.append(jnp.where(column < limit, product * scale, MASK_FILL))
    tops = [jnp.max(score, 1, keepdims=True) for score in scores]
    raised = [jnp.exp(score - top) for score, top in zip(scores, tops)]
    shares = [1.0 / jnp.sum(value, 1, keepdims=True) for value in raised]
    return [value * share for value, share in zip(raised, shares)]


def score_grads(probs, dprobs):
    weighted = [p * d for p, d in zip(probs, dprobs)]
    totals = [jnp.sum(value, 1, keepdims=True) for value in weighted]
    return [(value - p * total).astype(BF16) for value, p, total in zip(weighted, probs, totals)]


def at128(i):
    return pl.ds(pl.multiple_of(i * 128, 128), 128)


def load(near, far, w, sems, pieces, base):
    started = []
    used = 0
    for i, which in enumerate(pieces):
        begin, count, r, g = TILES[which]
        end = begin + count * r * g
        copies = []
        for owner in range(begin // SHARD, (end - 1) // SHARD + 1):
            first = max(begin, owner * SHARD)
            last = min(end, (owner + 1) * SHARD)
            middle = min(max(owner * SHARD + FAR, first), last)
            for source, lo, hi, at in (
                (near, first, middle, owner * (2 * G_HALF) + first - owner * SHARD),
                (far, middle, last, owner * (SHARD - FAR) + middle - owner * SHARD - FAR),
            ):
                if lo < hi:
                    copies.append(
                        pltpu.make_async_copy(
                            source.at[pl.ds(at, hi - lo)],
                            w.at[pl.ds(base[i] + lo - begin, hi - lo)],
                            sems.at[used],
                        )
                    )
                    copies[-1].start()
                    used += 1
        started.append(copies)
    return started


def arrive(copies):
    for copy in copies:
        copy.wait()


def tiles_of(which):
    _, count, r, g = TILES[which]
    return count * r * g


def co_body(len_ref, xv_ref, xt_ref, near, far, cv_ref, ct_ref, fv_ref, ft_ref, w, sems):
    base = (0, tiles_of(0))
    copies = load(near, far, w, sems, (0, 6), base)
    for which, at, x_ref, o_ref, copy in (
        (0, base[0], xv_ref, cv_ref, copies[0]),
        (6, base[1], xt_ref, ct_ref, copies[1]),
    ):
        _, count, r, g = TILES[which]
        arrive(copy)

        def column(i, carry, at=at, r=r, g=g, x_ref=x_ref, o_ref=o_ref):
            o_ref[:, at256(i)] = times(x_ref[...], w, at, r, g, i // g, i % g).astype(BF16)
            return carry

        lax.fori_loop(0, count * g, column, 0, unroll=2)
    scale = HEAD ** (-0.5)
    reg = len_ref[2]
    heads = BI // HEAD
    vis = [slice(pair * VIS_PAD, (pair + 1) * VIS_PAD) for pair in range(2)]
    text = [slice(pair * 128, (pair + 1) * 128) for pair in range(2)]
    limits = [len_ref[0], len_ref[1], reg, reg]

    def head(j, carry):
        qv, kv, vv = ([cv_ref[rows, at128(j + heads * s)] for rows in vis] for s in range(3))
        qt, kt, vt = ([ct_ref[rows, at128(j + heads * s)] for rows in text] for s in range(3))
        probs = softmax_all([dot(q, k, NT) for q, k in zip(qv + qt, kt + kv)], scale, limits)
        found = [dot(p.astype(BF16), v).astype(BF16) for p, v in zip(probs, vt + vv)]
        for pair in range(2):
            fv_ref[vis[pair], at128(j)] = found[pair]
            ft_ref[text[pair], at128(j)] = found[2 + pair]
        return carry

    lax.fori_loop(0, heads, head, 0, unroll=2)


def co_forward(lengths, x_vis, x_text, near, far):
    return pl.pallas_call(
        co_body,
        in_specs=[pl.BlockSpec(memory_space=pltpu.SMEM)] + whole(2) + [pl.BlockSpec(memory_space=pl.ANY)] * 2,
        out_specs=whole(4),
        out_shape=[
            jax.ShapeDtypeStruct((x_vis.shape[0], 3 * BI), BF16),
            jax.ShapeDtypeStruct((x_text.shape[0], 3 * BI), BF16),
            jax.ShapeDtypeStruct((x_vis.shape[0], BI), BF16),
            jax.ShapeDtypeStruct((x_text.shape[0], BI), BF16),
        ],
        scratch_shapes=[
            pltpu.VMEM((tiles_of(0) + tiles_of(6), SUB, WIDE), BF16),
            pltpu.SemaphoreType.DMA((16,)),
        ],
        compiler_params=params(),
        cost_estimate=cost(22),
    )(lengths, x_vis, x_text, near, far)


def co_back_body(
    len_ref, cv_ref, ct_ref, dv_ref, dt_ref, rv_ref, rt_ref, near, far,
    gv_ref, gt_ref, ov_ref, ot_ref, w, sems,
):
    base = (0, tiles_of(0))
    copies = load(near, far, w, sems, (0, 6), base)
    scale = HEAD ** (-0.5)
    reg = len_ref[2]
    heads = BI // HEAD
    vis = [slice(pair * VIS_PAD, (pair + 1) * VIS_PAD) for pair in range(2)]
    text = [slice(pair * 128, (pair + 1) * 128) for pair in range(2)]
    limits = [len_ref[0], len_ref[1], reg, reg]

    def head(j, carry):
        qv, kv, vv = ([cv_ref[rows, at128(j + heads * s)] for rows in vis] for s in range(3))
        qt, kt, vt = ([ct_ref[rows, at128(j + heads * s)] for rows in text] for s in range(3))
        up = [dv_ref[rows, at128(j)] for rows in vis] + [dt_ref[rows, at128(j)] for rows in text]
        queries, keys, values = qv + qt, kt + kv, vt + vv
        products = [dot(q, k, NT) for q, k in zip(queries, keys)]
        dprobs = [dot(u, v, NT) for u, v in zip(up, values)]
        probs = softmax_all(products, scale, limits)
        ds = score_grads(probs, dprobs)
        dvalues = [dot(p.astype(BF16), u, TN).astype(BF16) for p, u in zip(probs, up)]
        dqueries = [(dot(d, k) * scale).astype(BF16) for d, k in zip(ds, keys)]
        dkeys = [(dot(d, q, TN) * scale).astype(BF16) for d, q in zip(ds, queries)]
        for pair in range(2):
            gv_ref[vis[pair], at128(j)] = dqueries[pair]
            gt_ref[text[pair], at128(j + heads)] = dkeys[pair]
            gt_ref[text[pair], at128(j + 2 * heads)] = dvalues[pair]
            gt_ref[text[pair], at128(j)] = dqueries[2 + pair]
            gv_ref[vis[pair], at128(j + heads)] = dkeys[2 + pair]
            gv_ref[vis[pair], at128(j + 2 * heads)] = dvalues[2 + pair]
        return carry

    lax.fori_loop(0, heads, head, 0, unroll=2)
    for which, at, g_ref, r_ref, o_ref, copy in (
        (0, base[0], gv_ref, rv_ref, ov_ref, copies[0]),
        (6, base[1], gt_ref, rt_ref, ot_ref, copies[1]),
    ):
        _, count, r, g = TILES[which]
        arrive(copy)

        def rows4(i, carry, at=at, r=r, g=g, count=count, g_ref=g_ref, r_ref=r_ref, o_ref=o_ref):
            o_ref[:, at256(i)] = r_ref[:, at256(i)] + times_back(g_ref, w, at, r, g, count, i)
            return carry

        lax.fori_loop(0, r // 4, rows4, 0)


def co_backward(lengths, co_vis, co_text, dvis, dtext, resid_vis, resid_text, near, far):
    return pl.pallas_call(
        co_back_body,
        in_specs=[pl.BlockSpec(memory_space=pltpu.SMEM)] + whole(6) + [pl.BlockSpec(memory_space=pl.ANY)] * 2,
        out_specs=whole(4),
        out_shape=[
            jax.ShapeDtypeStruct(co_vis.shape, BF16),
            jax.ShapeDtypeStruct(co_text.shape, BF16),
            jax.ShapeDtypeStruct(resid_vis.shape, F32),
            jax.ShapeDtypeStruct(resid_text.shape, F32),
        ],
        scratch_shapes=[
            pltpu.VMEM((tiles_of(0) + tiles_of(6), SUB, WIDE), BF16),
            pltpu.SemaphoreType.DMA((16,)),
        ],
        compiler_params=params(),
        cost_estimate=cost(23),
    )(lengths, co_vis, co_text, dvis, dtext, resid_vis, resid_text, near, far)


def erf_parts(value):
    return 0.5 * (1.0 + lax.erf(value * 0.7071067811865476))


def middle_body(
    config,
    len_ref, ctx_ref, x_ref, cot_ref, norm_ref, near, far,
    out_ref, first_ref, act_ref, second_ref, sctx_ref,
    fback_ref, pback_ref, bback_ref, dself_ref, tback_ref,
    resid_ref, dctx_ref, sums_ref,
    w, sems, pre, n1, n2, n3, s1, s2, s3, wide, acc, selfs, probs, stat,
):
    begin, rows, span, head, chunk = config
    width = x_ref.shape[1]
    base = []
    at = 0
    for which in range(begin, begin + 5):
        base.append(at)
        at += tiles_of(which)
    copies = load(near, far, w, sems, tuple(range(begin, begin + 5)), base)
    shapes = [TILES[which][1:] for which in range(begin, begin + 5)]
    steps = rows // chunk

    def at_chunk(i):
        return pl.ds(pl.multiple_of(i * chunk, chunk), chunk)

    def norm(resid, which, i, kept, scales):
        mean = jnp.mean(resid, 1, keepdims=True)
        centered = resid - mean
        scale = lax.rsqrt(jnp.mean(centered * centered, 1, keepdims=True) + NORM_EPSILON)
        normed = centered * scale
        kept[at_chunk(i), :] = normed
        scales[at_chunk(i), :] = jnp.broadcast_to(scale, (chunk, 128))
        return normed * norm_ref[0, which : which + 1, :] + norm_ref[1, which : which + 1, :]

    def eight(value):
        return jnp.sum(value.reshape(chunk // 8, 8, width), 0)

    def norm_back(upstream, which, i, kept, scales):
        normed = kept[at_chunk(i), :]
        stat[which] = stat[which] + eight(upstream * normed)
        stat[3 + which] = stat[3 + which] + eight(upstream)
        scaled = upstream * norm_ref[0, which : which + 1, :]
        return scales[at_chunk(i), 0:1] * (
            scaled
            - jnp.mean(scaled, 1, keepdims=True)
            - normed * jnp.mean(scaled * normed, 1, keepdims=True)
        )

    def loop(count, body, unroll=1):
        lax.fori_loop(0, count, lambda i, carry: (body(i), carry)[1], 0, unroll=unroll)

    stat[...] = jnp.zeros(stat.shape, F32)
    count, r, g = shapes[0]
    arrive(copies[0])

    def co_out(i):
        wide[:, at256(i)] = times(ctx_ref[...], w, base[0], r, g, 0, i)

    loop(g, co_out, g)

    def norm_one(i):
        value = norm(wide[at_chunk(i), :] + x_ref[at_chunk(i), :].astype(F32), 0, i, n1, s1)
        wide[at_chunk(i), :] = value
        first_ref[at_chunk(i), :] = value.astype(BF16)

    loop(steps, norm_one, 2 if steps % 2 == 0 else steps)
    _, r_up, g_up = shapes[1]
    _, r_down, g_down = shapes[2]
    arrive(copies[1])
    arrive(copies[2])
    acc[...] = jnp.zeros(acc.shape, F32)

    def down_rows(i):
        return jnp.concatenate(
            [
                jnp.concatenate([w[base[2] + (4 * i + a) * g_down + col] for a in range(4)], 0)
                for col in range(g_down)
            ],
            1,
        )

    def feed(i):
        value = times(first_ref[...], w, base[1], r_up, g_up, 0, i)
        part = erf_parts(value)
        pre[i] = part + value * (0.3989422804014327 * jnp.exp(-0.5 * value * value))
        act = (value * part).astype(BF16)
        act_ref[:, at256(i)] = act
        acc[...] += dot(act, down_rows(i))

    loop(g_up, feed, 4)

    def norm_two(i):
        value = norm(wide[at_chunk(i), :] + acc[at_chunk(i), :], 1, i, n2, s2)
        wide[at_chunk(i), :] = value
        second_ref[at_chunk(i), :] = value.astype(BF16)

    loop(steps, norm_two, 2 if steps % 2 == 0 else steps)
    count_s, r_s, g_s = shapes[3]
    arrive(copies[3])

    def self_in(i):
        selfs[:, at256(i)] = times(second_ref[...], w, base[3], r_s, g_s, i // g_s, i % g_s).astype(BF16)

    loop(count_s * g_s, self_in, g_s)
    scale = head ** (-0.5)
    groups = width // 128
    per = 128 // head
    pairs = rows // span

    def halves(values):
        if per == 1:
            return values[0]
        low = lax.broadcasted_iota(jnp.int32, values[0].shape, 1) < head
        return jnp.where(low, values[0], values[1])

    def only(value, h):
        if per == 1:
            return value
        low = lax.broadcasted_iota(jnp.int32, value.shape, 1) < head
        keep = low if h == 0 else jnp.logical_not(low)
        return jnp.where(keep, value, jnp.zeros_like(value))

    own = [slice(pair * span, (pair + 1) * span) for pair in range(pairs)]
    each = [(pair, h) for pair in range(pairs) for h in range(per)]

    def attend(j):
        q, k, v = ([selfs[rows_of, at128(j + groups * s)] for rows_of in own] for s in range(3))
        products = [dot(only(q[pair], h), k[pair], NT) for pair, h in each]
        p = softmax_all(products, scale, [len_ref[pair] for pair, _ in each])
        found = [dot(value.astype(BF16), v[pair]) for value, (pair, _) in zip(p, each)]
        for i, value in enumerate(p):
            probs[j * len(each) + i] = value
        for pair in range(pairs):
            sctx_ref[own[pair], at128(j)] = halves(found[pair * per : (pair + 1) * per]).astype(BF16)

    loop(groups, attend, 2)
    _, r_o, g_o = shapes[4]
    arrive(copies[4])

    def self_out(i):
        acc[:, at256(i)] = times(sctx_ref[...], w, base[4], r_o, g_o, 0, i)

    loop(g_o, self_out, g_o)

    def norm_three(i):
        value = norm(wide[at_chunk(i), :] + acc[at_chunk(i), :], 2, i, n3, s3)
        out_ref[at_chunk(i), :] = value.astype(BF16)
        third = norm_back(cot_ref[at_chunk(i), :].astype(F32), 2, i, n3, s3)
        wide[at_chunk(i), :] = third
        tback_ref[at_chunk(i), :] = third.astype(BF16)

    loop(steps, norm_three, 2 if steps % 2 == 0 else steps)

    def self_out_back(i):
        dctx_ref[:, at256(i)] = times_back(tback_ref, w, base[4], r_o, g_o, 1, i).astype(BF16)

    loop(r_o // 4, self_out_back, r_o // 4)
    def attend_back(j):
        q, k, v = ([selfs[rows_of, at128(j + groups * s)] for rows_of in own] for s in range(3))
        up = [dctx_ref[rows_of, at128(j)] for rows_of in own]
        p = [probs[j * len(each) + i] for i in range(len(each))]
        dprobs = [dot(only(up[pair], h), v[pair], NT) for pair, h in each]
        dv = [dot(value.astype(BF16), up[pair], TN) for value, (pair, _) in zip(p, each)]
        ds = score_grads(p, dprobs)
        dq = [dot(value, k[pair]) for value, (pair, _) in zip(ds, each)]
        dk = [dot(value, q[pair], TN) for value, (pair, _) in zip(ds, each)]
        for pair in range(pairs):
            mine = slice(pair * per, (pair + 1) * per)
            dself_ref[own[pair], at128(j)] = (halves(dq[mine]) * scale).astype(BF16)
            dself_ref[own[pair], at128(j + groups)] = (halves(dk[mine]) * scale).astype(BF16)
            dself_ref[own[pair], at128(j + 2 * groups)] = halves(dv[mine]).astype(BF16)

    loop(groups, attend_back, 2)

    def self_in_back(i):
        acc[:, at256(i)] = times_back(dself_ref, w, base[3], r_s, g_s, count_s, i)

    loop(r_s // 4, self_in_back, r_s // 4)

    def norm_two_back(i):
        value = norm_back(wide[at_chunk(i), :] + acc[at_chunk(i), :], 1, i, n2, s2)
        wide[at_chunk(i), :] = value
        bback_ref[at_chunk(i), :] = value.astype(BF16)

    loop(steps, norm_two_back, 2 if steps % 2 == 0 else steps)

    def feed_back(i):
        act_grad = dot(bback_ref[...], down_rows(i), NT)
        pback_ref[:, at256(i)] = (act_grad * pre[i]).astype(BF16)

    loop(g_up, feed_back, 4)

    def up_back(i):
        acc[:, at256(i)] = times_back(pback_ref, w, base[1], r_up, g_up, 1, i)

    loop(r_up // 4, up_back, r_up // 4)

    def norm_one_back(i):
        value = norm_back(wide[at_chunk(i), :] + acc[at_chunk(i), :], 0, i, n1, s1)
        resid_ref[at_chunk(i), :] = value
        fback_ref[at_chunk(i), :] = value.astype(BF16)

    loop(steps, norm_one_back, 2 if steps % 2 == 0 else steps)

    def co_out_back(i):
        dctx_ref[:, at256(i)] = times_back(fback_ref, w, base[0], r, g, 1, i).astype(BF16)

    loop(r // 4, co_out_back, r // 4)
    sums_ref[...] = jnp.sum(stat[...], 1)


def middle(begin, lengths, context, x, cot, norms, near, far, span, head, chunk):
    rows, width = x.shape
    hidden = TILES[begin + 1][3] * WIDE
    number = sum(tiles_of(which) for which in range(begin, begin + 5))
    low = lambda columns: jax.ShapeDtypeStruct((rows, columns), BF16)
    return pl.pallas_call(
        functools.partial(middle_body, (begin, rows, span, head, chunk)),
        in_specs=[pl.BlockSpec(memory_space=pltpu.SMEM)] + whole(4) + [pl.BlockSpec(memory_space=pl.ANY)] * 2,
        out_specs=whole(13),
        out_shape=[
            low(width), low(width), low(hidden), low(width), low(width),
            low(width), low(hidden), low(width), low(3 * width), low(width),
            jax.ShapeDtypeStruct((rows, width), F32), low(BI),
            jax.ShapeDtypeStruct((6, width), F32),
        ],
        scratch_shapes=[
            pltpu.VMEM((number, SUB, WIDE), BF16),
            pltpu.SemaphoreType.DMA((24,)),
            pltpu.VMEM((hidden // WIDE, rows, WIDE), F32),
        ]
        + [pltpu.VMEM((rows, width), F32)] * 3
        + [pltpu.VMEM((rows, 128), F32)] * 3
        + [pltpu.VMEM((rows, width), F32)] * 2
        + [
            pltpu.VMEM((rows, 3 * width), BF16),
            pltpu.VMEM((rows // span * (width // head), span, span), F32),
            pltpu.VMEM((6, 8, width), F32),
        ],
        compiler_params=params(),
        cost_estimate=cost(40),
    )(lengths, context, x, cot, norms, near, far)


def weight_body(kinds, *refs):
    n = len(kinds)
    lefts, rights = refs[:n], refs[n : 2 * n]
    out, stage, across, sems = refs[2 * n :]
    offset = 0
    for which, a_ref, b_ref in zip(kinds, lefts, rights):
        _, count, r, g = TILES[which]
        size = 4 * g

        def copy(i, slot, offset=offset, size=size):
            return pltpu.make_async_copy(
                stage.at[slot, pl.ds(0, size)], out.at[pl.ds(offset + i * size, size)], sems.at[slot]
            )

        total = count * (r // 4)

        def step(i, carry, a_ref=a_ref, b_ref=b_ref, r=r, g=g, copy=copy):
            slot = lax.rem(i, 4)

            @pl.when(i >= 4)
            def _():
                copy(i - 4, slot).wait()

            part = i // (r // 4)
            r4 = lax.rem(i, r // 4)
            across[...] = jnp.transpose(a_ref[:, at256(r4)])
            left = across[...]
            for first in range(0, g, 4 if g % 4 == 0 else 3):
                columns = range(first, first + (4 if g % 4 == 0 else 3))
                made = [dot(left, b_ref[:, at256(part * g + col)]).astype(BF16) for col in columns]
                for col, value in zip(columns, made):
                    for a in range(4):
                        stage[slot, a * g + col] = value[a * SUB : (a + 1) * SUB]
            copy(i, slot).start()
            return carry

        lax.fori_loop(0, total, step, 0, unroll=2 if total % 2 == 0 else 3)
        for i in range(max(0, total - 4), total):
            copy(i, i % 4).wait()
        offset += count * r * g


def weight_grads(kinds, lefts, rights):
    number = sum(tiles_of(which) for which in kinds)
    most = max(4 * TILES[which][3] for which in kinds)
    return pl.pallas_call(
        functools.partial(weight_body, kinds),
        in_specs=whole(2 * len(kinds)),
        out_specs=pl.BlockSpec(memory_space=pl.ANY),
        out_shape=jax.ShapeDtypeStruct((number, SUB, WIDE), BF16),
        scratch_shapes=[
            pltpu.VMEM((4, most, SUB, WIDE), BF16),
            pltpu.VMEM((WIDE, lefts[0].shape[0]), BF16),
            pltpu.SemaphoreType.DMA((4,)),
        ],
        compiler_params=params(),
        cost_estimate=cost(number * 0.04),
    )(*lefts, *rights)


def spot():
    dp = lax.axis_index("dp")
    seq = lax.axis_index("seq")
    return dp // 2, dp % 2, seq // 2, seq % 2


def along_z(value, moves):
    return lax.ppermute(value, "dp", [(2 * a + x, 2 * b + x) for a, b in moves for x in (0, 1)])


def cut(value, begin, size):
    return lax.dynamic_slice_in_dim(value, begin, size, 0)


def join(parts):
    return jnp.concatenate(parts) if len(parts) > 1 else parts[0]


def add(left, right):
    return (left.astype(F32) + right.astype(F32)).astype(BF16)


def by_y(y, mine, other):
    return [jnp.where(y == 0, mine, other), jnp.where(y == 0, other, mine)]


def blank(shape):
    return pl.pallas_call(
        lambda out: None,
        out_specs=pl.BlockSpec(memory_space=pl.ANY),
        out_shape=jax.ShapeDtypeStruct(shape, BF16),
        compiler_params=params(),
    )()


def gather_tiles(master_blocks, others):
    z, x, y, core = spot()
    lone, both, half = G_LONE // 2, (G_HALF - 2 * G_LONE) // 2, G_HALF // 2
    fourth = (SHARD - FAR) // 4
    mine = prep(
        master_blocks,
        jnp.concatenate(
            [half * core + lone * y + jnp.arange(lone), half * core + 2 * lone + jnp.arange(both)]
        ).astype(jnp.int32),
    )
    last = prep(
        master_blocks,
        ((FAR + fourth * lax.axis_index("seq")) // 2 + jnp.arange(fourth // 2)).astype(jnp.int32),
    )
    far = lax.all_gather(last, ("dp", "seq"), axis=0, tiled=True)
    ring = [(0, 1), (1, 2), (2, 3), (3, 0)]
    near = blank((8, 2 * G_HALF, SUB, WIDE))
    rows = [mine]
    cross = []
    halves = []
    for phase in range(6):
        out = {}
        if phase < 3:
            out["z"] = along_z(rows[phase], ring)
        if phase < 4:
            out["x"] = lax.ppermute(rows[phase], "dp", SWAP_X)
        if 1 <= phase < 5:
            here = [rows[phase - 1], cross[phase - 1]]
            out["y"] = lax.ppermute(join([part[:G_LONE] for part in here]), "seq", SWAP_Y)
        if phase >= 2:
            out["core"] = lax.ppermute(join(halves[phase - 2]), "seq", SWAP_CORE)
        out, rows, cross, halves, near, others = lax.optimization_barrier(
            (out, rows, cross, halves, near, others)
        )
        if "z" in out:
            rows = rows + [out["z"]]
        if "x" in out:
            cross = cross + [out["x"]]
        if "y" in out:
            halves = halves + [
                [
                    join(by_y(y, part[:G_LONE], out["y"][G_LONE * i : G_LONE * (i + 1)]) + [part[G_LONE:]])
                    for i, part in enumerate(here)
                ]
            ]
        if "core" in out:
            step = phase - 2
            for side in range(2):
                owner = 2 * ((z - step) % 4) + (x + side) % 2
                own = halves[step][side][None]
                got = out["core"][None, G_HALF * side : G_HALF * (side + 1)]
                near = lax.dynamic_update_slice(near, own, (owner, G_HALF * core, 0, 0))
                near = lax.dynamic_update_slice(near, got, (owner, G_HALF * (1 - core), 0, 0))
    return near.reshape(-1, SUB, WIDE), far, others


ROUTES = (
    (((3, 2),), ((2, 1),), ((1, 0),)),
    (((3, 2), (0, 1)), ((2, 1),)),
    (((0, 1), (3, 2)), ((1, 2),)),
    (((0, 1),), ((1, 2),), ((2, 3),)),
)
LONE = R_LONE // CHUNKS
BOTH = R_BOTH // CHUNKS
GROUP_ORDER = [[0, 2, 1, 3]]


def lone_at(core):
    return 2 * R_LONE * core


def both_at(core):
    return 4 * R_LONE + (SHARD - 4 * R_LONE - R_BOTH) * core


def chunk_pairs(k):
    table = []
    for core in range(2):
        for y in range(2):
            table += [(lone_at(core) + R_LONE * y + LONE * k) // 2 + i for i in range(LONE // 2)]
        table += [(both_at(core) + BOTH * k) // 2 + i for i in range(BOTH // 2)]
    return jnp.asarray(table, jnp.int32)


def pieces_of(owner, ranges, begins):
    pieces = []
    at = 0
    for begin, size in ranges:
        first, last = SHARD * owner + begin, SHARD * owner + begin + size
        for which, (lo, hi) in enumerate(begins):
            start, end = max(first, lo), min(last, hi)
            if start < end:
                pieces.append((which, start - lo, end - start, at + start - first))
        at += size
    return pieces


def half_plan(owner, begins, other):
    return [
        pieces_of(owner, ((lone_at(core ^ other), 2 * R_LONE), (both_at(core ^ other), R_BOTH)), begins)
        for core in range(2)
    ]


def both_plan(owner, begins, other):
    plan = []
    for core in range(2):
        pieces = []
        for i in range(2):
            for which, begin, size, at in pieces_of(owner + i, ((both_at(core ^ other), R_BOTH),), begins):
                pieces.append((which, begin, size, at + R_BOTH * i))
        plan.append(pieces)
    return plan


def follow(core_ref, plans, arrays, outs, sems):
    for core in range(2):

        @pl.when(core_ref[0] == core)
        def _(core=core):
            copies = []
            for j, plan in enumerate(plans):
                for i, (which, begin, size, at) in enumerate(plan[core]):
                    copies.append(
                        pltpu.make_async_copy(
                            arrays[which].at[pl.ds(begin, size)], outs[j].at[pl.ds(at, size)], sems.at[j, i]
                        )
                    )
            for copy in copies:
                copy.start()
            for copy in copies:
                copy.wait()


def pick_body(plans, number, core_ref, *refs):
    follow(core_ref, plans, refs[:number], refs[number:-1], refs[-1])


def pick(core, sources, plans, sizes):
    arrays = [array for _, array in sources]
    return pl.pallas_call(
        functools.partial(pick_body, plans, len(arrays)),
        in_specs=[pl.BlockSpec(memory_space=pltpu.SMEM)] + [pl.BlockSpec(memory_space=pl.ANY)] * len(arrays),
        out_specs=whole(len(plans)),
        out_shape=[jax.ShapeDtypeStruct((size, SUB, WIDE), BF16) for size in sizes],
        scratch_shapes=[pltpu.SemaphoreType.DMA((len(plans), 6))],
        compiler_params=params(),
        cost_estimate=cost(2 * len(plans)),
    )(core.reshape(1), *arrays)


def begins_of(sources):
    return [(begin, begin + array.shape[0]) for begin, array in sources]


def merge_body(plans, number, core_ref, *refs):
    arrays, got = refs[:number], refs[number : number + 2]
    outs = refs[number + 2 : -2]
    own, sems = refs[-2:]
    follow(core_ref, plans, arrays, [own.at[0], own.at[1]], sems)

    def total(out, size, i, begin):
        def tile(t, carry):
            out[t] = add(own[i, begin + t], got[i][begin + t])
            return carry

        lax.fori_loop(0, size, tile, 0, unroll=4)

    for k in range(CHUNKS):
        for i in range(2):
            for y in range(2):
                total(outs[2 * k].at[y, i], LONE, i, R_LONE * y + LONE * k)
            total(outs[2 * k + 1].at[i], BOTH, i, 2 * R_LONE + BOTH * k)


def merge(core, sources, zi, got, chunks):
    arrays = [array for _, array in sources]
    plans = [half_plan(2 * zi + i, begins_of(sources), 0) for i in range(2)]
    shapes = []
    for _ in range(CHUNKS):
        shapes += [(2, 2, LONE, SUB, WIDE), (2, BOTH, SUB, WIDE)]
    made = pl.pallas_call(
        functools.partial(merge_body, plans, len(arrays)),
        in_specs=[pl.BlockSpec(memory_space=pltpu.SMEM)]
        + [pl.BlockSpec(memory_space=pl.ANY)] * len(arrays)
        + whole(2),
        out_specs=whole(len(shapes)),
        out_shape=[jax.ShapeDtypeStruct(shape, BF16) for shape in shapes],
        scratch_shapes=[
            pltpu.VMEM((2, R_HALF, SUB, WIDE), BF16),
            pltpu.SemaphoreType.DMA((2, 6)),
        ],
        compiler_params=params(),
        cost_estimate=cost(8),
    )(core.reshape(1), *arrays, *got)
    for k, chunk in enumerate(chunks):
        chunk.state["lone", zi], chunk.state["both", zi] = made[2 * k : 2 * k + 2]


def arrange_body(pieces, x_any, o_any, held, sems):
    arrivals = []
    at = 0
    for i, (begin, size) in enumerate(pieces):
        spot_of = pl.ds(at, size)
        arrivals.append(
            (
                pltpu.make_async_copy(x_any.at[pl.ds(begin, size)], held.at[spot_of], sems.at[0, i]),
                pltpu.make_async_copy(held.at[spot_of], o_any.at[spot_of], sems.at[1, i]),
            )
        )
        arrivals[-1][0].start()
        at += size
    for came, goes in arrivals:
        came.wait()
        goes.start()
    for _, goes in arrivals:
        goes.wait()


def arrange(array, pieces):
    number = sum(size for _, size in pieces)
    return pl.pallas_call(
        functools.partial(arrange_body, pieces),
        in_specs=[pl.BlockSpec(memory_space=pl.ANY)],
        out_specs=pl.BlockSpec(memory_space=pl.ANY),
        out_shape=jax.ShapeDtypeStruct((number, SUB, WIDE), BF16),
        scratch_shapes=[
            pltpu.VMEM((number, SUB, WIDE), BF16),
            pltpu.SemaphoreType.DMA((2, len(pieces))),
        ],
        compiler_params=params(),
        cost_estimate=cost(6),
    )(array)


def group_lone(array, offset):
    pieces = tuple(
        (offset + SHARD * o + R_LONE * part, R_LONE) for part in range(4) for o in range(2)
    )
    made = lax.psum_scatter(
        arrange(array, pieces), "seq", scatter_dimension=0, tiled=True, axis_index_groups=GROUP_ORDER
    )
    return made.reshape(2, R_LONE, SUB, WIDE)


def chunks_of(lone, both):
    return [
        (lone[:, LONE * k : LONE * (k + 1)], both[:, BOTH * k : BOTH * (k + 1)]) for k in range(CHUNKS)
    ]


class Sums:
    def __init__(self):
        self.at = spot()
        self.state = {}

    def send(self, task):
        z, x, y, core = self.at
        state = self.state
        kind, who = task[0], task[1]
        if kind == "Y":
            return lax.ppermute(cut(state["lone", who], 1 - y, 1)[0], "seq", SWAP_Y)
        if kind == "X":
            lone, both = state["kept", who]
            return lax.ppermute(join([cut(lone, 1 - x, 1)[0], cut(both, 1 - x, 1)[0]]), "dp", SWAP_X)
        if kind == "Z":
            return along_z(state["value", who], ROUTES[who][task[2]])
        if kind == "F":
            values = [state["value", zi] for zi in range(4)]
            mine = jnp.where(z == 0, values[0], jnp.where(z == 1, values[1], jnp.where(z == 2, values[2], values[3])))
            state["mine", 0] = mine
            return lax.ppermute(mine, "seq", SWAP_Y)
        if kind == "G":
            return lax.ppermute(state["whole", 0], "seq", SWAP_CORE)
        axis, step = (("seq", 1), ("seq", 2), ("dp", 1), ("dp", 2), ("dp", 4))[who]
        size = lax.axis_size(axis)
        return lax.ppermute(state["norms", 0], axis, [(i, i ^ step) for i in range(size)])

    def take(self, task, got):
        z, x, y, core = self.at
        state = self.state
        kind, who = task[0], task[1]
        if kind == "Y":
            state["kept", who] = (add(cut(state.pop(("lone", who)), y, 1)[0], got), state.pop(("both", who)))
        elif kind == "X":
            lone, both = state.pop(("kept", who))
            state["value", who] = add(join([cut(lone, x, 1)[0], cut(both, x, 1)[0]]), got)
        elif kind == "Z":
            state["value", who] = add(state["value", who], got)
        elif kind == "F":
            mine = state.pop(("mine", 0))
            state["whole", 0] = join(by_y(y, mine[:LONE], got[:LONE]) + [add(mine[LONE:], got[LONE:])])
        elif kind == "G":
            half = state.pop(("whole", 0))
            state["owned", 0] = join([jnp.where(core == 0, half, got), jnp.where(core == 0, got, half)])
        else:
            state["norms", 0] = state["norms", 0] + got

    def step(self, tasks):
        out = [self.send(task) for task in tasks]
        out, self.state = lax.optimization_barrier((out, self.state))
        for task, got in zip(tasks, out):
            self.take(task, got)


def beside(chunks, tasks, work):
    out = [chunks[k].send(task) for k, task in tasks]
    made = work()
    out, made, states = lax.optimization_barrier((out, made, [chunk.state for chunk in chunks]))
    for chunk, state in zip(chunks, states):
        chunk.state = state
    for (k, task), got in zip(tasks, out):
        chunks[k].take(task, got)
    return made


def pad_regions(value, pairs):
    reg = value.shape[0] // pairs
    cube = value.reshape(pairs, reg, value.shape[1])
    return jnp.pad(cube, ((0, 0), (0, VIS_PAD - reg), (0, 0))).reshape(pairs * VIS_PAD, -1)


def cut_regions(value, pairs, reg):
    return value.reshape(pairs, VIS_PAD, -1)[:, :reg].reshape(pairs * reg, -1)


def fast_shards(
    x_text, x_vis, caption_len, cot_text, cot_vis, master_blocks,
    stat_left, stat_right, root_left, root_right, norm_params, norm_second,
):
    pairs = caption_len.shape[0]
    reg = x_vis.shape[0] // pairs
    xv = pad_regions(x_vis, pairs)
    cv = pad_regions(cot_vis, pairs)
    near, far, (xv, cv) = gather_tiles(master_blocks, (xv, cv))
    lengths = jnp.concatenate([caption_len, jnp.full((2,), reg, jnp.int32)])
    regions = jnp.full((2,), reg, jnp.int32)
    vis_norms = norm_params[:, : 3 * VIS].reshape(2, 3, VIS)
    text_norms = norm_params[:, 3 * VIS :].reshape(2, 3, TXT)
    co_vis, co_text, vis_ctx, text_ctx = co_forward(lengths, xv, x_text, near, far)
    (out_vis, v_first, v_act, v_second, v_sctx, v_fback, v_pback, v_bback, v_dself, v_tback,
     v_resid, v_dctx, v_sums) = middle(1, regions, vis_ctx, xv, cv, vis_norms, near, far, VIS_PAD, HEAD_V, 32)
    vis_mid = weight_grads(
        (1, 2, 3, 4, 5), (vis_ctx, v_first, v_act, v_second, v_sctx),
        (v_fback, v_pback, v_bback, v_dself, v_tback),
    )
    _, _, _, core = spot()
    chunks = [Sums() for _ in range(CHUNKS)]
    vis_at, text_at = TILES[1][0], TILES[7][0]
    vis_pair, text_pair = (vis_mid, 2 * SHARD - vis_at), 6 * SHARD - text_at
    lone = group_lone(*vis_pair)
    vis_source = (vis_at, vis_mid)

    def pick_both(source, owner):
        begins = begins_of([source])
        plans = [both_plan(owner, begins, 1), both_plan(owner, begins, 0)]
        send, own = pick(core, [source], plans, [2 * R_BOTH] * 2)
        return own, lax.ppermute(send, "seq", SWAP_CORE)

    def both_sum(own, got):
        return add(own, got).reshape(2, R_BOTH, SUB, WIDE)

    own_both, far_both = pick_both(vis_source, 2)
    (out_text, t_first, t_act, t_second, t_sctx, t_fback, t_pback, t_bback, t_dself, t_tback,
     t_resid, t_dctx, t_sums) = middle(
        7, lengths, text_ctx, x_text, cot_text, text_norms, near, far, x_text.shape[0] // pairs, HEAD_T, 32
    )
    chunks[0].state["norms", 0] = jnp.concatenate([v_sums.reshape(2, -1), t_sums.reshape(2, -1)], 1)
    lefts = (text_ctx, t_first, t_act, t_second, t_sctx)
    rights = (t_fback, t_pback, t_bback, t_dself, t_tback)
    lefts, rights, far_both = lax.optimization_barrier((lefts, rights, far_both))
    text_mid = weight_grads((7, 8, 9, 10, 11), lefts, rights)
    text_source = (text_at, text_mid)
    both = both_sum(own_both, far_both)
    own_both, far_both = pick_both(text_source, 6)
    back = (co_vis, co_text, v_dctx, t_dctx, v_resid, t_resid)
    back, both, text_mid = lax.optimization_barrier((back, both, text_mid))
    for k, kept in enumerate(chunks_of(lone, both)):
        chunks[k].state["kept", 1] = kept
    lone = group_lone(text_mid, text_pair)
    def swap_halves(sources, owners):
        plans = [half_plan(o, begins_of(sources), 1) for o in owners]
        return [
            lax.ppermute(part, "seq", SWAP_CORE) for part in pick(core, sources, plans, [R_HALF] * len(owners))
        ]

    dco_vis, dco_text, grad_vis, grad_text, far_both, far_half = beside(
        chunks,
        [(0, ("X", 1)), (0, ("N", 0))],
        lambda: (*co_backward(lengths, *back, near, far), far_both, swap_halves([text_source], (5,))[0]),
    )
    early_sources = [None, vis_source]
    late_sources = [vis_source, None, text_source]

    def co_grads():
        text_co = weight_grads((6,), (x_text,), (dco_text,))
        late_sources[1] = (TILES[6][0], text_co)
        far_four = swap_halves(late_sources, (4,))[0]
        early_sources[0] = (0, weight_grads((0,), (xv,), (dco_vis,)))
        return text_co, far_four

    text_co, far_four = beside(
        chunks, [(1, ("X", 1)), (0, ("Z", 1, 0)), (0, ("N", 1))], co_grads
    )
    late_sources[1] = (TILES[6][0], text_co)

    def merge_late():
        merge(core, late_sources, 2, [far_four, far_half], chunks)
        return swap_halves(early_sources, (0, 1))

    got = beside(chunks, [(0, ("Z", 1, 1)), (1, ("Z", 1, 0))], merge_late)
    for k, kept in enumerate(chunks_of(lone, both_sum(own_both, far_both))):
        chunks[k].state["kept", 3] = kept
    beside(
        chunks,
        [(0, ("Y", 2)), (0, ("X", 3)), (1, ("Z", 1, 1))],
        lambda: merge(core, early_sources, 0, got, chunks),
    )
    beside(chunks, [(0, ("Y", 0)), (0, ("X", 2)), (0, ("Z", 3, 0)), (0, ("N", 2))], lambda: ())
    chunks[1].step([("Y", 2), ("X", 3)])
    chunks[0].step([("X", 0), ("Z", 2, 0), ("Z", 3, 1), ("N", 3)])
    chunks[1].step([("Y", 0), ("X", 2), ("Z", 3, 0)])
    chunks[0].step([("Z", 0, 0), ("Z", 2, 1), ("Z", 3, 2), ("N", 4)])
    chunks[1].step([("X", 0), ("Z", 2, 0), ("Z", 3, 1)])
    chunks[0].step([("Z", 0, 1)])
    chunks[1].step([("Z", 0, 0), ("Z", 2, 1), ("Z", 3, 2)])
    chunks[0].step([("Z", 0, 2)])
    chunks[1].step([("Z", 0, 1)])
    chunks[0].step([("F", 0)])
    chunks[0].step([("G", 0)])
    statistics = (master_blocks, stat_left, stat_right, root_left, root_right)
    early = chunk_pairs(0)
    count = early.shape[0] // 2
    owned = chunks[0].state["owned", 0]
    renewed = beside(
        chunks, [(1, ("Z", 0, 2))], lambda: renew(early[:count], owned[: 2 * count], *statistics, ())
    )
    renewed = beside(
        chunks, [(1, ("F", 0))], lambda: renew(early[count:], owned[2 * count :], *statistics, renewed)
    )
    chunks[1].step([("G", 0)])
    grad_blocks, left_new, right_new, master_new = renew(
        chunk_pairs(1), chunks[1].state["owned", 0], *statistics, renewed
    )
    norm_grads = chunks[0].state["norms", 0]
    second_new = STAT_DECAY * norm_second + (1.0 - STAT_DECAY) * norm_grads * norm_grads
    norm_new = norm_params - NORM_RATE * norm_grads / (jnp.sqrt(second_new) + MOMENT_EPSILON)
    return (
        out_text,
        cut_regions(out_vis, pairs, reg),
        grad_text,
        cut_regions(grad_vis, pairs, reg),
        grad_blocks,
        left_new,
        right_new,
        master_new,
        norm_grads,
        second_new,
        norm_new,
    )


def fits(mesh):
    return mesh.shape["dp"] == 8 and mesh.shape["seq"] == 4


def solution(mesh):
    placed = (
        P(("dp", "seq"), None),
        P(("dp", "seq"), None),
        P(("dp", "seq")),
        P(("dp", "seq"), None),
        P(("dp", "seq"), None),
        P("dp", None),
        P("dp", None),
        P("dp", None),
        P("dp", None),
        P("dp", None),
        P(),
        P(),
    )
    step = fast_shards if fits(mesh) else shards
    return jax.shard_map(
        step,
        mesh=mesh,
        in_specs=placed,
        out_specs=(
            P(("dp", "seq"), None),
            P(("dp", "seq"), None),
            P(("dp", "seq"), None),
            P(("dp", "seq"), None),
            P("dp", None),
            P("dp", None),
            P("dp", None),
            P("dp", None),
            P(),
            P(),
            P(),
        ),
        check_vma=False,
    )
```

```python
import functools

import jax
import jax.numpy as jnp
from jax import lax
from jax.experimental import pallas as pl
from jax.experimental.pallas import tpu as pltpu
from jax.sharding import PartitionSpec as P

TXT = 768
VIS = 1024
BI = 1024
FFT = 3072
FFV = 1024
HEAD = 128
HEAD_T = 64
HEAD_V = 128
BLK = 64


MASK_FILL = -1000000000.0
STAT_DECAY = 0.9
WEIGHT_RATE = 0.3
NORM_RATE = 0.2
NORM_EPSILON = 1e-05
MOMENT_EPSILON = 1e-08
HIGHEST = lax.Precision.HIGHEST
CONTRACT_COLS = (((1,), (1,)), ((), ()))


def weight_layout():
    return (
        (VIS, BI, 3),
        (BI, VIS, 1),
        (VIS, FFV, 1),
        (FFV, VIS, 1),
        (VIS, VIS, 3),
        (VIS, VIS, 1),
        (TXT, BI, 3),
        (BI, TXT, 1),
        (TXT, FFT, 1),
        (FFT, TXT, 1),
        (TXT, TXT, 3),
        (TXT, TXT, 1),
    )


def unpack_weights(flat):
    size = BLK
    blocks = flat.reshape(flat.shape[0], size, size)
    begin = 0
    matrices = []
    for rows, columns, count in weight_layout():
        number = count * rows * columns // (size * size)
        shaped = blocks[begin : begin + number].reshape(
            count, rows // size, columns // size, size, size
        )
        matrices.append(shaped.transpose(1, 3, 0, 2, 4).reshape(rows, count * columns))
        begin += number
    return matrices


def block_grad(inputs, grads, count):
    size = BLK
    left = inputs.reshape(inputs.shape[0], inputs.shape[1] // size, size)
    right = grads.reshape(grads.shape[0], count, grads.shape[1] // (count * size), size)
    return jnp.einsum("nai,nkbj->kabij", left, right, preferred_element_type=jnp.float32).reshape(
        -1, size * size
    )


def norm_columns(values, stream, which):
    if stream == 0:
        begin = which * VIS
        width = VIS
    else:
        begin = 3 * VIS + which * TXT
        width = TXT
    return values[:, begin : begin + width]


def gelu_exact(value):
    return jax.nn.gelu(value, approximate=False)


def heads_of(side, which, head):
    part = side[:, :, which, :]
    return part.reshape(part.shape[0], part.shape[1], part.shape[2] // head, head)


def scores_of(query, keys, live, head):
    scores = jnp.einsum(
        "gqhd,gkhd->ghqk", query, keys, preferred_element_type=jnp.float32
    ) * head ** (-0.5)
    if live is not None:
        scores = jnp.where(live[:, None, None, :], scores, MASK_FILL)
    return scores


def attend_one(query, keys, values, live, head):
    scores = scores_of(query, keys, live, head)
    top = jnp.max(scores, axis=3, keepdims=True)
    raised = jnp.exp(scores - top)
    total = jnp.sum(raised, axis=3, keepdims=True)
    found = jnp.einsum(
        "ghqk,gkhd->gqhd",
        (raised / total).astype(jnp.bfloat16),
        values,
        preferred_element_type=jnp.float32,
    ).astype(jnp.bfloat16)
    return (found.reshape(found.shape[0], found.shape[1], -1), top + jnp.log(total))


def attend_one_back(query, keys, values, live, head, logsum, dfound):
    scale = head ** (-0.5)
    probs = jnp.exp(scores_of(query, keys, live, head) - logsum)
    upstream = dfound.reshape(dfound.shape[0], dfound.shape[1], -1, head)
    dprobs = jnp.einsum("gqhd,gkhd->ghqk", upstream, values, preferred_element_type=jnp.float32)
    dvalues = jnp.einsum(
        "ghqk,gqhd->gkhd", probs.astype(jnp.bfloat16), upstream, preferred_element_type=jnp.float32
    )
    dscores = (probs * (dprobs - jnp.sum(probs * dprobs, axis=3, keepdims=True))).astype(
        jnp.bfloat16
    )
    dquery = (
        jnp.einsum("ghqk,gkhd->gqhd", dscores, keys, preferred_element_type=jnp.float32) * scale
    )
    dkeys = (
        jnp.einsum("ghqk,gqhd->gkhd", dscores, query, preferred_element_type=jnp.float32) * scale
    )
    return (dquery, dkeys, dvalues)


def attention_plan(vis_side, text_side, lengths, cross):
    live = (
        lax.broadcasted_iota(jnp.int32, (lengths.shape[0], text_side.shape[1]), 1)
        < lengths[:, None]
    )
    if cross:
        return ((vis_side, text_side, live, HEAD), (text_side, vis_side, None, HEAD))
    return ((vis_side, vis_side, None, HEAD_V), (text_side, text_side, live, HEAD_T))


def pair_attend(vis_side, text_side, lengths, cross):
    results = []
    for query_side, key_side, live, head in attention_plan(vis_side, text_side, lengths, cross):
        results.append(
            attend_one(
                heads_of(query_side, 0, head),
                heads_of(key_side, 1, head),
                heads_of(key_side, 2, head),
                live,
                head,
            )
        )
    return (results[0][0], results[1][0], results[0][1], results[1][1])


def pair_attend_back(
    vis_side, text_side, lengths, cross, vis_logsum, text_logsum, vis_dfound, text_dfound
):
    plan = attention_plan(vis_side, text_side, lengths, cross)
    parts = []
    for (query_side, key_side, live, head), logsum, dfound in zip(
        plan, (vis_logsum, text_logsum), (vis_dfound, text_dfound)
    ):
        parts.append(
            attend_one_back(
                heads_of(query_side, 0, head),
                heads_of(key_side, 1, head),
                heads_of(key_side, 2, head),
                live,
                head,
                logsum,
                dfound,
            )
        )
    if cross:
        vis_parts = (parts[0][0], parts[1][1], parts[1][2])
        text_parts = (parts[1][0], parts[0][1], parts[0][2])
    else:
        vis_parts = parts[0]
        text_parts = parts[1]
    vis_grad = jnp.stack(vis_parts, axis=2).reshape(vis_side.shape).astype(jnp.bfloat16)
    text_grad = jnp.stack(text_parts, axis=2).reshape(text_side.shape).astype(jnp.bfloat16)
    return (vis_grad, text_grad)


def to_heads(vis_side, text_side):
    return (vis_side, text_side)


def from_heads(vis_found, text_found):
    return (vis_found, text_found)


def dfound_to_heads(vis_dfound, text_dfound):
    return (vis_dfound, text_dfound)


def grads_from_heads(vis_grad, text_grad):
    return (vis_grad, text_grad)


def side_of(rows_in, weight, pairs):
    made = jnp.dot(rows_in, weight, preferred_element_type=jnp.float32).astype(jnp.bfloat16)
    return made.reshape(pairs, -1, 3, weight.shape[1] // 3)


def norm_forward(resid, columns):
    mean = jnp.mean(resid, -1, keepdims=True)
    centered = resid - mean
    scale = lax.rsqrt(jnp.mean(centered * centered, -1, keepdims=True) + NORM_EPSILON)
    normed = centered * scale
    return (normed, scale, normed * columns[0] + columns[1])


def norm_backward(upstream, normed, scale, gain):
    scaled = upstream * gain
    resid_grad = scale * (
        scaled
        - jnp.mean(scaled, -1, keepdims=True)
        - normed * jnp.mean(scaled * normed, -1, keepdims=True)
    )
    return (resid_grad, jnp.sum(upstream * normed, 0), jnp.sum(upstream, 0))


def stream_middle(context_rows, x_rows, weights, values, stream, pairs):
    resid = x_rows.astype(jnp.float32) + jnp.dot(
        context_rows, weights[1], preferred_element_type=jnp.float32
    )
    normed_one, scale_one, first = norm_forward(resid, norm_columns(values, stream, 0))
    first_low = first.astype(jnp.bfloat16)
    pre = jnp.dot(first_low, weights[2], preferred_element_type=jnp.float32)
    act = gelu_exact(pre).astype(jnp.bfloat16)
    resid = first + jnp.dot(act, weights[3], preferred_element_type=jnp.float32)
    normed_two, scale_two, second = norm_forward(resid, norm_columns(values, stream, 1))
    second_low = second.astype(jnp.bfloat16)
    side = side_of(second_low, weights[4], pairs)
    return (
        side,
        (normed_one, scale_one, first_low, pre, act, normed_two, scale_two, second, second_low),
    )


def stream_end(self_rows, second, out_weight, values, stream):
    resid = second + jnp.dot(self_rows, out_weight, preferred_element_type=jnp.float32)
    normed_three, scale_three, third = norm_forward(resid, norm_columns(values, stream, 2))
    return (third.astype(jnp.bfloat16), normed_three, scale_three)


def stream_back_end(
    cotangent, normed_three, scale_three, self_rows, out_weight, values, stream, pairs
):
    resid_three, gain_three, bias_three = norm_backward(
        cotangent.astype(jnp.float32), normed_three, scale_three, norm_columns(values, stream, 2)[0]
    )
    third_back = resid_three.astype(jnp.bfloat16)
    grad_self_out = block_grad(self_rows, third_back, 1)
    dself = lax.dot_general(
        third_back, out_weight, CONTRACT_COLS, preferred_element_type=jnp.float32
    )
    dself = dself.astype(jnp.bfloat16).reshape(pairs, -1, out_weight.shape[0])
    return (resid_three, dself, grad_self_out, gain_three, bias_three)


def stream_back_middle(resid_three, dself_side, kept, context_rows, weights, values, stream, pairs):
    normed_one, scale_one, first_low, pre, act, normed_two, scale_two, second, second_low = kept
    dself_rows = dself_side.reshape(-1, dself_side.shape[2] * dself_side.shape[3])
    grad_self_qkv = block_grad(second_low, dself_rows, 3)
    second_in = resid_three + lax.dot_general(
        dself_rows, weights[4], CONTRACT_COLS, preferred_element_type=jnp.float32
    )
    resid_two, gain_two, bias_two = norm_backward(
        second_in, normed_two, scale_two, norm_columns(values, stream, 1)[0]
    )
    branch_back = resid_two.astype(jnp.bfloat16)
    grad_down = block_grad(act, branch_back, 1)
    act_grad = lax.dot_general(
        branch_back, weights[3], CONTRACT_COLS, preferred_element_type=jnp.float32
    )
    pre_grad = jax.vjp(gelu_exact, pre)[1](act_grad)[0].astype(jnp.bfloat16)
    grad_up = block_grad(first_low, pre_grad, 1)
    first_in = resid_two + lax.dot_general(
        pre_grad, weights[2], CONTRACT_COLS, preferred_element_type=jnp.float32
    )
    resid_one, gain_one, bias_one = norm_backward(
        first_in, normed_one, scale_one, norm_columns(values, stream, 0)[0]
    )
    first_back = resid_one.astype(jnp.bfloat16)
    grad_co_out = block_grad(context_rows, first_back, 1)
    dcontext = lax.dot_general(
        first_back, weights[1], CONTRACT_COLS, preferred_element_type=jnp.float32
    )
    dcontext = dcontext.astype(jnp.bfloat16).reshape(pairs, -1, BI)
    return (
        resid_one,
        dcontext,
        (grad_co_out, grad_up, grad_down, grad_self_qkv),
        (gain_one, gain_two),
        (bias_one, bias_two),
    )


def shards(
    x_text,
    x_vis,
    caption_len,
    cot_text,
    cot_vis,
    master_blocks,
    stat_left,
    stat_right,
    root_left,
    root_right,
    norm_params,
    norm_second,
):
    pairs = caption_len.shape[0]
    width = master_blocks.shape[1] // lax.axis_size("seq")
    mine = lax.dynamic_slice_in_dim(master_blocks, lax.axis_index("seq") * width, width, 1).astype(
        jnp.bfloat16
    )
    partial_value = lax.all_gather(mine, "dp", axis=0, tiled=True)
    every = lax.all_gather(partial_value, "seq", axis=1, tiled=True)
    matrices = unpack_weights(every)
    vis_weights = matrices[:6]
    text_weights = matrices[6:]
    vis_co = side_of(x_vis, vis_weights[0], pairs)
    text_co = side_of(x_text, text_weights[0], pairs)
    lengths = caption_len
    vis_co_use, text_co_use = to_heads(vis_co, text_co)
    vis_found, text_found, vis_co_sum, text_co_sum = pair_attend(
        vis_co_use, text_co_use, lengths, True
    )
    vis_context, text_context = from_heads(vis_found, text_found)
    vis_context_rows = vis_context.reshape(-1, BI)
    text_context_rows = text_context.reshape(-1, BI)
    vis_self, vis_kept = stream_middle(vis_context_rows, x_vis, vis_weights, norm_params, 0, pairs)
    text_self, text_kept = stream_middle(
        text_context_rows, x_text, text_weights, norm_params, 1, pairs
    )
    vis_self_use, text_self_use = to_heads(vis_self, text_self)
    vis_found, text_found, vis_self_sum, text_self_sum = pair_attend(
        vis_self_use, text_self_use, lengths, False
    )
    vis_self_context, text_self_context = from_heads(vis_found, text_found)
    vis_self_rows = vis_self_context.reshape(-1, VIS)
    text_self_rows = text_self_context.reshape(-1, TXT)
    out_vis, vis_normed_three, vis_scale_three = stream_end(
        vis_self_rows, vis_kept[7], vis_weights[5], norm_params, 0
    )
    out_text, text_normed_three, text_scale_three = stream_end(
        text_self_rows, text_kept[7], text_weights[5], norm_params, 1
    )
    vis_resid_three, vis_dself, vis_grad_so, vis_gain_three, vis_bias_three = stream_back_end(
        cot_vis,
        vis_normed_three,
        vis_scale_three,
        vis_self_rows,
        vis_weights[5],
        norm_params,
        0,
        pairs,
    )
    text_resid_three, text_dself, text_grad_so, text_gain_three, text_bias_three = stream_back_end(
        cot_text,
        text_normed_three,
        text_scale_three,
        text_self_rows,
        text_weights[5],
        norm_params,
        1,
        pairs,
    )
    vis_dheads, text_dheads = dfound_to_heads(vis_dself, text_dself)
    vis_dgot, text_dgot = pair_attend_back(
        vis_self_use,
        text_self_use,
        lengths,
        False,
        vis_self_sum,
        text_self_sum,
        vis_dheads,
        text_dheads,
    )
    vis_dself_side, text_dself_side = grads_from_heads(vis_dgot, text_dgot)
    vis_resid_one, vis_dcontext, vis_grads_mid, vis_gains_mid, vis_biases_mid = stream_back_middle(
        vis_resid_three,
        vis_dself_side,
        vis_kept,
        vis_context_rows,
        vis_weights,
        norm_params,
        0,
        pairs,
    )
    text_resid_one, text_dcontext, text_grads_mid, text_gains_mid, text_biases_mid = (
        stream_back_middle(
            text_resid_three,
            text_dself_side,
            text_kept,
            text_context_rows,
            text_weights,
            norm_params,
            1,
            pairs,
        )
    )
    vis_dheads, text_dheads = dfound_to_heads(vis_dcontext, text_dcontext)
    vis_dgot, text_dgot = pair_attend_back(
        vis_co_use, text_co_use, lengths, True, vis_co_sum, text_co_sum, vis_dheads, text_dheads
    )
    vis_dco, text_dco = grads_from_heads(vis_dgot, text_dgot)
    vis_dco_rows = vis_dco.reshape(-1, 3 * BI)
    text_dco_rows = text_dco.reshape(-1, 3 * BI)
    grad_vis = vis_resid_one + lax.dot_general(
        vis_dco_rows, vis_weights[0], CONTRACT_COLS, preferred_element_type=jnp.float32
    )
    grad_text = text_resid_one + lax.dot_general(
        text_dco_rows, text_weights[0], CONTRACT_COLS, preferred_element_type=jnp.float32
    )
    vis_grad_co = block_grad(x_vis, vis_dco_rows, 3)
    text_grad_co = block_grad(x_text, text_dco_rows, 3)
    local_blocks = jnp.concatenate(
        [vis_grad_co]
        + list(vis_grads_mid)
        + [vis_grad_so]
        + [text_grad_co]
        + list(text_grads_mid)
        + [text_grad_so],
        0,
    )
    norm_local = jnp.stack(
        [
            jnp.concatenate(
                [
                    vis_gains_mid[0],
                    vis_gains_mid[1],
                    vis_gain_three,
                    text_gains_mid[0],
                    text_gains_mid[1],
                    text_gain_three,
                ]
            ),
            jnp.concatenate(
                [
                    vis_biases_mid[0],
                    vis_biases_mid[1],
                    vis_bias_three,
                    text_biases_mid[0],
                    text_biases_mid[1],
                    text_bias_three,
                ]
            ),
        ]
    )
    columns = lax.psum_scatter(
        local_blocks.astype(jnp.bfloat16), "seq", scatter_dimension=1, tiled=True
    ).astype(jnp.float32)
    owned_columns = lax.psum_scatter(columns, "dp", scatter_dimension=0, tiled=True)
    owned = lax.all_gather(owned_columns.astype(jnp.bfloat16), "seq", axis=1, tiled=True).astype(
        owned_columns.dtype
    )
    norm_grads = lax.psum(norm_local, ("dp", "seq"))
    number = owned.shape[0]
    grad_cube = owned.reshape(number, BLK, BLK)
    left_cube = stat_left.reshape(number, BLK, BLK)
    right_cube = stat_right.reshape(number, BLK, BLK)
    rootl_cube = root_left.reshape(number, BLK, BLK)
    rootr_cube = root_right.reshape(number, BLK, BLK)
    left_new = STAT_DECAY * left_cube + (1.0 - STAT_DECAY) * jnp.einsum(
        "bij,bkj->bik", grad_cube, grad_cube, precision=HIGHEST
    )
    right_new = STAT_DECAY * right_cube + (1.0 - STAT_DECAY) * jnp.einsum(
        "bji,bjk->bik", grad_cube, grad_cube, precision=HIGHEST
    )
    half = jnp.einsum("bij,bjk->bik", rootl_cube, grad_cube, precision=HIGHEST)
    direction = jnp.einsum("bij,bjk->bik", half, rootr_cube, precision=HIGHEST)
    master_new = master_blocks - WEIGHT_RATE * direction.reshape(number, BLK * BLK)
    second_new = STAT_DECAY * norm_second + (1.0 - STAT_DECAY) * norm_grads * norm_grads
    norm_new = norm_params - NORM_RATE * norm_grads / (jnp.sqrt(second_new) + MOMENT_EPSILON)
    return (
        out_text,
        out_vis,
        grad_text,
        grad_vis,
        owned,
        left_new.reshape(number, BLK * BLK),
        right_new.reshape(number, BLK * BLK),
        master_new,
        norm_grads,
        second_new,
        norm_new,
    )


SUB = 64
WIDE = 256
QUAD = 4
F32 = jnp.float32
BF16 = jnp.bfloat16
VIS_PAD = 48
VMEM_LIMIT = 60 * 1024 * 1024
NT = (((1,), (1,)), ((), ()))
TN = (((0,), (0,)), ((), ()))


def tile_table():
    begin = 0
    table = []
    for rows, columns, count in weight_layout():
        r, g = rows // SUB, columns // WIDE
        table.append((begin, count, r, g))
        begin += count * r * g
    return table


TILES = tile_table()
SHARD = 158
FAR = 62
G_HALF = 32
G_LONE = 8
R_LONE = 32
R_BOTH = 16
R_HALF = 2 * R_LONE + R_BOTH
CHUNKS = 2
SWAP_CORE = [(i, i ^ 1) for i in range(4)]
SWAP_Y = [(i, i ^ 2) for i in range(4)]
SWAP_X = [(i, i ^ 1) for i in range(8)]


def dot(left, right, how=None):
    if how is None:
        return jnp.dot(left, right, preferred_element_type=F32)
    return lax.dot_general(left, right, how, preferred_element_type=F32)


def params(**more):
    return pltpu.CompilerParams(vmem_limit_bytes=VMEM_LIMIT, **more)


def cost(micros):
    return pl.CostEstimate(flops=0, bytes_accessed=int(micros * 3.4e6), transcendentals=0)


def whole(count):
    return [pl.BlockSpec(memory_space=pltpu.VMEM)] * count


def linear(value):
    groups = value.shape[0] // 8
    return value.reshape(groups, 8, 32, 128).transpose(0, 2, 1, 3).reshape(groups * 256, 128)


def unlinear(value):
    groups = value.shape[0] // 256
    return value.reshape(groups, 32, 8, 128).transpose(0, 2, 1, 3).reshape(groups * 8, SUB * SUB)


def lanes_low(rows):
    return lax.broadcasted_iota(jnp.int32, (rows, 2 * SUB), 1) < SUB


def spread_of(ref, b):
    return ref[pl.ds(b, 32, stride=8), :]


def natural_order():
    row = lax.broadcasted_iota(jnp.int32, (SUB, SUB), 0)
    column = lax.broadcasted_iota(jnp.int32, (SUB, SUB), 1)
    return jnp.where(row == 2 * (column % 32) + column // 32, 1.0, 0.0).astype(BF16)


def prep_rows(number, pairs_ref, x_any, o_ref, rows_in, sems):
    def fetch(i):
        rows = pl.ds(pl.multiple_of(pairs_ref[i] * 256, 256), 256)
        return pltpu.make_async_copy(x_any.at[rows], rows_in.at[i], sems.at[i])

    for i in range(number):
        fetch(i).start()
    low = lanes_low(32)
    order = natural_order()

    def step(i, carry):
        fetch(i).wait()
        x_ref = rows_in.at[i]
        spots = range(4)
        one = [spread_of(x_ref, 2 * m) for m in spots]
        two = [spread_of(x_ref, 2 * m + 1) for m in spots]
        rows = [
            jnp.concatenate(
                [
                    jnp.where(low, one[m], pltpu.roll(two[m], SUB, 1)),
                    jnp.where(low, pltpu.roll(one[m], SUB, 1), two[m]),
                ],
                0,
            ).astype(BF16)
            for m in spots
        ]
        made = [dot(order, rows[m]).astype(BF16) for m in spots]
        for m in spots:
            o_ref[2 * i + m // 2, :, (m % 2) * 128 : (m % 2 + 1) * 128] = made[m]
        return carry

    lax.fori_loop(0, number, step, 0, unroll=2 if number % 2 == 0 else 3)


def prep(master_blocks, pairs):
    number = pairs.shape[0]
    return pl.pallas_call(
        functools.partial(prep_rows, number),
        in_specs=[pl.BlockSpec(memory_space=pltpu.SMEM), pl.BlockSpec(memory_space=pl.ANY)],
        out_specs=pl.BlockSpec(memory_space=pltpu.VMEM),
        out_shape=jax.ShapeDtypeStruct((number * 2, SUB, WIDE), BF16),
        scratch_shapes=[pltpu.VMEM((number, 256, 128), F32), pltpu.SemaphoreType.DMA((number,))],
        compiler_params=params(),
        cost_estimate=cost(0.4 * number),
    )(pairs, linear(master_blocks))


def renew_eight(g_ref, m_ref, sl_ref, sr_ref, rl_ref, rr_ref, go_ref, lo_ref, ro_ref, mo_ref, place):
    low = lanes_low(SUB)
    low_half = lanes_low(32)
    nothing = jnp.zeros((SUB, 128), F32)
    pairs = range(4)

    def diagonal(pair):
        return jnp.concatenate([jnp.where(low, pair, nothing), jnp.where(low, nothing, pair)], 0).astype(BF16)

    def mixed(even, odd):
        return (
            jnp.where(low_half, even, pltpu.roll(odd, SUB, 1)),
            jnp.where(low_half, pltpu.roll(even, SUB, 1), odd),
        )

    def natural(ref, pair, spot):
        even, odd = mixed(spread_of(ref, 2 * pair), spread_of(ref, 2 * pair + 1))
        spot[pl.ds(0, 32, stride=2), :] = even
        spot[pl.ds(1, 32, stride=2), :] = odd
        return spot[...]

    def spread(value, spot):
        spot[...] = value
        return mixed(spot[pl.ds(0, 32, stride=2), :], spot[pl.ds(1, 32, stride=2), :])

    tiles = [g_ref[pair // 2, :, (pair % 2) * 128 : (pair % 2 + 1) * 128] for pair in pairs]
    wide = [tile.astype(F32) for tile in tiles]
    grads = [diagonal(value) for value in wide]
    lefts = [natural(rl_ref, pair, place.at[pair, 0]).astype(BF16) for pair in pairs]
    rights = [diagonal(natural(rr_ref, pair, place.at[pair, 1])) for pair in pairs]
    halves = [dot(lefts[pair], grads[pair]).astype(BF16) for pair in pairs]
    left_parts = [dot(tiles[pair], grads[pair], NT) for pair in pairs]
    squares = [dot(tiles[pair], tiles[pair], TN) for pair in pairs]
    right_parts = [jnp.where(low, square[:SUB], square[SUB:]) for square in squares]
    steps = [dot(halves[pair], rights[pair]) for pair in pairs]
    for pair in pairs:
        made = [
            spread(value[pair], place.at[pair, 2 + k])
            for k, value in enumerate((wide, left_parts, right_parts, steps))
        ]
        for i in range(2):
            at = pl.ds(2 * pair + i, 32, stride=8)
            go_ref[at, :] = made[0][i]
            lo_ref[at, :] = STAT_DECAY * sl_ref[at, :] + (1.0 - STAT_DECAY) * made[1][i]
            ro_ref[at, :] = STAT_DECAY * sr_ref[at, :] + (1.0 - STAT_DECAY) * made[2][i]
            mo_ref[at, :] = m_ref[at, :] - WEIGHT_RATE * made[3][i]


SLOTS = 4


def renew_body(steps, which_ref, g_any, *refs):
    ins = refs[:5]
    outs = refs[-9:-5]
    gbuf, inbuf, outbuf, place, sems = refs[-5:]

    def rows(i):
        return pl.ds(pl.multiple_of(which_ref[i] * 256, 256), 256)

    def fetch(i):
        slot = lax.rem(i, SLOTS)
        copies = [pltpu.make_async_copy(g_any.at[pl.ds(2 * i, 2)], gbuf.at[slot], sems.at[slot, 0])]
        for k, ref in enumerate(ins):
            copies.append(
                pltpu.make_async_copy(ref.at[rows(i)], inbuf.at[slot, k], sems.at[slot, 1 + k])
            )
        return copies

    def put(i):
        slot = lax.rem(i, SLOTS)
        return [
            pltpu.make_async_copy(outbuf.at[slot, k], ref.at[rows(i)], sems.at[slot, 6 + k])
            for k, ref in enumerate(outs)
        ]

    def start(copies):
        for copy in copies:
            copy.start()

    def wait(copies):
        for copy in copies:
            copy.wait()

    for i in range(min(SLOTS, steps)):
        start(fetch(i))

    def step(i, carry):
        slot = lax.rem(i, SLOTS)
        wait(fetch(i))

        @pl.when(i >= SLOTS)
        def _():
            wait(put(i - SLOTS))

        renew_eight(
            gbuf.at[slot], *(inbuf.at[slot, k] for k in range(5)), *(outbuf.at[slot, k] for k in range(4)), place
        )
        start(put(i))

        @pl.when(i + SLOTS < steps)
        def _():
            start(fetch(i + SLOTS))

        return carry

    lax.fori_loop(0, steps, step, 0)
    for i in range(max(0, steps - SLOTS), steps):
        wait(put(i))


def renew(which, owned, master_blocks, stat_left, stat_right, root_left, root_right, before):
    steps = which.shape[0]
    shape = jax.ShapeDtypeStruct((master_blocks.shape[0] * 32, 128), F32)
    anywhere = pl.BlockSpec(memory_space=pl.ANY)
    made = pl.pallas_call(
        functools.partial(renew_body, steps),
        in_specs=[pl.BlockSpec(memory_space=pltpu.SMEM)] + [anywhere] * (6 + len(before)),
        out_specs=[anywhere] * 4,
        out_shape=[shape] * 4,
        scratch_shapes=[
            pltpu.VMEM((SLOTS, 2, SUB, WIDE), BF16),
            pltpu.VMEM((SLOTS, 5, 256, 128), F32),
            pltpu.VMEM((SLOTS, 4, 256, 128), F32),
            pltpu.VMEM((4, 6, SUB, 128), F32),
            pltpu.SemaphoreType.DMA((SLOTS, 10)),
        ],
        input_output_aliases={7 + i: i for i in range(len(before))},
        compiler_params=params(),
        cost_estimate=cost(0.7 * steps),
    )(
        which,
        owned,
        *(linear(value) for value in (master_blocks, stat_left, stat_right, root_left, root_right)),
        *(linear(value) for value in before),
    )
    return [unlinear(value) for value in made]


def times(rows_in, w, base, r, g, part, col):
    first = base + part * r * g + col
    return dot(rows_in, jnp.concatenate([w[first + a * g] for a in range(r)], 0))


def times_back(d_ref, w, base, r, g, count, r4):
    total = None
    for part in range(count):
        first = base + (part * r + 4 * r4) * g
        wide = jnp.concatenate(
            [
                jnp.concatenate([w[first + a * g + col] for a in range(4)], 0)
                for col in range(g)
            ],
            1,
        )
        made = dot(d_ref[:, part * g * WIDE : (part + 1) * g * WIDE], wide, NT)
        total = made if total is None else total + made
    return total


def at256(i):
    return pl.ds(pl.multiple_of(i * WIDE, WIDE), WIDE)


def softmax_all(products, scale, limits):
    scores = []
    for product, limit in zip(products, limits):
        column = lax.broadcasted_iota(jnp.int32, product.shape, 1)
        scores.append(jnp.where(column < limit, product * scale, MASK_FILL))
    tops = [jnp.max(score, 1, keepdims=True) for score in scores]
    raised = [jnp.exp(score - top) for score, top in zip(scores, tops)]
    shares = [1.0 / jnp.sum(value, 1, keepdims=True) for value in raised]
    return [value * share for value, share in zip(raised, shares)]


def score_grads(probs, dprobs):
    weighted = [p * d for p, d in zip(probs, dprobs)]
    totals = [jnp.sum(value, 1, keepdims=True) for value in weighted]
    return [(value - p * total).astype(BF16) for value, p, total in zip(weighted, probs, totals)]


def at128(i):
    return pl.ds(pl.multiple_of(i * 128, 128), 128)


def load(near, far, w, sems, pieces, base):
    started = []
    used = 0
    for i, which in enumerate(pieces):
        begin, count, r, g = TILES[which]
        end = begin + count * r * g
        copies = []
        for owner in range(begin // SHARD, (end - 1) // SHARD + 1):
            first = max(begin, owner * SHARD)
            last = min(end, (owner + 1) * SHARD)
            middle = min(max(owner * SHARD + FAR, first), last)
            for source, lo, hi, at in (
                (near, first, middle, owner * (2 * G_HALF) + first - owner * SHARD),
                (far, middle, last, owner * (SHARD - FAR) + middle - owner * SHARD - FAR),
            ):
                if lo < hi:
                    copies.append(
                        pltpu.make_async_copy(
                            source.at[pl.ds(at, hi - lo)],
                            w.at[pl.ds(base[i] + lo - begin, hi - lo)],
                            sems.at[used],
                        )
                    )
                    copies[-1].start()
                    used += 1
        started.append(copies)
    return started


def arrive(copies):
    for copy in copies:
        copy.wait()


def tiles_of(which):
    _, count, r, g = TILES[which]
    return count * r * g


def co_body(len_ref, xv_ref, xt_ref, near, far, cv_ref, ct_ref, fv_ref, ft_ref, w, sems):
    base = (0, tiles_of(0))
    copies = load(near, far, w, sems, (0, 6), base)
    for which, at, x_ref, o_ref, copy in (
        (0, base[0], xv_ref, cv_ref, copies[0]),
        (6, base[1], xt_ref, ct_ref, copies[1]),
    ):
        _, count, r, g = TILES[which]
        arrive(copy)

        def column(i, carry, at=at, r=r, g=g, x_ref=x_ref, o_ref=o_ref):
            o_ref[:, at256(i)] = times(x_ref[...], w, at, r, g, i // g, i % g).astype(BF16)
            return carry

        lax.fori_loop(0, count * g, column, 0, unroll=2)
    scale = HEAD ** (-0.5)
    reg = len_ref[2]
    heads = BI // HEAD
    vis = [slice(pair * VIS_PAD, (pair + 1) * VIS_PAD) for pair in range(2)]
    text = [slice(pair * 128, (pair + 1) * 128) for pair in range(2)]
    limits = [len_ref[0], len_ref[1], reg, reg]

    def head(j, carry):
        qv, kv, vv = ([cv_ref[rows, at128(j + heads * s)] for rows in vis] for s in range(3))
        qt, kt, vt = ([ct_ref[rows, at128(j + heads * s)] for rows in text] for s in range(3))
        probs = softmax_all([dot(q, k, NT) for q, k in zip(qv + qt, kt + kv)], scale, limits)
        found = [dot(p.astype(BF16), v).astype(BF16) for p, v in zip(probs, vt + vv)]
        for pair in range(2):
            fv_ref[vis[pair], at128(j)] = found[pair]
            ft_ref[text[pair], at128(j)] = found[2 + pair]
        return carry

    lax.fori_loop(0, heads, head, 0, unroll=2)


def co_forward(lengths, x_vis, x_text, near, far):
    return pl.pallas_call(
        co_body,
        in_specs=[pl.BlockSpec(memory_space=pltpu.SMEM)] + whole(2) + [pl.BlockSpec(memory_space=pl.ANY)] * 2,
        out_specs=whole(4),
        out_shape=[
            jax.ShapeDtypeStruct((x_vis.shape[0], 3 * BI), BF16),
            jax.ShapeDtypeStruct((x_text.shape[0], 3 * BI), BF16),
            jax.ShapeDtypeStruct((x_vis.shape[0], BI), BF16),
            jax.ShapeDtypeStruct((x_text.shape[0], BI), BF16),
        ],
        scratch_shapes=[
            pltpu.VMEM((tiles_of(0) + tiles_of(6), SUB, WIDE), BF16),
            pltpu.SemaphoreType.DMA((16,)),
        ],
        compiler_params=params(),
        cost_estimate=cost(22),
    )(lengths, x_vis, x_text, near, far)


def co_back_body(
    len_ref, cv_ref, ct_ref, dv_ref, dt_ref, rv_ref, rt_ref, near, far,
    gv_ref, gt_ref, ov_ref, ot_ref, w, sems,
):
    base = (0, tiles_of(0))
    copies = load(near, far, w, sems, (0, 6), base)
    scale = HEAD ** (-0.5)
    reg = len_ref[2]
    heads = BI // HEAD
    vis = [slice(pair * VIS_PAD, (pair + 1) * VIS_PAD) for pair in range(2)]
    text = [slice(pair * 128, (pair + 1) * 128) for pair in range(2)]
    limits = [len_ref[0], len_ref[1], reg, reg]

    def head(j, carry):
        qv, kv, vv = ([cv_ref[rows, at128(j + heads * s)] for rows in vis] for s in range(3))
        qt, kt, vt = ([ct_ref[rows, at128(j + heads * s)] for rows in text] for s in range(3))
        up = [dv_ref[rows, at128(j)] for rows in vis] + [dt_ref[rows, at128(j)] for rows in text]
        queries, keys, values = qv + qt, kt + kv, vt + vv
        products = [dot(q, k, NT) for q, k in zip(queries, keys)]
        dprobs = [dot(u, v, NT) for u, v in zip(up, values)]
        probs = softmax_all(products, scale, limits)
        ds = score_grads(probs, dprobs)
        dvalues = [dot(p.astype(BF16), u, TN).astype(BF16) for p, u in zip(probs, up)]
        dqueries = [(dot(d, k) * scale).astype(BF16) for d, k in zip(ds, keys)]
        dkeys = [(dot(d, q, TN) * scale).astype(BF16) for d, q in zip(ds, queries)]
        for pair in range(2):
            gv_ref[vis[pair], at128(j)] = dqueries[pair]
            gt_ref[text[pair], at128(j + heads)] = dkeys[pair]
            gt_ref[text[pair], at128(j + 2 * heads)] = dvalues[pair]
            gt_ref[text[pair], at128(j)] = dqueries[2 + pair]
            gv_ref[vis[pair], at128(j + heads)] = dkeys[2 + pair]
            gv_ref[vis[pair], at128(j + 2 * heads)] = dvalues[2 + pair]
        return carry

    lax.fori_loop(0, heads, head, 0, unroll=2)
    for which, at, g_ref, r_ref, o_ref, copy in (
        (0, base[0], gv_ref, rv_ref, ov_ref, copies[0]),
        (6, base[1], gt_ref, rt_ref, ot_ref, copies[1]),
    ):
        _, count, r, g = TILES[which]
        arrive(copy)

        def rows4(i, carry, at=at, r=r, g=g, count=count, g_ref=g_ref, r_ref=r_ref, o_ref=o_ref):
            o_ref[:, at256(i)] = r_ref[:, at256(i)] + times_back(g_ref, w, at, r, g, count, i)
            return carry

        lax.fori_loop(0, r // 4, rows4, 0)


def co_backward(lengths, co_vis, co_text, dvis, dtext, resid_vis, resid_text, near, far):
    return pl.pallas_call(
        co_back_body,
        in_specs=[pl.BlockSpec(memory_space=pltpu.SMEM)] + whole(6) + [pl.BlockSpec(memory_space=pl.ANY)] * 2,
        out_specs=whole(4),
        out_shape=[
            jax.ShapeDtypeStruct(co_vis.shape, BF16),
            jax.ShapeDtypeStruct(co_text.shape, BF16),
            jax.ShapeDtypeStruct(resid_vis.shape, F32),
            jax.ShapeDtypeStruct(resid_text.shape, F32),
        ],
        scratch_shapes=[
            pltpu.VMEM((tiles_of(0) + tiles_of(6), SUB, WIDE), BF16),
            pltpu.SemaphoreType.DMA((16,)),
        ],
        compiler_params=params(),
        cost_estimate=cost(23),
    )(lengths, co_vis, co_text, dvis, dtext, resid_vis, resid_text, near, far)


def erf_parts(value):
    return 0.5 * (1.0 + lax.erf(value * 0.7071067811865476))


def middle_body(
    config,
    len_ref, ctx_ref, x_ref, cot_ref, norm_ref, near, far,
    out_ref, first_ref, act_ref, second_ref, sctx_ref,
    fback_ref, pback_ref, bback_ref, dself_ref, tback_ref,
    resid_ref, dctx_ref, sums_ref,
    w, sems, pre, n1, n2, n3, s1, s2, s3, wide, acc, selfs, probs, stat,
):
    begin, rows, span, head, chunk = config
    width = x_ref.shape[1]
    base = []
    at = 0
    for which in range(begin, begin + 5):
        base.append(at)
        at += tiles_of(which)
    copies = load(near, far, w, sems, tuple(range(begin, begin + 5)), base)
    shapes = [TILES[which][1:] for which in range(begin, begin + 5)]
    steps = rows // chunk

    def at_chunk(i):
        return pl.ds(pl.multiple_of(i * chunk, chunk), chunk)

    def norm(resid, which, i, kept, scales):
        mean = jnp.mean(resid, 1, keepdims=True)
        centered = resid - mean
        scale = lax.rsqrt(jnp.mean(centered * centered, 1, keepdims=True) + NORM_EPSILON)
        normed = centered * scale
        kept[at_chunk(i), :] = normed
        scales[at_chunk(i), :] = jnp.broadcast_to(scale, (chunk, 128))
        return normed * norm_ref[0, which : which + 1, :] + norm_ref[1, which : which + 1, :]

    def eight(value):
        return jnp.sum(value.reshape(chunk // 8, 8, width), 0)

    def norm_back(upstream, which, i, kept, scales):
        normed = kept[at_chunk(i), :]
        stat[which] = stat[which] + eight(upstream * normed)
        stat[3 + which] = stat[3 + which] + eight(upstream)
        scaled = upstream * norm_ref[0, which : which + 1, :]
        return scales[at_chunk(i), 0:1] * (
            scaled
            - jnp.mean(scaled, 1, keepdims=True)
            - normed * jnp.mean(scaled * normed, 1, keepdims=True)
        )

    def loop(count, body, unroll=1):
        lax.fori_loop(0, count, lambda i, carry: (body(i), carry)[1], 0, unroll=unroll)

    stat[...] = jnp.zeros(stat.shape, F32)
    count, r, g = shapes[0]
    arrive(copies[0])

    def co_out(i):
        wide[:, at256(i)] = times(ctx_ref[...], w, base[0], r, g, 0, i)

    loop(g, co_out, g)

    def norm_one(i):
        value = norm(wide[at_chunk(i), :] + x_ref[at_chunk(i), :].astype(F32), 0, i, n1, s1)
        wide[at_chunk(i), :] = value
        first_ref[at_chunk(i), :] = value.astype(BF16)

    loop(steps, norm_one, 2 if steps % 2 == 0 else steps)
    _, r_up, g_up = shapes[1]
    _, r_down, g_down = shapes[2]
    arrive(copies[1])
    arrive(copies[2])
    acc[...] = jnp.zeros(acc.shape, F32)

    def down_rows(i):
        return jnp.concatenate(
            [
                jnp.concatenate([w[base[2] + (4 * i + a) * g_down + col] for a in range(4)], 0)
                for col in range(g_down)
            ],
            1,
        )

    def feed(i):
        value = times(first_ref[...], w, base[1], r_up, g_up, 0, i)
        part = erf_parts(value)
        pre[i] = part + value * (0.3989422804014327 * jnp.exp(-0.5 * value * value))
        act = (value * part).astype(BF16)
        act_ref[:, at256(i)] = act
        acc[...] += dot(act, down_rows(i))

    loop(g_up, feed, 4)

    def norm_two(i):
        value = norm(wide[at_chunk(i), :] + acc[at_chunk(i), :], 1, i, n2, s2)
        wide[at_chunk(i), :] = value
        second_ref[at_chunk(i), :] = value.astype(BF16)

    loop(steps, norm_two, 2 if steps % 2 == 0 else steps)
    count_s, r_s, g_s = shapes[3]
    arrive(copies[3])

    def self_in(i):
        selfs[:, at256(i)] = times(second_ref[...], w, base[3], r_s, g_s, i // g_s, i % g_s).astype(BF16)

    loop(count_s * g_s, self_in, g_s)
    scale = head ** (-0.5)
    groups = width // 128
    per = 128 // head
    pairs = rows // span

    def halves(values):
        if per == 1:
            return values[0]
        low = lax.broadcasted_iota(jnp.int32, values[0].shape, 1) < head
        return jnp.where(low, values[0], values[1])

    def only(value, h):
        if per == 1:
            return value
        low = lax.broadcasted_iota(jnp.int32, value.shape, 1) < head
        keep = low if h == 0 else jnp.logical_not(low)
        return jnp.where(keep, value, jnp.zeros_like(value))

    own = [slice(pair * span, (pair + 1) * span) for pair in range(pairs)]
    each = [(pair, h) for pair in range(pairs) for h in range(per)]

    def attend(j):
        q, k, v = ([selfs[rows_of, at128(j + groups * s)] for rows_of in own] for s in range(3))
        products = [dot(only(q[pair], h), k[pair], NT) for pair, h in each]
        p = softmax_all(products, scale, [len_ref[pair] for pair, _ in each])
        found = [dot(value.astype(BF16), v[pair]) for value, (pair, _) in zip(p, each)]
        for i, value in enumerate(p):
            probs[j * len(each) + i] = value
        for pair in range(pairs):
            sctx_ref[own[pair], at128(j)] = halves(found[pair * per : (pair + 1) * per]).astype(BF16)

    loop(groups, attend, 2)
    _, r_o, g_o = shapes[4]
    arrive(copies[4])

    def self_out(i):
        acc[:, at256(i)] = times(sctx_ref[...], w, base[4], r_o, g_o, 0, i)

    loop(g_o, self_out, g_o)

    def norm_three(i):
        value = norm(wide[at_chunk(i), :] + acc[at_chunk(i), :], 2, i, n3, s3)
        out_ref[at_chunk(i), :] = value.astype(BF16)
        third = norm_back(cot_ref[at_chunk(i), :].astype(F32), 2, i, n3, s3)
        wide[at_chunk(i), :] = third
        tback_ref[at_chunk(i), :] = third.astype(BF16)

    loop(steps, norm_three, 2 if steps % 2 == 0 else steps)

    def self_out_back(i):
        dctx_ref[:, at256(i)] = times_back(tback_ref, w, base[4], r_o, g_o, 1, i).astype(BF16)

    loop(r_o // 4, self_out_back, r_o // 4)
    def attend_back(j):
        q, k, v = ([selfs[rows_of, at128(j + groups * s)] for rows_of in own] for s in range(3))
        up = [dctx_ref[rows_of, at128(j)] for rows_of in own]
        p = [probs[j * len(each) + i] for i in range(len(each))]
        dprobs = [dot(only(up[pair], h), v[pair], NT) for pair, h in each]
        dv = [dot(value.astype(BF16), up[pair], TN) for value, (pair, _) in zip(p, each)]
        ds = score_grads(p, dprobs)
        dq = [dot(value, k[pair]) for value, (pair, _) in zip(ds, each)]
        dk = [dot(value, q[pair], TN) for value, (pair, _) in zip(ds, each)]
        for pair in range(pairs):
            mine = slice(pair * per, (pair + 1) * per)
            dself_ref[own[pair], at128(j)] = (halves(dq[mine]) * scale).astype(BF16)
            dself_ref[own[pair], at128(j + groups)] = (halves(dk[mine]) * scale).astype(BF16)
            dself_ref[own[pair], at128(j + 2 * groups)] = halves(dv[mine]).astype(BF16)

    loop(groups, attend_back, 2)

    def self_in_back(i):
        acc[:, at256(i)] = times_back(dself_ref, w, base[3], r_s, g_s, count_s, i)

    loop(r_s // 4, self_in_back, r_s // 4)

    def norm_two_back(i):
        value = norm_back(wide[at_chunk(i), :] + acc[at_chunk(i), :], 1, i, n2, s2)
        wide[at_chunk(i), :] = value
        bback_ref[at_chunk(i), :] = value.astype(BF16)

    loop(steps, norm_two_back, 2 if steps % 2 == 0 else steps)

    def feed_back(i):
        act_grad = dot(bback_ref[...], down_rows(i), NT)
        pback_ref[:, at256(i)] = (act_grad * pre[i]).astype(BF16)

    loop(g_up, feed_back, 4)

    def up_back(i):
        acc[:, at256(i)] = times_back(pback_ref, w, base[1], r_up, g_up, 1, i)

    loop(r_up // 4, up_back, r_up // 4)

    def norm_one_back(i):
        value = norm_back(wide[at_chunk(i), :] + acc[at_chunk(i), :], 0, i, n1, s1)
        resid_ref[at_chunk(i), :] = value
        fback_ref[at_chunk(i), :] = value.astype(BF16)

    loop(steps, norm_one_back, 2 if steps % 2 == 0 else steps)

    def co_out_back(i):
        dctx_ref[:, at256(i)] = times_back(fback_ref, w, base[0], r, g, 1, i).astype(BF16)

    loop(r // 4, co_out_back, r // 4)
    sums_ref[...] = jnp.sum(stat[...], 1)


def middle(begin, lengths, context, x, cot, norms, near, far, span, head, chunk):
    rows, width = x.shape
    hidden = TILES[begin + 1][3] * WIDE
    number = sum(tiles_of(which) for which in range(begin, begin + 5))
    low = lambda columns: jax.ShapeDtypeStruct((rows, columns), BF16)
    return pl.pallas_call(
        functools.partial(middle_body, (begin, rows, span, head, chunk)),
        in_specs=[pl.BlockSpec(memory_space=pltpu.SMEM)] + whole(4) + [pl.BlockSpec(memory_space=pl.ANY)] * 2,
        out_specs=whole(13),
        out_shape=[
            low(width), low(width), low(hidden), low(width), low(width),
            low(width), low(hidden), low(width), low(3 * width), low(width),
            jax.ShapeDtypeStruct((rows, width), F32), low(BI),
            jax.ShapeDtypeStruct((6, width), F32),
        ],
        scratch_shapes=[
            pltpu.VMEM((number, SUB, WIDE), BF16),
            pltpu.SemaphoreType.DMA((24,)),
            pltpu.VMEM((hidden // WIDE, rows, WIDE), F32),
        ]
        + [pltpu.VMEM((rows, width), F32)] * 3
        + [pltpu.VMEM((rows, 128), F32)] * 3
        + [pltpu.VMEM((rows, width), F32)] * 2
        + [
            pltpu.VMEM((rows, 3 * width), BF16),
            pltpu.VMEM((rows // span * (width // head), span, span), F32),
            pltpu.VMEM((6, 8, width), F32),
        ],
        compiler_params=params(),
        cost_estimate=cost(40),
    )(lengths, context, x, cot, norms, near, far)


def weight_body(kinds, *refs):
    n = len(kinds)
    lefts, rights = refs[:n], refs[n : 2 * n]
    out, stage, across, sems = refs[2 * n :]
    offset = 0
    for which, a_ref, b_ref in zip(kinds, lefts, rights):
        _, count, r, g = TILES[which]
        size = 4 * g

        def copy(i, slot, offset=offset, size=size):
            return pltpu.make_async_copy(
                stage.at[slot, pl.ds(0, size)], out.at[pl.ds(offset + i * size, size)], sems.at[slot]
            )

        total = count * (r // 4)

        def step(i, carry, a_ref=a_ref, b_ref=b_ref, r=r, g=g, copy=copy):
            slot = lax.rem(i, 4)

            @pl.when(i >= 4)
            def _():
                copy(i - 4, slot).wait()

            part = i // (r // 4)
            r4 = lax.rem(i, r // 4)
            across[...] = jnp.transpose(a_ref[:, at256(r4)])
            left = across[...]
            for first in range(0, g, 4 if g % 4 == 0 else 3):
                columns = range(first, first + (4 if g % 4 == 0 else 3))
                made = [dot(left, b_ref[:, at256(part * g + col)]).astype(BF16) for col in columns]
                for col, value in zip(columns, made):
                    for a in range(4):
                        stage[slot, a * g + col] = value[a * SUB : (a + 1) * SUB]
            copy(i, slot).start()
            return carry

        lax.fori_loop(0, total, step, 0, unroll=2 if total % 2 == 0 else 3)
        for i in range(max(0, total - 4), total):
            copy(i, i % 4).wait()
        offset += count * r * g


def weight_grads(kinds, lefts, rights):
    number = sum(tiles_of(which) for which in kinds)
    most = max(4 * TILES[which][3] for which in kinds)
    return pl.pallas_call(
        functools.partial(weight_body, kinds),
        in_specs=whole(2 * len(kinds)),
        out_specs=pl.BlockSpec(memory_space=pl.ANY),
        out_shape=jax.ShapeDtypeStruct((number, SUB, WIDE), BF16),
        scratch_shapes=[
            pltpu.VMEM((4, most, SUB, WIDE), BF16),
            pltpu.VMEM((WIDE, lefts[0].shape[0]), BF16),
            pltpu.SemaphoreType.DMA((4,)),
        ],
        compiler_params=params(),
        cost_estimate=cost(number * 0.04),
    )(*lefts, *rights)


def spot():
    dp = lax.axis_index("dp")
    seq = lax.axis_index("seq")
    return dp // 2, dp % 2, seq // 2, seq % 2


def along_z(value, moves):
    return lax.ppermute(value, "dp", [(2 * a + x, 2 * b + x) for a, b in moves for x in (0, 1)])


def cut(value, begin, size):
    return lax.dynamic_slice_in_dim(value, begin, size, 0)


def join(parts):
    return jnp.concatenate(parts) if len(parts) > 1 else parts[0]


def add(left, right):
    return (left.astype(F32) + right.astype(F32)).astype(BF16)


def by_y(y, mine, other):
    return [jnp.where(y == 0, mine, other), jnp.where(y == 0, other, mine)]


def blank(shape):
    return pl.pallas_call(
        lambda out: None,
        out_specs=pl.BlockSpec(memory_space=pl.ANY),
        out_shape=jax.ShapeDtypeStruct(shape, BF16),
        compiler_params=params(),
    )()


def gather_tiles(master_blocks, others):
    z, x, y, core = spot()
    lone, both, half = G_LONE // 2, (G_HALF - 2 * G_LONE) // 2, G_HALF // 2
    fourth = (SHARD - FAR) // 4
    mine = prep(
        master_blocks,
        jnp.concatenate(
            [half * core + lone * y + jnp.arange(lone), half * core + 2 * lone + jnp.arange(both)]
        ).astype(jnp.int32),
    )
    last = prep(
        master_blocks,
        ((FAR + fourth * lax.axis_index("seq")) // 2 + jnp.arange(fourth // 2)).astype(jnp.int32),
    )
    far = lax.all_gather(last, ("dp", "seq"), axis=0, tiled=True)
    ring = [(0, 1), (1, 2), (2, 3), (3, 0)]
    near = blank((8, 2 * G_HALF, SUB, WIDE))
    rows = [mine]
    cross = []
    halves = []
    for phase in range(6):
        out = {}
        if phase < 3:
            out["z"] = along_z(rows[phase], ring)
        if phase < 4:
            out["x"] = lax.ppermute(rows[phase], "dp", SWAP_X)
        if 1 <= phase < 5:
            here = [rows[phase - 1], cross[phase - 1]]
            out["y"] = lax.ppermute(join([part[:G_LONE] for part in here]), "seq", SWAP_Y)
        if phase >= 2:
            out["core"] = lax.ppermute(join(halves[phase - 2]), "seq", SWAP_CORE)
        out, rows, cross, halves, near, others = lax.optimization_barrier(
            (out, rows, cross, halves, near, others)
        )
        if "z" in out:
            rows = rows + [out["z"]]
        if "x" in out:
            cross = cross + [out["x"]]
        if "y" in out:
            halves = halves + [
                [
                    join(by_y(y, part[:G_LONE], out["y"][G_LONE * i : G_LONE * (i + 1)]) + [part[G_LONE:]])
                    for i, part in enumerate(here)
                ]
            ]
        if "core" in out:
            step = phase - 2
            for side in range(2):
                owner = 2 * ((z - step) % 4) + (x + side) % 2
                own = halves[step][side][None]
                got = out["core"][None, G_HALF * side : G_HALF * (side + 1)]
                near = lax.dynamic_update_slice(near, own, (owner, G_HALF * core, 0, 0))
                near = lax.dynamic_update_slice(near, got, (owner, G_HALF * (1 - core), 0, 0))
    return near.reshape(-1, SUB, WIDE), far, others


ROUTES = (
    (((3, 2),), ((2, 1),), ((1, 0),)),
    (((3, 2), (0, 1)), ((2, 1),)),
    (((0, 1), (3, 2)), ((1, 2),)),
    (((0, 1),), ((1, 2),), ((2, 3),)),
)
LONE = R_LONE // CHUNKS
BOTH = R_BOTH // CHUNKS
GROUP_ORDER = [[0, 2, 1, 3]]


def lone_at(core):
    return 2 * R_LONE * core


def both_at(core):
    return 4 * R_LONE + (SHARD - 4 * R_LONE - R_BOTH) * core


def chunk_pairs(k):
    table = []
    for core in range(2):
        for y in range(2):
            table += [(lone_at(core) + R_LONE * y + LONE * k) // 2 + i for i in range(LONE // 2)]
        table += [(both_at(core) + BOTH * k) // 2 + i for i in range(BOTH // 2)]
    return jnp.asarray(table, jnp.int32)


def pieces_of(owner, ranges, begins):
    pieces = []
    at = 0
    for begin, size in ranges:
        first, last = SHARD * owner + begin, SHARD * owner + begin + size
        for which, (lo, hi) in enumerate(begins):
            start, end = max(first, lo), min(last, hi)
            if start < end:
                pieces.append((which, start - lo, end - start, at + start - first))
        at += size
    return pieces


def half_plan(owner, begins, other):
    return [
        pieces_of(owner, ((lone_at(core ^ other), 2 * R_LONE), (both_at(core ^ other), R_BOTH)), begins)
        for core in range(2)
    ]


def both_plan(owner, begins, other):
    plan = []
    for core in range(2):
        pieces = []
        for i in range(2):
            for which, begin, size, at in pieces_of(owner + i, ((both_at(core ^ other), R_BOTH),), begins):
                pieces.append((which, begin, size, at + R_BOTH * i))
        plan.append(pieces)
    return plan


def follow(core_ref, plans, arrays, outs, sems):
    for core in range(2):

        @pl.when(core_ref[0] == core)
        def _(core=core):
            copies = []
            for j, plan in enumerate(plans):
                for i, (which, begin, size, at) in enumerate(plan[core]):
                    copies.append(
                        pltpu.make_async_copy(
                            arrays[which].at[pl.ds(begin, size)], outs[j].at[pl.ds(at, size)], sems.at[j, i]
                        )
                    )
            for copy in copies:
                copy.start()
            for copy in copies:
                copy.wait()


def pick_body(plans, number, core_ref, *refs):
    follow(core_ref, plans, refs[:number], refs[number:-1], refs[-1])


def pick(core, sources, plans, sizes):
    arrays = [array for _, array in sources]
    return pl.pallas_call(
        functools.partial(pick_body, plans, len(arrays)),
        in_specs=[pl.BlockSpec(memory_space=pltpu.SMEM)] + [pl.BlockSpec(memory_space=pl.ANY)] * len(arrays),
        out_specs=whole(len(plans)),
        out_shape=[jax.ShapeDtypeStruct((size, SUB, WIDE), BF16) for size in sizes],
        scratch_shapes=[pltpu.SemaphoreType.DMA((len(plans), 6))],
        compiler_params=params(),
        cost_estimate=cost(2 * len(plans)),
    )(core.reshape(1), *arrays)


def begins_of(sources):
    return [(begin, begin + array.shape[0]) for begin, array in sources]


def merge_body(plans, number, core_ref, *refs):
    arrays, got = refs[:number], refs[number : number + 2]
    outs = refs[number + 2 : -2]
    own, sems = refs[-2:]
    follow(core_ref, plans, arrays, [own.at[0], own.at[1]], sems)

    def total(out, size, i, begin):
        def tile(t, carry):
            out[t] = add(own[i, begin + t], got[i][begin + t])
            return carry

        lax.fori_loop(0, size, tile, 0, unroll=4)

    for k in range(CHUNKS):
        for i in range(2):
            for y in range(2):
                total(outs[2 * k].at[y, i], LONE, i, R_LONE * y + LONE * k)
            total(outs[2 * k + 1].at[i], BOTH, i, 2 * R_LONE + BOTH * k)


def merge(core, sources, zi, got, chunks):
    arrays = [array for _, array in sources]
    plans = [half_plan(2 * zi + i, begins_of(sources), 0) for i in range(2)]
    shapes = []
    for _ in range(CHUNKS):
        shapes += [(2, 2, LONE, SUB, WIDE), (2, BOTH, SUB, WIDE)]
    made = pl.pallas_call(
        functools.partial(merge_body, plans, len(arrays)),
        in_specs=[pl.BlockSpec(memory_space=pltpu.SMEM)]
        + [pl.BlockSpec(memory_space=pl.ANY)] * len(arrays)
        + whole(2),
        out_specs=whole(len(shapes)),
        out_shape=[jax.ShapeDtypeStruct(shape, BF16) for shape in shapes],
        scratch_shapes=[
            pltpu.VMEM((2, R_HALF, SUB, WIDE), BF16),
            pltpu.SemaphoreType.DMA((2, 6)),
        ],
        compiler_params=params(),
        cost_estimate=cost(8),
    )(core.reshape(1), *arrays, *got)
    for k, chunk in enumerate(chunks):
        chunk.state["lone", zi], chunk.state["both", zi] = made[2 * k : 2 * k + 2]


def arrange_body(pieces, x_any, o_any, held, sems):
    arrivals = []
    at = 0
    for i, (begin, size) in enumerate(pieces):
        spot_of = pl.ds(at, size)
        arrivals.append(
            (
                pltpu.make_async_copy(x_any.at[pl.ds(begin, size)], held.at[spot_of], sems.at[0, i]),
                pltpu.make_async_copy(held.at[spot_of], o_any.at[spot_of], sems.at[1, i]),
            )
        )
        arrivals[-1][0].start()
        at += size
    for came, goes in arrivals:
        came.wait()
        goes.start()
    for _, goes in arrivals:
        goes.wait()


def arrange(array, pieces):
    number = sum(size for _, size in pieces)
    return pl.pallas_call(
        functools.partial(arrange_body, pieces),
        in_specs=[pl.BlockSpec(memory_space=pl.ANY)],
        out_specs=pl.BlockSpec(memory_space=pl.ANY),
        out_shape=jax.ShapeDtypeStruct((number, SUB, WIDE), BF16),
        scratch_shapes=[
            pltpu.VMEM((number, SUB, WIDE), BF16),
            pltpu.SemaphoreType.DMA((2, len(pieces))),
        ],
        compiler_params=params(),
        cost_estimate=cost(6),
    )(array)


def group_lone(array, offset):
    pieces = tuple(
        (offset + SHARD * o + R_LONE * part, R_LONE) for part in range(4) for o in range(2)
    )
    made = lax.psum_scatter(
        arrange(array, pieces), "seq", scatter_dimension=0, tiled=True, axis_index_groups=GROUP_ORDER
    )
    return made.reshape(2, R_LONE, SUB, WIDE)


def chunks_of(lone, both):
    return [
        (lone[:, LONE * k : LONE * (k + 1)], both[:, BOTH * k : BOTH * (k + 1)]) for k in range(CHUNKS)
    ]


class Sums:
    def __init__(self):
        self.at = spot()
        self.state = {}

    def send(self, task):
        z, x, y, core = self.at
        state = self.state
        kind, who = task[0], task[1]
        if kind == "Y":
            return lax.ppermute(cut(state["lone", who], 1 - y, 1)[0], "seq", SWAP_Y)
        if kind == "X":
            lone, both = state["kept", who]
            return lax.ppermute(join([cut(lone, 1 - x, 1)[0], cut(both, 1 - x, 1)[0]]), "dp", SWAP_X)
        if kind == "Z":
            return along_z(state["value", who], ROUTES[who][task[2]])
        if kind == "F":
            values = [state["value", zi] for zi in range(4)]
            mine = jnp.where(z == 0, values[0], jnp.where(z == 1, values[1], jnp.where(z == 2, values[2], values[3])))
            state["mine", 0] = mine
            return lax.ppermute(mine, "seq", SWAP_Y)
        if kind == "G":
            return lax.ppermute(state["whole", 0], "seq", SWAP_CORE)
        axis, step = (("seq", 1), ("seq", 2), ("dp", 1), ("dp", 2), ("dp", 4))[who]
        size = lax.axis_size(axis)
        return lax.ppermute(state["norms", 0], axis, [(i, i ^ step) for i in range(size)])

    def take(self, task, got):
        z, x, y, core = self.at
        state = self.state
        kind, who = task[0], task[1]
        if kind == "Y":
            state["kept", who] = (add(cut(state.pop(("lone", who)), y, 1)[0], got), state.pop(("both", who)))
        elif kind == "X":
            lone, both = state.pop(("kept", who))
            state["value", who] = add(join([cut(lone, x, 1)[0], cut(both, x, 1)[0]]), got)
        elif kind == "Z":
            state["value", who] = add(state["value", who], got)
        elif kind == "F":
            mine = state.pop(("mine", 0))
            state["whole", 0] = join(by_y(y, mine[:LONE], got[:LONE]) + [add(mine[LONE:], got[LONE:])])
        elif kind == "G":
            half = state.pop(("whole", 0))
            state["owned", 0] = join([jnp.where(core == 0, half, got), jnp.where(core == 0, got, half)])
        else:
            state["norms", 0] = state["norms", 0] + got

    def step(self, tasks):
        out = [self.send(task) for task in tasks]
        out, self.state = lax.optimization_barrier((out, self.state))
        for task, got in zip(tasks, out):
            self.take(task, got)


def beside(chunks, tasks, work):
    out = [chunks[k].send(task) for k, task in tasks]
    made = work()
    out, made, states = lax.optimization_barrier((out, made, [chunk.state for chunk in chunks]))
    for chunk, state in zip(chunks, states):
        chunk.state = state
    for (k, task), got in zip(tasks, out):
        chunks[k].take(task, got)
    return made


def pad_regions(value, pairs):
    reg = value.shape[0] // pairs
    cube = value.reshape(pairs, reg, value.shape[1])
    return jnp.pad(cube, ((0, 0), (0, VIS_PAD - reg), (0, 0))).reshape(pairs * VIS_PAD, -1)


def cut_regions(value, pairs, reg):
    return value.reshape(pairs, VIS_PAD, -1)[:, :reg].reshape(pairs * reg, -1)


def fast_shards(
    x_text, x_vis, caption_len, cot_text, cot_vis, master_blocks,
    stat_left, stat_right, root_left, root_right, norm_params, norm_second,
):
    pairs = caption_len.shape[0]
    reg = x_vis.shape[0] // pairs
    xv = pad_regions(x_vis, pairs)
    cv = pad_regions(cot_vis, pairs)
    near, far, (xv, cv) = gather_tiles(master_blocks, (xv, cv))
    lengths = jnp.concatenate([caption_len, jnp.full((2,), reg, jnp.int32)])
    regions = jnp.full((2,), reg, jnp.int32)
    vis_norms = norm_params[:, : 3 * VIS].reshape(2, 3, VIS)
    text_norms = norm_params[:, 3 * VIS :].reshape(2, 3, TXT)
    co_vis, co_text, vis_ctx, text_ctx = co_forward(lengths, xv, x_text, near, far)
    (out_vis, v_first, v_act, v_second, v_sctx, v_fback, v_pback, v_bback, v_dself, v_tback,
     v_resid, v_dctx, v_sums) = middle(1, regions, vis_ctx, xv, cv, vis_norms, near, far, VIS_PAD, HEAD_V, 32)
    vis_mid = weight_grads(
        (1, 2, 3, 4, 5), (vis_ctx, v_first, v_act, v_second, v_sctx),
        (v_fback, v_pback, v_bback, v_dself, v_tback),
    )
    _, _, _, core = spot()
    chunks = [Sums() for _ in range(CHUNKS)]
    vis_at, text_at = TILES[1][0], TILES[7][0]
    vis_pair, text_pair = (vis_mid, 2 * SHARD - vis_at), 6 * SHARD - text_at
    lone = group_lone(*vis_pair)
    vis_source = (vis_at, vis_mid)

    def pick_both(source, owner):
        begins = begins_of([source])
        plans = [both_plan(owner, begins, 1), both_plan(owner, begins, 0)]
        send, own = pick(core, [source], plans, [2 * R_BOTH] * 2)
        return own, lax.ppermute(send, "seq", SWAP_CORE)

    def both_sum(own, got):
        return add(own, got).reshape(2, R_BOTH, SUB, WIDE)

    own_both, far_both = pick_both(vis_source, 2)
    (out_text, t_first, t_act, t_second, t_sctx, t_fback, t_pback, t_bback, t_dself, t_tback,
     t_resid, t_dctx, t_sums) = middle(
        7, lengths, text_ctx, x_text, cot_text, text_norms, near, far, x_text.shape[0] // pairs, HEAD_T, 32
    )
    chunks[0].state["norms", 0] = jnp.concatenate([v_sums.reshape(2, -1), t_sums.reshape(2, -1)], 1)
    lefts = (text_ctx, t_first, t_act, t_second, t_sctx)
    rights = (t_fback, t_pback, t_bback, t_dself, t_tback)
    lefts, rights, far_both = lax.optimization_barrier((lefts, rights, far_both))
    text_mid = weight_grads((7, 8, 9, 10, 11), lefts, rights)
    text_source = (text_at, text_mid)
    both = both_sum(own_both, far_both)
    own_both, far_both = pick_both(text_source, 6)
    back = (co_vis, co_text, v_dctx, t_dctx, v_resid, t_resid)
    back, both, text_mid = lax.optimization_barrier((back, both, text_mid))
    for k, kept in enumerate(chunks_of(lone, both)):
        chunks[k].state["kept", 1] = kept
    lone = group_lone(text_mid, text_pair)
    def swap_halves(sources, owners):
        plans = [half_plan(o, begins_of(sources), 1) for o in owners]
        return [
            lax.ppermute(part, "seq", SWAP_CORE) for part in pick(core, sources, plans, [R_HALF] * len(owners))
        ]

    dco_vis, dco_text, grad_vis, grad_text, far_both, far_half = beside(
        chunks,
        [(0, ("X", 1)), (0, ("N", 0))],
        lambda: (*co_backward(lengths, *back, near, far), far_both, swap_halves([text_source], (5,))[0]),
    )
    early_sources = [None, vis_source]
    late_sources = [vis_source, None, text_source]

    def co_grads():
        text_co = weight_grads((6,), (x_text,), (dco_text,))
        late_sources[1] = (TILES[6][0], text_co)
        far_parts.append(swap_halves(late_sources, (4,))[0])
        early_sources[0] = (0, weight_grads((0,), (xv,), (dco_vis,)))
        return text_co

    far_parts = []
    beside(
        chunks, [(1, ("X", 1)), (0, ("Z", 1, 0)), (0, ("N", 1))], co_grads
    )
    def merge_late():
        merge(core, late_sources, 2, [far_parts[0], far_half], chunks)
        return swap_halves(early_sources, (0, 1))

    got = beside(chunks, [(0, ("Z", 1, 1)), (1, ("Z", 1, 0))], merge_late)
    for k, kept in enumerate(chunks_of(lone, both_sum(own_both, far_both))):
        chunks[k].state["kept", 3] = kept
    beside(
        chunks,
        [(0, ("Y", 2)), (0, ("X", 3)), (1, ("Z", 1, 1))],
        lambda: merge(core, early_sources, 0, got, chunks),
    )
    beside(chunks, [(0, ("Y", 0)), (0, ("X", 2)), (0, ("Z", 3, 0)), (0, ("N", 2))], lambda: ())
    chunks[1].step([("Y", 2), ("X", 3)])
    chunks[0].step([("X", 0), ("Z", 2, 0), ("Z", 3, 1), ("N", 3)])
    chunks[1].step([("Y", 0), ("X", 2), ("Z", 3, 0)])
    chunks[0].step([("Z", 0, 0), ("Z", 2, 1), ("Z", 3, 2), ("N", 4)])
    chunks[1].step([("X", 0), ("Z", 2, 0), ("Z", 3, 1)])
    chunks[0].step([("Z", 0, 1)])
    chunks[1].step([("Z", 0, 0), ("Z", 2, 1), ("Z", 3, 2)])
    chunks[0].step([("Z", 0, 2)])
    chunks[1].step([("Z", 0, 1)])
    chunks[0].step([("F", 0)])
    chunks[0].step([("G", 0)])
    statistics = (master_blocks, stat_left, stat_right, root_left, root_right)
    early = chunk_pairs(0)
    count = early.shape[0] // 2
    owned = chunks[0].state["owned", 0]
    renewed = beside(
        chunks, [(1, ("Z", 0, 2))], lambda: renew(early[:count], owned[: 2 * count], *statistics, ())
    )
    renewed = beside(
        chunks, [(1, ("F", 0))], lambda: renew(early[count:], owned[2 * count :], *statistics, renewed)
    )
    chunks[1].step([("G", 0)])
    grad_blocks, left_new, right_new, master_new = renew(
        chunk_pairs(1), chunks[1].state["owned", 0], *statistics, renewed
    )
    norm_grads = chunks[0].state["norms", 0]
    second_new = STAT_DECAY * norm_second + (1.0 - STAT_DECAY) * norm_grads * norm_grads
    norm_new = norm_params - NORM_RATE * norm_grads / (jnp.sqrt(second_new) + MOMENT_EPSILON)
    return (
        out_text,
        cut_regions(out_vis, pairs, reg),
        grad_text,
        cut_regions(grad_vis, pairs, reg),
        grad_blocks,
        left_new,
        right_new,
        master_new,
        norm_grads,
        second_new,
        norm_new,
    )


def fits(mesh):
    return mesh.shape["dp"] == 8 and mesh.shape["seq"] == 4


def solution(mesh):
    placed = (
        P(("dp", "seq"), None),
        P(("dp", "seq"), None),
        P(("dp", "seq")),
        P(("dp", "seq"), None),
        P(("dp", "seq"), None),
        P("dp", None),
        P("dp", None),
        P("dp", None),
        P("dp", None),
        P("dp", None),
        P(),
        P(),
    )
    step = fast_shards if fits(mesh) else shards
    return jax.shard_map(
        step,
        mesh=mesh,
        in_specs=placed,
        out_specs=(
            P(("dp", "seq"), None),
            P(("dp", "seq"), None),
            P(("dp", "seq"), None),
            P(("dp", "seq"), None),
            P("dp", None),
            P("dp", None),
            P("dp", None),
            P("dp", None),
            P(),
            P(),
            P(),
        ),
        check_vma=False,
    )
```
